128 devices in a mesh: shard: 8 (over x, y_lo), ctx: 2 (over y_hi), tp: 8 (over z, core).
Axes of the slice: x: 4, y: 4 (y_hi: 2, y_lo: 2; y = y_hi * 2 + y_lo), z: 4, core: 2. Of those that a mesh axis runs over, the one named last changes fastest.
Arguments:
- tokens: bfloat16 [8, 1024, 2048], P('shard', 'ctx'), may hold values from -6 to 6
- out_grad: bfloat16 [8, 1024, 2048], P('shard', 'ctx'), may hold values from -6 to 6
- segments: int32 [8, 1024], P('shard'), may hold values from 0 to 4, as said below
- routes: int32 [8, 1024, 8], P('shard', 'ctx'), may hold values from 0 to 15, all different within a row; in each aligned block of 512 rows (0 to 511, 512 to 1023, ..., all dimensions but the last counted through in order) at most 288 rows name the same one
- query_weight: bfloat16 [2048, 2048], P('shard', 'tp'), may hold values from -0.125 to 0.125
- key_weight: bfloat16 [2048, 2048], P('shard', 'tp'), may hold values from -0.125 to 0.125
- value_weight: bfloat16 [2048, 2048], P('shard', 'tp'), may hold values from -0.125 to 0.125
- out_weight: bfloat16 [2048, 2048], P('tp', 'shard'), may hold values from -0.5 to 0.5
- router_weight: bfloat16 [2048, 16], P('shard'), may hold values from -0.0625 to 0.0625
- attn_gain: bfloat16 [2048], P('shard'), may hold values from 0.099609375 to 1.8984375
- moe_gain: bfloat16 [2048], P('shard'), may hold values from 0.099609375 to 1.8984375
- query_gain: bfloat16 [16, 128], P('tp', 'shard'), may hold values from 0.099609375 to 1.8984375
- key_gain: bfloat16 [16, 128], P('tp', 'shard'), may hold values from 0.099609375 to 1.8984375
- gate_weight: bfloat16 [16, 2048, 1024], P(None, 'shard', 'tp'), may hold values from -0.125 to 0.125
- up_weight: bfloat16 [16, 2048, 1024], P(None, 'shard', 'tp'), may hold values from -0.125 to 0.125
- down_weight: bfloat16 [16, 1024, 2048], P(None, 'tp', 'shard'), may hold values from -0.75 to 0.75
Outputs:
- layer_out: bfloat16 [8, 1024, 2048], P('shard', 'ctx')
- input_grad: bfloat16 [8, 1024, 2048], P('shard', 'ctx')
- query_weight_grad: float32 [2048, 2048], P('shard', 'tp')
- key_weight_grad: float32 [2048, 2048], P('shard', 'tp')
- value_weight_grad: float32 [2048, 2048], P('shard', 'tp')
- out_weight_grad: float32 [2048, 2048], P('tp', 'shard')
- router_weight_grad: float32 [2048, 16], P('shard')
- attn_gain_grad: float32 [2048], P('shard')
- moe_gain_grad: float32 [2048], P('shard')
- query_gain_grad: float32 [16, 128], P('tp', 'shard')
- key_gain_grad: float32 [16, 128], P('tp', 'shard')
- gate_weight_grad: float32 [16, 2048, 1024], P(None, 'shard', 'tp')
- up_weight_grad: float32 [16, 2048, 1024], P(None, 'shard', 'tp')
- down_weight_grad: float32 [16, 1024, 2048], P(None, 'tp', 'shard')
The draws below stay inside these ranges and needn't reach their ends.
Inputs may be any that keep to these rules, and one draw needn't show every extreme that they name: `segments`: segment numbers start at 0, never fall along a sequence and rise by one from document to document; every sequence holds exactly five documents, one of them exactly 768 positions long, the other four sharing the remaining 1024 - 768 positions, each at least one eighth of them. `routes`: each token names 8 different experts; within the 512 positions of one block of one sequence no expert is named by more than 288 tokens, and in some blocks one expert is named by exactly 288.
All inputs are finite; a program needn't handle non-finite values.
Results may differ from the reference program's by a relative error of at most 0.035.
Values may be sent and summed in bfloat16 or wider, within the bound.
A program may use at most 384 MiB of HBM per device.

```python
import math
import jax
import jax.numpy as jnp
import numpy as np
from jax import lax

D = 2048
HEADS = 16
HD = 128
FF = 1024
EXPERTS = 16
TOP = 8
LEN = 1024
SEQS = 8
BLK = 512
CAP = 288
SEG_MOST = 768


def draw_segments(key, part):
    key = jax.random.fold_in(key, 11)
    key_weights, key_place = jax.random.split(key)
    remaining = LEN - SEG_MOST
    least_len = remaining // 8
    spare = remaining - 4 * least_len
    weights = jnp.left_shift(jnp.ones((SEQS, 4), jnp.int32), jax.random.randint(key_weights, (SEQS, 4), 0, 5))
    total = jnp.sum(weights, axis=1, keepdims=True)
    shares = spare * weights // total
    leftover = spare - jnp.sum(shares, axis=1, keepdims=True)
    last_col = (jnp.arange(4, dtype=jnp.int32)[None, :] == 3).astype(jnp.int32)
    small_lens = least_len + shares + leftover * last_col
    place = jax.random.randint(key_place, (SEQS, 1), 0, 5)
    slots = jnp.arange(5, dtype=jnp.int32)[None, :]
    index = jnp.clip(slots - (slots > place).astype(jnp.int32), 0, 3)
    doc_lens = jnp.where(slots == place, SEG_MOST, jnp.take_along_axis(small_lens, jnp.broadcast_to(index, (SEQS, 5)), axis=1))
    ends = jnp.cumsum(doc_lens, axis=1).astype(jnp.int32)
    places = jnp.arange(LEN, dtype=jnp.int32)[None, :, None]
    return jnp.sum((places >= ends[:, None, :4]).astype(jnp.int32), axis=-1).astype(jnp.int32)


def levels(rng, extent, pieces, low, high):
    gain = 1.0
    for dim, parts in pieces:
        draws = jax.random.uniform(jax.random.fold_in(jax.random.fold_in(rng, 6), dim), (parts,), jnp.float32, low / len(pieces), high / len(pieces))
        gain = gain * jnp.repeat(jnp.exp(draws), extent[dim] // parts).reshape((-1,) + (1,) * (len(extent) - 1 - dim))
    return gain


def shared_out(stream_key, own, number, rows, count, top, reach, slope):
    sequence = jax.random.permutation(stream_key, count)
    heavy_load, common = portions_of(count, rows * top, reach, slope, True), portions_of(count, rows * top, reach, slope, False)
    places = jnp.arange(count)

    def named(lengths, turn):
        used = int((lengths > 0).sum())
        fixed = max(1, used // 4)
        passed = fixed + (places - fixed + turn * (used - fixed)) % max(1, count - fixed)
        return jnp.zeros((count,), jnp.int32).at[sequence[jnp.where(places < fixed, places, passed)]].set(jnp.asarray(lengths, jnp.int32))

    lengths = jnp.where(number % 4 == 0, named(heavy_load, number // 4), named(common, number - number // 4 - 1))
    mixed = jax.random.permutation(jax.random.fold_in(own, 3), count)
    source_of, taker = mixed[0:count // 2 * 2:2], mixed[1:count // 2 * 2:2]
    room = jnp.minimum(lengths[source_of] - 1, reach - lengths[taker]) // 2
    room = jnp.where((source_of == sequence[0]) | (taker == sequence[0]) | (lengths[taker] == 0), 0, jnp.maximum(room, 0))
    passed = jax.random.randint(jax.random.fold_in(own, 4), (count // 2,), 0, 1 << 20) % (room + 1)
    lengths = lengths.at[source_of].add(-passed).at[taker].add(passed)
    members = jnp.searchsorted(jnp.cumsum(lengths), jnp.arange(rows * top), side="right").astype(jnp.int32)
    grid = members.reshape(top, rows).T
    grid = grid[jax.random.permutation(jax.random.fold_in(own, 1), rows)]
    turn = jax.random.randint(jax.random.fold_in(own, 2), (rows, 1), 0, top)
    return jnp.take_along_axis(grid, (jnp.arange(top)[None, :] + turn) % top, axis=1)


def portions_of(amount, total, limit, skew, full):
    portions = [(1 << 20) // math.isqrt(grade ** skew) + 1 for grade in range(1, amount + 1)]
    largest = limit if full else min(limit, max(-(-total // amount), total * portions[0] // sum(portions)))
    least = 1 if total - largest >= amount - 1 else 0
    holding, spare = [largest] + [least] * (amount - 1), total - largest - least * (amount - 1)
    while spare > 0:
        candidates = [i for i in range(1, amount) if holding[i] < largest] or [i for i in range(1, amount) if holding[i] < limit]
        mass, left = sum([portions[i] for i in candidates]), spare
        for i in candidates:
            addition = min(limit - holding[i], max(1, left * portions[i] // mass), spare)
            holding[i] = holding[i] + addition
            spare = spare - addition
    return np.array(holding)


def normal_values(rng, shape, deviation, most, pieces=(), kind=jnp.bfloat16):
    values = deviation * jax.random.normal(rng, shape, jnp.float32)
    if pieces:
        values = values * levels(rng, shape, pieces, -0.22, 0.18)
    return jnp.clip(values, -most, most).astype(kind)


def setup_inputs(seed: int = 0) -> dict:
    splits = jax.random.split(jax.random.key(seed), 17)
    tokens = normal_values(splits[0], (SEQS, LEN, D), 1.0, 6.0, ((0, 8), (1, 2)))
    out_grad = normal_values(splits[1], (SEQS, LEN, D), 1.0, 6.0, ((0, 8), (1, 2)))
    segments = draw_segments(jax.random.fold_in(splits[16], 71), 0)
    routes_keys = jax.random.split(jax.random.fold_in(splits[3], 1), SEQS * LEN // BLK)
    routes_turns = jax.random.permutation(jax.random.fold_in(splits[3], 3), SEQS * LEN // BLK)
    routes = jax.vmap(lambda own, number: shared_out(jax.random.fold_in(splits[3], 2), own, number, BLK, EXPERTS, TOP, CAP, 2))(routes_keys, routes_turns).reshape((SEQS, LEN, TOP))
    query_weight = normal_values(splits[4], (D, D), D ** -0.5, 0.125, ((0, 8), (1, 8)))
    key_weight = normal_values(splits[5], (D, D), D ** -0.5, 0.125, ((0, 8), (1, 8)))
    value_weight = normal_values(splits[6], (D, D), D ** -0.5, 0.125, ((0, 8), (1, 8)))
    out_weight = normal_values(splits[7], (D, D), (D // 16) ** -0.5, 0.5, ((0, 8), (1, 8)))
    router_weight = normal_values(splits[8], (D, EXPERTS), (4 * D) ** -0.5, 0.0625, ((0, 8),))
    attn_gain = jnp.clip(1.0 + 0.18 * jax.random.normal(splits[9], (D,), jnp.float32), 0.099609375, 1.8984375).astype(jnp.bfloat16)
    moe_gain = jnp.clip(1.0 + 0.18 * jax.random.normal(splits[10], (D,), jnp.float32), 0.099609375, 1.8984375).astype(jnp.bfloat16)
    query_gain = jnp.clip(1.0 + 0.18 * jax.random.normal(splits[11], (HEADS, HD), jnp.float32), 0.099609375, 1.8984375).astype(jnp.bfloat16)
    key_gain = jnp.clip(1.0 + 0.18 * jax.random.normal(splits[12], (HEADS, HD), jnp.float32), 0.099609375, 1.8984375).astype(jnp.bfloat16)
    gate_weight = normal_values(splits[13], (EXPERTS, D, FF), D ** -0.5, 0.125, ((1, 8), (2, 8)))
    up_weight = normal_values(splits[14], (EXPERTS, D, FF), D ** -0.5, 0.125, ((1, 8), (2, 8)))
    down_weight = normal_values(splits[15], (EXPERTS, FF, D), (FF // 16) ** -0.5, 0.75, ((1, 8), (2, 8)))
    return {"tokens": tokens, "out_grad": out_grad, "segments": segments, "routes": routes, "query_weight": query_weight, "key_weight": key_weight, "value_weight": value_weight, "out_weight": out_weight, "router_weight": router_weight, "attn_gain": attn_gain, "moe_gain": moe_gain, "query_gain": query_gain, "key_gain": key_gain, "gate_weight": gate_weight, "up_weight": up_weight, "down_weight": down_weight}


@jax.custom_vjp
def low(v):
    return lax.optimization_barrier(v.astype(jnp.bfloat16)).astype(jnp.float32)

@jax.custom_vjp
def low_back(v):
    return v

def low_keep(v):
    return (low(v), None)

def low_pass(kept, grad):
    return (grad,)

def back_keep(v):
    return (v, None)

def back_low(kept, grad):
    return (low(grad),)
low.defvjp(low_keep, low_pass)
low_back.defvjp(back_keep, back_low)
EPSILON = 1e-05
ROPE_BASE = 10000.0
PRECISE = lax.Precision.HIGHEST

def product(left, right):
    return jnp.dot(left, right, precision=PRECISE)

def rms_norm(values, gain_row):
    scale_row = lax.rsqrt(lax.optimization_barrier(jnp.mean(values * values, axis=-1, keepdims=True)) + EPSILON)
    return values * scale_row * gain_row

def rope_tables(positions, head_width):
    frequency = ROPE_BASE ** (-(jnp.arange(0, head_width, 2, dtype=jnp.float32) / head_width))
    angles = positions.astype(jnp.float32)[:, None] * frequency[None, :]
    return (jnp.cos(angles), jnp.sin(angles))

def rotate(values, cosine, sine_table):
    half_width = values.shape[-1] // 2
    first_half = values[..., :half_width]
    second_half = values[..., half_width:]
    return jnp.concatenate([first_half * cosine - second_half * sine_table, second_half * cosine + first_half * sine_table], axis=-1)

def sequence_forward(weights, tokens, segment, route):
    query_weight, key_weight, value_weight, out_weight, router_weight, attn_gain, moe_gain, query_gain, key_gain, gate_weight, up_weight, down_weight = weights
    normed = low(rms_norm(tokens, attn_gain))
    query_pre = low_back(product(normed, query_weight)).reshape(LEN, HEADS, HD)
    key_pre = low_back(product(normed, key_weight)).reshape(LEN, HEADS, HD)
    value_heads = low(low_back(product(normed, value_weight))).reshape(LEN, HEADS, HD)
    cosine, sine_table = rope_tables(jnp.arange(LEN), HD)
    cosine = cosine[:, None, :]
    sine_table = sine_table[:, None, :]
    query_rot = low(low_back(rotate(rms_norm(query_pre, query_gain), cosine, sine_table)))
    key_rot = low(low_back(rotate(rms_norm(key_pre, key_gain), cosine, sine_table)))
    scores = low_back(jnp.einsum('qhd,khd->hqk', query_rot, key_rot, precision=PRECISE) * HD ** (-0.5))
    places = jnp.arange(LEN)
    allowed = (places[:, None] >= places[None, :]) & (segment[:, None] == segment[None, :])
    scores = jnp.where(allowed[None], scores, -1e+30)
    attn_probs = jax.nn.softmax(scores, axis=-1)
    mixed_heads = jnp.einsum('hqk,khd->qhd', low(attn_probs), value_heads, precision=PRECISE)
    mixed_heads = low(low_back(mixed_heads)).reshape(LEN, D)
    hidden = tokens + low_back(product(mixed_heads, out_weight))
    moe_in = low(rms_norm(hidden, moe_gain))
    logits = low_back(product(moe_in, router_weight))
    chosen = jnp.take_along_axis(logits, route, axis=1)
    gate_probs = jax.nn.softmax(chosen, axis=1)
    picked = (route[:, :, None] == jnp.arange(EXPERTS)[None, None, :]).astype(jnp.float32)
    dense_gates = jnp.einsum('tk,tke->te', gate_probs, picked, precision=PRECISE)
    gate_pre = low_back(jnp.einsum('td,edf->etf', moe_in, gate_weight, precision=PRECISE))
    up_pre = low_back(jnp.einsum('td,edf->etf', moe_in, up_weight, precision=PRECISE))
    activated = low(jax.nn.silu(gate_pre) * up_pre)
    expert_out = low_back(jnp.einsum('etf,efd->etd', activated, down_weight, precision=PRECISE))
    return hidden + jnp.einsum('te,etd->td', dense_gates, expert_out, precision=PRECISE)

def reference(tokens, out_grad, segments, routes, query_weight, key_weight, value_weight, out_weight, router_weight, attn_gain, moe_gain, query_gain, key_gain, gate_weight, up_weight, down_weight):
    weights = tuple((weight_array.astype(jnp.float32) for weight_array in (query_weight, key_weight, value_weight, out_weight, router_weight, attn_gain, moe_gain, query_gain, key_gain, gate_weight, up_weight, down_weight)))

    def forward(token_values, weight_values):
        checked = jax.checkpoint(sequence_forward)

        def advance(running, sequence_item):
            return (running, checked(weight_values, sequence_item[0], sequence_item[1], sequence_item[2]))
        running, outputs = lax.scan(advance, jnp.zeros((), jnp.float32), (token_values, segments, routes))
        return outputs
    outputs, pullback = jax.vjp(forward, tokens.astype(jnp.float32), weights)
    token_grads, weight_grads = pullback(out_grad.astype(jnp.float32))
    return (outputs.astype(jnp.bfloat16), token_grads.astype(jnp.bfloat16), weight_grads[0], weight_grads[1], weight_grads[2], weight_grads[3], weight_grads[4], weight_grads[5], weight_grads[6], weight_grads[7], weight_grads[8], weight_grads[9], weight_grads[10], weight_grads[11])
```

```python
import jax
import jax.numpy as jnp
from jax import lax
from jax.sharding import PartitionSpec as P

EPSILON = 1e-05
ROPE_BASE = 10000.0
MASKED_SCORE = -1e30
AXES = ("shard", "ctx", "tp")
BF = jnp.bfloat16
F32 = jnp.float32


def place_of(index):
    shard, rest = divmod(index, 16)
    ctx, tp = divmod(rest, 8)
    return shard // 2, ctx * 2 + shard % 2, tp // 2, tp % 2


def index_of(x, y, z, c):
    x, y, z, c = x % 4, y % 4, z % 4, c % 2
    return (x * 2 + y % 2) * 16 + (y // 2) * 8 + z * 2 + c


def hop(value, dx=0, dy=0, dz=0, dc=0, only=None):
    pairs = []
    for index in range(128):
        x, y, z, c = place_of(index)
        if only is None or only(x, y, z, c):
            pairs.append((index, index_of(x + dx, y + dy, z + dz, c + dc)))
    return lax.ppermute(value, AXES, pairs)


def step_of(axis, amount):
    return {"d" + axis: amount}


def halves(value):
    middle = value.shape[0] // 2
    return value[:middle], value[middle:]


def ring_gather(block, axis):
    from_before = hop(block, **step_of(axis, 1))
    from_after = hop(block, **step_of(axis, -1))
    first = hop(halves(from_before)[0], **step_of(axis, 1))
    second = hop(halves(from_after)[1], **step_of(axis, -1))
    return [block, from_after, jnp.concatenate([first, second], axis=0), from_before]


def direct_gather(block, axis):
    return [
        block,
        hop(block, **step_of(axis, -1)),
        hop(block, **step_of(axis, 2)),
        hop(block, **step_of(axis, 1)),
    ]


def in_order(blocks, start):
    whole = jnp.zeros((4,) + blocks[0].shape, blocks[0].dtype)
    for distance, block in enumerate(blocks):
        whole = lax.dynamic_update_index_in_dim(whole, block, (start + distance) % 4, 0)
    return whole


def by_distance(whole, start):
    return [
        lax.dynamic_index_in_dim(whole, (start + distance) % 4, 0, keepdims=False)
        for distance in range(4)
    ]


def added(*values):
    total = values[0].astype(F32)
    for value in values[1:]:
        total = total + value.astype(F32)
    return total


def ring_scatter(chunks, axis):
    far_first, far_second = halves(chunks[2])
    got_first = hop(far_first, **step_of(axis, 1))
    got_second = hop(far_second, **step_of(axis, -1))
    after_first, after_second = halves(chunks[1])
    before_first, before_second = halves(chunks[3])
    to_after = jnp.concatenate([added(after_first, got_first).astype(BF), after_second], axis=0)
    to_before = jnp.concatenate([before_first, added(before_second, got_second).astype(BF)], axis=0)
    from_before = hop(to_after, **step_of(axis, 1))
    from_after = hop(to_before, **step_of(axis, -1))
    return added(chunks[0], from_before, from_after)


def direct_scatter(chunks, axis):
    return added(
        chunks[0],
        hop(chunks[1], **step_of(axis, 1)),
        hop(chunks[2], **step_of(axis, 2)),
        hop(chunks[3], **step_of(axis, -1)),
    )


def with_partner(own, other, number):
    return jnp.where(
        number == 0, jnp.concatenate([own, other], 0), jnp.concatenate([other, own], 0)
    )


def rms_scale(values):
    return lax.rsqrt(jnp.mean(values * values, axis=-1, keepdims=True) + EPSILON)


def norm_back(grad_normed, source, scale_row, gain_row):
    unit_values = source * scale_row
    grad_unit = grad_normed * gain_row
    grad_source = scale_row * (
        grad_unit - unit_values * jnp.mean(grad_unit * unit_values, axis=-1, keepdims=True)
    )
    return (grad_source, grad_normed * unit_values)


def rope_tables(positions, head_width):
    frequency = ROPE_BASE ** (-(jnp.arange(0, head_width, 2, dtype=F32) / head_width))
    angles = positions.astype(F32)[:, None] * frequency[None, :]
    return (jnp.cos(angles), jnp.sin(angles))


def rotate(values, cosine, sine_table):
    half_width = values.shape[-1] // 2
    first_half = values[..., :half_width]
    second_half = values[..., half_width:]
    return jnp.concatenate(
        [
            first_half * cosine - second_half * sine_table,
            second_half * cosine + first_half * sine_table,
        ],
        axis=-1,
    )


def dot(left, right):
    return jnp.dot(left, right, preferred_element_type=F32)


def dot_nt(left, right):
    return lax.dot_general(left, right, (((1,), (1,)), ((), ())), preferred_element_type=F32)


def dot_tn(left, right):
    return lax.dot_general(left, right, (((0,), (0,)), ((), ())), preferred_element_type=F32)


def body(
    tokens,
    out_grad,
    segments,
    routes,
    query_weight,
    key_weight,
    value_weight,
    out_weight,
    router_weight,
    attn_gain,
    moe_gain,
    query_gain,
    key_gain,
    gate_weight,
    up_weight,
    down_weight,
):
    rows, width = tokens.shape[1], tokens.shape[2]
    experts = gate_weight.shape[0]
    own_experts = experts // 4
    hidden_units = gate_weight.shape[2]
    span = own_experts * hidden_units
    shard, ctx, tp = lax.axis_index("shard"), lax.axis_index("ctx"), lax.axis_index("tp")
    x, y_low, z, core = shard // 2, shard % 2, tp // 2, tp % 2
    y = ctx * 2 + y_low
    home = rows // 8
    head_dim = 128
    local_width = 256
    score_scale = head_dim ** (-0.5)

    def spread_rows(part):
        lane = in_order(direct_gather(part, "z"), z).reshape(4 * part.shape[0], -1)
        return with_partner(lane, hop(lane, dc=1), core)

    def gather_tokens(part):
        lane = jnp.concatenate(direct_gather(part, "z"), axis=0)
        near = ring_gather(lane, "y")
        mine = jnp.concatenate(near, axis=0)
        return jnp.concatenate([mine, hop(mine, dc=1)], axis=0)

    def home_sum(terms):
        keep = lax.dynamic_slice_in_dim(terms, core * 256, 256, 0)
        give = lax.dynamic_slice_in_dim(terms, (1 - core) * 256, 256, 0)
        lane = added(keep, hop(give, dc=1)).astype(BF).reshape(4, home, -1)
        return direct_scatter(by_distance(lane, z), "z")

    def tokens_sum(terms):
        half = 2 * rows
        lane = added(terms[:half], hop(terms[half:], dc=1)).astype(BF)
        mine = ring_scatter([lane[256 * k : 256 * k + 256] for k in range(4)], "y").astype(BF)
        return direct_scatter([mine[home * k : home * k + home] for k in range(4)], "z")

    small = jnp.zeros((256, 128), BF)
    small = small.at[:, 0].set(attn_gain).at[:, 1].set(moe_gain)
    head_gains = jnp.stack([query_gain, key_gain]).reshape(-1)
    small = small.at[: head_gains.shape[0], 2].set(head_gains)
    attn_own = jnp.concatenate([query_weight, key_weight, value_weight, small, out_weight.T], axis=1)
    attn_pair = with_partner(
        attn_own,
        jnp.concatenate([hop(attn_own[:128], dy=1), hop(attn_own[128:], dy=-1)], axis=0),
        y_low,
    )
    attn_all = in_order(ring_gather(attn_pair, "x"), x).reshape(width, -1)
    w_stacked = attn_all[:, : 3 * local_width]
    small_all = attn_all[:, 3 * local_width : 3 * local_width + 128]
    w_out_t = attn_all[:, 3 * local_width + 128 :]
    attn_gains = small_all[:, 0].astype(F32)
    moe_gains = small_all[:, 1].astype(F32)
    gains = small_all[:, 2].reshape(8, 256)[:, :64].reshape(8, 2, 2, 16)
    gains = gains.transpose(1, 2, 0, 3).reshape(2, 2 * head_dim).astype(F32)
    query_gains, key_gains = gains[0][None], gains[1][None]

    def grouped(weight):
        parted = weight.reshape(4, own_experts, 256, hidden_units)
        return parted.transpose(0, 2, 1, 3).reshape(4, 256, span)

    router_pad = jnp.pad(router_weight, ((0, 0), (0, 128 - experts)))
    moe_groups = jnp.concatenate(
        [
            grouped(gate_weight),
            grouped(up_weight),
            jnp.broadcast_to(router_pad[None], (4, 256, 128)),
            grouped(down_weight.transpose(0, 2, 1)),
        ],
        axis=2,
    )
    moe_groups, _ = lax.optimization_barrier((moe_groups, attn_pair))
    moe_own, to_after, _, to_before = by_distance(moe_groups, y)
    moe_pair = with_partner(
        moe_own,
        jnp.concatenate([hop(to_after[:128], dy=1), hop(to_before[128:], dy=-1)], axis=0),
        y_low,
    )
    moe_pair, _ = lax.optimization_barrier((moe_pair, attn_all))
    moe_all = in_order(ring_gather(moe_pair, "x"), x).reshape(width, -1)
    w_in = moe_all[:, : 2 * span + 128]
    w_down_t = moe_all[:, 2 * span + 128 :]

    own_grad = out_grad.reshape(rows, width)
    route_rows = routes.reshape(rows, -1)
    own_picked = jnp.any(
        route_rows[:, :, None] == jnp.arange(128, dtype=jnp.int32)[None, None, :], axis=1
    ).astype(BF)

    def lane_rows(whole):
        half = lax.dynamic_slice_in_dim(whole, core * (rows // 2), rows // 2, 0)
        twice = jnp.concatenate([half, half], axis=0)
        return lax.dynamic_slice_in_dim(twice, z * home, rows // 2, 0)

    grad_half, _ = lax.optimization_barrier((lane_rows(own_grad), attn_pair))
    grad_lane = jnp.concatenate(ring_gather(grad_half, "y"), axis=0)
    grad_all = jnp.concatenate([grad_lane, hop(grad_lane, dc=1)], axis=0)
    picked_lane = jnp.concatenate(direct_gather(lane_rows(own_picked), "y"), axis=0)
    picked = jnp.concatenate([picked_lane, hop(picked_lane, dc=1)], axis=0)[:, :experts] > 0

    inputs = tokens.reshape(rows, width).astype(F32)
    scale_one = rms_scale(inputs)
    normed = (inputs * scale_one * attn_gains).astype(BF)
    projected = dot(normed, w_stacked)
    query_pre = [projected[:, h * 128 : h * 128 + 128] for h in range(2)]
    key_pre = [projected[:, 256 + h * 128 : 384 + h * 128] for h in range(2)]
    value_low = projected[:, 512:].astype(BF)
    first_row = ctx * rows
    places = first_row + jnp.arange(rows, dtype=jnp.int32)
    cosine, sine_table = rope_tables(places, head_dim)
    scale_query = [rms_scale(v) for v in query_pre]
    scale_key = [rms_scale(v) for v in key_pre]
    gain_q = [query_gains[:, h * 128 : h * 128 + 128] for h in range(2)]
    gain_k = [key_gains[:, h * 128 : h * 128 + 128] for h in range(2)]
    query_low = [
        rotate(query_pre[h] * scale_query[h] * gain_q[h], cosine, sine_table).astype(BF)
        for h in range(2)
    ]
    key_low = [
        rotate(key_pre[h] * scale_key[h] * gain_k[h], cosine, sine_table).astype(BF)
        for h in range(2)
    ]
    keys_values = jnp.concatenate(key_low + [value_low], axis=1)
    earlier = hop(keys_values, dy=2, only=lambda x, y, z, c: y < 2)
    both = jnp.concatenate([earlier, keys_values], axis=0)
    keys = [both[:, h * 128 : h * 128 + 128] for h in range(2)]
    values = [both[:, 256 + h * 128 : 384 + h * 128] for h in range(2)]
    key_places = first_row - rows + jnp.arange(2 * rows, dtype=jnp.int32)
    own_segments = lax.dynamic_slice_in_dim(segments[0], first_row, rows, 0)
    key_segments = jnp.concatenate([segments[0, :rows], own_segments])
    allowed = (
        (places[:, None] >= key_places[None, :])
        & (key_places[None, :] >= 0)
        & (own_segments[:, None] == key_segments[None, :])
    )
    probs, mixed = [], []
    for h in range(2):
        scores = jnp.where(allowed, dot_nt(query_low[h], keys[h]) * score_scale, MASKED_SCORE)
        exponents = jnp.exp(scores - jnp.max(scores, axis=-1, keepdims=True))
        probs.append(exponents / jnp.sum(exponents, axis=-1, keepdims=True))
        mixed.append(dot(probs[h].astype(BF), values[h]))
    mixed_low = jnp.concatenate(mixed, axis=1).astype(BF)
    attn_part = dot_nt(mixed_low, w_out_t).astype(BF)

    home_row = (core * 4 + z) * home
    home_inputs = lax.dynamic_slice_in_dim(tokens.reshape(rows, width), home_row, home, 0).astype(F32)
    home_scale_one = lax.dynamic_slice_in_dim(scale_one, home_row, home, 0)
    home_grad = lax.dynamic_slice_in_dim(own_grad, home_row, home, 0).astype(F32)
    hidden = home_inputs + home_sum(attn_part)
    scale_two = rms_scale(hidden)
    moe_in = gather_tokens((hidden * scale_two * moe_gains).astype(BF))

    joined = dot(moe_in, w_in)
    logits = jnp.where(picked, joined[:, 2 * span : 2 * span + experts], -jnp.inf)
    gates = jax.nn.softmax(logits, axis=-1)
    own_gates = lax.dynamic_slice_in_dim(gates, y * own_experts, own_experts, 1)
    wide_gates = jnp.repeat(own_gates, hidden_units, axis=1)
    gate_pre, up_pre = joined[:, :span], joined[:, span : 2 * span]
    logistic = jax.nn.sigmoid(gate_pre)
    silu_gate = gate_pre * logistic
    silu_slope = logistic * (1.0 + gate_pre * (1.0 - logistic))
    act = silu_gate * up_pre
    act_back = dot(grad_all, w_down_t)
    gate_terms = jnp.sum(
        (act.astype(BF).astype(F32) * act_back).reshape(-1, own_experts, hidden_units), axis=-1
    )
    gate_grad = lax.dynamic_update_slice_in_dim(
        jnp.zeros_like(gates), gate_terms, y * own_experts, 1
    )
    logit_grad = gates * (gate_grad - jnp.sum(gates * gate_grad, axis=-1, keepdims=True))
    act_grad = act_back * wide_gates
    pre_grad = jnp.concatenate(
        [
            (act_grad * up_pre * silu_slope).astype(BF),
            (act_grad * silu_gate).astype(BF),
            jnp.pad(logit_grad.astype(BF), ((0, 0), (0, 128 - experts))),
        ],
        axis=1,
    )
    gated_act = (act * wide_gates).astype(BF)
    moe_in_part = dot_nt(pre_grad, w_in).astype(BF)
    moe_in_grad = tokens_sum(moe_in_part)
    moe_part = dot_nt(gated_act, w_down_t).astype(BF)
    moe_part, _ = lax.optimization_barrier((moe_part, moe_in_grad))
    layer_rows = (hidden + tokens_sum(moe_part)).astype(BF)
    layer_out = spread_rows(layer_rows).reshape(tokens.shape)
    grad_in = dot_tn(moe_in, pre_grad).astype(BF)
    grad_down_t = dot_tn(grad_all, gated_act).astype(BF)
    grad_in, grad_down_t, _ = lax.optimization_barrier((grad_in, grad_down_t, moe_in_grad))
    grad_moe = ring_scatter(
        [
            jnp.concatenate([a[:, : 2 * span], b], axis=1)
            for a, b in zip(
                by_distance(grad_in.reshape(4, 512, -1), x),
                by_distance(grad_down_t.reshape(4, 512, -1), x),
            )
        ],
        "x",
    ).astype(BF)
    grad_moe = grad_moe.reshape(2, 256, -1)
    keep = lax.dynamic_index_in_dim(grad_moe, y_low, 0, keepdims=False)
    give = lax.dynamic_index_in_dim(grad_moe, 1 - y_low, 0, keepdims=False)
    grad_groups = in_order(
        [keep, hop(give, dy=-1), hop(keep, dy=2), hop(give, dy=1)], y
    )

    def ungrouped(part):
        parted = part.reshape(4, 256, own_experts, hidden_units)
        return parted.transpose(0, 2, 1, 3).reshape(experts, 256, hidden_units).astype(F32)

    grad_gate_weight = ungrouped(grad_groups[:, :, :span])
    grad_up_weight = ungrouped(grad_groups[:, :, span : 2 * span])
    grad_down_weight = (
        grad_groups[:, :, 2 * span :]
        .reshape(4, 256, own_experts, hidden_units)
        .transpose(0, 2, 3, 1)
        .reshape(experts, hidden_units, 256)
        .astype(F32)
    )

    hidden_norm_grad, moe_gain_rows = norm_back(moe_in_grad, hidden, scale_two, moe_gains)
    hidden_grad = home_grad + hidden_norm_grad
    hidden_low = spread_rows(hidden_grad.astype(BF))
    grad_router = grad_in[:, 2 * span : 2 * span + experts]
    early = jnp.concatenate([grad_router.T.astype(F32), jnp.sum(moe_gain_rows, axis=0)[None]], axis=0)
    early = early.reshape(-1, 128)
    early = early + hop(early, dc=1)
    for axis in "zyx":
        early = direct_scatter([early] * 4, axis)
    early = early.reshape(experts + 1, width)
    early = lax.dynamic_slice_in_dim(early, shard * 256, 256, 1)

    mixed_grad = dot(hidden_low, w_out_t).astype(BF)
    grad_out_t = dot_tn(hidden_low, mixed_low)
    query_grads, key_terms, value_terms = [], [], []
    for h in range(2):
        grad_h = mixed_grad[:, h * 128 : h * 128 + 128]
        prob_grad = dot_nt(grad_h, values[h])
        row_delta = jnp.sum(probs[h] * prob_grad, axis=-1, keepdims=True)
        score_grad = (probs[h] * (prob_grad - row_delta)).astype(BF)
        query_grads.append((dot(score_grad, keys[h]) * score_scale).astype(BF).astype(F32))
        key_terms.append(dot_tn(score_grad, query_low[h]) * score_scale)
        value_terms.append(dot_tn(probs[h].astype(BF), grad_h))
    terms = jnp.concatenate(key_terms + value_terms, axis=1)
    later = hop(terms[:rows].astype(BF), dy=2, only=lambda x, y, z, c: y >= 2)
    key_value_grad = added(terms[rows:], later).astype(BF)
    stacked, gain_sums = [], []
    for pre, scale, gain, grads in (
        (query_pre, scale_query, gain_q, query_grads),
        (key_pre, scale_key, gain_k, [key_value_grad[:, :128], key_value_grad[:, 128:256]]),
    ):
        for h in range(2):
            unit_grad = rotate(grads[h].astype(F32), cosine, -sine_table)
            pre_back, gain_rows = norm_back(unit_grad, pre[h], scale[h], gain[h])
            stacked.append(pre_back.astype(BF))
            gain_sums.append(jnp.sum(gain_rows, axis=0))
    stacked = jnp.concatenate(stacked + [key_value_grad[:, 256:]], axis=1)
    normed_part = dot_nt(stacked, w_stacked).astype(BF)
    grad_stacked = dot_tn(normed, stacked)
    normed_grad = home_sum(normed_part)
    input_norm_grad, attn_gain_rows = norm_back(
        normed_grad, home_inputs, home_scale_one, attn_gains
    )
    input_grad = spread_rows((hidden_grad + input_norm_grad).astype(BF)).reshape(tokens.shape)
    grad_attn = jnp.concatenate([grad_stacked, grad_out_t], axis=1).astype(BF)
    grad_attn = ring_scatter(by_distance(grad_attn.reshape(4, 512, -1), x), "x").astype(BF)
    grad_attn = grad_attn.reshape(2, 256, -1)
    keep = lax.dynamic_index_in_dim(grad_attn, y_low, 0, keepdims=False)
    give = lax.dynamic_index_in_dim(grad_attn, 1 - y_low, 0, keepdims=False)
    got = jnp.concatenate([hop(give[:128], dy=1), hop(give[128:], dy=-1)], axis=0)
    keep = added(keep, got).astype(BF)
    grad_attn = added(keep, hop(keep, dy=2))
    head_gain_sums = jnp.stack(gain_sums).reshape(2, 1, 2, 128)
    mine = (jnp.arange(8) == tp).astype(F32)[None, :, None, None]
    late = jnp.concatenate(
        [jnp.sum(attn_gain_rows, axis=0), (mine * head_gain_sums).reshape(-1)]
    ).reshape(48, 128)
    late = late + hop(late, dc=1)
    for axis in "zyx":
        late = direct_scatter([late] * 4, axis)
    grad_attn_gain = lax.dynamic_slice_in_dim(late[:16].reshape(-1), shard * 256, 256, 0)
    late_heads = late[16:].reshape(2, 8, 2, 128)
    late_heads = lax.dynamic_index_in_dim(late_heads, tp, 1, keepdims=False)
    late_heads = lax.dynamic_slice_in_dim(late_heads, shard * 16, 16, 2)
    return (
        layer_out,
        input_grad,
        grad_attn[:, :256],
        grad_attn[:, 256:512],
        grad_attn[:, 512:768],
        grad_attn[:, 768:].T,
        early[:experts].T,
        grad_attn_gain,
        early[experts],
        late_heads[0],
        late_heads[1],
        grad_gate_weight,
        grad_up_weight,
        grad_down_weight,
    )


def solution(mesh):
    return jax.shard_map(
        body,
        mesh=mesh,
        in_specs=(
            P("shard", "ctx", None),
            P("shard", "ctx", None),
            P("shard", None),
            P("shard", "ctx", None),
            P("shard", "tp"),
            P("shard", "tp"),
            P("shard", "tp"),
            P("tp", "shard"),
            P("shard", None),
            P("shard"),
            P("shard"),
            P("tp", "shard"),
            P("tp", "shard"),
            P(None, "shard", "tp"),
            P(None, "shard", "tp"),
            P(None, "tp", "shard"),
        ),
        out_specs=(
            P("shard", "ctx", None),
            P("shard", "ctx", None),
            P("shard", "tp"),
            P("shard", "tp"),
            P("shard", "tp"),
            P("tp", "shard"),
            P("shard", None),
            P("shard"),
            P("shard"),
            P("tp", "shard"),
            P("tp", "shard"),
            P(None, "shard", "tp"),
            P(None, "shard", "tp"),
            P(None, "tp", "shard"),
        ),
        check_vma=False,
    )
```

```python
import jax
import jax.numpy as jnp
import numpy as np
from jax import lax
from jax.experimental import pallas as pl
from jax.experimental.pallas import tpu as pltpu
from jax.sharding import PartitionSpec as P

EPSILON = 1e-05
ROPE_BASE = 10000.0
MASKED_SCORE = -1e30
AXES = ("shard", "ctx", "tp")
BF = jnp.bfloat16
F32 = jnp.float32


def place_of(index):
    shard, rest = divmod(index, 16)
    ctx, tp = divmod(rest, 8)
    return shard // 2, ctx * 2 + shard % 2, tp // 2, tp % 2


def index_of(x, y, z, c):
    x, y, z, c = x % 4, y % 4, z % 4, c % 2
    return (x * 2 + y % 2) * 16 + (y // 2) * 8 + z * 2 + c


def hop(value, dx=0, dy=0, dz=0, dc=0, only=None):
    pairs = []
    for index in range(128):
        x, y, z, c = place_of(index)
        if only is None or only(x, y, z, c):
            pairs.append((index, index_of(x + dx, y + dy, z + dz, c + dc)))
    return lax.ppermute(value, AXES, pairs)


def step_of(axis, amount):
    return {"d" + axis: amount}


def halves(value):
    middle = value.shape[0] // 2
    return value[:middle], value[middle:]


def ring_gather(block, axis):
    from_before = hop(block, **step_of(axis, 1))
    from_after = hop(block, **step_of(axis, -1))
    first = hop(halves(from_before)[0], **step_of(axis, 1))
    second = hop(halves(from_after)[1], **step_of(axis, -1))
    return [block, from_after, jnp.concatenate([first, second], axis=0), from_before]


def direct_gather(block, axis):
    return [
        block,
        hop(block, **step_of(axis, -1)),
        hop(block, **step_of(axis, 2)),
        hop(block, **step_of(axis, 1)),
    ]


def in_order(blocks, start):
    whole = jnp.zeros((4,) + blocks[0].shape, blocks[0].dtype)
    for distance, block in enumerate(blocks):
        whole = lax.dynamic_update_index_in_dim(whole, block, (start + distance) % 4, 0)
    return whole


def by_distance(whole, start):
    return [
        lax.dynamic_index_in_dim(whole, (start + distance) % 4, 0, keepdims=False)
        for distance in range(4)
    ]


def added(*values):
    total = values[0].astype(F32)
    for value in values[1:]:
        total = total + value.astype(F32)
    return total


def ring_scatter(chunks, axis):
    far_first, far_second = halves(chunks[2])
    got_first = hop(far_first, **step_of(axis, 1))
    got_second = hop(far_second, **step_of(axis, -1))
    after_first, after_second = halves(chunks[1])
    before_first, before_second = halves(chunks[3])
    to_after = jnp.concatenate([added(after_first, got_first).astype(BF), after_second], axis=0)
    to_before = jnp.concatenate([before_first, added(before_second, got_second).astype(BF)], axis=0)
    from_before = hop(to_after, **step_of(axis, 1))
    from_after = hop(to_before, **step_of(axis, -1))
    return added(chunks[0], from_before, from_after)


def direct_scatter(chunks, axis):
    return added(
        chunks[0],
        hop(chunks[1], **step_of(axis, 1)),
        hop(chunks[2], **step_of(axis, 2)),
        hop(chunks[3], **step_of(axis, -1)),
    )


def with_partner(own, other, number):
    return jnp.where(
        number == 0, jnp.concatenate([own, other], 0), jnp.concatenate([other, own], 0)
    )


def rms_scale(values):
    return lax.rsqrt(jnp.mean(values * values, axis=-1, keepdims=True) + EPSILON)


def norm_back(grad_normed, source, scale_row, gain_row):
    unit_values = source * scale_row
    grad_unit = grad_normed * gain_row
    grad_source = scale_row * (
        grad_unit - unit_values * jnp.mean(grad_unit * unit_values, axis=-1, keepdims=True)
    )
    return (grad_source, grad_normed * unit_values)


def rope_tables(positions, head_width):
    frequency = ROPE_BASE ** (-(jnp.arange(0, head_width, 2, dtype=F32) / head_width))
    angles = positions.astype(F32)[:, None] * frequency[None, :]
    return (jnp.cos(angles), jnp.sin(angles))


def rotate(values, cosine, sine_table):
    half_width = values.shape[-1] // 2
    first_half = values[..., :half_width]
    second_half = values[..., half_width:]
    return jnp.concatenate(
        [
            first_half * cosine - second_half * sine_table,
            second_half * cosine + first_half * sine_table,
        ],
        axis=-1,
    )


def dot(left, right):
    return jnp.dot(left, right, preferred_element_type=F32)


def dot_nt(left, right):
    return lax.dot_general(left, right, (((1,), (1,)), ((), ())), preferred_element_type=F32)


def dot_tn(left, right):
    return lax.dot_general(left, right, (((0,), (0,)), ((), ())), preferred_element_type=F32)


ANY = pl.BlockSpec(memory_space=pl.ANY)
VMEM = pl.BlockSpec(memory_space=pltpu.VMEM)
MIB = 1024 * 1024
ROWS, WIDTH, HOME, HALF = 512, 2048, 64, 256
WROWS, WCOLS = 272, 1152


def places():
    shard, ctx, tp = lax.axis_index("shard"), lax.axis_index("ctx"), lax.axis_index("tp")
    return shard // 2, ctx * 2 + shard % 2, tp // 2, tp % 2


def device(x, y, z, c):
    x, y, z, c = lax.rem(x + 4, 4), lax.rem(y + 4, 4), lax.rem(z + 4, 4), lax.rem(c + 2, 2)
    return {"shard": x * 2 + lax.rem(y, 2), "ctx": y // 2, "tp": z * 2 + c}


class Links:
    def __init__(self, send_sems, recv_sems):
        self.here = places()
        self.send_sems, self.recv_sems, self.made = send_sems, recv_sems, []

    def send(self, source, target, dx=0, dy=0, dz=0, dc=0, start=True):
        x, y, z, c = self.here
        number = len(self.made)
        copy = pltpu.make_async_remote_copy(
            src_ref=source,
            dst_ref=target,
            send_sem=self.send_sems.at[number],
            recv_sem=self.recv_sems.at[number],
            device_id=device(x + dx, y + dy, z + dz, c + dc),
            device_id_type=pl.DeviceIdType.MESH,
        )
        self.made.append(copy)
        if start:
            copy.start()
        return copy

    def finish(self):
        for copy in self.made:
            copy.wait_send()

    def greet(self, steps):
        x, y, z, c = self.here
        barrier = pltpu.get_barrier_semaphore()
        for dx, dy, dz, dc in steps:
            pl.semaphore_signal(
                barrier,
                inc=1,
                device_id=device(x + dx, y + dy, z + dz, c + dc),
                device_id_type=pl.DeviceIdType.MESH,
            )
        pl.semaphore_wait(barrier, len(steps))


STEPS_X = [(1, 0, 0, 0), (-1, 0, 0, 0)]
STEPS_Y = [(0, 1, 0, 0), (0, -1, 0, 0), (0, 2, 0, 0)]
STEPS_Z = [(0, 0, 1, 0), (0, 0, -1, 0), (0, 0, 2, 0)]
STEPS_C = [(0, 0, 0, 1)]


def arrived(copies):
    for copy in copies:
        copy.wait_recv()


def turned(values, cosine, sine):
    return values * cosine + pltpu.roll(values, 64, 1) * sine


def spread(links, array, home_ref, y, z, c):
    first, second = pl.ds(0, 32), pl.ds(32, 32)
    y_after, y_before, y_far = lax.rem(y + 1, 4), lax.rem(y + 3, 4), lax.rem(y + 2, 4)
    z_after, z_before, z_far = lax.rem(z + 1, 4), lax.rem(z + 3, 4), lax.rem(z + 2, 4)
    p_one = [
        links.send(home_ref.at[first], array.at[y, c, z, first], dz=d) for d in (1, -1, 2)
    ]
    q_one = [
        links.send(home_ref.at[second], array.at[y, c, z, second], dy=d) for d in (1, -1, 2)
    ]

    def p_block(place):
        return array.at[place, c, :, first]

    def q_block(place):
        return array.at[:, c, place, second]

    arrived(p_one)
    p_two = [links.send(p_block(y), p_block(y), dy=d) for d in (1, -1)]
    sibling = [links.send(p_block(y), p_block(y), dc=1)]
    arrived(q_one)
    q_two = [links.send(q_block(z), q_block(z), dz=d) for d in (1, -1)]
    sibling.append(links.send(q_block(z), q_block(z), dc=1))
    p_two[0].wait_recv()
    low, high = pl.ds(0, 2), pl.ds(2, 2)
    ahead = array.at[y_before, c, low, first]
    p_far = [links.send(ahead, ahead, dy=1)]
    sibling.append(links.send(p_block(y_before), p_block(y_before), dc=1))
    q_two[0].wait_recv()
    ahead = array.at[low, c, z_before, second]
    q_far = [links.send(ahead, ahead, dz=1)]
    sibling.append(links.send(q_block(z_before), q_block(z_before), dc=1))
    p_two[1].wait_recv()
    behind = array.at[y_after, c, high, first]
    p_far.append(links.send(behind, behind, dy=-1))
    sibling.append(links.send(p_block(y_after), p_block(y_after), dc=1))
    q_two[1].wait_recv()
    behind = array.at[high, c, z_after, second]
    q_far.append(links.send(behind, behind, dz=-1))
    sibling.append(links.send(q_block(z_after), q_block(z_after), dc=1))
    arrived(p_far)
    sibling.append(links.send(p_block(y_far), p_block(y_far), dc=1))
    arrived(q_far)
    sibling.append(links.send(q_block(z_far), q_block(z_far), dc=1))
    return sibling


def front(
    tok, own_weights, cosine_ref, sine_ref, segment_rows, segment_row, gate, up, down, grad, picked,
    weights_out, experts_in, experts_out, grad_all, picked_all, moe_in_all,
    normed_out, pre_out, rot_out, kv_out, mixed_out, lse_out, hidden_out, home_scale_out,
    weights, kv_far, biases, accs, part, part_core, part_z, home_ref,
    send_sems, recv_sems, local_sems,
):
    links = Links(send_sems, recv_sems)
    x, y, z, c = links.here
    ctx, y_low = y // 2, lax.rem(y, 2)
    x_after, x_before = lax.rem(x + 1, 4), lax.rem(x + 3, 4)
    y_after, y_before, y_far = lax.rem(y + 1, 4), lax.rem(y + 3, 4), lax.rem(y + 2, 4)
    own = c * HALF
    links.greet(STEPS_X + STEPS_Y + STEPS_Z + STEPS_C)

    low, high = pl.ds(0, 128), pl.ds(128, WROWS - 128)
    slot = weights.at[x, y_low]
    pair = [
        links.send(own_weights.at[low], slot.at[low], dy=1),
        links.send(own_weights.at[high], slot.at[high], dy=-1),
    ]
    local = [pltpu.make_async_copy(own_weights, slot, local_sems.at[0])]

    def mine(array, group):
        return array.at[pl.ds(group * 4, 4)]

    def columns(place, low_place):
        return pl.ds(pl.multiple_of(place * 512 + low_place * 256, 256), 256)

    local.append(
        pltpu.make_async_copy(
            mine(gate, y), experts_in.at[:, x, y_low, :, pl.ds(0, 128)], local_sems.at[1]
        )
    )
    local.append(
        pltpu.make_async_copy(
            mine(up, y), experts_in.at[:, x, y_low, :, pl.ds(128, 128)], local_sems.at[2]
        )
    )
    local.append(
        pltpu.make_async_copy(
            mine(down, y), experts_out.at[:, :, columns(x, y_low)], local_sems.at[3]
        )
    )
    own_rows = pl.ds(pl.multiple_of(own, HALF), HALF)
    local.append(pltpu.make_async_copy(grad, grad_all.at[y], local_sems.at[4]))
    local.append(pltpu.make_async_copy(picked, picked_all.at[y], local_sems.at[5]))
    for copy in local:
        copy.start()
    local[0].wait()
    arrived(pair)
    near = [links.send(weights.at[x], weights.at[x], dx=d) for d in (1, -1)]

    expert_pair = []
    for group, start, step in ((y_after, 0, 1), (y_before, 2, -1)):
        some = pl.ds(group * 4 + start, 2)
        there = pl.ds(start, 2)
        expert_pair += [
            links.send(
                gate.at[some], experts_in.at[there, x, y_low, :, pl.ds(0, 128)], dy=step
            ),
            links.send(
                up.at[some], experts_in.at[there, x, y_low, :, pl.ds(128, 128)], dy=step
            ),
            links.send(down.at[some], experts_out.at[there, :, columns(x, y_low)], dy=step),
        ]
    grad_near = [
        links.send(grad.at[own_rows], grad_all.at[y, own_rows], dy=d) for d in (1, -1)
    ]
    picked_near = [links.send(picked, picked_all.at[y], dy=d) for d in (1, -1, 2)]

    rows_at = lax.broadcasted_iota(jnp.int32, (ROWS, ROWS), 0)
    cols_at = lax.broadcasted_iota(jnp.int32, (ROWS, ROWS), 1)
    own_first = pl.ds(pl.multiple_of(ctx * ROWS, ROWS), ROWS)
    same = segment_rows[own_first, :] == segment_row[:, own_first]
    biases[0] = jnp.where(same & (rows_at >= cols_at), 0.0, MASKED_SCORE)
    earlier = segment_rows[own_first, :] == segment_row[:, pl.ds(0, ROWS)]
    biases[1] = jnp.where(earlier, 0.0, MASKED_SCORE)
    tokens = tok[...].astype(F32)
    scale_one = rms_scale(tokens)

    near[0].wait_recv()
    far = [links.send(weights.at[x_before, 0], weights.at[x_before, 0], dx=1)]
    near[1].wait_recv()
    far.append(links.send(weights.at[x_after, 1], weights.at[x_after, 1], dx=-1))
    arrived(far)
    for copy in local[1:4]:
        copy.wait()
    arrived(expert_pair)

    def expert_blocks(place, low_place=None):
        if low_place is None:
            cols = pl.ds(pl.multiple_of(place * 512, 512), 512)
            return experts_in.at[:, place], experts_out.at[:, :, cols]
        return experts_in.at[:, place, low_place], experts_out.at[:, :, columns(place, low_place)]

    expert_near = [
        [links.send(block, block, dx=d) for block in expert_blocks(x)] for d in (1, -1)
    ]

    gain_blocks = [weights[s // 2, s % 2, 256:272, 0:256].astype(F32) for s in range(8)]
    gains = jnp.concatenate([block[0:1] for block in gain_blocks], axis=1)
    moe_gains = jnp.concatenate([block[1:2] for block in gain_blocks], axis=1)
    head_gains = sum(block[:, 0:128] for block in gain_blocks)
    normed_out[...] = (tokens * scale_one * gains).astype(BF)

    def project(column):
        block = weights[:, :, 0:256, column * 256 : column * 256 + 256].reshape(WIDTH, 256)
        return jnp.dot(normed_out[...], block, preferred_element_type=F32)

    cosine, sine = cosine_ref[own_first, :], sine_ref[own_first, :]

    def heads(pre, first_gain, base):
        for h in range(2):
            part_h = pre[:, h * 128 : h * 128 + 128]
            unit = part_h * rms_scale(part_h) * head_gains[first_gain + h : first_gain + h + 1]
            rot_out[:, base + h * 128 : base + h * 128 + 128] = turned(unit, cosine, sine).astype(BF)

    key_pre = project(1)
    pre_out[:, 256:512] = key_pre
    heads(key_pre, 4, 256)
    kv_out[:, 0:256] = rot_out[:, 256:512]
    kv_out[:, 256:512] = project(2).astype(BF)
    later = links.send(kv_out, kv_far, dy=2, start=False)

    @pl.when(ctx == 0)
    def _():
        later.start()

    query_pre = project(0)
    pre_out[:, 0:256] = query_pre
    heads(query_pre, 2, 0)
    score_scale = 128 ** (-0.5)
    peaks, totals = [], []
    for h in range(2):
        lane = slice(h * 128, h * 128 + 128)
        scores = dot_nt(rot_out[:, lane], kv_out[:, lane]) * score_scale + biases[0]
        peak = jnp.max(scores, axis=-1, keepdims=True)
        exponents = jnp.exp(scores - peak)
        lse_out[h] = jnp.broadcast_to(peak, (ROWS, 128))
        lse_out[2 + h] = jnp.broadcast_to(
            jnp.sum(exponents, axis=-1, keepdims=True), (ROWS, 128)
        )
        accs[h] = dot(exponents.astype(BF), kv_out[:, 256 + h * 128 : 384 + h * 128])

    arrived(grad_near)
    grad_lane = grad_all.at[:, own_rows]
    quarter = pl.multiple_of(own, HALF)
    first_half, second_half = pl.ds(quarter, 128), pl.ds(pl.multiple_of(quarter + 128, 128), 128)
    grad_far = [
        links.send(grad_all.at[y_before, first_half], grad_all.at[y_before, first_half], dy=1),
        links.send(grad_all.at[y_after, second_half], grad_all.at[y_after, second_half], dy=-1),
    ]
    siblings = [
        links.send(grad_all.at[place, own_rows], grad_all.at[place, own_rows], dc=1)
        for place in (y_before, y_after)
    ]

    @pl.when(ctx == 1)
    def _():
        later.wait_recv()
        for h in range(2):
            lane = slice(h * 128, h * 128 + 128)
            scores = dot_nt(rot_out[:, lane], kv_far[:, lane]) * score_scale + biases[1]
            old_peak = lse_out[h][:, 0:1]
            peak = jnp.maximum(old_peak, jnp.max(scores, axis=-1, keepdims=True))
            exponents = jnp.exp(scores - peak)
            old = jnp.exp(old_peak - peak)
            lse_out[h] = jnp.broadcast_to(peak, (ROWS, 128))
            lse_out[2 + h] = lse_out[2 + h] * old + jnp.sum(exponents, axis=-1, keepdims=True)
            accs[h] = accs[h] * old + dot(
                exponents.astype(BF), kv_far[:, 256 + h * 128 : 384 + h * 128]
            )

    for h in range(2):
        total = lse_out[2 + h]
        mixed_out[:, h * 128 : h * 128 + 128] = (accs[h] / total).astype(BF)
        lse_out[h] = lse_out[h] + jnp.log(total)

    other = pl.multiple_of((1 - c) * HALF, HALF)
    give_rows = mixed_out[pl.ds(other, HALF), :]
    for s in range(8):
        block = weights[s // 2, s % 2, 0:256, 896:1152]
        part[1, :, s * 256 : s * 256 + 256] = dot(give_rows, block).astype(BF)
    core_sum = links.send(part.at[1], part_core, dc=1)
    keep_rows = mixed_out[pl.ds(quarter, HALF), :]
    for s in range(8):
        block = weights[s // 2, s % 2, 0:256, 896:1152]
        part[0, :, s * 256 : s * 256 + 256] = dot(keep_rows, block).astype(BF)
    core_sum.wait_recv()
    part[0] = (part[0].astype(F32) + part_core[...].astype(F32)).astype(BF)
    z_sum = []
    for k, d in enumerate((1, -1, 2)):
        there = pl.multiple_of(lax.rem(z + d + 4, 4) * HOME, HOME)
        z_sum.append(links.send(part.at[0, pl.ds(there, HOME)], part_z.at[k], dz=d))

    for copies in expert_near:
        arrived(copies)
    expert_far = [links.send(block, block, dx=1) for block in expert_blocks(x_before, 0)]
    expert_far += [links.send(block, block, dx=-1) for block in expert_blocks(x_after, 1)]
    arrived(grad_far)
    siblings.append(links.send(grad_all.at[y_far, own_rows], grad_all.at[y_far, own_rows], dc=1))

    arrived(z_sum)
    home_first = pl.multiple_of(quarter + z * HOME, HOME)
    home_rows = pl.ds(home_first, HOME)
    summed = part[0, pl.ds(pl.multiple_of(z * HOME, HOME), HOME), :].astype(F32)
    for k in range(3):
        summed = summed + part_z[k].astype(F32)
    home_tokens = tok[home_rows, :].astype(F32)
    hidden = home_tokens + summed
    hidden_out[...] = hidden
    home_scale_out[...] = jnp.broadcast_to(rms_scale(home_tokens), (HOME, 128))
    home_ref[...] = (hidden * rms_scale(hidden) * moe_gains).astype(BF)
    place_home = pltpu.make_async_copy(home_ref, moe_in_all.at[y, c, z], local_sems.at[6])
    place_home.start()
    keep_weights = pltpu.make_async_copy(weights, weights_out, local_sems.at[7])
    keep_weights.start()
    place_home.wait()
    siblings += spread(links, moe_in_all, home_ref, y, z, c)
    arrived(expert_far)
    arrived(picked_near)
    arrived(siblings)
    local[4].wait()
    local[5].wait()
    keep_weights.wait()

    for copy in links.made:
        if copy is not later:
            copy.wait_send()

    @pl.when(ctx == 0)
    def _():
        later.wait_send()


FRONT_COPIES = 6 + 14 + 8 + 3 + 1 + 4 + 24


def run_front(tok, own_weights, tables, segments, gate, up, down, grad, picked):
    shape = jax.ShapeDtypeStruct
    outs = (
        (shape((4, 2, WROWS, WCOLS), BF), ANY),
        (shape((4, 4, 2, 256, 256), BF), ANY),
        (shape((4, 128, WIDTH), BF), ANY),
        (shape((4, ROWS, WIDTH), BF), ANY),
        (shape((4, ROWS, 128), BF), ANY),
        (shape((4, 2, 4, HOME, WIDTH), BF), ANY),
        (shape((ROWS, WIDTH), BF), VMEM),
        (shape((ROWS, 512), F32), VMEM),
        (shape((ROWS, 512), BF), VMEM),
        (shape((ROWS, 512), BF), VMEM),
        (shape((ROWS, 256), BF), VMEM),
        (shape((4, ROWS, 128), F32), VMEM),
        (shape((HOME, WIDTH), F32), VMEM),
        (shape((HOME, 128), F32), VMEM),
    )
    return pl.pallas_call(
        front,
        out_shape=[o for o, _ in outs],
        in_specs=[VMEM] * 6 + [ANY] * 5,
        out_specs=[spec for _, spec in outs],
        scratch_shapes=[
            pltpu.VMEM((4, 2, WROWS, WCOLS), BF),
            pltpu.VMEM((ROWS, 512), BF),
            pltpu.VMEM((2, ROWS, ROWS), F32),
            pltpu.VMEM((2, ROWS, 128), F32),
            pltpu.VMEM((2, HALF, WIDTH), BF),
            pltpu.VMEM((HALF, WIDTH), BF),
            pltpu.VMEM((3, HOME, WIDTH), BF),
            pltpu.VMEM((HOME, WIDTH), BF),
            pltpu.SemaphoreType.DMA((FRONT_COPIES,)),
            pltpu.SemaphoreType.DMA((FRONT_COPIES,)),
            pltpu.SemaphoreType.DMA((8,)),
        ],
        compiler_params=pltpu.CompilerParams(
            collective_id=1, has_side_effects=True, vmem_limit_bytes=56 * MIB
        ),
        name="front",
    )(
        tok,
        own_weights,
        jnp.asarray(tables[0]),
        jnp.asarray(tables[1]),
        segments.reshape(-1, 1),
        segments,
        gate,
        up,
        down,
        grad,
        picked,
    )


def turn_tables():
    frequency = ROPE_BASE ** (-(np.arange(0, 128, 2, dtype=np.float64) / 128))
    angles = np.arange(1024, dtype=np.float64)[:, None] * frequency[None, :]
    cosine, sine = np.cos(angles), np.sin(angles)
    return (
        np.concatenate([cosine, cosine], axis=1).astype(np.float32),
        np.concatenate([-sine, sine], axis=1).astype(np.float32),
    )


def body(
    tokens,
    out_grad,
    segments,
    routes,
    query_weight,
    key_weight,
    value_weight,
    out_weight,
    router_weight,
    attn_gain,
    moe_gain,
    query_gain,
    key_gain,
    gate_weight,
    up_weight,
    down_weight,
):
    rows, width = tokens.shape[1], tokens.shape[2]
    experts = gate_weight.shape[0]
    own_experts = experts // 4
    hidden_units = gate_weight.shape[2]
    span = own_experts * hidden_units
    shard, ctx, tp = lax.axis_index("shard"), lax.axis_index("ctx"), lax.axis_index("tp")
    x, y_low, z, core = shard // 2, shard % 2, tp // 2, tp % 2
    y = ctx * 2 + y_low
    home = rows // 8
    head_dim = 128
    local_width = 256
    score_scale = head_dim ** (-0.5)

    def spread_rows(part):
        lane = in_order(direct_gather(part, "z"), z).reshape(4 * part.shape[0], -1)
        return with_partner(lane, hop(lane, dc=1), core)

    def home_sum(terms):
        keep = lax.dynamic_slice_in_dim(terms, core * 256, 256, 0)
        give = lax.dynamic_slice_in_dim(terms, (1 - core) * 256, 256, 0)
        lane = added(keep, hop(give, dc=1)).astype(BF).reshape(4, home, -1)
        return direct_scatter(by_distance(lane, z), "z")

    def tokens_sum(terms):
        terms = terms.reshape(4, rows, -1)
        keep = lax.dynamic_slice_in_dim(terms, core * 256, 256, 1)
        give = lax.dynamic_slice_in_dim(terms, (1 - core) * 256, 256, 1)
        lane = added(keep, hop(give, dc=1)).astype(BF)
        mine = ring_scatter(by_distance(lane, y), "y").astype(BF).reshape(4, home, -1)
        return direct_scatter(by_distance(mine, z), "z")

    lanes = jnp.zeros((4, 128), BF)
    head_gains = jnp.concatenate([query_gain, key_gain], axis=0)
    lanes = lax.dynamic_update_slice_in_dim(lanes, head_gains, shard * 16, 1)
    gain_rows = jnp.zeros((16, WCOLS), BF)
    gain_rows = gain_rows.at[0, :256].set(attn_gain).at[1, :256].set(moe_gain)
    gain_rows = gain_rows.at[2:6, :128].set(lanes)
    router_pad = jnp.pad(router_weight, ((0, 0), (0, 128 - experts)))
    own_weights = jnp.concatenate(
        [
            jnp.concatenate([query_weight, key_weight, value_weight, router_pad, out_weight], axis=1),
            gain_rows,
        ],
        axis=0,
    )
    own_grad = out_grad.reshape(rows, width)
    route_rows = routes.reshape(rows, -1)
    own_picked = jnp.any(
        route_rows[:, :, None] == jnp.arange(128, dtype=jnp.int32)[None, None, :], axis=1
    ).astype(BF)
    (
        weights, experts_in, experts_out, grad_all, picked_all, moe_in_all,
        normed, pre, rot, key_value, mixed_low, lse, hidden, home_scale_one,
    ) = run_front(
        tokens.reshape(rows, width), own_weights, turn_tables(), segments,
        gate_weight, up_weight, down_weight, own_grad, own_picked,
    )
    weights = weights.reshape(8, WROWS, WCOLS)
    w_stacked = weights[:, :256, :768].reshape(width, -1)
    w_router = weights[:, :256, 768:896].reshape(width, -1)
    w_out_t = weights[:, :256, 896:].transpose(0, 2, 1).reshape(width, -1)
    gain_rows = weights[:, 256:].astype(F32)
    attn_gains = gain_rows[:, 0, :256].reshape(-1)
    moe_gains = gain_rows[:, 1, :256].reshape(-1)
    head_gains = jnp.sum(gain_rows[:, 2:6, :128], axis=0)

    def wide(part):
        return part.transpose(1, 2, 3, 0, 4).reshape(width, -1)

    w_in = jnp.concatenate(
        [wide(experts_in[..., :128]), wide(experts_in[..., 128:]), w_router], axis=1
    )
    w_down_t = experts_out.reshape(-1, width).T
    grad_all = grad_all.reshape(4 * rows, width)
    picked = picked_all.reshape(4 * rows, -1)[:, :experts] > 0
    moe_in = moe_in_all.reshape(4 * rows, width)
    inputs = tokens.reshape(rows, width).astype(F32)
    first_row = ctx * rows
    places = first_row + jnp.arange(rows, dtype=jnp.int32)
    cosine, sine_table = rope_tables(places, head_dim)
    query_pre = [pre[:, h * 128 : h * 128 + 128] for h in range(2)]
    key_pre = [pre[:, 256 + h * 128 : 384 + h * 128] for h in range(2)]
    scale_query = [rms_scale(v) for v in query_pre]
    scale_key = [rms_scale(v) for v in key_pre]
    gain_q = [head_gains[h][None] for h in range(2)]
    gain_k = [head_gains[2 + h][None] for h in range(2)]
    query_low = [rot[:, h * 128 : h * 128 + 128] for h in range(2)]
    earlier = hop(key_value, dy=2, only=lambda x, y, z, c: y < 2)
    both = jnp.concatenate([earlier, key_value], axis=0)
    keys = [both[:, h * 128 : h * 128 + 128] for h in range(2)]
    values = [both[:, 256 + h * 128 : 384 + h * 128] for h in range(2)]
    key_places = first_row - rows + jnp.arange(2 * rows, dtype=jnp.int32)
    own_segments = lax.dynamic_slice_in_dim(segments[0], first_row, rows, 0)
    key_segments = jnp.concatenate([segments[0, :rows], own_segments])
    allowed = (
        (places[:, None] >= key_places[None, :])
        & (key_places[None, :] >= 0)
        & (own_segments[:, None] == key_segments[None, :])
    )
    probs = []
    for h in range(2):
        scores = jnp.where(allowed, dot_nt(query_low[h], keys[h]) * score_scale, MASKED_SCORE)
        probs.append(jnp.exp(scores - lse[h][:, :1]))
    home_row = (core * 4 + z) * home
    home_inputs = lax.dynamic_slice_in_dim(tokens.reshape(rows, width), home_row, home, 0).astype(F32)
    home_scale_one = home_scale_one[:, :1]
    home_grad = lax.dynamic_slice_in_dim(own_grad, home_row, home, 0).astype(F32)
    scale_two = rms_scale(hidden)

    joined = dot(moe_in, w_in)
    logits = jnp.where(picked, joined[:, 2 * span : 2 * span + experts], -jnp.inf)
    gates = jax.nn.softmax(logits, axis=-1)
    own_gates = lax.dynamic_slice_in_dim(gates, y * own_experts, own_experts, 1)
    wide_gates = jnp.repeat(own_gates, hidden_units, axis=1)
    gate_pre, up_pre = joined[:, :span], joined[:, span : 2 * span]
    logistic = jax.nn.sigmoid(gate_pre)
    silu_gate = gate_pre * logistic
    silu_slope = logistic * (1.0 + gate_pre * (1.0 - logistic))
    act = silu_gate * up_pre
    act_back = dot(grad_all, w_down_t)
    gate_terms = jnp.sum(
        (act.astype(BF).astype(F32) * act_back).reshape(-1, own_experts, hidden_units), axis=-1
    )
    gate_grad = lax.dynamic_update_slice_in_dim(
        jnp.zeros_like(gates), gate_terms, y * own_experts, 1
    )
    logit_grad = gates * (gate_grad - jnp.sum(gates * gate_grad, axis=-1, keepdims=True))
    act_grad = act_back * wide_gates
    pre_grad = jnp.concatenate(
        [
            (act_grad * up_pre * silu_slope).astype(BF),
            (act_grad * silu_gate).astype(BF),
            jnp.pad(logit_grad.astype(BF), ((0, 0), (0, 128 - experts))),
        ],
        axis=1,
    )
    gated_act = (act * wide_gates).astype(BF)
    moe_in_part = dot_nt(pre_grad, w_in).astype(BF)
    moe_in_grad = tokens_sum(moe_in_part)
    moe_part = dot_nt(gated_act, w_down_t).astype(BF)
    moe_part, _ = lax.optimization_barrier((moe_part, moe_in_grad))
    layer_rows = (hidden + tokens_sum(moe_part)).astype(BF)
    layer_out = spread_rows(layer_rows).reshape(tokens.shape)
    grad_in = dot_tn(moe_in, pre_grad).astype(BF)
    grad_down_t = dot_tn(grad_all, gated_act).astype(BF)
    grad_in, grad_down_t, _ = lax.optimization_barrier((grad_in, grad_down_t, moe_in_grad))
    grad_moe = ring_scatter(
        [
            jnp.concatenate([a[:, : 2 * span], b], axis=1)
            for a, b in zip(
                by_distance(grad_in.reshape(4, 512, -1), x),
                by_distance(grad_down_t.reshape(4, 512, -1), x),
            )
        ],
        "x",
    ).astype(BF)
    grad_moe = grad_moe.reshape(2, 256, -1)
    keep = lax.dynamic_index_in_dim(grad_moe, y_low, 0, keepdims=False)
    give = lax.dynamic_index_in_dim(grad_moe, 1 - y_low, 0, keepdims=False)
    grad_groups = in_order(
        [keep, hop(give, dy=-1), hop(keep, dy=2), hop(give, dy=1)], y
    )

    def ungrouped(part):
        parted = part.reshape(4, 256, own_experts, hidden_units)
        return parted.transpose(0, 2, 1, 3).reshape(experts, 256, hidden_units).astype(F32)

    grad_gate_weight = ungrouped(grad_groups[:, :, :span])
    grad_up_weight = ungrouped(grad_groups[:, :, span : 2 * span])
    grad_down_weight = (
        grad_groups[:, :, 2 * span :]
        .reshape(4, 256, own_experts, hidden_units)
        .transpose(0, 2, 3, 1)
        .reshape(experts, hidden_units, 256)
        .astype(F32)
    )

    hidden_norm_grad, moe_gain_rows = norm_back(moe_in_grad, hidden, scale_two, moe_gains)
    hidden_grad = home_grad + hidden_norm_grad
    hidden_low = spread_rows(hidden_grad.astype(BF))
    grad_router = grad_in[:, 2 * span : 2 * span + experts]
    early = jnp.concatenate([grad_router.T.astype(F32), jnp.sum(moe_gain_rows, axis=0)[None]], axis=0)
    early = early.reshape(-1, 128)
    early = early + hop(early, dc=1)
    for axis in "zyx":
        early = direct_scatter([early] * 4, axis)
    early = early.reshape(experts + 1, width)
    early = lax.dynamic_slice_in_dim(early, shard * 256, 256, 1)

    mixed_grad = dot(hidden_low, w_out_t).astype(BF)
    grad_out_t = dot_tn(hidden_low, mixed_low)
    query_grads, key_terms, value_terms = [], [], []
    for h in range(2):
        grad_h = mixed_grad[:, h * 128 : h * 128 + 128]
        prob_grad = dot_nt(grad_h, values[h])
        row_delta = jnp.sum(probs[h] * prob_grad, axis=-1, keepdims=True)
        score_grad = (probs[h] * (prob_grad - row_delta)).astype(BF)
        query_grads.append((dot(score_grad, keys[h]) * score_scale).astype(BF).astype(F32))
        key_terms.append(dot_tn(score_grad, query_low[h]) * score_scale)
        value_terms.append(dot_tn(probs[h].astype(BF), grad_h))
    terms = jnp.concatenate(key_terms + value_terms, axis=1)
    later = hop(terms[:rows].astype(BF), dy=2, only=lambda x, y, z, c: y >= 2)
    key_value_grad = added(terms[rows:], later).astype(BF)
    stacked, gain_sums = [], []
    for pre, scale, gain, grads in (
        (query_pre, scale_query, gain_q, query_grads),
        (key_pre, scale_key, gain_k, [key_value_grad[:, :128], key_value_grad[:, 128:256]]),
    ):
        for h in range(2):
            unit_grad = rotate(grads[h].astype(F32), cosine, -sine_table)
            pre_back, gain_rows = norm_back(unit_grad, pre[h], scale[h], gain[h])
            stacked.append(pre_back.astype(BF))
            gain_sums.append(jnp.sum(gain_rows, axis=0))
    stacked = jnp.concatenate(stacked + [key_value_grad[:, 256:]], axis=1)
    normed_part = dot_nt(stacked, w_stacked).astype(BF)
    grad_stacked = dot_tn(normed, stacked)
    normed_grad = home_sum(normed_part)
    input_norm_grad, attn_gain_rows = norm_back(
        normed_grad, home_inputs, home_scale_one, attn_gains
    )
    input_grad = spread_rows((hidden_grad + input_norm_grad).astype(BF)).reshape(tokens.shape)
    grad_attn = jnp.concatenate([grad_stacked, grad_out_t], axis=1).astype(BF)
    grad_attn = ring_scatter(by_distance(grad_attn.reshape(4, 512, -1), x), "x").astype(BF)
    grad_attn = grad_attn.reshape(2, 256, -1)
    keep = lax.dynamic_index_in_dim(grad_attn, y_low, 0, keepdims=False)
    give = lax.dynamic_index_in_dim(grad_attn, 1 - y_low, 0, keepdims=False)
    got = jnp.concatenate([hop(give[:128], dy=1), hop(give[128:], dy=-1)], axis=0)
    keep = added(keep, got).astype(BF)
    grad_attn = added(keep, hop(keep, dy=2))
    head_gain_sums = jnp.stack(gain_sums).reshape(2, 1, 2, 128)
    mine = (jnp.arange(8) == tp).astype(F32)[None, :, None, None]
    late = jnp.concatenate(
        [jnp.sum(attn_gain_rows, axis=0), (mine * head_gain_sums).reshape(-1)]
    ).reshape(48, 128)
    late = late + hop(late, dc=1)
    for axis in "zyx":
        late = direct_scatter([late] * 4, axis)
    grad_attn_gain = lax.dynamic_slice_in_dim(late[:16].reshape(-1), shard * 256, 256, 0)
    late_heads = late[16:].reshape(2, 8, 2, 128)
    late_heads = lax.dynamic_index_in_dim(late_heads, tp, 1, keepdims=False)
    late_heads = lax.dynamic_slice_in_dim(late_heads, shard * 16, 16, 2)
    return (
        layer_out,
        input_grad,
        grad_attn[:, :256],
        grad_attn[:, 256:512],
        grad_attn[:, 512:768],
        grad_attn[:, 768:].T,
        early[:experts].T,
        grad_attn_gain,
        early[experts],
        late_heads[0],
        late_heads[1],
        grad_gate_weight,
        grad_up_weight,
        grad_down_weight,
    )


def solution(mesh):
    return jax.shard_map(
        body,
        mesh=mesh,
        in_specs=(
            P("shard", "ctx", None),
            P("shard", "ctx", None),
            P("shard", None),
            P("shard", "ctx", None),
            P("shard", "tp"),
            P("shard", "tp"),
            P("shard", "tp"),
            P("tp", "shard"),
            P("shard", None),
            P("shard"),
            P("shard"),
            P("tp", "shard"),
            P("tp", "shard"),
            P(None, "shard", "tp"),
            P(None, "shard", "tp"),
            P(None, "tp", "shard"),
        ),
        out_specs=(
            P("shard", "ctx", None),
            P("shard", "ctx", None),
            P("shard", "tp"),
            P("shard", "tp"),
            P("shard", "tp"),
            P("tp", "shard"),
            P("shard", None),
            P("shard"),
            P("shard"),
            P("tp", "shard"),
            P("tp", "shard"),
            P(None, "shard", "tp"),
            P(None, "shard", "tp"),
            P(None, "tp", "shard"),
        ),
        check_vma=False,
    )
```

```python
import jax
import jax.numpy as jnp
import numpy as np
from jax import lax
from jax.experimental import pallas as pl
from jax.experimental.pallas import tpu as pltpu
from jax.sharding import PartitionSpec as P

EPSILON = 1e-05
ROPE_BASE = 10000.0
MASKED_SCORE = -1e30
AXES = ("shard", "ctx", "tp")
BF = jnp.bfloat16
F32 = jnp.float32


def place_of(index):
    shard, rest = divmod(index, 16)
    ctx, tp = divmod(rest, 8)
    return shard // 2, ctx * 2 + shard % 2, tp // 2, tp % 2


def index_of(x, y, z, c):
    x, y, z, c = x % 4, y % 4, z % 4, c % 2
    return (x * 2 + y % 2) * 16 + (y // 2) * 8 + z * 2 + c


def hop(value, dx=0, dy=0, dz=0, dc=0, only=None):
    pairs = []
    for index in range(128):
        x, y, z, c = place_of(index)
        if only is None or only(x, y, z, c):
            pairs.append((index, index_of(x + dx, y + dy, z + dz, c + dc)))
    return lax.ppermute(value, AXES, pairs)


def step_of(axis, amount):
    return {"d" + axis: amount}


def halves(value):
    middle = value.shape[0] // 2
    return value[:middle], value[middle:]


def ring_gather(block, axis):
    from_before = hop(block, **step_of(axis, 1))
    from_after = hop(block, **step_of(axis, -1))
    first = hop(halves(from_before)[0], **step_of(axis, 1))
    second = hop(halves(from_after)[1], **step_of(axis, -1))
    return [block, from_after, jnp.concatenate([first, second], axis=0), from_before]


def direct_gather(block, axis):
    return [
        block,
        hop(block, **step_of(axis, -1)),
        hop(block, **step_of(axis, 2)),
        hop(block, **step_of(axis, 1)),
    ]


def in_order(blocks, start):
    whole = jnp.zeros((4,) + blocks[0].shape, blocks[0].dtype)
    for distance, block in enumerate(blocks):
        whole = lax.dynamic_update_index_in_dim(whole, block, (start + distance) % 4, 0)
    return whole


def by_distance(whole, start):
    return [
        lax.dynamic_index_in_dim(whole, (start + distance) % 4, 0, keepdims=False)
        for distance in range(4)
    ]


def added(*values):
    total = values[0].astype(F32)
    for value in values[1:]:
        total = total + value.astype(F32)
    return total


def ring_scatter(chunks, axis):
    far_first, far_second = halves(chunks[2])
    got_first = hop(far_first, **step_of(axis, 1))
    got_second = hop(far_second, **step_of(axis, -1))
    after_first, after_second = halves(chunks[1])
    before_first, before_second = halves(chunks[3])
    to_after = jnp.concatenate([added(after_first, got_first).astype(BF), after_second], axis=0)
    to_before = jnp.concatenate([before_first, added(before_second, got_second).astype(BF)], axis=0)
    from_before = hop(to_after, **step_of(axis, 1))
    from_after = hop(to_before, **step_of(axis, -1))
    return added(chunks[0], from_before, from_after)


def direct_scatter(chunks, axis):
    return added(
        chunks[0],
        hop(chunks[1], **step_of(axis, 1)),
        hop(chunks[2], **step_of(axis, 2)),
        hop(chunks[3], **step_of(axis, -1)),
    )


def with_partner(own, other, number):
    return jnp.where(
        number == 0, jnp.concatenate([own, other], 0), jnp.concatenate([other, own], 0)
    )


def rms_scale(values):
    return lax.rsqrt(jnp.mean(values * values, axis=-1, keepdims=True) + EPSILON)


def norm_back(grad_normed, source, scale_row, gain_row):
    unit_values = source * scale_row
    grad_unit = grad_normed * gain_row
    grad_source = scale_row * (
        grad_unit - unit_values * jnp.mean(grad_unit * unit_values, axis=-1, keepdims=True)
    )
    return (grad_source, grad_normed * unit_values)


def rope_tables(positions, head_width):
    frequency = ROPE_BASE ** (-(jnp.arange(0, head_width, 2, dtype=F32) / head_width))
    angles = positions.astype(F32)[:, None] * frequency[None, :]
    return (jnp.cos(angles), jnp.sin(angles))


def rotate(values, cosine, sine_table):
    half_width = values.shape[-1] // 2
    first_half = values[..., :half_width]
    second_half = values[..., half_width:]
    return jnp.concatenate(
        [
            first_half * cosine - second_half * sine_table,
            second_half * cosine + first_half * sine_table,
        ],
        axis=-1,
    )


def dot(left, right):
    return jnp.dot(left, right, preferred_element_type=F32)


def dot_nt(left, right):
    return lax.dot_general(left, right, (((1,), (1,)), ((), ())), preferred_element_type=F32)


def dot_tn(left, right):
    return lax.dot_general(left, right, (((0,), (0,)), ((), ())), preferred_element_type=F32)


ANY = pl.BlockSpec(memory_space=pl.ANY)
VMEM = pl.BlockSpec(memory_space=pltpu.VMEM)
MIB = 1024 * 1024
ROWS, WIDTH, HOME, HALF = 512, 2048, 64, 256
WROWS, WCOLS = 272, 1152


def places():
    shard, ctx, tp = lax.axis_index("shard"), lax.axis_index("ctx"), lax.axis_index("tp")
    return shard // 2, ctx * 2 + shard % 2, tp // 2, tp % 2


def device(x, y, z, c):
    x, y, z, c = lax.rem(x + 4, 4), lax.rem(y + 4, 4), lax.rem(z + 4, 4), lax.rem(c + 2, 2)
    return {"shard": x * 2 + lax.rem(y, 2), "ctx": y // 2, "tp": z * 2 + c}


class Links:
    def __init__(self, send_sems, recv_sems):
        self.here = places()
        self.send_sems, self.recv_sems, self.made = send_sems, recv_sems, []

    def send(self, source, target, dx=0, dy=0, dz=0, dc=0, start=True):
        x, y, z, c = self.here
        number = len(self.made)
        copy = pltpu.make_async_remote_copy(
            src_ref=source,
            dst_ref=target,
            send_sem=self.send_sems.at[number],
            recv_sem=self.recv_sems.at[number],
            device_id=device(x + dx, y + dy, z + dz, c + dc),
            device_id_type=pl.DeviceIdType.MESH,
        )
        self.made.append(copy)
        if start:
            copy.start()
        return copy

    def finish(self):
        for copy in self.made:
            copy.wait_send()

    def greet(self, steps):
        x, y, z, c = self.here
        barrier = pltpu.get_barrier_semaphore()
        for dx, dy, dz, dc in steps:
            pl.semaphore_signal(
                barrier,
                inc=1,
                device_id=device(x + dx, y + dy, z + dz, c + dc),
                device_id_type=pl.DeviceIdType.MESH,
            )
        pl.semaphore_wait(barrier, len(steps))


STEPS_X = [(1, 0, 0, 0), (-1, 0, 0, 0)]
STEPS_Y = [(0, 1, 0, 0), (0, -1, 0, 0), (0, 2, 0, 0)]
STEPS_Z = [(0, 0, 1, 0), (0, 0, -1, 0), (0, 0, 2, 0)]
STEPS_C = [(0, 0, 0, 1)]


def arrived(copies):
    for copy in copies:
        copy.wait_recv()


def turned(values, cosine, sine):
    return values * cosine + pltpu.roll(values, 64, 1) * sine


def spread(links, array, home_ref, y, z, c):
    first, second = pl.ds(0, 32), pl.ds(32, 32)
    y_after, y_before, y_far = lax.rem(y + 1, 4), lax.rem(y + 3, 4), lax.rem(y + 2, 4)
    z_after, z_before, z_far = lax.rem(z + 1, 4), lax.rem(z + 3, 4), lax.rem(z + 2, 4)
    p_one = [
        links.send(home_ref.at[first], array.at[y, c, z, first], dz=d) for d in (1, -1, 2)
    ]
    q_one = [
        links.send(home_ref.at[second], array.at[y, c, z, second], dy=d) for d in (1, -1, 2)
    ]

    def p_block(place):
        return array.at[place, c, :, first]

    def q_block(place):
        return array.at[:, c, place, second]

    arrived(p_one)
    p_two = [links.send(p_block(y), p_block(y), dy=d) for d in (1, -1)]
    sibling = [links.send(p_block(y), p_block(y), dc=1)]
    arrived(q_one)
    q_two = [links.send(q_block(z), q_block(z), dz=d) for d in (1, -1)]
    sibling.append(links.send(q_block(z), q_block(z), dc=1))
    p_two[0].wait_recv()
    low, high = pl.ds(0, 2), pl.ds(2, 2)
    ahead = array.at[y_before, c, low, first]
    p_far = [links.send(ahead, ahead, dy=1)]
    sibling.append(links.send(p_block(y_before), p_block(y_before), dc=1))
    q_two[0].wait_recv()
    ahead = array.at[low, c, z_before, second]
    q_far = [links.send(ahead, ahead, dz=1)]
    sibling.append(links.send(q_block(z_before), q_block(z_before), dc=1))
    p_two[1].wait_recv()
    behind = array.at[y_after, c, high, first]
    p_far.append(links.send(behind, behind, dy=-1))
    sibling.append(links.send(p_block(y_after), p_block(y_after), dc=1))
    q_two[1].wait_recv()
    behind = array.at[high, c, z_after, second]
    q_far.append(links.send(behind, behind, dz=-1))
    sibling.append(links.send(q_block(z_after), q_block(z_after), dc=1))
    arrived(p_far)
    sibling.append(links.send(p_block(y_far), p_block(y_far), dc=1))
    arrived(q_far)
    sibling.append(links.send(q_block(z_far), q_block(z_far), dc=1))
    return sibling


def front(
    tok, own_weights, cosine_ref, sine_ref, segment_rows, segment_row, gate, up, down, grad, picked,
    weights_out, experts_in, experts_out, grad_all, picked_all, moe_in_all,
    normed_out, pre_out, rot_out, kv_out, mixed_out, lse_out, hidden_out, home_scale_out,
    weights, kv_far, biases, accs, part, part_core, part_z, home_ref,
    send_sems, recv_sems, local_sems,
):
    links = Links(send_sems, recv_sems)
    x, y, z, c = links.here
    ctx, y_low = y // 2, lax.rem(y, 2)
    x_after, x_before = lax.rem(x + 1, 4), lax.rem(x + 3, 4)
    y_after, y_before, y_far = lax.rem(y + 1, 4), lax.rem(y + 3, 4), lax.rem(y + 2, 4)
    own = c * HALF
    links.greet(STEPS_X + STEPS_Y + STEPS_Z + STEPS_C)

    low, high = pl.ds(0, 128), pl.ds(128, WROWS - 128)
    slot = weights.at[x, y_low]
    pair = [
        links.send(own_weights.at[low], slot.at[low], dy=1),
        links.send(own_weights.at[high], slot.at[high], dy=-1),
    ]
    local = [pltpu.make_async_copy(own_weights, slot, local_sems.at[0])]

    def mine(array, group):
        return array.at[pl.ds(group * 4, 4)]

    def columns(place, low_place):
        return pl.ds(pl.multiple_of(place * 512 + low_place * 256, 256), 256)

    local.append(
        pltpu.make_async_copy(
            mine(gate, y), experts_in.at[:, x, y_low, :, pl.ds(0, 128)], local_sems.at[1]
        )
    )
    local.append(
        pltpu.make_async_copy(
            mine(up, y), experts_in.at[:, x, y_low, :, pl.ds(128, 128)], local_sems.at[2]
        )
    )
    local.append(
        pltpu.make_async_copy(
            mine(down, y), experts_out.at[:, :, columns(x, y_low)], local_sems.at[3]
        )
    )
    own_rows = pl.ds(pl.multiple_of(own, HALF), HALF)
    local.append(pltpu.make_async_copy(grad, grad_all.at[y], local_sems.at[4]))
    local.append(pltpu.make_async_copy(picked, picked_all.at[y], local_sems.at[5]))
    for copy in local:
        copy.start()
    local[0].wait()
    arrived(pair)
    near = [links.send(weights.at[x], weights.at[x], dx=d) for d in (1, -1)]

    expert_pair = []
    for group, start, step in ((y_after, 0, 1), (y_before, 2, -1)):
        some = pl.ds(group * 4 + start, 2)
        there = pl.ds(start, 2)
        expert_pair += [
            links.send(
                gate.at[some], experts_in.at[there, x, y_low, :, pl.ds(0, 128)], dy=step
            ),
            links.send(
                up.at[some], experts_in.at[there, x, y_low, :, pl.ds(128, 128)], dy=step
            ),
            links.send(down.at[some], experts_out.at[there, :, columns(x, y_low)], dy=step),
        ]
    grad_near = [
        links.send(grad.at[own_rows], grad_all.at[y, own_rows], dy=d) for d in (1, -1)
    ]
    picked_near = [links.send(picked, picked_all.at[y], dy=d) for d in (1, -1, 2)]

    rows_at = lax.broadcasted_iota(jnp.int32, (ROWS, ROWS), 0)
    cols_at = lax.broadcasted_iota(jnp.int32, (ROWS, ROWS), 1)
    own_first = pl.ds(pl.multiple_of(ctx * ROWS, ROWS), ROWS)
    same = segment_rows[own_first, :] == segment_row[:, own_first]
    biases[0] = jnp.where(same & (rows_at >= cols_at), 0.0, MASKED_SCORE)
    earlier = segment_rows[own_first, :] == segment_row[:, pl.ds(0, ROWS)]
    biases[1] = jnp.where(earlier, 0.0, MASKED_SCORE)
    tokens = tok[...].astype(F32)
    scale_one = rms_scale(tokens)

    near[0].wait_recv()
    far = [links.send(weights.at[x_before, 0], weights.at[x_before, 0], dx=1)]
    near[1].wait_recv()
    far.append(links.send(weights.at[x_after, 1], weights.at[x_after, 1], dx=-1))
    arrived(far)
    for copy in local[1:4]:
        copy.wait()
    arrived(expert_pair)

    def expert_blocks(place, low_place=None):
        if low_place is None:
            cols = pl.ds(pl.multiple_of(place * 512, 512), 512)
            return experts_in.at[:, place], experts_out.at[:, :, cols]
        return experts_in.at[:, place, low_place], experts_out.at[:, :, columns(place, low_place)]

    expert_near = [
        [links.send(block, block, dx=d) for block in expert_blocks(x)] for d in (1, -1)
    ]

    gain_blocks = [weights[s // 2, s % 2, 256:272, 0:256].astype(F32) for s in range(8)]
    gains = jnp.concatenate([block[0:1] for block in gain_blocks], axis=1)
    moe_gains = jnp.concatenate([block[1:2] for block in gain_blocks], axis=1)
    head_gains = sum(block[:, 0:128] for block in gain_blocks)
    normed_out[...] = (tokens * scale_one * gains).astype(BF)

    def project(column):
        block = weights[:, :, 0:256, column * 256 : column * 256 + 256].reshape(WIDTH, 256)
        return jnp.dot(normed_out[...], block, preferred_element_type=F32)

    cosine, sine = cosine_ref[own_first, :], sine_ref[own_first, :]

    def heads(pre, first_gain, base):
        for h in range(2):
            part_h = pre[:, h * 128 : h * 128 + 128]
            unit = part_h * rms_scale(part_h) * head_gains[first_gain + h : first_gain + h + 1]
            rot_out[:, base + h * 128 : base + h * 128 + 128] = turned(unit, cosine, sine).astype(BF)

    key_pre = project(1)
    pre_out[:, 256:512] = key_pre
    heads(key_pre, 4, 256)
    kv_out[:, 0:256] = rot_out[:, 256:512]
    kv_out[:, 256:512] = project(2).astype(BF)
    later = links.send(kv_out, kv_far, dy=2, start=False)

    @pl.when(ctx == 0)
    def _():
        later.start()

    query_pre = project(0)
    pre_out[:, 0:256] = query_pre
    heads(query_pre, 2, 0)
    score_scale = 128 ** (-0.5)
    peaks, totals = [], []
    for h in range(2):
        lane = slice(h * 128, h * 128 + 128)
        scores = dot_nt(rot_out[:, lane], kv_out[:, lane]) * score_scale + biases[0]
        peak = jnp.max(scores, axis=-1, keepdims=True)
        exponents = jnp.exp(scores - peak)
        lse_out[h] = jnp.broadcast_to(peak, (ROWS, 128))
        lse_out[2 + h] = jnp.broadcast_to(
            jnp.sum(exponents, axis=-1, keepdims=True), (ROWS, 128)
        )
        accs[h] = dot(exponents.astype(BF), kv_out[:, 256 + h * 128 : 384 + h * 128])

    arrived(grad_near)
    grad_lane = grad_all.at[:, own_rows]
    quarter = pl.multiple_of(own, HALF)
    first_half, second_half = pl.ds(quarter, 128), pl.ds(pl.multiple_of(quarter + 128, 128), 128)
    grad_far = [
        links.send(grad_all.at[y_before, first_half], grad_all.at[y_before, first_half], dy=1),
        links.send(grad_all.at[y_after, second_half], grad_all.at[y_after, second_half], dy=-1),
    ]
    siblings = [
        links.send(grad_all.at[place, own_rows], grad_all.at[place, own_rows], dc=1)
        for place in (y_before, y_after)
    ]

    @pl.when(ctx == 1)
    def _():
        later.wait_recv()
        for h in range(2):
            lane = slice(h * 128, h * 128 + 128)
            scores = dot_nt(rot_out[:, lane], kv_far[:, lane]) * score_scale + biases[1]
            old_peak = lse_out[h][:, 0:1]
            peak = jnp.maximum(old_peak, jnp.max(scores, axis=-1, keepdims=True))
            exponents = jnp.exp(scores - peak)
            old = jnp.exp(old_peak - peak)
            lse_out[h] = jnp.broadcast_to(peak, (ROWS, 128))
            lse_out[2 + h] = lse_out[2 + h] * old + jnp.sum(exponents, axis=-1, keepdims=True)
            accs[h] = accs[h] * old + dot(
                exponents.astype(BF), kv_far[:, 256 + h * 128 : 384 + h * 128]
            )

    for h in range(2):
        total = lse_out[2 + h]
        mixed_out[:, h * 128 : h * 128 + 128] = (accs[h] / total).astype(BF)
        lse_out[h] = lse_out[h] + jnp.log(total)

    other = pl.multiple_of((1 - c) * HALF, HALF)
    give_rows = mixed_out[pl.ds(other, HALF), :]
    for s in range(8):
        block = weights[s // 2, s % 2, 0:256, 896:1152]
        part[1, :, s * 256 : s * 256 + 256] = dot(give_rows, block).astype(BF)
    core_sum = links.send(part.at[1], part_core, dc=1)
    keep_rows = mixed_out[pl.ds(quarter, HALF), :]
    for s in range(8):
        block = weights[s // 2, s % 2, 0:256, 896:1152]
        part[0, :, s * 256 : s * 256 + 256] = dot(keep_rows, block).astype(BF)
    core_sum.wait_recv()
    part[0] = (part[0].astype(F32) + part_core[...].astype(F32)).astype(BF)
    z_sum = []
    for k, d in enumerate((1, -1, 2)):
        there = pl.multiple_of(lax.rem(z + d + 4, 4) * HOME, HOME)
        z_sum.append(links.send(part.at[0, pl.ds(there, HOME)], part_z.at[k], dz=d))

    for copies in expert_near:
        arrived(copies)
    expert_far = [links.send(block, block, dx=1) for block in expert_blocks(x_before, 0)]
    expert_far += [links.send(block, block, dx=-1) for block in expert_blocks(x_after, 1)]
    arrived(grad_far)
    siblings.append(links.send(grad_all.at[y_far, own_rows], grad_all.at[y_far, own_rows], dc=1))

    arrived(z_sum)
    home_first = pl.multiple_of(quarter + z * HOME, HOME)
    home_rows = pl.ds(home_first, HOME)
    summed = part[0, pl.ds(pl.multiple_of(z * HOME, HOME), HOME), :].astype(F32)
    for k in range(3):
        summed = summed + part_z[k].astype(F32)
    home_tokens = tok[home_rows, :].astype(F32)
    hidden = home_tokens + summed
    hidden_out[...] = hidden
    home_scale_out[...] = jnp.broadcast_to(rms_scale(home_tokens), (HOME, 128))
    home_ref[...] = (hidden * rms_scale(hidden) * moe_gains).astype(BF)
    place_home = pltpu.make_async_copy(home_ref, moe_in_all.at[y, c, z], local_sems.at[6])
    place_home.start()
    keep_weights = pltpu.make_async_copy(weights, weights_out, local_sems.at[7])
    keep_weights.start()
    place_home.wait()
    siblings += spread(links, moe_in_all, home_ref, y, z, c)
    arrived(expert_far)
    arrived(picked_near)
    arrived(siblings)
    local[4].wait()
    local[5].wait()
    keep_weights.wait()

    for copy in links.made:
        if copy is not later:
            copy.wait_send()

    @pl.when(ctx == 0)
    def _():
        later.wait_send()


FRONT_COPIES = 6 + 14 + 8 + 3 + 1 + 4 + 24


def run_front(tok, own_weights, tables, segments, gate, up, down, grad, picked):
    shape = jax.ShapeDtypeStruct
    outs = (
        (shape((4, 2, WROWS, WCOLS), BF), ANY),
        (shape((4, 4, 2, 256, 256), BF), ANY),
        (shape((4, 128, WIDTH), BF), ANY),
        (shape((4, ROWS, WIDTH), BF), ANY),
        (shape((4, ROWS, 128), BF), ANY),
        (shape((4, 2, 4, HOME, WIDTH), BF), ANY),
        (shape((ROWS, WIDTH), BF), VMEM),
        (shape((ROWS, 512), F32), VMEM),
        (shape((ROWS, 512), BF), VMEM),
        (shape((ROWS, 512), BF), VMEM),
        (shape((ROWS, 256), BF), VMEM),
        (shape((4, ROWS, 128), F32), VMEM),
        (shape((HOME, WIDTH), F32), VMEM),
        (shape((HOME, 128), F32), VMEM),
    )
    return pl.pallas_call(
        front,
        out_shape=[o for o, _ in outs],
        in_specs=[VMEM] * 6 + [ANY] * 5,
        out_specs=[spec for _, spec in outs],
        scratch_shapes=[
            pltpu.VMEM((4, 2, WROWS, WCOLS), BF),
            pltpu.VMEM((ROWS, 512), BF),
            pltpu.VMEM((2, ROWS, ROWS), F32),
            pltpu.VMEM((2, ROWS, 128), F32),
            pltpu.VMEM((2, HALF, WIDTH), BF),
            pltpu.VMEM((HALF, WIDTH), BF),
            pltpu.VMEM((3, HOME, WIDTH), BF),
            pltpu.VMEM((HOME, WIDTH), BF),
            pltpu.SemaphoreType.DMA((FRONT_COPIES,)),
            pltpu.SemaphoreType.DMA((FRONT_COPIES,)),
            pltpu.SemaphoreType.DMA((8,)),
        ],
        compiler_params=pltpu.CompilerParams(
            collective_id=1, has_side_effects=True, vmem_limit_bytes=56 * MIB
        ),
        name="front",
    )(
        tok,
        own_weights,
        jnp.asarray(tables[0]),
        jnp.asarray(tables[1]),
        segments.reshape(-1, 1),
        segments,
        gate,
        up,
        down,
        grad,
        picked,
    )


MCOLS = 1664


def at(first, size):
    return pl.ds(pl.multiple_of(first, size), size)


def scatter_buffers():
    return [
        pltpu.VMEM((4, HALF, WIDTH), BF),
        pltpu.VMEM((2, 2, 32, WIDTH), BF),
        pltpu.VMEM((2, 4, 32, WIDTH), BF),
        pltpu.VMEM((3, 32, WIDTH), BF),
        pltpu.VMEM((4, 3, 32, WIDTH), BF),
        pltpu.VMEM((3, 32, WIDTH), BF),
    ]


class TokenSum:
    def __init__(self, links, give, keep, landings):
        self.links, self.give, self.keep = links, give, keep
        self.core_in, self.p_one_in, self.p_two_in, self.p_three_in, self.q_one_in, self.q_two_in = landings
        self.core, self.p_one, self.p_two, self.q_one, self.q_two = {}, [], [], {}, []

    def give_core(self, k):
        self.core[k] = self.links.send(self.give.at[k], self.core_in.at[k], dc=1)

    def q_part(self, k, place):
        return self.keep.at[k, at(place * HOME + 32, 32)]

    def add(self, k):
        links, keep = self.links, self.keep
        z = links.here[2]
        self.core[k].wait_recv()
        keep[k] = (keep[k].astype(F32) + self.core_in[k].astype(F32)).astype(BF)
        self.q_one[k] = [
            links.send(
                self.q_part(k, lax.rem(z + d + 4, 4)), self.q_one_in.at[k, n], dz=d
            )
            for n, d in enumerate((1, -1, 2))
        ]
        rows = keep.at[k].reshape(4, HOME, WIDTH)
        first = pl.ds(0, 32)
        if k == 0:
            self.p_one = [
                links.send(rows.at[pl.ds(0, 2), first], self.p_one_in.at[0], dy=1),
                links.send(rows.at[pl.ds(2, 2), first], self.p_one_in.at[1], dy=-1),
            ]
        elif k < 3:
            n = k - 1
            self.p_one[n].wait_recv()
            for i in range(2):
                row = (2 * n + i) * HOME
                keep[k, row : row + 32] = (
                    keep[k, row : row + 32].astype(F32) + self.p_one_in[n, i].astype(F32)
                ).astype(BF)
            self.p_two.append(
                links.send(rows.at[:, first], self.p_two_in.at[n], dy=(1, -1)[n])
            )

    def q_sum(self, k):
        z = self.links.here[2]
        for copy in self.q_one[k]:
            copy.wait_recv()
        part = self.keep[k, at(z * HOME + 32, 32), :].astype(F32)
        for n in range(3):
            part = part + self.q_one_in[k, n].astype(F32)
        return part

    def q_send(self, k, buffer):
        buffer[k] = self.q_sum(k).astype(BF)
        self.q_two.append(
            self.links.send(buffer.at[k], self.q_two_in.at[k], dy=(2, 1, -1)[k])
        )

    def p_send(self):
        links, keep = self.links, self.keep
        z = links.here[2]
        arrived(self.p_two)
        for place in range(4):
            row = place * HOME
            keep[3, row : row + 32] = (
                keep[3, row : row + 32].astype(F32)
                + self.p_two_in[0, place].astype(F32)
                + self.p_two_in[1, place].astype(F32)
            ).astype(BF)
        self.p_three = [
            links.send(
                keep.at[3, at(lax.rem(z + d + 4, 4) * HOME, 32)], self.p_three_in.at[n], dz=d
            )
            for n, d in enumerate((1, -1, 2))
        ]

    def home(self):
        z = self.links.here[2]
        second = self.q_sum(3)
        arrived(self.q_two)
        for n in range(3):
            second = second + self.q_two_in[n].astype(F32)
        arrived(self.p_three)
        first = self.keep[3, at(z * HOME, 32), :].astype(F32)
        for n in range(3):
            first = first + self.p_three_in[n].astype(F32)
        return first, second


TOKEN_SUM_COPIES = 4 + 12 + 2 + 2 + 3 + 3


def spread_home(links, array, home_ref):
    x, y, z, c = links.here
    return [links.send(home_ref, array.at[c, z], dz=d) for d in (1, -1, 2)]


def experts(
    x_all, g_all, picked_all, w_in_hbm, w_out_hbm, weights, hidden_ref,
    gated_out, grad_out, grad_near_out, low_all, hidden_grad_out, gain_out,
    w_in, w_out, gain_ref, x_ref, g_ref, picked_ref, gates_ref, gate_grad_ref, back_ref, pre_ref,
    gated_ref, give, keep, grad_ref, q_buffer, home_ref,
    core_in, p_one_in, p_two_in, p_three_in, q_one_in, q_two_in,
    send_sems, recv_sems, local_sems,
):
    links = Links(send_sems, recv_sems)
    x, y, z, c = links.here
    x_after, x_before, x_far = lax.rem(x + 1, 4), lax.rem(x + 3, 4), lax.rem(x + 2, 4)
    order = (lax.rem(y + 2, 4), lax.rem(y + 1, 4), lax.rem(y + 3, 4), y)
    loads = []

    def load(source, target):
        copy = pltpu.make_async_copy(source, target, local_sems.at[len(loads)])
        copy.start()
        loads.append(copy)
        return copy

    first = [load(g_all.at[order[0]], g_ref.at[0]), load(w_out_hbm, w_out)]
    first += [load(picked_all.at[place], picked_ref.at[k]) for k, place in enumerate(order)]
    first.append(load(weights.at[:, :, pl.ds(0, 256), pl.ds(768, 128)], w_in.at[:, :, :, pl.ds(1024, 128)]))
    first.append(load(weights.at[:, :, pl.ds(256, 16), pl.ds(0, 256)], gain_ref))
    first.append(load(x_all.at[order[0]], x_ref.at[0]))
    first += [
        load(w_in_hbm.at[e], w_in.at[:, :, :, pl.ds(e * 256, 256)]) for e in range(4)
    ]
    rest = [
        [load(g_all.at[order[k]], g_ref.at[k]), load(x_all.at[order[k]], x_ref.at[k])]
        for k in range(1, 4)
    ]
    links.greet(STEPS_X + STEPS_Y + STEPS_Z + STEPS_C)
    for copy in first:
        copy.wait()

    sums = TokenSum(links, give, keep, (core_in, p_one_in, p_two_in, p_three_in, q_one_in, q_two_in))
    lanes = lax.broadcasted_iota(jnp.int32, (ROWS, 128), 1)
    own_rows = at(c * HALF, HALF)
    other_rows = at((1 - c) * HALF, HALF)

    def in_block(first_column, size):
        return w_in[:, :, :, pl.ds(first_column, size)].reshape(WIDTH, size)

    for k in range(4):
        if k:
            for copy in rest[k - 1]:
                copy.wait()
        logits = dot(x_ref[k], in_block(1024, 128))
        logits = jnp.where(picked_ref[k].astype(F32) > 0.5, logits, MASKED_SCORE)
        exponents = jnp.exp(logits - jnp.max(logits, axis=-1, keepdims=True))
        gates_ref[...] = exponents / jnp.sum(exponents, axis=-1, keepdims=True)
        gate_grad_ref[...] = jnp.zeros_like(gate_grad_ref)
        back_ref[...] = dot_nt(g_ref[k], w_out[...].reshape(512, WIDTH))

        def one_expert(e, carry, k=k):
            joined = dot(x_ref[k], in_block(pl.multiple_of(e * 256, 256), 256))
            gate_pre, up_pre = joined[:, :128], joined[:, 128:]
            logistic = 1.0 / (1.0 + jnp.exp(-gate_pre))
            silu_gate = gate_pre * logistic
            silu_slope = logistic * (1.0 + gate_pre * (1.0 - logistic))
            act = silu_gate * up_pre
            back = back_ref[:, at(e * 128, 128)]
            mine = lanes == y * 4 + e
            gate = jnp.sum(jnp.where(mine, gates_ref[...], 0.0), axis=-1, keepdims=True)
            term = jnp.sum(act.astype(BF).astype(F32) * back, axis=-1, keepdims=True)
            gate_grad_ref[...] += jnp.where(mine, term, 0.0)
            act_grad = back * gate
            pre_ref[k, :, pl.ds(pl.multiple_of(e * 256, 256), 128)] = (
                act_grad * up_pre * silu_slope
            ).astype(BF)
            pre_ref[k, :, pl.ds(pl.multiple_of(e * 256 + 128, 128), 128)] = (
                act_grad * silu_gate
            ).astype(BF)
            gated_ref[k, :, at(e * 128, 128)] = (act * gate).astype(BF)
            return carry

        lax.fori_loop(0, 4, one_expert, 0)
        gates, gate_grad = gates_ref[...], gate_grad_ref[...]
        logit_grad = gates * (gate_grad - jnp.sum(gates * gate_grad, axis=-1, keepdims=True))
        pre_ref[k, :, 1024:1152] = logit_grad.astype(BF)

        def back_rows(rows, target, k=k):
            def one_block(s, carry):
                block = w_in[s // 2, lax.rem(s, 2)]
                target[k, :, at(s * 256, 256)] = dot_nt(pre_ref[k, rows, :], block).astype(BF)
                return carry

            lax.fori_loop(0, 8, one_block, 0)

        back_rows(other_rows, give)
        sums.give_core(k)
        back_rows(own_rows, keep)
        if k:
            sums.q_send(k - 1, q_buffer)
        sums.add(k)
    sums.p_send()
    keep_gated = pltpu.make_async_copy(gated_ref, gated_out, local_sems.at[len(loads)])
    keep_gated.start()

    def weight_grad(slot):
        columns = at(slot * 256, 256)
        rows = x_ref[:, :, columns].reshape(4 * ROWS, 256)
        grad_ref[slot, :, 0:1152] = dot_tn(rows, pre_ref[...].reshape(4 * ROWS, 1152)).astype(BF)
        rows = g_ref[:, :, columns].reshape(4 * ROWS, 256)
        grad_ref[slot, :, 1152:MCOLS] = dot_tn(rows, gated_ref[...].reshape(4 * ROWS, 512)).astype(BF)

    def weight_grads(place):
        def one_slot(i, carry):
            weight_grad(place * 2 + i)
            return carry

        lax.fori_loop(0, 2, one_slot, 0)

    weight_grads(x_far)
    near = [
        links.send(grad_ref.at[x_far * 2], grad_near_out.at[0], dx=1),
        links.send(grad_ref.at[x_far * 2 + 1], grad_near_out.at[1], dx=-1),
    ]

    moe_gains = jnp.concatenate(
        [gain_ref[s // 2, s % 2].astype(F32)[1:2] for s in range(8)], axis=1
    )
    moe_grad = jnp.concatenate(sums.home(), axis=0)
    hidden = hidden_ref[...]
    home_grad = g_ref[3, at(c * HALF + z * HOME, HOME), :].astype(F32)
    back, gain_rows = norm_back(moe_grad, hidden, rms_scale(hidden), moe_gains)
    hidden_grad = home_grad + back
    hidden_grad_out[...] = hidden_grad
    gain_out[...] = jnp.broadcast_to(jnp.sum(gain_rows, axis=0, keepdims=True), (8, WIDTH))
    home_ref[...] = hidden_grad.astype(BF)
    place_home = pltpu.make_async_copy(home_ref, low_all.at[c, z], local_sems.at[len(loads) + 1])
    place_home.start()
    low_near = spread_home(links, low_all, home_ref)

    def other_grads(i, carry):
        weight_grad(lax.rem(x_far * 2 + 2 + i, 8))
        return carry

    lax.fori_loop(0, 6, other_grads, 0)
    arrived(low_near)
    place_home.wait()
    sibling = links.send(low_all.at[c], low_all.at[c], dc=1)
    keep_grad = pltpu.make_async_copy(grad_ref, grad_out, local_sems.at[len(loads) + 2])
    keep_grad.start()
    arrived(near)
    sibling.wait_recv()
    keep_gated.wait()
    keep_grad.wait()
    links.finish()


EXPERT_COPIES = TOKEN_SUM_COPIES + 2 + 3 + 1


def run_experts(moe_in_all, grad_all, picked_all, experts_in, experts_out, weights, hidden):
    shape = jax.ShapeDtypeStruct
    outs = (
        (shape((4, ROWS, 512), BF), ANY),
        (shape((8, 256, MCOLS), BF), ANY),
        (shape((2, 256, MCOLS), BF), ANY),
        (shape((2, 4, HOME, WIDTH), BF), ANY),
        (shape((HOME, WIDTH), F32), VMEM),
        (shape((8, WIDTH), F32), VMEM),
    )
    return pl.pallas_call(
        experts,
        out_shape=[o for o, _ in outs],
        in_specs=[ANY] * 6 + [VMEM],
        out_specs=[spec for _, spec in outs],
        scratch_shapes=[
            pltpu.VMEM((4, 2, 256, 1152), BF),
            pltpu.VMEM((4, 128, WIDTH), BF),
            pltpu.VMEM((4, 2, 16, 256), BF),
            pltpu.VMEM((4, ROWS, WIDTH), BF),
            pltpu.VMEM((4, ROWS, WIDTH), BF),
            pltpu.VMEM((4, ROWS, 128), BF),
            pltpu.VMEM((ROWS, 128), F32),
            pltpu.VMEM((ROWS, 128), F32),
            pltpu.VMEM((ROWS, 512), F32),
            pltpu.VMEM((4, ROWS, 1152), BF),
            pltpu.VMEM((4, ROWS, 512), BF),
            pltpu.VMEM((4, HALF, WIDTH), BF),
            pltpu.VMEM((4, HALF, WIDTH), BF),
            pltpu.VMEM((8, 256, MCOLS), BF),
            pltpu.VMEM((3, 32, WIDTH), BF),
            pltpu.VMEM((HOME, WIDTH), BF),
            *scatter_buffers(),
            pltpu.SemaphoreType.DMA((EXPERT_COPIES,)),
            pltpu.SemaphoreType.DMA((EXPERT_COPIES,)),
            pltpu.SemaphoreType.DMA((24,)),
        ],
        compiler_params=pltpu.CompilerParams(
            collective_id=2, has_side_effects=True, vmem_limit_bytes=62 * MIB
        ),
        name="experts",
    )(
        moe_in_all.reshape(4, ROWS, WIDTH),
        grad_all,
        picked_all,
        experts_in,
        experts_out,
        weights,
        hidden,
    )


def turn_tables():
    frequency = ROPE_BASE ** (-(np.arange(0, 128, 2, dtype=np.float64) / 128))
    angles = np.arange(1024, dtype=np.float64)[:, None] * frequency[None, :]
    cosine, sine = np.cos(angles), np.sin(angles)
    return (
        np.concatenate([cosine, cosine], axis=1).astype(np.float32),
        np.concatenate([-sine, sine], axis=1).astype(np.float32),
    )


def body(
    tokens,
    out_grad,
    segments,
    routes,
    query_weight,
    key_weight,
    value_weight,
    out_weight,
    router_weight,
    attn_gain,
    moe_gain,
    query_gain,
    key_gain,
    gate_weight,
    up_weight,
    down_weight,
):
    rows, width = tokens.shape[1], tokens.shape[2]
    experts = gate_weight.shape[0]
    own_experts = experts // 4
    hidden_units = gate_weight.shape[2]
    span = own_experts * hidden_units
    shard, ctx, tp = lax.axis_index("shard"), lax.axis_index("ctx"), lax.axis_index("tp")
    x, y_low, z, core = shard // 2, shard % 2, tp // 2, tp % 2
    y = ctx * 2 + y_low
    home = rows // 8
    head_dim = 128
    local_width = 256
    score_scale = head_dim ** (-0.5)

    def spread_rows(part):
        lane = in_order(direct_gather(part, "z"), z).reshape(4 * part.shape[0], -1)
        return with_partner(lane, hop(lane, dc=1), core)

    def home_sum(terms):
        keep = lax.dynamic_slice_in_dim(terms, core * 256, 256, 0)
        give = lax.dynamic_slice_in_dim(terms, (1 - core) * 256, 256, 0)
        lane = added(keep, hop(give, dc=1)).astype(BF).reshape(4, home, -1)
        return direct_scatter(by_distance(lane, z), "z")

    def tokens_sum(terms):
        terms = terms.reshape(4, rows, -1)
        keep = lax.dynamic_slice_in_dim(terms, core * 256, 256, 1)
        give = lax.dynamic_slice_in_dim(terms, (1 - core) * 256, 256, 1)
        lane = added(keep, hop(give, dc=1)).astype(BF)
        mine = ring_scatter(by_distance(lane, y), "y").astype(BF).reshape(4, home, -1)
        return direct_scatter(by_distance(mine, z), "z")

    lanes = jnp.zeros((4, 128), BF)
    head_gains = jnp.concatenate([query_gain, key_gain], axis=0)
    lanes = lax.dynamic_update_slice_in_dim(lanes, head_gains, shard * 16, 1)
    gain_rows = jnp.zeros((16, WCOLS), BF)
    gain_rows = gain_rows.at[0, :256].set(attn_gain).at[1, :256].set(moe_gain)
    gain_rows = gain_rows.at[2:6, :128].set(lanes)
    router_pad = jnp.pad(router_weight, ((0, 0), (0, 128 - experts)))
    own_weights = jnp.concatenate(
        [
            jnp.concatenate([query_weight, key_weight, value_weight, router_pad, out_weight], axis=1),
            gain_rows,
        ],
        axis=0,
    )
    own_grad = out_grad.reshape(rows, width)
    route_rows = routes.reshape(rows, -1)
    own_picked = jnp.any(
        route_rows[:, :, None] == jnp.arange(128, dtype=jnp.int32)[None, None, :], axis=1
    ).astype(BF)
    (
        weights, experts_in, experts_out, grad_all, picked_all, moe_in_all,
        normed, pre, rot, key_value, mixed_low, lse, hidden, home_scale_one,
    ) = run_front(
        tokens.reshape(rows, width), own_weights, turn_tables(), segments,
        gate_weight, up_weight, down_weight, own_grad, own_picked,
    )
    gated, grad_moe, grad_near, hidden_low, hidden_grad, gain_sum = run_experts(
        moe_in_all, grad_all, picked_all, experts_in, experts_out, weights, hidden
    )
    hidden_low = hidden_low.reshape(rows, width)
    weights = weights.reshape(8, WROWS, WCOLS)
    w_stacked = weights[:, :256, :768].reshape(width, -1)
    w_out_t = weights[:, :256, 896:].transpose(0, 2, 1).reshape(width, -1)
    gain_rows = weights[:, 256:].astype(F32)
    attn_gains = gain_rows[:, 0, :256].reshape(-1)
    moe_gains = gain_rows[:, 1, :256].reshape(-1)
    head_gains = jnp.sum(gain_rows[:, 2:6, :128], axis=0)

    inputs = tokens.reshape(rows, width).astype(F32)
    first_row = ctx * rows
    places = first_row + jnp.arange(rows, dtype=jnp.int32)
    cosine, sine_table = rope_tables(places, head_dim)
    query_pre = [pre[:, h * 128 : h * 128 + 128] for h in range(2)]
    key_pre = [pre[:, 256 + h * 128 : 384 + h * 128] for h in range(2)]
    scale_query = [rms_scale(v) for v in query_pre]
    scale_key = [rms_scale(v) for v in key_pre]
    gain_q = [head_gains[h][None] for h in range(2)]
    gain_k = [head_gains[2 + h][None] for h in range(2)]
    query_low = [rot[:, h * 128 : h * 128 + 128] for h in range(2)]
    earlier = hop(key_value, dy=2, only=lambda x, y, z, c: y < 2)
    both = jnp.concatenate([earlier, key_value], axis=0)
    keys = [both[:, h * 128 : h * 128 + 128] for h in range(2)]
    values = [both[:, 256 + h * 128 : 384 + h * 128] for h in range(2)]
    key_places = first_row - rows + jnp.arange(2 * rows, dtype=jnp.int32)
    own_segments = lax.dynamic_slice_in_dim(segments[0], first_row, rows, 0)
    key_segments = jnp.concatenate([segments[0, :rows], own_segments])
    allowed = (
        (places[:, None] >= key_places[None, :])
        & (key_places[None, :] >= 0)
        & (own_segments[:, None] == key_segments[None, :])
    )
    probs = []
    for h in range(2):
        scores = jnp.where(allowed, dot_nt(query_low[h], keys[h]) * score_scale, MASKED_SCORE)
        probs.append(jnp.exp(scores - lse[h][:, :1]))
    home_row = (core * 4 + z) * home
    home_inputs = lax.dynamic_slice_in_dim(tokens.reshape(rows, width), home_row, home, 0).astype(F32)
    home_scale_one = home_scale_one[:, :1]

    moe_part = dot(gated.reshape(4 * rows, -1), experts_out.reshape(-1, width)).astype(BF)
    far, after, before, mine = [moe_part[k * rows : k * rows + rows] for k in range(4)]
    moe_part = in_order([mine, after, far, before], y).reshape(4 * rows, width)
    layer_rows = (hidden + tokens_sum(moe_part)).astype(BF)
    layer_out = spread_rows(layer_rows).reshape(tokens.shape)
    own_chunk, to_after, _, to_before = by_distance(grad_moe.reshape(4, 2, 256, -1), x)
    to_after = jnp.stack([added(to_after[0], grad_near[0]).astype(BF), to_after[1]])
    to_before = jnp.stack([to_before[0], added(to_before[1], grad_near[1]).astype(BF)])
    grad_moe = added(own_chunk, hop(to_after, dx=1), hop(to_before, dx=-1))
    grad_router = jnp.concatenate(
        [grad_moe[0, :, 1024 : 1024 + experts], grad_moe[1, :, 1024 : 1024 + experts]], axis=0
    ).T.reshape(-1, 128)
    grad_moe = grad_moe.astype(BF)
    keep = lax.dynamic_index_in_dim(grad_moe, y_low, 0, keepdims=False)
    give = lax.dynamic_index_in_dim(grad_moe, 1 - y_low, 0, keepdims=False)
    grad_groups = in_order(
        [keep, hop(give, dy=-1), hop(keep, dy=2), hop(give, dy=1)], y
    )
    joined = grad_groups[:, :, :1024].reshape(4, 256, own_experts, 256).transpose(0, 2, 1, 3)
    grad_gate_weight = joined[..., :128].reshape(experts, 256, hidden_units).astype(F32)
    grad_up_weight = joined[..., 128:].reshape(experts, 256, hidden_units).astype(F32)
    grad_down_weight = (
        grad_groups[:, :, 1152:]
        .reshape(4, 256, own_experts, hidden_units)
        .transpose(0, 2, 3, 1)
        .reshape(experts, hidden_units, 256)
        .astype(F32)
    )
    grad_router = grad_router + hop(grad_router, dc=1)
    for axis in "zy":
        grad_router = direct_scatter([grad_router] * 4, axis)
    grad_router = grad_router.reshape(experts, 2, 256)
    grad_router = lax.dynamic_index_in_dim(grad_router, y_low, 1, keepdims=False).T
    early = gain_sum[0].reshape(-1, 128)
    early = early + hop(early, dc=1)
    for axis in "zyx":
        early = direct_scatter([early] * 4, axis)
    grad_moe_gain = lax.dynamic_slice_in_dim(early.reshape(-1), shard * 256, 256, 0)

    mixed_grad = dot(hidden_low, w_out_t).astype(BF)
    grad_out_t = dot_tn(hidden_low, mixed_low)
    query_grads, key_terms, value_terms = [], [], []
    for h in range(2):
        grad_h = mixed_grad[:, h * 128 : h * 128 + 128]
        prob_grad = dot_nt(grad_h, values[h])
        row_delta = jnp.sum(probs[h] * prob_grad, axis=-1, keepdims=True)
        score_grad = (probs[h] * (prob_grad - row_delta)).astype(BF)
        query_grads.append((dot(score_grad, keys[h]) * score_scale).astype(BF).astype(F32))
        key_terms.append(dot_tn(score_grad, query_low[h]) * score_scale)
        value_terms.append(dot_tn(probs[h].astype(BF), grad_h))
    terms = jnp.concatenate(key_terms + value_terms, axis=1)
    later = hop(terms[:rows].astype(BF), dy=2, only=lambda x, y, z, c: y >= 2)
    key_value_grad = added(terms[rows:], later).astype(BF)
    stacked, gain_sums = [], []
    for pre, scale, gain, grads in (
        (query_pre, scale_query, gain_q, query_grads),
        (key_pre, scale_key, gain_k, [key_value_grad[:, :128], key_value_grad[:, 128:256]]),
    ):
        for h in range(2):
            unit_grad = rotate(grads[h].astype(F32), cosine, -sine_table)
            pre_back, gain_rows = norm_back(unit_grad, pre[h], scale[h], gain[h])
            stacked.append(pre_back.astype(BF))
            gain_sums.append(jnp.sum(gain_rows, axis=0))
    stacked = jnp.concatenate(stacked + [key_value_grad[:, 256:]], axis=1)
    normed_part = dot_nt(stacked, w_stacked).astype(BF)
    grad_stacked = dot_tn(normed, stacked)
    normed_grad = home_sum(normed_part)
    input_norm_grad, attn_gain_rows = norm_back(
        normed_grad, home_inputs, home_scale_one, attn_gains
    )
    input_grad = spread_rows((hidden_grad + input_norm_grad).astype(BF)).reshape(tokens.shape)
    grad_attn = jnp.concatenate([grad_stacked, grad_out_t], axis=1).astype(BF)
    grad_attn = ring_scatter(by_distance(grad_attn.reshape(4, 512, -1), x), "x").astype(BF)
    grad_attn = grad_attn.reshape(2, 256, -1)
    keep = lax.dynamic_index_in_dim(grad_attn, y_low, 0, keepdims=False)
    give = lax.dynamic_index_in_dim(grad_attn, 1 - y_low, 0, keepdims=False)
    got = jnp.concatenate([hop(give[:128], dy=1), hop(give[128:], dy=-1)], axis=0)
    keep = added(keep, got).astype(BF)
    grad_attn = added(keep, hop(keep, dy=2))
    head_gain_sums = jnp.stack(gain_sums).reshape(2, 1, 2, 128)
    mine = (jnp.arange(8) == tp).astype(F32)[None, :, None, None]
    late = jnp.concatenate(
        [jnp.sum(attn_gain_rows, axis=0), (mine * head_gain_sums).reshape(-1)]
    ).reshape(48, 128)
    late = late + hop(late, dc=1)
    for axis in "zyx":
        late = direct_scatter([late] * 4, axis)
    grad_attn_gain = lax.dynamic_slice_in_dim(late[:16].reshape(-1), shard * 256, 256, 0)
    late_heads = late[16:].reshape(2, 8, 2, 128)
    late_heads = lax.dynamic_index_in_dim(late_heads, tp, 1, keepdims=False)
    late_heads = lax.dynamic_slice_in_dim(late_heads, shard * 16, 16, 2)
    return (
        layer_out,
        input_grad,
        grad_attn[:, :256],
        grad_attn[:, 256:512],
        grad_attn[:, 512:768],
        grad_attn[:, 768:].T,
        grad_router,
        grad_attn_gain,
        grad_moe_gain,
        late_heads[0],
        late_heads[1],
        grad_gate_weight,
        grad_up_weight,
        grad_down_weight,
    )


def solution(mesh):
    return jax.shard_map(
        body,
        mesh=mesh,
        in_specs=(
            P("shard", "ctx", None),
            P("shard", "ctx", None),
            P("shard", None),
            P("shard", "ctx", None),
            P("shard", "tp"),
            P("shard", "tp"),
            P("shard", "tp"),
            P("tp", "shard"),
            P("shard", None),
            P("shard"),
            P("shard"),
            P("tp", "shard"),
            P("tp", "shard"),
            P(None, "shard", "tp"),
            P(None, "shard", "tp"),
            P(None, "tp", "shard"),
        ),
        out_specs=(
            P("shard", "ctx", None),
            P("shard", "ctx", None),
            P("shard", "tp"),
            P("shard", "tp"),
            P("shard", "tp"),
            P("tp", "shard"),
            P("shard", None),
            P("shard"),
            P("shard"),
            P("tp", "shard"),
            P("tp", "shard"),
            P(None, "shard", "tp"),
            P(None, "shard", "tp"),
            P(None, "tp", "shard"),
        ),
        check_vma=False,
    )
```

```python
import jax
import jax.numpy as jnp
import numpy as np
from jax import lax
from jax.experimental import pallas as pl
from jax.experimental.pallas import tpu as pltpu
from jax.sharding import PartitionSpec as P

EPSILON = 1e-05
ROPE_BASE = 10000.0
MASKED_SCORE = -1e30
AXES = ("shard", "ctx", "tp")
BF = jnp.bfloat16
F32 = jnp.float32

def rms_scale(values):
    return lax.rsqrt(jnp.mean(values * values, axis=-1, keepdims=True) + EPSILON)


def norm_back(grad_normed, source, scale_row, gain_row):
    unit_values = source * scale_row
    grad_unit = grad_normed * gain_row
    grad_source = scale_row * (
        grad_unit - unit_values * jnp.mean(grad_unit * unit_values, axis=-1, keepdims=True)
    )
    return (grad_source, grad_normed * unit_values)


def dot(left, right):
    return jnp.dot(left, right, preferred_element_type=F32)


def dot_nt(left, right):
    return lax.dot_general(left, right, (((1,), (1,)), ((), ())), preferred_element_type=F32)


def dot_tn(left, right):
    return lax.dot_general(left, right, (((0,), (0,)), ((), ())), preferred_element_type=F32)


ANY = pl.BlockSpec(memory_space=pl.ANY)
VMEM = pl.BlockSpec(memory_space=pltpu.VMEM)
MIB = 1024 * 1024
ROWS, WIDTH, HOME, HALF = 512, 2048, 64, 256
WROWS, WCOLS = 272, 1152


def places():
    shard, ctx, tp = lax.axis_index("shard"), lax.axis_index("ctx"), lax.axis_index("tp")
    return shard // 2, ctx * 2 + shard % 2, tp // 2, tp % 2


def device(x, y, z, c):
    x, y, z, c = lax.rem(x + 4, 4), lax.rem(y + 4, 4), lax.rem(z + 4, 4), lax.rem(c + 2, 2)
    return {"shard": x * 2 + lax.rem(y, 2), "ctx": y // 2, "tp": z * 2 + c}


def at(first, size):
    return pl.ds(pl.multiple_of(first, size), size)


class Links:
    def __init__(self, send_sems, recv_sems):
        self.here = places()
        self.send_sems, self.recv_sems, self.made, self.count = send_sems, recv_sems, [], 0

    def send(self, source, target, dx=0, dy=0, dz=0, dc=0, start=True):
        x, y, z, c = self.here
        number = self.count
        self.count += 1
        copy = pltpu.make_async_remote_copy(
            src_ref=source,
            dst_ref=target,
            send_sem=self.send_sems.at[number],
            recv_sem=self.recv_sems.at[number],
            device_id=device(x + dx, y + dy, z + dz, c + dc),
            device_id_type=pl.DeviceIdType.MESH,
        )
        self.made.append(copy)
        if start:
            copy.start()
        return copy

    def left(self, copy):
        copy.wait_send()
        self.made = [other for other in self.made if other is not copy]

    def finish(self):
        for copy in self.made:
            copy.wait_send()

    def greet(self, steps):
        x, y, z, c = self.here
        barrier = pltpu.get_barrier_semaphore()
        for dx, dy, dz, dc in steps:
            pl.semaphore_signal(
                barrier,
                inc=1,
                device_id=device(x + dx, y + dy, z + dz, c + dc),
                device_id_type=pl.DeviceIdType.MESH,
            )
        pl.semaphore_wait(barrier, len(steps))


STEPS_X = [(1, 0, 0, 0), (-1, 0, 0, 0)]
STEPS_Y = [(0, 1, 0, 0), (0, -1, 0, 0), (0, 2, 0, 0)]
STEPS_Z = [(0, 0, 1, 0), (0, 0, -1, 0), (0, 0, 2, 0)]
STEPS_C = [(0, 0, 0, 1)]


def arrived(copies):
    for copy in copies:
        copy.wait_recv()


def turned(values, cosine, sine):
    return values * cosine + pltpu.roll(values, 64, 1) * sine


def spread(links, array, home_ref, y, z, c):
    first, second = pl.ds(0, 32), pl.ds(32, 32)
    y_after, y_before, y_far = lax.rem(y + 1, 4), lax.rem(y + 3, 4), lax.rem(y + 2, 4)
    z_after, z_before, z_far = lax.rem(z + 1, 4), lax.rem(z + 3, 4), lax.rem(z + 2, 4)
    p_one = [
        links.send(home_ref.at[first], array.at[y, c, z, first], dz=d) for d in (1, -1, 2)
    ]
    q_one = [
        links.send(home_ref.at[second], array.at[y, c, z, second], dy=d) for d in (1, -1, 2)
    ]

    def p_block(place):
        return array.at[place, c, :, first]

    def q_block(place):
        return array.at[:, c, place, second]

    arrived(p_one)
    p_two = [links.send(p_block(y), p_block(y), dy=d) for d in (1, -1)]
    sibling = [links.send(p_block(y), p_block(y), dc=1)]
    arrived(q_one)
    q_two = [links.send(q_block(z), q_block(z), dz=d) for d in (1, -1)]
    sibling.append(links.send(q_block(z), q_block(z), dc=1))
    p_two[0].wait_recv()
    low, high = pl.ds(0, 2), pl.ds(2, 2)
    ahead = array.at[y_before, c, low, first]
    p_far = [links.send(ahead, ahead, dy=1)]
    sibling.append(links.send(p_block(y_before), p_block(y_before), dc=1))
    q_two[0].wait_recv()
    ahead = array.at[low, c, z_before, second]
    q_far = [links.send(ahead, ahead, dz=1)]
    sibling.append(links.send(q_block(z_before), q_block(z_before), dc=1))
    p_two[1].wait_recv()
    behind = array.at[y_after, c, high, first]
    p_far.append(links.send(behind, behind, dy=-1))
    sibling.append(links.send(p_block(y_after), p_block(y_after), dc=1))
    q_two[1].wait_recv()
    behind = array.at[high, c, z_after, second]
    q_far.append(links.send(behind, behind, dz=-1))
    sibling.append(links.send(q_block(z_after), q_block(z_after), dc=1))
    arrived(p_far)
    sibling.append(links.send(p_block(y_far), p_block(y_far), dc=1))
    arrived(q_far)
    sibling.append(links.send(q_block(z_far), q_block(z_far), dc=1))
    return sibling


def own_mask(segment_rows, segment_row, own_first):
    rows_at = lax.broadcasted_iota(jnp.int32, (ROWS, ROWS), 0)
    cols_at = lax.broadcasted_iota(jnp.int32, (ROWS, ROWS), 1)
    same = segment_rows[own_first, :] == segment_row[:, own_first]
    return jnp.where(same & (rows_at >= cols_at), 0.0, MASKED_SCORE)


def earlier_mask(segment_rows, segment_row, own_first):
    same = segment_rows[own_first, :] == segment_row[:, pl.ds(0, ROWS)]
    return jnp.where(same, 0.0, MASKED_SCORE)


def front(
    tok, own_weights, cosine_ref, sine_ref, segment_rows, segment_row, gate, up, down, grad, picked,
    weights_out, experts_in, experts_out, grad_all, picked_all, moe_in_all,
    normed_out, pre_out, rot_out, kv_out, kv_far, mixed_out, lse_out, hidden_out, home_scale_out,
    weights, biases, accs, part, part_core, part_z, home_ref,
    send_sems, recv_sems, local_sems,
):
    links = Links(send_sems, recv_sems)
    x, y, z, c = links.here
    ctx, y_low = y // 2, lax.rem(y, 2)
    x_after, x_before = lax.rem(x + 1, 4), lax.rem(x + 3, 4)
    y_after, y_before, y_far = lax.rem(y + 1, 4), lax.rem(y + 3, 4), lax.rem(y + 2, 4)
    own = c * HALF
    links.greet(STEPS_X + STEPS_Y + STEPS_Z + STEPS_C)

    low, high = pl.ds(0, 128), pl.ds(128, WROWS - 128)
    slot = weights.at[x, y_low]
    pair = [
        links.send(own_weights.at[low], slot.at[low], dy=1),
        links.send(own_weights.at[high], slot.at[high], dy=-1),
    ]
    local = [pltpu.make_async_copy(own_weights, slot, local_sems.at[0])]

    def mine(array, group):
        return array.at[pl.ds(group * 4, 4)]

    def columns(place, low_place):
        return pl.ds(pl.multiple_of(place * 512 + low_place * 256, 256), 256)

    local.append(
        pltpu.make_async_copy(
            mine(gate, y), experts_in.at[:, x, y_low, :, pl.ds(0, 128)], local_sems.at[1]
        )
    )
    local.append(
        pltpu.make_async_copy(
            mine(up, y), experts_in.at[:, x, y_low, :, pl.ds(128, 128)], local_sems.at[2]
        )
    )
    local.append(
        pltpu.make_async_copy(
            mine(down, y), experts_out.at[:, :, columns(x, y_low)], local_sems.at[3]
        )
    )
    own_rows = pl.ds(pl.multiple_of(own, HALF), HALF)
    local.append(pltpu.make_async_copy(grad, grad_all.at[y], local_sems.at[4]))
    local.append(pltpu.make_async_copy(picked, picked_all.at[y], local_sems.at[5]))
    for copy in local:
        copy.start()
    local[0].wait()
    arrived(pair)
    near = [links.send(weights.at[x], weights.at[x], dx=d) for d in (1, -1)]

    expert_pair = []
    for group, start, step in ((y_after, 0, 1), (y_before, 2, -1)):
        some = pl.ds(group * 4 + start, 2)
        there = pl.ds(start, 2)
        expert_pair += [
            links.send(
                gate.at[some], experts_in.at[there, x, y_low, :, pl.ds(0, 128)], dy=step
            ),
            links.send(
                up.at[some], experts_in.at[there, x, y_low, :, pl.ds(128, 128)], dy=step
            ),
            links.send(down.at[some], experts_out.at[there, :, columns(x, y_low)], dy=step),
        ]
    grad_near = [
        links.send(grad.at[own_rows], grad_all.at[y, own_rows], dy=d) for d in (1, -1)
    ]
    picked_near = [links.send(picked, picked_all.at[y], dy=d) for d in (1, -1, 2)]

    own_first = at(ctx * ROWS, ROWS)
    biases[0] = own_mask(segment_rows, segment_row, own_first)
    biases[1] = earlier_mask(segment_rows, segment_row, own_first)
    tokens = tok[...].astype(F32)
    scale_one = rms_scale(tokens)

    near[0].wait_recv()
    far = [links.send(weights.at[x_before, 0], weights.at[x_before, 0], dx=1)]
    near[1].wait_recv()
    far.append(links.send(weights.at[x_after, 1], weights.at[x_after, 1], dx=-1))
    arrived(far)
    for copy in local[1:4]:
        copy.wait()
    arrived(expert_pair)

    def expert_blocks(place, low_place=None):
        if low_place is None:
            cols = pl.ds(pl.multiple_of(place * 512, 512), 512)
            return experts_in.at[:, place], experts_out.at[:, :, cols]
        return experts_in.at[:, place, low_place], experts_out.at[:, :, columns(place, low_place)]

    expert_near = [
        [links.send(block, block, dx=d) for block in expert_blocks(x)] for d in (1, -1)
    ]

    gain_blocks = [weights[s // 2, s % 2, 256:272, 0:256].astype(F32) for s in range(8)]
    gains = jnp.concatenate([block[0:1] for block in gain_blocks], axis=1)
    moe_gains = jnp.concatenate([block[1:2] for block in gain_blocks], axis=1)
    head_gains = sum(block[:, 0:128] for block in gain_blocks)
    normed_out[...] = (tokens * scale_one * gains).astype(BF)

    def project(column):
        block = weights[:, :, 0:256, column * 256 : column * 256 + 256].reshape(WIDTH, 256)
        return jnp.dot(normed_out[...], block, preferred_element_type=F32)

    cosine, sine = cosine_ref[own_first, :], sine_ref[own_first, :]

    def heads(pre, first_gain, base):
        for h in range(2):
            part_h = pre[:, h * 128 : h * 128 + 128]
            unit = part_h * rms_scale(part_h) * head_gains[first_gain + h : first_gain + h + 1]
            rot_out[:, base + h * 128 : base + h * 128 + 128] = turned(unit, cosine, sine).astype(BF)

    key_pre = project(1)
    pre_out[:, 256:512] = key_pre
    heads(key_pre, 4, 256)
    kv_out[:, 0:256] = rot_out[:, 256:512]
    kv_out[:, 256:512] = project(2).astype(BF)
    later = links.send(kv_out, kv_far, dy=2, start=False)

    @pl.when(ctx == 0)
    def _():
        later.start()
        kv_far[...] = jnp.zeros_like(kv_far)

    query_pre = project(0)
    pre_out[:, 0:256] = query_pre
    heads(query_pre, 2, 0)
    score_scale = 128 ** (-0.5)
    peaks, totals = [], []
    for h in range(2):
        lane = slice(h * 128, h * 128 + 128)
        scores = dot_nt(rot_out[:, lane], kv_out[:, lane]) * score_scale + biases[0]
        peak = jnp.max(scores, axis=-1, keepdims=True)
        exponents = jnp.exp(scores - peak)
        lse_out[h] = jnp.broadcast_to(peak, (ROWS, 128))
        lse_out[2 + h] = jnp.broadcast_to(
            jnp.sum(exponents, axis=-1, keepdims=True), (ROWS, 128)
        )
        accs[h] = dot(exponents.astype(BF), kv_out[:, 256 + h * 128 : 384 + h * 128])

    arrived(grad_near)
    grad_lane = grad_all.at[:, own_rows]
    quarter = pl.multiple_of(own, HALF)
    first_half, second_half = pl.ds(quarter, 128), pl.ds(pl.multiple_of(quarter + 128, 128), 128)
    grad_far = [
        links.send(grad_all.at[y_before, first_half], grad_all.at[y_before, first_half], dy=1),
        links.send(grad_all.at[y_after, second_half], grad_all.at[y_after, second_half], dy=-1),
    ]
    siblings = [
        links.send(grad_all.at[place, own_rows], grad_all.at[place, own_rows], dc=1)
        for place in (y_before, y_after)
    ]

    @pl.when(ctx == 1)
    def _():
        later.wait_recv()
        for h in range(2):
            lane = slice(h * 128, h * 128 + 128)
            scores = dot_nt(rot_out[:, lane], kv_far[:, lane]) * score_scale + biases[1]
            old_peak = lse_out[h][:, 0:1]
            peak = jnp.maximum(old_peak, jnp.max(scores, axis=-1, keepdims=True))
            exponents = jnp.exp(scores - peak)
            old = jnp.exp(old_peak - peak)
            lse_out[h] = jnp.broadcast_to(peak, (ROWS, 128))
            lse_out[2 + h] = lse_out[2 + h] * old + jnp.sum(exponents, axis=-1, keepdims=True)
            accs[h] = accs[h] * old + dot(
                exponents.astype(BF), kv_far[:, 256 + h * 128 : 384 + h * 128]
            )

    for h in range(2):
        total = lse_out[2 + h]
        mixed_out[:, h * 128 : h * 128 + 128] = (accs[h] / total).astype(BF)
        lse_out[h] = lse_out[h] + jnp.log(total)

    other = pl.multiple_of((1 - c) * HALF, HALF)
    give_rows = mixed_out[pl.ds(other, HALF), :]
    for s in range(8):
        block = weights[s // 2, s % 2, 0:256, 896:1152]
        part[1, :, s * 256 : s * 256 + 256] = dot(give_rows, block).astype(BF)
    core_sum = links.send(part.at[1], part_core, dc=1)
    keep_rows = mixed_out[pl.ds(quarter, HALF), :]
    for s in range(8):
        block = weights[s // 2, s % 2, 0:256, 896:1152]
        part[0, :, s * 256 : s * 256 + 256] = dot(keep_rows, block).astype(BF)
    core_sum.wait_recv()
    part[0] = (part[0].astype(F32) + part_core[...].astype(F32)).astype(BF)
    z_sum = []
    for k, d in enumerate((1, -1, 2)):
        there = pl.multiple_of(lax.rem(z + d + 4, 4) * HOME, HOME)
        z_sum.append(links.send(part.at[0, pl.ds(there, HOME)], part_z.at[k], dz=d))

    for copies in expert_near:
        arrived(copies)
    expert_far = [links.send(block, block, dx=1) for block in expert_blocks(x_before, 0)]
    expert_far += [links.send(block, block, dx=-1) for block in expert_blocks(x_after, 1)]
    arrived(grad_far)
    siblings.append(links.send(grad_all.at[y_far, own_rows], grad_all.at[y_far, own_rows], dc=1))

    arrived(z_sum)
    home_first = pl.multiple_of(quarter + z * HOME, HOME)
    home_rows = pl.ds(home_first, HOME)
    summed = part[0, pl.ds(pl.multiple_of(z * HOME, HOME), HOME), :].astype(F32)
    for k in range(3):
        summed = summed + part_z[k].astype(F32)
    home_tokens = tok[home_rows, :].astype(F32)
    hidden = home_tokens + summed
    hidden_out[...] = hidden
    home_scale_out[...] = jnp.broadcast_to(rms_scale(home_tokens), (HOME, 128))
    home_ref[...] = (hidden * rms_scale(hidden) * moe_gains).astype(BF)
    place_home = pltpu.make_async_copy(home_ref, moe_in_all.at[y, c, z], local_sems.at[6])
    place_home.start()
    keep_weights = pltpu.make_async_copy(weights, weights_out, local_sems.at[7])
    keep_weights.start()
    place_home.wait()
    siblings += spread(links, moe_in_all, home_ref, y, z, c)
    arrived(expert_far)
    arrived(picked_near)
    arrived(siblings)
    local[4].wait()
    local[5].wait()
    keep_weights.wait()

    for copy in links.made:
        if copy is not later:
            copy.wait_send()

    @pl.when(ctx == 0)
    def _():
        later.wait_send()


FRONT_COPIES = 6 + 14 + 8 + 3 + 1 + 4 + 24


def run_front(tok, own_weights, tables, segments, gate, up, down, grad, picked):
    shape = jax.ShapeDtypeStruct
    outs = (
        (shape((4, 2, WROWS, WCOLS), BF), ANY),
        (shape((4, 4, 2, 256, 256), BF), ANY),
        (shape((4, 128, WIDTH), BF), ANY),
        (shape((4, ROWS, WIDTH), BF), ANY),
        (shape((4, ROWS, 128), BF), ANY),
        (shape((4, 2, 4, HOME, WIDTH), BF), ANY),
        (shape((ROWS, WIDTH), BF), VMEM),
        (shape((ROWS, 512), F32), VMEM),
        (shape((ROWS, 512), BF), VMEM),
        (shape((ROWS, 512), BF), VMEM),
        (shape((ROWS, 512), BF), VMEM),
        (shape((ROWS, 256), BF), VMEM),
        (shape((4, ROWS, 128), F32), VMEM),
        (shape((HOME, WIDTH), F32), VMEM),
        (shape((HOME, 128), F32), VMEM),
    )
    return pl.pallas_call(
        front,
        out_shape=[o for o, _ in outs],
        in_specs=[VMEM] * 6 + [ANY] * 5,
        out_specs=[spec for _, spec in outs],
        scratch_shapes=[
            pltpu.VMEM((4, 2, WROWS, WCOLS), BF),
            pltpu.VMEM((2, ROWS, ROWS), F32),
            pltpu.VMEM((2, ROWS, 128), F32),
            pltpu.VMEM((2, HALF, WIDTH), BF),
            pltpu.VMEM((HALF, WIDTH), BF),
            pltpu.VMEM((3, HOME, WIDTH), BF),
            pltpu.VMEM((HOME, WIDTH), BF),
            pltpu.SemaphoreType.DMA((FRONT_COPIES,)),
            pltpu.SemaphoreType.DMA((FRONT_COPIES,)),
            pltpu.SemaphoreType.DMA((8,)),
        ],
        compiler_params=pltpu.CompilerParams(
            collective_id=1, has_side_effects=True, vmem_limit_bytes=56 * MIB
        ),
        name="front",
    )(
        tok,
        own_weights,
        jnp.asarray(tables[0]),
        jnp.asarray(tables[1]),
        segments.reshape(-1, 1),
        segments,
        gate,
        up,
        down,
        grad,
        picked,
    )


MCOLS = 1664


def scatter_buffers():
    return [
        pltpu.VMEM((4, HALF, WIDTH), BF),
        pltpu.VMEM((2, 2, 32, WIDTH), BF),
        pltpu.VMEM((2, 4, 32, WIDTH), BF),
        pltpu.VMEM((3, 32, WIDTH), BF),
        pltpu.VMEM((4, 3, 32, WIDTH), BF),
        pltpu.VMEM((3, 32, WIDTH), BF),
    ]


class TokenSum:
    def __init__(self, links, give, keep, landings):
        self.links, self.give, self.keep = links, give, keep
        self.core_in, self.p_one_in, self.p_two_in, self.p_three_in, self.q_one_in, self.q_two_in = landings
        self.core, self.p_one, self.p_two, self.q_one, self.q_two = {}, [], [], {}, []

    def give_slot(self, k):
        slots = self.give.shape[0]
        if k >= slots:
            self.links.left(self.core[k - slots])
        return k % slots

    def give_core(self, k):
        self.core[k] = self.links.send(
            self.give.at[k % self.give.shape[0]], self.core_in.at[k], dc=1
        )

    def q_part(self, k, place):
        return self.keep.at[k, at(place * HOME + 32, 32)]

    def add(self, k):
        links, keep = self.links, self.keep
        z = links.here[2]
        self.core[k].wait_recv()
        keep[k] = (keep[k].astype(F32) + self.core_in[k].astype(F32)).astype(BF)
        self.q_one[k] = [
            links.send(
                self.q_part(k, lax.rem(z + d + 4, 4)), self.q_one_in.at[k, n], dz=d
            )
            for n, d in enumerate((1, -1, 2))
        ]
        rows = keep.at[k].reshape(4, HOME, WIDTH)
        first = pl.ds(0, 32)
        if k == 0:
            self.p_one = [
                links.send(rows.at[pl.ds(0, 2), first], self.p_one_in.at[0], dy=1),
                links.send(rows.at[pl.ds(2, 2), first], self.p_one_in.at[1], dy=-1),
            ]
        elif k < 3:
            n = k - 1
            self.p_one[n].wait_recv()
            for i in range(2):
                row = (2 * n + i) * HOME
                keep[k, row : row + 32] = (
                    keep[k, row : row + 32].astype(F32) + self.p_one_in[n, i].astype(F32)
                ).astype(BF)
            self.p_two.append(
                links.send(rows.at[:, first], self.p_two_in.at[n], dy=(1, -1)[n])
            )

    def q_sum(self, k):
        z = self.links.here[2]
        for copy in self.q_one[k]:
            copy.wait_recv()
        part = self.keep[k, at(z * HOME + 32, 32), :].astype(F32)
        for n in range(3):
            part = part + self.q_one_in[k, n].astype(F32)
        return part

    def q_send(self, k, buffer):
        buffer[k] = self.q_sum(k).astype(BF)
        self.q_two.append(
            self.links.send(buffer.at[k], self.q_two_in.at[k], dy=(2, 1, -1)[k])
        )

    def p_send(self):
        links, keep = self.links, self.keep
        z = links.here[2]
        arrived(self.p_two)
        for place in range(4):
            row = place * HOME
            keep[3, row : row + 32] = (
                keep[3, row : row + 32].astype(F32)
                + self.p_two_in[0, place].astype(F32)
                + self.p_two_in[1, place].astype(F32)
            ).astype(BF)
        self.p_three = [
            links.send(
                keep.at[3, at(lax.rem(z + d + 4, 4) * HOME, 32)], self.p_three_in.at[n], dz=d
            )
            for n, d in enumerate((1, -1, 2))
        ]

    def home(self):
        z = self.links.here[2]
        second = self.q_sum(3)
        arrived(self.q_two)
        for n in range(3):
            second = second + self.q_two_in[n].astype(F32)
        arrived(self.p_three)
        first = self.keep[3, at(z * HOME, 32), :].astype(F32)
        for n in range(3):
            first = first + self.p_three_in[n].astype(F32)
        return first, second


TOKEN_SUM_COPIES = 4 + 12 + 2 + 2 + 3 + 3


def spread_home(links, array, home_ref):
    x, y, z, c = links.here
    return [links.send(home_ref, array.at[c, z], dz=d) for d in (1, -1, 2)]


def experts(
    x_all, g_all, picked_all, w_in_hbm, w_out_hbm, weights, hidden_ref,
    gated_out, grad_out, grad_near_out, low_all, hidden_grad_out, gain_out,
    w_in, w_out, gain_ref, x_ref, g_ref, picked_ref, gates_ref, gate_grad_ref, back_ref, pre_ref,
    gated_ref, give, keep, grad_ref, q_buffer, home_ref,
    core_in, p_one_in, p_two_in, p_three_in, q_one_in, q_two_in,
    send_sems, recv_sems, local_sems,
):
    links = Links(send_sems, recv_sems)
    x, y, z, c = links.here
    x_after, x_before, x_far = lax.rem(x + 1, 4), lax.rem(x + 3, 4), lax.rem(x + 2, 4)
    order = (lax.rem(y + 2, 4), lax.rem(y + 1, 4), lax.rem(y + 3, 4), y)
    loads = []

    def load(source, target):
        copy = pltpu.make_async_copy(source, target, local_sems.at[len(loads)])
        copy.start()
        loads.append(copy)
        return copy

    first = [load(g_all.at[order[0]], g_ref.at[0]), load(w_out_hbm, w_out)]
    first += [load(picked_all.at[place], picked_ref.at[k]) for k, place in enumerate(order)]
    first.append(load(weights.at[:, :, pl.ds(0, 256), pl.ds(768, 128)], w_in.at[:, :, :, pl.ds(1024, 128)]))
    first.append(load(weights.at[:, :, pl.ds(256, 16), pl.ds(0, 256)], gain_ref))
    first.append(load(x_all.at[order[0]], x_ref.at[0]))
    first += [
        load(w_in_hbm.at[e], w_in.at[:, :, :, pl.ds(e * 256, 256)]) for e in range(4)
    ]
    rest = [
        [load(g_all.at[order[k]], g_ref.at[k]), load(x_all.at[order[k]], x_ref.at[k])]
        for k in range(1, 4)
    ]
    links.greet(STEPS_X + STEPS_Y + STEPS_Z + STEPS_C)
    for copy in first:
        copy.wait()

    sums = TokenSum(links, give, keep, (core_in, p_one_in, p_two_in, p_three_in, q_one_in, q_two_in))
    lanes = lax.broadcasted_iota(jnp.int32, (ROWS, 128), 1)
    own_rows = at(c * HALF, HALF)
    other_rows = at((1 - c) * HALF, HALF)

    def in_block(first_column, size):
        return w_in[:, :, :, pl.ds(first_column, size)].reshape(WIDTH, size)

    for k in range(4):
        if k:
            for copy in rest[k - 1]:
                copy.wait()
        logits = dot(x_ref[k], in_block(1024, 128))
        logits = jnp.where(picked_ref[k].astype(F32) > 0.5, logits, MASKED_SCORE)
        exponents = jnp.exp(logits - jnp.max(logits, axis=-1, keepdims=True))
        gates_ref[...] = exponents / jnp.sum(exponents, axis=-1, keepdims=True)
        gate_grad_ref[...] = jnp.zeros_like(gate_grad_ref)
        back_ref[...] = dot_nt(g_ref[k], w_out[...].reshape(512, WIDTH))

        def one_expert(e, carry, k=k):
            joined = dot(x_ref[k], in_block(pl.multiple_of(e * 256, 256), 256))
            gate_pre, up_pre = joined[:, :128], joined[:, 128:]
            logistic = 1.0 / (1.0 + jnp.exp(-gate_pre))
            silu_gate = gate_pre * logistic
            silu_slope = logistic * (1.0 + gate_pre * (1.0 - logistic))
            act = silu_gate * up_pre
            back = back_ref[:, at(e * 128, 128)]
            mine = lanes == y * 4 + e
            gate = jnp.sum(jnp.where(mine, gates_ref[...], 0.0), axis=-1, keepdims=True)
            term = jnp.sum(act.astype(BF).astype(F32) * back, axis=-1, keepdims=True)
            gate_grad_ref[...] += jnp.where(mine, term, 0.0)
            act_grad = back * gate
            pre_ref[k, :, pl.ds(pl.multiple_of(e * 256, 256), 128)] = (
                act_grad * up_pre * silu_slope
            ).astype(BF)
            pre_ref[k, :, pl.ds(pl.multiple_of(e * 256 + 128, 128), 128)] = (
                act_grad * silu_gate
            ).astype(BF)
            gated_ref[k, :, at(e * 128, 128)] = (act * gate).astype(BF)
            return carry

        lax.fori_loop(0, 4, one_expert, 0)
        gates, gate_grad = gates_ref[...], gate_grad_ref[...]
        logit_grad = gates * (gate_grad - jnp.sum(gates * gate_grad, axis=-1, keepdims=True))
        pre_ref[k, :, 1024:1152] = logit_grad.astype(BF)

        def back_rows(rows, target, k=k):
            def one_block(s, carry):
                block = w_in[s // 2, lax.rem(s, 2)]
                target[k, :, at(s * 256, 256)] = dot_nt(pre_ref[k, rows, :], block).astype(BF)
                return carry

            lax.fori_loop(0, 8, one_block, 0)

        back_rows(other_rows, give)
        sums.give_core(k)
        back_rows(own_rows, keep)
        if k:
            sums.q_send(k - 1, q_buffer)
        sums.add(k)
    sums.p_send()
    keep_gated = pltpu.make_async_copy(gated_ref, gated_out, local_sems.at[len(loads)])
    keep_gated.start()

    def weight_grad(slot):
        columns = at(slot * 256, 256)
        rows = x_ref[:, :, columns].reshape(4 * ROWS, 256)
        grad_ref[slot, :, 0:1152] = dot_tn(rows, pre_ref[...].reshape(4 * ROWS, 1152)).astype(BF)
        rows = g_ref[:, :, columns].reshape(4 * ROWS, 256)
        grad_ref[slot, :, 1152:MCOLS] = dot_tn(rows, gated_ref[...].reshape(4 * ROWS, 512)).astype(BF)

    def weight_grads(place):
        def one_slot(i, carry):
            weight_grad(place * 2 + i)
            return carry

        lax.fori_loop(0, 2, one_slot, 0)

    weight_grads(x_far)
    near = [
        links.send(grad_ref.at[x_far * 2], grad_near_out.at[0], dx=1),
        links.send(grad_ref.at[x_far * 2 + 1], grad_near_out.at[1], dx=-1),
    ]

    moe_gains = jnp.concatenate(
        [gain_ref[s // 2, s % 2].astype(F32)[1:2] for s in range(8)], axis=1
    )
    moe_grad = jnp.concatenate(sums.home(), axis=0)
    hidden = hidden_ref[...]
    home_grad = g_ref[3, at(c * HALF + z * HOME, HOME), :].astype(F32)
    back, gain_rows = norm_back(moe_grad, hidden, rms_scale(hidden), moe_gains)
    hidden_grad = home_grad + back
    hidden_grad_out[...] = hidden_grad
    gain_out[...] = jnp.broadcast_to(jnp.sum(gain_rows, axis=0, keepdims=True), (8, WIDTH))
    home_ref[...] = hidden_grad.astype(BF)
    place_home = pltpu.make_async_copy(home_ref, low_all.at[c, z], local_sems.at[len(loads) + 1])
    place_home.start()
    low_near = spread_home(links, low_all, home_ref)

    def other_grads(i, carry):
        weight_grad(lax.rem(x_far * 2 + 2 + i, 8))
        return carry

    lax.fori_loop(0, 6, other_grads, 0)
    arrived(low_near)
    place_home.wait()
    sibling = links.send(low_all.at[c], low_all.at[c], dc=1)
    keep_grad = pltpu.make_async_copy(grad_ref, grad_out, local_sems.at[len(loads) + 2])
    keep_grad.start()
    arrived(near)
    sibling.wait_recv()
    keep_gated.wait()
    keep_grad.wait()
    links.finish()


EXPERT_COPIES = TOKEN_SUM_COPIES + 2 + 3 + 1


def run_experts(moe_in_all, grad_all, picked_all, experts_in, experts_out, weights, hidden):
    shape = jax.ShapeDtypeStruct
    outs = (
        (shape((4, ROWS, 512), BF), ANY),
        (shape((8, 256, MCOLS), BF), ANY),
        (shape((2, 256, MCOLS), BF), ANY),
        (shape((2, 4, HOME, WIDTH), BF), ANY),
        (shape((HOME, WIDTH), F32), VMEM),
        (shape((8, WIDTH), F32), VMEM),
    )
    return pl.pallas_call(
        experts,
        out_shape=[o for o, _ in outs],
        in_specs=[ANY] * 6 + [VMEM],
        out_specs=[spec for _, spec in outs],
        scratch_shapes=[
            pltpu.VMEM((4, 2, 256, 1152), BF),
            pltpu.VMEM((4, 128, WIDTH), BF),
            pltpu.VMEM((4, 2, 16, 256), BF),
            pltpu.VMEM((4, ROWS, WIDTH), BF),
            pltpu.VMEM((4, ROWS, WIDTH), BF),
            pltpu.VMEM((4, ROWS, 128), BF),
            pltpu.VMEM((ROWS, 128), F32),
            pltpu.VMEM((ROWS, 128), F32),
            pltpu.VMEM((ROWS, 512), F32),
            pltpu.VMEM((4, ROWS, 1152), BF),
            pltpu.VMEM((4, ROWS, 512), BF),
            pltpu.VMEM((4, HALF, WIDTH), BF),
            pltpu.VMEM((4, HALF, WIDTH), BF),
            pltpu.VMEM((8, 256, MCOLS), BF),
            pltpu.VMEM((3, 32, WIDTH), BF),
            pltpu.VMEM((HOME, WIDTH), BF),
            *scatter_buffers(),
            pltpu.SemaphoreType.DMA((EXPERT_COPIES,)),
            pltpu.SemaphoreType.DMA((EXPERT_COPIES,)),
            pltpu.SemaphoreType.DMA((24,)),
        ],
        compiler_params=pltpu.CompilerParams(
            collective_id=2, has_side_effects=True, vmem_limit_bytes=62 * MIB
        ),
        name="experts",
    )(
        moe_in_all.reshape(4, ROWS, WIDTH),
        grad_all,
        picked_all,
        experts_in,
        experts_out,
        weights,
        hidden,
    )


SMALL = 264


def back(
    grad_moe, grad_near, low_hbm, weights, mixed_hbm, rot_hbm, kv_hbm, kv_far_hbm, lse_hbm, pre_hbm,
    normed_hbm, gated_hbm, w_out_hbm, tok_hbm,
    hidden_ref, hidden_grad_ref, home_scale_ref, gain_ref, cosine_ref, sine_ref, segment_rows, segment_row,
    layer_all, input_all, groups_in, groups_out, moe_in,
    grad_q, grad_k, grad_v, grad_o, small_out, heads_out,
    w_ref, w_gains, low, mixed, rot, kv, kv_far, lse, pre, gated, w_out, home_tok,
    bias, mixed_grad, dq, dkv, kv_give, kv_got, stacked,
    moe_after, moe_before, moe_near, pay_in, pay_out,
    attn_grad, attn_one, attn_two, attn_give, attn_keep, attn_y_one, attn_y_two,
    part, part_core, part_z, home_in, home_layer,
    give, keep, q_buffer, core_in, p_one_in, p_two_in, p_three_in, q_one_in, q_two_in,
    sums_ref, sums_x, sums_y, pair_ref, small_ref, small_z, small_c, routed,
    send_sems, recv_sems, local_sems,
):
    links = Links(send_sems, recv_sems)
    x, y, z, c = links.here
    ctx, y_low = y // 2, lax.rem(y, 2)
    x_after, x_before, x_far = lax.rem(x + 1, 4), lax.rem(x + 3, 4), lax.rem(x + 2, 4)
    own_rows, other_rows = at(c * HALF, HALF), at((1 - c) * HALF, HALF)
    loads = []

    def load(source, target):
        copy = pltpu.make_async_copy(source, target, local_sems.at[len(loads)])
        copy.start()
        loads.append(copy)
        return copy

    def pair_of(array, place):
        return array.at[at(place * 2, 2)]

    near_loads = [
        load(pair_of(grad_moe, x_after), moe_after),
        load(pair_of(grad_moe, x_before), moe_before),
        load(grad_near, moe_near),
    ]
    every = pl.ds(0, 256)
    out_loads = [
        load(low_hbm, low),
        load(weights.at[:, :, every, pl.ds(896, 256)], w_ref.at[:, :, :, pl.ds(768, 256)]),
        load(mixed_hbm, mixed),
        load(rot_hbm, rot),
        load(kv_hbm, kv),
        load(kv_far_hbm, kv_far),
        load(lse_hbm.at[pl.ds(0, 2)], lse),
    ]
    next_loads = [
        load(pre_hbm, pre),
        load(weights.at[:, :, every, pl.ds(0, 768)], w_ref.at[:, :, :, pl.ds(0, 768)]),
        load(weights.at[:, :, pl.ds(256, 16), every], w_gains),
        load(tok_hbm.at[at(c * HALF + z * HOME, HOME)], home_tok),
    ]
    last_loads = [
        load(gated_hbm, gated),
        load(w_out_hbm, w_out),
    ]
    links.greet(STEPS_X + [(2, 0, 0, 0)] + STEPS_Y + STEPS_Z + STEPS_C)

    for copy in near_loads:
        copy.wait()
    moe_after[0] = (moe_after[0].astype(F32) + moe_near[0].astype(F32)).astype(BF)
    moe_two = [links.send(moe_after, moe_in.at[0], dx=1)]
    moe_before[1] = (moe_before[1].astype(F32) + moe_near[1].astype(F32)).astype(BF)
    moe_two.append(links.send(moe_before, moe_in.at[1], dx=-1))
    moe_own = moe_near
    own_load = load(pair_of(grad_moe, x), moe_own)

    own_first = at(ctx * ROWS, ROWS)
    for copy in out_loads:
        copy.wait()
    total = jnp.zeros((ROWS, 256), F32)
    for s in range(8):
        total = total + dot_nt(low[:, s * 256 : s * 256 + 256], w_ref[s // 2, s % 2, :, 768:1024])
    mixed_grad[...] = total.astype(BF)

    score_scale = 128 ** (-0.5)
    deltas = []
    for h in range(2):
        lane = slice(h * 128, h * 128 + 128)
        deltas.append(
            jnp.sum(
                mixed_grad[:, lane].astype(F32) * mixed[:, lane].astype(F32), axis=-1, keepdims=True
            )
        )

    def scores_back(h, keys_values):
        lane = slice(h * 128, h * 128 + 128)
        keys, values = keys_values[:, lane], keys_values[:, 256 + h * 128 : 384 + h * 128]
        scores = dot_nt(rot[:, lane], keys) * score_scale + bias[...]
        probs = jnp.exp(scores - lse[h][:, 0:1])
        prob_grad = dot_nt(mixed_grad[:, lane], values)
        score_grad = (probs * (prob_grad - deltas[h])).astype(BF)
        query_part = dot(score_grad, keys) * score_scale
        key_part = dot_tn(score_grad, rot[:, lane]) * score_scale
        value_part = dot_tn(probs.astype(BF), mixed_grad[:, lane])
        return query_part, key_part, value_part

    earlier = links.send(kv_give, kv_got, dy=2, start=False)

    @pl.when(ctx == 1)
    def _():
        bias[...] = earlier_mask(segment_rows, segment_row, own_first)
        for h in range(2):
            query_part, key_part, value_part = scores_back(h, kv_far)
            dq[:, h * 128 : h * 128 + 128] = query_part
            kv_give[:, h * 128 : h * 128 + 128] = key_part.astype(BF)
            kv_give[:, 256 + h * 128 : 384 + h * 128] = value_part.astype(BF)
        earlier.start()

    @pl.when(ctx == 0)
    def _():
        dq[...] = jnp.zeros_like(dq)

    bias[...] = own_mask(segment_rows, segment_row, own_first)
    for h in range(2):
        query_part, key_part, value_part = scores_back(h, kv)
        dq[:, h * 128 : h * 128 + 128] += query_part
        dkv[:, h * 128 : h * 128 + 128] = key_part
        dkv[:, 256 + h * 128 : 384 + h * 128] = value_part

    def out_grad_block(s, carry):
        attn_grad[s, :, 768:1024] = dot_tn(mixed[...], low[:, at(s * 256, 256)]).astype(BF)
        return carry

    lax.fori_loop(0, 8, out_grad_block, 0)
    normed = low
    normed_load = load(normed_hbm, normed)
    for copy in next_loads:
        copy.wait()
    head_gains = jnp.zeros((16, 128), F32)
    for s in range(8):
        head_gains = head_gains + w_gains[s // 2, s % 2, :, 0:128].astype(F32)
    cosine, sine = cosine_ref[own_first, :], sine_ref[own_first, :]

    def head_back(grads, first, first_gain):
        for h in range(2):
            lane = slice(first + h * 128, first + h * 128 + 128)
            unit_grad = turned(
                grads[:, h * 128 : h * 128 + 128].astype(BF).astype(F32), cosine, -sine
            )
            source = pre[:, lane]
            gain = head_gains[first_gain + h : first_gain + h + 1]
            grad, gain_rows = norm_back(unit_grad, source, rms_scale(source), gain)
            stacked[:, lane] = grad.astype(BF)
            row = first_gain - 2 + h
            heads_row = jnp.sum(gain_rows, axis=0, keepdims=True)
            for s in range(8):
                sums_ref[s // 2, s % 2, row + 2 : row + 3, 0:128] = heads_row
                sums_ref[s // 2, s % 2, row + 2 : row + 3, 128:256] = jnp.zeros_like(heads_row)

    head_back(dq, 0, 2)

    @pl.when(ctx == 0)
    def _():
        earlier.wait_recv()
        dkv[...] += kv_got[...].astype(F32)

    head_back(dkv, 256, 4)
    stacked[:, 512:768] = dkv[:, 256:512].astype(BF)

    def input_rows(rows, target):
        def one_block(s, carry):
            block = w_ref[s // 2, lax.rem(s, 2), :, 0:768]
            part[target, :, at(s * 256, 256)] = dot_nt(stacked[rows, :], block).astype(BF)
            return carry

        lax.fori_loop(0, 8, one_block, 0)

    input_rows(other_rows, 1)
    core_sum = links.send(part.at[1], part_core, dc=1)
    input_rows(own_rows, 0)

    def weight_block(slot):
        attn_grad[slot, :, 0:768] = dot_tn(normed[:, at(slot * 256, 256)], stacked[...]).astype(BF)

    normed_load.wait()
    weight_block(x_far * 2)
    weight_block(x_far * 2 + 1)
    attn_first = [
        links.send(attn_grad.at[x_far * 2], attn_one.at[0], dx=1),
        links.send(attn_grad.at[x_far * 2 + 1], attn_one.at[1], dx=-1),
    ]
    core_sum.wait_recv()
    part[0] = (part[0].astype(F32) + part_core[...].astype(F32)).astype(BF)
    z_sum = [
        links.send(part.at[0, at(lax.rem(z + d + 4, 4) * HOME, HOME)], part_z.at[k], dz=d)
        for k, d in enumerate((1, -1, 2))
    ]

    def other_blocks(i, carry):
        weight_block(lax.rem(x_far * 2 + 2 + i, 8))
        return carry

    lax.fori_loop(0, 6, other_blocks, 0)

    for copy in last_loads:
        copy.wait()
    sums = TokenSum(links, give, keep, (core_in, p_one_in, p_two_in, p_three_in, q_one_in, q_two_in))

    def expert_rows(k, rows, target):
        def one_block(s, carry):
            block = w_out[:, :, at(s * 256, 256)].reshape(512, 256)
            target[:, at(s * 256, 256)] = dot(gated[k, rows, :], block).astype(BF)
            return carry

        lax.fori_loop(0, 8, one_block, 0)

    def expert_chunk(k):
        expert_rows(k, other_rows, give.at[sums.give_slot(k)])
        sums.give_core(k)
        expert_rows(k, own_rows, keep.at[k])
        if k:
            sums.q_send(k - 1, q_buffer)
        sums.add(k)

    expert_chunk(0)
    expert_chunk(1)

    arrived(z_sum)
    normed_grad = part[0, at(z * HOME, HOME), :].astype(F32)
    for k in range(3):
        normed_grad = normed_grad + part_z[k].astype(F32)
    gains = jnp.concatenate(
        [w_gains[s // 2, s % 2].astype(F32)[0:1] for s in range(8)], axis=1
    )
    input_back, gain_rows = norm_back(
        normed_grad, home_tok[...].astype(F32), home_scale_ref[:, 0:1], gains
    )
    home_in[...] = (hidden_grad_ref[...] + input_back).astype(BF)
    gain_row = jnp.sum(gain_rows, axis=0, keepdims=True)
    for s in range(8):
        columns = slice(s * 256, s * 256 + 256)
        sums_ref[s // 2, s % 2, 0:1, :] = gain_row[:, columns]
        sums_ref[s // 2, s % 2, 1:2, :] = gain_ref[0:1, columns]
        sums_ref[s // 2, s % 2, 6:16, :] = jnp.zeros((10, 256), F32)
    place_in = load(home_in, input_all.at[c, z])
    input_near = spread_home(links, input_all, home_in)
    sum_x = [
        links.send(sums_ref.at[lax.rem(x + d + 4, 4)], sums_x.at[k], dx=d)
        for k, d in enumerate((1, -1, 2))
    ]
    expert_chunk(2)
    expert_chunk(3)
    sums.p_send()

    arrived(moe_two)
    arrivals = []
    for n, target in enumerate((moe_after, moe_before)):
        links.left(moe_two[n])
        arrivals.append(load(moe_in.at[n], target))
    own_load.wait()
    for copy in arrivals:
        copy.wait()
    for i in range(2):
        total = moe_own[i].astype(F32) + moe_after[i].astype(F32) + moe_before[i].astype(F32)
        for e in range(4):
            pay_in[i, e] = total[:, e * 256 : e * 256 + 128].astype(BF)
            pay_in[i, 4 + e] = total[:, e * 256 + 128 : e * 256 + 256].astype(BF)
            pay_out[i, e] = total[:, 1152 + e * 128 : 1280 + e * 128].T.astype(BF)
        pay_in[i, 8] = total[:, 1024:1152].astype(BF)
    groups = []
    for d, low_place in ((1, 1 - y_low), (-1, 1 - y_low), (2, y_low)):
        groups.append(links.send(pay_in.at[low_place], groups_in.at[y], dy=d))
        groups.append(links.send(pay_out.at[low_place], groups_out.at[y], dy=d))
    place_groups = [load(pay_in.at[y_low], groups_in.at[y]), load(pay_out.at[y_low], groups_out.at[y])]

    arrived(attn_first)
    slot = x_after * 2
    attn_grad[slot] = (attn_grad[slot].astype(F32) + attn_one[0].astype(F32)).astype(BF)
    attn_next = [links.send(pair_of(attn_grad, x_after), attn_two.at[0], dx=1)]
    slot = x_before * 2 + 1
    attn_grad[slot] = (attn_grad[slot].astype(F32) + attn_one[1].astype(F32)).astype(BF)
    attn_next.append(links.send(pair_of(attn_grad, x_before), attn_two.at[1], dx=-1))

    first, second = sums.home()
    home_layer[...] = (hidden_ref[...] + jnp.concatenate([first, second], axis=0)).astype(BF)
    place_layer = load(home_layer, layer_all.at[c, z])
    layer_near = spread_home(links, layer_all, home_layer)
    arrived(input_near)
    place_in.wait()
    siblings = [links.send(input_all.at[c], input_all.at[c], dc=1)]

    arrived(sum_x)
    pair_ref[...] = sums_ref[x] + sums_x[0] + sums_x[1] + sums_x[2]
    sum_y = [
        links.send(pair_ref.at[low_place], sums_y.at[k], dy=d)
        for k, (d, low_place) in enumerate(((1, 1 - y_low), (-1, 1 - y_low), (2, y_low)))
    ]
    arrived(layer_near)
    place_layer.wait()
    siblings.append(links.send(layer_all.at[c], layer_all.at[c], dc=1))
    arrived(groups)
    for copy in place_groups:
        copy.wait()
    get_routed = load(groups_in.at[:, 8], routed)
    arrived(sum_y)
    summed = pair_ref[y_low] + sums_y[0] + sums_y[1] + sums_y[2]
    heads_out[...] = jnp.concatenate([summed[2:6, 0:128], jnp.zeros((4, 128), F32)], axis=0)
    get_routed.wait()
    small_ref[0:256] = (
        routed[0].astype(F32) + routed[1].astype(F32) + routed[2].astype(F32) + routed[3].astype(F32)
    )
    small_ref[256:SMALL] = jnp.concatenate(
        [summed[0:2, 0:128], summed[0:2, 128:256], jnp.zeros((4, 128), F32)], axis=0
    )
    small_sums = [
        links.send(small_ref, small_z.at[k], dz=d) for k, d in enumerate((1, -1, 2))
    ]

    arrived(attn_next)
    def attn_total(low_place):
        slot = x * 2 + low_place
        return (
            attn_grad[slot].astype(F32)
            + attn_two[0, low_place].astype(F32)
            + attn_two[1, low_place].astype(F32)
        )

    attn_give[...] = attn_total(1 - y_low).astype(BF)
    top, bottom = pl.ds(0, 128), pl.ds(128, 128)
    y_first = [
        links.send(attn_give.at[top], attn_y_one.at[top], dy=1),
        links.send(attn_give.at[bottom], attn_y_one.at[bottom], dy=-1),
    ]
    kept = attn_total(y_low)
    arrived(small_sums)
    small_ref_total = small_ref[...] + small_z[0] + small_z[1] + small_z[2]
    small_out[...] = small_ref_total
    small_core = links.send(small_out, small_c, dc=1)
    arrived(y_first)
    attn_keep[...] = (kept + attn_y_one[...].astype(F32)).astype(BF)
    y_second = links.send(attn_keep, attn_y_two, dy=2)
    small_core.wait()
    small_out[...] = small_ref_total + small_c[...]
    arrived(siblings)
    y_second.wait_recv()
    for n, target in enumerate((grad_q, grad_k, grad_v, grad_o)):
        columns = slice(n * 256, n * 256 + 256)
        target[...] = attn_keep[:, columns].astype(F32) + attn_y_two[:, columns].astype(F32)

    for copy in links.made:
        if copy is not earlier and copy is not small_core:
            copy.wait_send()

    @pl.when(ctx == 1)
    def _():
        earlier.wait_send()


BACK_COPIES = 2 + 1 + 1 + 3 + 2 + TOKEN_SUM_COPIES + 3 + 3 + 6 + 2 + 3 + 2 + 3 + 3 + 1 + 3


def run_back(hbm, vmem):
    shape = jax.ShapeDtypeStruct
    outs = (
        (shape((2, 4, HOME, WIDTH), BF), ANY),
        (shape((2, 4, HOME, WIDTH), BF), ANY),
        (shape((4, 9, 256, 128), BF), ANY),
        (shape((4, 4, 128, 256), BF), ANY),
        (shape((2, 2, 256, MCOLS), BF), ANY),
        (shape((256, 256), F32), VMEM),
        (shape((256, 256), F32), VMEM),
        (shape((256, 256), F32), VMEM),
        (shape((256, 256), F32), VMEM),
        (shape((SMALL, 128), F32), VMEM),
        (shape((8, 128), F32), VMEM),
    )

    def buffer(*dims, kind=BF):
        return pltpu.VMEM(dims, kind)

    return pl.pallas_call(
        back,
        out_shape=[o for o, _ in outs],
        in_specs=[ANY] * len(hbm) + [VMEM] * len(vmem),
        out_specs=[spec for _, spec in outs],
        scratch_shapes=[
            buffer(4, 2, 256, 1024),
            buffer(4, 2, 16, 256),
            buffer(ROWS, WIDTH),
            buffer(ROWS, 256),
            buffer(ROWS, 512),
            buffer(ROWS, 512),
            buffer(ROWS, 512),
            buffer(2, ROWS, 128, kind=F32),
            buffer(ROWS, 512, kind=F32),
            buffer(4, ROWS, 512),
            buffer(4, 128, WIDTH),
            buffer(HOME, WIDTH),
            buffer(ROWS, ROWS, kind=F32),
            buffer(ROWS, 256),
            buffer(ROWS, 256, kind=F32),
            buffer(ROWS, 512, kind=F32),
            buffer(ROWS, 512),
            buffer(ROWS, 512),
            buffer(ROWS, 768),
            buffer(2, 256, MCOLS),
            buffer(2, 256, MCOLS),
            buffer(2, 256, MCOLS),
            buffer(2, 9, 256, 128),
            buffer(2, 4, 128, 256),
            buffer(8, 256, 1024),
            buffer(2, 256, 1024),
            buffer(2, 2, 256, 1024),
            buffer(256, 1024),
            buffer(256, 1024),
            buffer(256, 1024),
            buffer(256, 1024),
            buffer(2, HALF, WIDTH),
            buffer(HALF, WIDTH),
            buffer(3, HOME, WIDTH),
            buffer(HOME, WIDTH),
            buffer(HOME, WIDTH),
            buffer(2, HALF, WIDTH),
            buffer(4, HALF, WIDTH),
            buffer(3, 32, WIDTH),
            *scatter_buffers(),
            buffer(4, 2, 16, 256, kind=F32),
            buffer(3, 2, 16, 256, kind=F32),
            buffer(3, 16, 256, kind=F32),
            buffer(2, 16, 256, kind=F32),
            buffer(SMALL, 128, kind=F32),
            buffer(3, SMALL, 128, kind=F32),
            buffer(SMALL, 128, kind=F32),
            buffer(4, 256, 128),
            pltpu.SemaphoreType.DMA((BACK_COPIES,)),
            pltpu.SemaphoreType.DMA((BACK_COPIES,)),
            pltpu.SemaphoreType.DMA((32,)),
        ],
        compiler_params=pltpu.CompilerParams(
            collective_id=3, has_side_effects=True, vmem_limit_bytes=62 * MIB
        ),
        name="back",
    )(*hbm, *vmem)


def turn_tables():
    frequency = ROPE_BASE ** (-(np.arange(0, 128, 2, dtype=np.float64) / 128))
    angles = np.arange(1024, dtype=np.float64)[:, None] * frequency[None, :]
    cosine, sine = np.cos(angles), np.sin(angles)
    return (
        np.concatenate([cosine, cosine], axis=1).astype(np.float32),
        np.concatenate([-sine, sine], axis=1).astype(np.float32),
    )


def body(
    tokens,
    out_grad,
    segments,
    routes,
    query_weight,
    key_weight,
    value_weight,
    out_weight,
    router_weight,
    attn_gain,
    moe_gain,
    query_gain,
    key_gain,
    gate_weight,
    up_weight,
    down_weight,
):
    rows, width = tokens.shape[1], tokens.shape[2]
    experts_count = gate_weight.shape[0]
    shard = lax.axis_index("shard")

    lanes = jnp.zeros((4, 128), BF)
    head_gains = jnp.concatenate([query_gain, key_gain], axis=0)
    lanes = lax.dynamic_update_slice_in_dim(lanes, head_gains, shard * 16, 1)
    gain_rows = jnp.zeros((16, WCOLS), BF)
    gain_rows = gain_rows.at[0, :256].set(attn_gain).at[1, :256].set(moe_gain)
    gain_rows = gain_rows.at[2:6, :128].set(lanes)
    router_pad = jnp.pad(router_weight, ((0, 0), (0, 128 - experts_count)))
    own_weights = jnp.concatenate(
        [
            jnp.concatenate([query_weight, key_weight, value_weight, router_pad, out_weight], axis=1),
            gain_rows,
        ],
        axis=0,
    )
    own_grad = out_grad.reshape(rows, width)
    route_rows = routes.reshape(rows, -1)
    own_picked = jnp.any(
        route_rows[:, :, None] == jnp.arange(128, dtype=jnp.int32)[None, None, :], axis=1
    ).astype(BF)
    (
        weights, experts_in, experts_out, grad_all, picked_all, moe_in_all,
        normed, pre, rot, key_value, key_value_far, mixed, lse, hidden, home_scale,
    ) = run_front(
        tokens.reshape(rows, width), own_weights, turn_tables(), segments,
        gate_weight, up_weight, down_weight, own_grad, own_picked,
    )
    gated, grad_moe, grad_near, hidden_low, hidden_grad, gain_sum = run_experts(
        moe_in_all, grad_all, picked_all, experts_in, experts_out, weights, hidden
    )
    tables = turn_tables()
    (
        layer_all, input_all, groups_in, groups_out, _, grad_q, grad_k, grad_v, grad_o, small, heads,
    ) = run_back(
        [
            grad_moe, grad_near, hidden_low.reshape(rows, width), weights, mixed, rot, key_value,
            key_value_far, lse, pre, normed, gated, experts_out, tokens.reshape(rows, width),
        ],
        [
            hidden, hidden_grad, home_scale, gain_sum, jnp.asarray(tables[0]), jnp.asarray(tables[1]),
            segments.reshape(-1, 1), segments,
        ],
    )
    head_grads = lax.dynamic_slice_in_dim(heads[:4], shard * 16, 16, 1)

    def grown(groups):
        return groups.reshape((experts_count,) + groups.shape[2:]).astype(F32)

    return (
        layer_all.reshape(tokens.shape),
        input_all.reshape(tokens.shape),
        grad_q,
        grad_k,
        grad_v,
        grad_o,
        small[:256, :experts_count],
        small[256::2][:2].reshape(-1),
        small[257::2][:2].reshape(-1),
        head_grads[:2],
        head_grads[2:],
        grown(groups_in[:, :4]),
        grown(groups_in[:, 4:8]),
        grown(groups_out),
    )


def solution(mesh):
    return jax.shard_map(
        body,
        mesh=mesh,
        in_specs=(
            P("shard", "ctx", None),
            P("shard", "ctx", None),
            P("shard", None),
            P("shard", "ctx", None),
            P("shard", "tp"),
            P("shard", "tp"),
            P("shard", "tp"),
            P("tp", "shard"),
            P("shard", None),
            P("shard"),
            P("shard"),
            P("tp", "shard"),
            P("tp", "shard"),
            P(None, "shard", "tp"),
            P(None, "shard", "tp"),
            P(None, "tp", "shard"),
        ),
        out_specs=(
            P("shard", "ctx", None),
            P("shard", "ctx", None),
            P("shard", "tp"),
            P("shard", "tp"),
            P("shard", "tp"),
            P("tp", "shard"),
            P("shard", None),
            P("shard"),
            P("shard"),
            P("tp", "shard"),
            P("tp", "shard"),
            P(None, "shard", "tp"),
            P(None, "shard", "tp"),
            P(None, "tp", "shard"),
        ),
        check_vma=False,
    )
```

```python
import jax
import jax.numpy as jnp
import numpy as np
from jax import lax
from jax.experimental import pallas as pl
from jax.experimental.pallas import tpu as pltpu
from jax.sharding import PartitionSpec as P

EPSILON = 1e-05
ROPE_BASE = 10000.0
MASKED_SCORE = -1e30
AXES = ("shard", "ctx", "tp")
BF = jnp.bfloat16
F32 = jnp.float32

def rms_scale(values):
    return lax.rsqrt(jnp.mean(values * values, axis=-1, keepdims=True) + EPSILON)


def norm_back(grad_normed, source, scale_row, gain_row):
    unit_values = source * scale_row
    grad_unit = grad_normed * gain_row
    grad_source = scale_row * (
        grad_unit - unit_values * jnp.mean(grad_unit * unit_values, axis=-1, keepdims=True)
    )
    return (grad_source, grad_normed * unit_values)


def dot(left, right):
    return jnp.dot(left, right, preferred_element_type=F32)


def dot_nt(left, right):
    return lax.dot_general(left, right, (((1,), (1,)), ((), ())), preferred_element_type=F32)


def dot_tn(left, right):
    return lax.dot_general(left, right, (((0,), (0,)), ((), ())), preferred_element_type=F32)


ANY = pl.BlockSpec(memory_space=pl.ANY)
VMEM = pl.BlockSpec(memory_space=pltpu.VMEM)
MIB = 1024 * 1024
ROWS, WIDTH, HOME, HALF = 512, 2048, 64, 256
WROWS = 272


def places():
    shard, ctx, tp = lax.axis_index("shard"), lax.axis_index("ctx"), lax.axis_index("tp")
    return shard // 2, ctx * 2 + shard % 2, tp // 2, tp % 2


def device(x, y, z, c):
    x, y, z, c = lax.rem(x + 4, 4), lax.rem(y + 4, 4), lax.rem(z + 4, 4), lax.rem(c + 2, 2)
    return {"shard": x * 2 + lax.rem(y, 2), "ctx": y // 2, "tp": z * 2 + c}


def at(first, size):
    return pl.ds(pl.multiple_of(first, size), size)


class Links:
    def __init__(self, send_sems, recv_sems):
        self.here = places()
        self.send_sems, self.recv_sems, self.made, self.count = send_sems, recv_sems, [], 0

    def send(self, source, target, dx=0, dy=0, dz=0, dc=0, start=True):
        x, y, z, c = self.here
        number = self.count
        self.count += 1
        copy = pltpu.make_async_remote_copy(
            src_ref=source,
            dst_ref=target,
            send_sem=self.send_sems.at[number],
            recv_sem=self.recv_sems.at[number],
            device_id=device(x + dx, y + dy, z + dz, c + dc),
            device_id_type=pl.DeviceIdType.MESH,
        )
        self.made.append(copy)
        if start:
            copy.start()
        return copy

    def left(self, copy):
        copy.wait_send()
        self.made = [other for other in self.made if other is not copy]

    def finish(self):
        for copy in self.made:
            copy.wait_send()

    def greet(self, steps):
        x, y, z, c = self.here
        barrier = pltpu.get_barrier_semaphore()
        for dx, dy, dz, dc in steps:
            pl.semaphore_signal(
                barrier,
                inc=1,
                device_id=device(x + dx, y + dy, z + dz, c + dc),
                device_id_type=pl.DeviceIdType.MESH,
            )
        pl.semaphore_wait(barrier, len(steps))


STEPS_X = [(1, 0, 0, 0), (-1, 0, 0, 0)]
STEPS_Y = [(0, 1, 0, 0), (0, -1, 0, 0), (0, 2, 0, 0)]
STEPS_Z = [(0, 0, 1, 0), (0, 0, -1, 0), (0, 0, 2, 0)]
STEPS_C = [(0, 0, 0, 1)]


def arrived(copies):
    for copy in copies:
        copy.wait_recv()


def turned(values, cosine, sine):
    return values * cosine + pltpu.roll(values, 64, 1) * sine


class Spread:
    def __init__(self, links, array, home_ref, first, start):
        self.links, self.first, self.second = links, first, "z" if first == "y" else "y"
        rows = pl.ds(start, 32)
        x, y, z, c = links.here
        self.source = home_ref.at[rows]
        if first == "z":
            self.block = lambda one, two: array.at[
                lax.rem(y + two + 4, 4), c, lax.rem(z + one + 4, 4), rows
            ]
            self.blocks = lambda two: array.at[lax.rem(y + two + 4, 4), c, :, rows]
        else:
            self.block = lambda one, two: array.at[
                lax.rem(y + one + 4, 4), c, lax.rem(z + two + 4, 4), rows
            ]
            self.blocks = lambda two: array.at[:, c, lax.rem(z + two + 4, 4), rows]
        self.near, self.siblings = {}, []

    def pass_on(self, one):
        block = self.block(one, 0)
        self.near[one] = {
            d: self.links.send(block, block, **{"d" + self.second: d}) for d in (1, -1)
        }

    def to_sibling(self, two):
        self.siblings.append(self.links.send(self.blocks(two), self.blocks(two), dc=1))

    def begin(self):
        self.coming = {
            -d if d != 2 else 2: self.links.send(
                self.source, self.block(0, 0), **{"d" + self.first: d}
            )
            for d in (1, -1, 2)
        }
        block = self.block(0, 0)
        self.near[0] = {
            d: self.links.send(self.source, block, **{"d" + self.second: d}) for d in (1, -1)
        }

    def neighbours(self):
        for one in (-1, 1):
            self.coming[one].wait_recv()
            self.pass_on(one)

    def opposite(self):
        self.coming[2].wait_recv()
        self.pass_on(2)
        self.to_sibling(0)

    def onward(self):
        self.far = []
        for one, d in ((0, 1), (1, -1), (-1, 1), (2, -1)):
            self.near[one][d].wait_recv()
            block = self.block(one, -d)
            self.far.append(self.links.send(block, block, **{"d" + self.second: d}))

    def rest(self):
        for one, d in ((0, -1), (1, 1), (-1, -1), (2, 1)):
            self.near[one][d].wait_recv()
        self.to_sibling(-1)
        self.to_sibling(1)

    def end(self):
        arrived(self.far)
        self.to_sibling(2)


def spread(links, array, home_ref, between):
    halves = (Spread(links, array, home_ref, "z", 0), Spread(links, array, home_ref, "y", 32))
    for step in ("begin", "neighbours", "opposite", "onward", "rest", "end"):
        for half in halves:
            getattr(half, step)()
        if step == "opposite":
            between()
    return halves[0].siblings + halves[1].siblings


class SlotGather:
    def __init__(self, links, array, first, size):
        x, y, z, c = links.here
        self.links, self.array, self.place, self.low = links, array, x, lax.rem(y, 2)
        self.all = pl.ds(first, size)
        self.halves = pl.ds(first, size // 2), pl.ds(first + size // 2, size // 2)
        self.along_y = []

    def part(self, d, rows):
        return self.array.at[lax.rem(self.place + d + 4, 4), self.low, rows]

    def to_pair(self, d):
        for rows, step in zip(self.halves, (1, -1)):
            block = self.part(d, rows)
            self.along_y.append(self.links.send(block, block, dy=step))

    def begin(self):
        block = self.part(0, self.all)
        self.near = {d: self.links.send(block, block, dx=d) for d in (1, -1)}
        self.to_pair(0)

    def onward(self):
        self.far = []
        for rows, d in zip(self.halves, (1, -1)):
            self.near[d].wait_recv()
            block = self.part(-d, rows)
            self.far.append(self.links.send(block, block, dx=d))
            self.to_pair(-d)

    def end(self):
        arrived(self.far)
        self.to_pair(2)


def wide_column(segment_row, first):
    blocks = []
    for n in range(4):
        row = segment_row[:, pl.ds(pl.multiple_of(first + n * 128, 128), 128)].astype(F32)
        block = jnp.broadcast_to(row, (128, 128)).T
        blocks.append(jnp.concatenate([block] * 4, axis=1))
    return jnp.concatenate(blocks, axis=0)


def own_mask(segment_row, first):
    rows_at = lax.broadcasted_iota(jnp.int32, (ROWS, ROWS), 0)
    cols_at = lax.broadcasted_iota(jnp.int32, (ROWS, ROWS), 1)
    same = wide_column(segment_row, first) == segment_row[:, at(first, ROWS)].astype(F32)
    return jnp.where(same & (rows_at >= cols_at), 0.0, MASKED_SCORE)


def earlier_mask(segment_row, first):
    same = wide_column(segment_row, first) == segment_row[:, pl.ds(0, ROWS)].astype(F32)
    return jnp.where(same, 0.0, MASKED_SCORE)


def front(
    tok, router, gain_pair, query_gain, key_gain, cosine_ref, sine_ref, segment_row, routes,
    query_weight, key_weight, value_weight, out_weight, gate, up, down, grad,
    weights_out, others_out, experts_in, experts_out, grad_all, picked_all, moe_in_all,
    normed_out, pre_out, rot_out, kv_out, kv_far, mixed_out, lse_out, hidden_out, home_scale_out,
    weights, others, picked, stage_in, stage_out, biases, accs, totals, part, part_core, part_z, home_ref,
    send_sems, recv_sems, local_sems,
):
    links = Links(send_sems, recv_sems)
    x, y, z, c = links.here
    ctx, y_low = y // 2, lax.rem(y, 2)
    x_after, x_before = lax.rem(x + 1, 4), lax.rem(x + 3, 4)
    y_after, y_before, y_far = lax.rem(y + 1, 4), lax.rem(y + 3, 4), lax.rem(y + 2, 4)
    own = c * HALF
    own_rows = pl.ds(pl.multiple_of(own, HALF), HALF)
    loads = []

    def load(source, target):
        copy = pltpu.make_async_copy(source, target, local_sems.at[len(loads)])
        copy.start()
        loads.append(copy)
        return copy

    slot, other_slot = weights.at[x, y_low], others.at[x, y_low]
    every = pl.ds(0, 256)
    slot_loads = [
        load(array, slot.at[every, pl.ds(n * 256, 256)])
        for n, array in enumerate((query_weight, key_weight, value_weight))
    ]
    other_load = load(out_weight, other_slot.at[:, pl.ds(128, 256)])

    def mine(array, group):
        return array.at[pl.ds(group * 4, 4)]

    def columns(place, low_place):
        return pl.ds(pl.multiple_of(place * 512 + low_place * 256, 256), 256)

    staged = [
        load(mine(gate, y), stage_in.at[:, :, pl.ds(0, 128)]),
        load(mine(up, y), stage_in.at[:, :, pl.ds(128, 128)]),
        load(mine(down, y), stage_out),
    ]
    lanes = lax.broadcasted_iota(jnp.int32, (16, 128), 1)
    rows_of = lax.broadcasted_iota(jnp.int32, (16, 128), 0)
    turned_to = (lanes == (x * 2 + y_low) * 16 + rows_of).astype(BF)
    head_rows = dot(jnp.concatenate([query_gain[...], key_gain[...]], axis=0), turned_to)
    gain_block = jnp.concatenate(
        [
            gain_pair[...].astype(F32),
            jnp.concatenate([head_rows, jnp.zeros((4, 128), F32)], axis=1),
            jnp.zeros((10, 256), F32),
        ],
        axis=0,
    )
    weights[x, y_low, 256:272, 0:256] = gain_block.astype(BF)
    weights[x, y_low, 256:272, 256:768] = jnp.zeros((16, 512), BF)
    others[x, y_low, :, 0:128] = jnp.concatenate(
        [router[...].astype(F32), jnp.zeros((256, 112), F32)], axis=1
    ).astype(BF)
    links.greet(STEPS_X + STEPS_Y + STEPS_Z + STEPS_C)
    for copy in slot_loads:
        copy.wait()

    first_rows = pl.ds(0, 80)
    pair = [
        links.send(slot.at[pl.ds(0, 48)], slot.at[pl.ds(0, 48)], dy=1),
        links.send(slot.at[pl.ds(48, 32)], slot.at[pl.ds(48, 32)], dy=-1),
    ]
    most = SlotGather(links, weights, 80, WROWS - 80)
    most.begin()
    other_load.wait()
    behind = SlotGather(links, others, 0, 256)

    def grad_block(dy, dz, first=0, size=HOME):
        start = own + lax.rem(z + dz + 4, 4) * HOME + first
        return grad_all.at[lax.rem(y + dy + 4, 4), pl.ds(pl.multiple_of(start, 32), size)]

    home_rows = pl.ds(pl.multiple_of(own + z * HOME, HOME), HOME)
    grad_near = {
        -d if d != 2 else 2: links.send(grad.at[home_rows], grad_block(0, 0), dy=d)
        for d in (1, -1, 2)
    }
    for copy in staged:
        copy.wait()
    place_staged = [
        load(stage_in, experts_in.at[:, x, y_low]),
        load(stage_out, experts_out.at[:, :, columns(x, y_low)]),
    ]
    arrived(pair)
    both = weights.at[x, :, first_rows]
    near = [links.send(both, both, dx=d) for d in (1, -1)]
    behind.begin()

    expert_lanes = lax.broadcasted_iota(jnp.int32, (ROWS, 128), 1)
    marked = expert_lanes == routes[:, 0:1]
    for k in range(1, 8):
        marked = marked | (expert_lanes == routes[:, k : k + 1])
    picked[...] = jnp.where(marked, 1.0, 0.0).T[0:16].astype(BF)
    place_picked = load(picked, picked_all.at[y])
    most.onward()
    first_row = ctx * ROWS
    own_first = at(first_row, ROWS)
    biases[0] = own_mask(segment_row, first_row)
    biases[1] = earlier_mask(segment_row, first_row)
    far = []
    for n, (d, place) in enumerate(((1, x_before), (-1, x_after))):
        near[n].wait_recv()
        block = weights.at[place, n, first_rows]
        far.append(links.send(block, block, dx=d))
    tokens = tok[...].astype(F32)
    scale_one = rms_scale(tokens)
    most.end()
    grad_next = {}
    for dy in (-1, 1, 2):
        grad_near[dy].wait_recv()
        block = grad_block(dy, 0)
        grad_next[dy] = {d: links.send(block, block, dz=d) for d in (1, -1)}
    behind.onward()

    def expert_block(place, low_place):
        return [
            experts_in.at[:, place, low_place],
            experts_out.at[:, :, columns(place, low_place)],
        ]

    for copy in place_staged:
        copy.wait()
    expert_near = {
        d: [links.send(block, block, dx=d) for block in expert_block(x, y_low)] for d in (1, -1)
    }
    expert_pair = []
    for group, start, step in ((y_after, 0, 1), (y_before, 2, -1)):
        some = pl.ds(group * 4 + start, 2)
        there = pl.ds(start, 2)
        expert_pair += [
            links.send(
                gate.at[some], experts_in.at[there, x, y_low, :, pl.ds(0, 128)], dy=step
            ),
            links.send(
                up.at[some], experts_in.at[there, x, y_low, :, pl.ds(128, 128)], dy=step
            ),
            links.send(down.at[some], experts_out.at[there, :, columns(x, y_low)], dy=step),
        ]
    arrived(most.along_y)
    arrived(far)

    gain_blocks = [weights[s // 2, s % 2, 256:272, 0:256].astype(F32) for s in range(8)]
    gains = jnp.concatenate([block[0:1] for block in gain_blocks], axis=1)
    moe_gains = jnp.concatenate([block[1:2] for block in gain_blocks], axis=1)
    head_gains = sum(block[:, 0:128] for block in gain_blocks)
    normed_out[...] = (tokens * scale_one * gains).astype(BF)

    def project(column):
        block = weights[:, :, 0:256, column * 256 : column * 256 + 256].reshape(WIDTH, 256)
        return jnp.dot(normed_out[...], block, preferred_element_type=F32)

    cosine, sine = cosine_ref[own_first, :], sine_ref[own_first, :]

    def heads(pre, first_gain, base):
        for h in range(2):
            part_h = pre[:, h * 128 : h * 128 + 128]
            unit = part_h * rms_scale(part_h) * head_gains[first_gain + h : first_gain + h + 1]
            rot_out[:, base + h * 128 : base + h * 128 + 128] = turned(unit, cosine, sine).astype(BF)

    key_pre = project(1)
    pre_out[:, 256:512] = key_pre
    heads(key_pre, 4, 256)
    kv_out[:, 0:256] = rot_out[:, 256:512]
    kv_out[:, 256:512] = project(2).astype(BF)
    later = links.send(kv_out, kv_far, dy=2, start=False)

    @pl.when(ctx == 0)
    def _():
        later.start()
        kv_far[...] = jnp.zeros_like(kv_far)

    picked_near = [links.send(picked, picked_all.at[y], dy=d) for d in (1, -1, 2)]
    query_pre = project(0)
    pre_out[:, 0:256] = query_pre
    heads(query_pre, 2, 0)
    score_scale = 128 ** (-0.5)
    for h in range(2):
        lane = slice(h * 128, h * 128 + 128)
        scores = dot_nt(rot_out[:, lane], kv_out[:, lane]) * score_scale + biases[0]
        peak = jnp.max(scores, axis=-1, keepdims=True)
        exponents = jnp.exp(scores - peak)
        lse_out[h] = jnp.broadcast_to(peak, (ROWS, 128))
        totals[h] = jnp.broadcast_to(jnp.sum(exponents, axis=-1, keepdims=True), (ROWS, 128))
        accs[h] = dot(exponents.astype(BF), kv_out[:, 256 + h * 128 : 384 + h * 128])

    behind.end()
    grad_far = []
    for dy in (-1, 1, 2):
        for d, first in ((1, 0), (-1, 32)):
            grad_next[dy][d].wait_recv()
            block = grad_block(dy, -d, first, 32)
            grad_far.append(links.send(block, block, dz=d))
    arrived(expert_pair)
    expert_pair_near = {
        d: [links.send(block, block, dx=d) for block in expert_block(x, 1 - y_low)] for d in (1, -1)
    }
    @pl.when(ctx == 1)
    def _():
        later.wait_recv()
        for h in range(2):
            lane = slice(h * 128, h * 128 + 128)
            scores = dot_nt(rot_out[:, lane], kv_far[:, lane]) * score_scale + biases[1]
            old_peak = lse_out[h][:, 0:1]
            peak = jnp.maximum(old_peak, jnp.max(scores, axis=-1, keepdims=True))
            exponents = jnp.exp(scores - peak)
            old = jnp.exp(old_peak - peak)
            lse_out[h] = jnp.broadcast_to(peak, (ROWS, 128))
            totals[h] = totals[h] * old + jnp.sum(exponents, axis=-1, keepdims=True)
            accs[h] = accs[h] * old + dot(
                exponents.astype(BF), kv_far[:, 256 + h * 128 : 384 + h * 128]
            )

    for h in range(2):
        total = totals[h]
        mixed_out[:, h * 128 : h * 128 + 128] = (accs[h] / total).astype(BF)
        lse_out[h] = lse_out[h] + jnp.log(total)

    quarter = pl.multiple_of(own, HALF)
    arrived(behind.along_y)
    other = pl.multiple_of((1 - c) * HALF, HALF)
    give_rows = mixed_out[pl.ds(other, HALF), :]
    for s in range(8):
        block = others[s // 2, s % 2, :, 128:384]
        part[1, :, s * 256 : s * 256 + 256] = dot(give_rows, block).astype(BF)
    core_sum = links.send(part.at[1], part_core, dc=1)
    keep_rows = mixed_out[pl.ds(quarter, HALF), :]
    for s in range(8):
        block = others[s // 2, s % 2, :, 128:384]
        part[0, :, s * 256 : s * 256 + 256] = dot(keep_rows, block).astype(BF)
    core_sum.wait_recv()
    part[0] = (part[0].astype(F32) + part_core[...].astype(F32)).astype(BF)
    z_sum = []
    for k, d in enumerate((1, -1, 2)):
        there = pl.multiple_of(lax.rem(z + d + 4, 4) * HOME, HOME)
        z_sum.append(links.send(part.at[0, pl.ds(there, HOME)], part_z.at[k], dz=d))

    arrived(grad_far)
    siblings = [
        links.send(grad_all.at[place, own_rows], grad_all.at[place, own_rows], dc=1)
        for place in (y_before, y_after, y_far)
    ]
    arrived(expert_near[1] + expert_near[-1])
    expert_far = [links.send(block, block, dx=1) for block in expert_block(x_before, y_low)]
    arrived(z_sum)
    summed = part[0, pl.ds(pl.multiple_of(z * HOME, HOME), HOME), :].astype(F32)
    for k in range(3):
        summed = summed + part_z[k].astype(F32)
    home_tokens = tok[home_rows, :].astype(F32)
    hidden = home_tokens + summed
    hidden_out[...] = hidden
    home_scale_out[...] = jnp.broadcast_to(rms_scale(home_tokens), (HOME, 128))
    home_ref[...] = (hidden * rms_scale(hidden) * moe_gains).astype(BF)
    place_home = load(home_ref, moe_in_all.at[y, c, z])
    keep_weights = [load(weights, weights_out), load(others, others_out)]
    place_home.wait()

    def onward():
        arrived(expert_pair_near[1] + expert_pair_near[-1])
        expert_far.extend(
            links.send(block, block, dx=-1) for block in expert_block(x_after, 1 - y_low)
        )

    siblings += spread(links, moe_in_all, home_ref, lambda: onward())
    arrived(expert_far)
    arrived(picked_near)
    arrived(siblings)
    place_picked.wait()
    for copy in keep_weights:
        copy.wait()

    for copy in links.made:
        if copy is not later:
            copy.wait_send()

    @pl.when(ctx == 0)
    def _():
        later.wait_send()


FRONT_COPIES = 6 + 12 + 12 + 18 + 18 + 3 + 1 + 4 + 38


def run_front(vmem, hbm):
    shape = jax.ShapeDtypeStruct
    outs = (
        (shape((4, 2, WROWS, 768), BF), ANY),
        (shape((4, 2, 256, 384), BF), ANY),
        (shape((4, 4, 2, 256, 256), BF), ANY),
        (shape((4, 128, WIDTH), BF), ANY),
        (shape((4, ROWS, WIDTH), BF), ANY),
        (shape((4, 16, ROWS), BF), ANY),
        (shape((4, 2, 4, HOME, WIDTH), BF), ANY),
        (shape((ROWS, WIDTH), BF), VMEM),
        (shape((ROWS, 512), F32), VMEM),
        (shape((ROWS, 512), BF), VMEM),
        (shape((ROWS, 512), BF), VMEM),
        (shape((ROWS, 512), BF), VMEM),
        (shape((ROWS, 256), BF), VMEM),
        (shape((2, ROWS, 128), F32), VMEM),
        (shape((HOME, WIDTH), F32), VMEM),
        (shape((HOME, 128), F32), VMEM),
    )
    return pl.pallas_call(
        front,
        out_shape=[o for o, _ in outs],
        in_specs=[VMEM] * len(vmem) + [ANY] * len(hbm),
        out_specs=[spec for _, spec in outs],
        scratch_shapes=[
            pltpu.VMEM((4, 2, WROWS, 768), BF),
            pltpu.VMEM((4, 2, 256, 384), BF),
            pltpu.VMEM((16, ROWS), BF),
            pltpu.VMEM((4, 256, 256), BF),
            pltpu.VMEM((4, 128, 256), BF),
            pltpu.VMEM((2, ROWS, ROWS), F32),
            pltpu.VMEM((2, ROWS, 128), F32),
            pltpu.VMEM((2, ROWS, 128), F32),
            pltpu.VMEM((2, HALF, WIDTH), BF),
            pltpu.VMEM((HALF, WIDTH), BF),
            pltpu.VMEM((3, HOME, WIDTH), BF),
            pltpu.VMEM((HOME, WIDTH), BF),
            pltpu.SemaphoreType.DMA((FRONT_COPIES,)),
            pltpu.SemaphoreType.DMA((FRONT_COPIES,)),
            pltpu.SemaphoreType.DMA((16,)),
        ],
        compiler_params=pltpu.CompilerParams(
            collective_id=1, has_side_effects=True, vmem_limit_bytes=56 * MIB
        ),
        name="front",
    )(*vmem, *hbm)


MCOLS = 1664


def scatter_buffers():
    return [
        pltpu.VMEM((2, HALF, WIDTH), BF),
        pltpu.VMEM((2, 2, 32, WIDTH), BF),
        pltpu.VMEM((2, 4, 32, WIDTH), BF),
        pltpu.VMEM((3, 32, WIDTH), BF),
        pltpu.VMEM((4, 2, 16, WIDTH), BF),
        pltpu.VMEM((4, 2, 32, WIDTH), BF),
        pltpu.VMEM((3, 32, WIDTH), BF),
    ]


class TokenSum:
    def __init__(self, links, give, keep, landings, credit):
        self.links, self.give, self.keep, self.credit = links, give, keep, credit
        (
            self.core_in, self.p_one_in, self.p_two_in, self.p_three_in,
            self.q_one_in, self.q_two_in, self.q_three_in,
        ) = landings
        self.core, self.p_one, self.p_two, self.q_one, self.q_two, self.q_three = {}, [], [], {}, {}, []

    def free(self, k):
        if k:
            self.links.left(self.core[k - 1])

    def give_core(self, k):
        if k >= 2:
            pl.semaphore_wait(self.credit, 1)
        self.core[k] = self.links.send(self.give, self.core_in.at[k % 2], dc=1)

    def q_rows(self, d, first=0, size=32):
        place = lax.rem(self.links.here[2] + d + 4, 4)
        return pl.ds(pl.multiple_of(place * HOME + 32 + first, 16), size)

    def add(self, k):
        links, keep = self.links, self.keep
        self.core[k].wait_recv()
        keep[k] = keep[k] + self.core_in[k % 2]
        if k < 2:
            x, y, z, c = links.here
            pl.semaphore_signal(
                self.credit,
                inc=1,
                device_id=device(x, y, z, c + 1),
                device_id_type=pl.DeviceIdType.MESH,
            )
        self.q_one[k] = [
            links.send(keep.at[k, self.q_rows(2, 16 * n, 16)], self.q_one_in.at[k, n], dz=d)
            for n, d in enumerate((1, -1))
        ]
        if k == 0:
            rows = keep.at[0].reshape(4, HOME, WIDTH)
            first = pl.ds(0, 32)
            self.p_one = [
                links.send(rows.at[pl.ds(0, 2), first], self.p_one_in.at[0], dy=1),
                links.send(rows.at[pl.ds(2, 2), first], self.p_one_in.at[1], dy=-1),
            ]

    def p_step(self, k):
        links, keep, n = self.links, self.keep, k - 1
        self.p_one[n].wait_recv()
        for i in range(2):
            row = (2 * n + i) * HOME
            keep[k, row : row + 32] = keep[k, row : row + 32] + self.p_one_in[n, i]
        rows = keep.at[k].reshape(4, HOME, WIDTH)
        self.p_two.append(
            links.send(rows.at[:, pl.ds(0, 32)], self.p_two_in.at[n], dy=(1, -1)[n])
        )

    def second(self, k):
        links, keep = self.links, self.keep
        self.q_two[k] = []
        for n, d in enumerate((1, -1)):
            self.q_one[k][n].wait_recv()
            rows = self.q_rows(d, 16 * n, 16)
            keep[k, rows, :] = keep[k, rows, :] + self.q_one_in[k, n]
            self.q_two[k].append(
                links.send(keep.at[k, self.q_rows(d)], self.q_two_in.at[k, n], dz=d)
            )

    def q_sum(self, k):
        arrived(self.q_two[k])
        part = self.keep[k, self.q_rows(0), :].astype(F32)
        for n in range(2):
            part = part + self.q_two_in[k, n].astype(F32)
        return part

    def third(self, k, buffer):
        buffer[k] = self.q_sum(k).astype(BF)
        self.q_three.append(
            self.links.send(buffer.at[k], self.q_three_in.at[k], dy=(2, 1, -1)[k])
        )

    def p_send(self):
        links, keep = self.links, self.keep
        z = links.here[2]
        arrived(self.p_two)
        for place in range(4):
            row = place * HOME
            keep[3, row : row + 32] = (
                keep[3, row : row + 32].astype(F32)
                + self.p_two_in[0, place].astype(F32)
                + self.p_two_in[1, place].astype(F32)
            ).astype(BF)
        self.p_three = [
            links.send(
                keep.at[3, at(lax.rem(z + d + 4, 4) * HOME, 32)], self.p_three_in.at[n], dz=d
            )
            for n, d in enumerate((1, -1, 2))
        ]

    def home(self):
        z = self.links.here[2]
        second = self.q_sum(3)
        arrived(self.q_three)
        for n in range(3):
            second = second + self.q_three_in[n].astype(F32)
        arrived(self.p_three)
        first = self.keep[3, at(z * HOME, 32), :].astype(F32)
        for n in range(3):
            first = first + self.p_three_in[n].astype(F32)
        return first, second


TOKEN_SUM_COPIES = 4 + 8 + 8 + 2 + 2 + 3 + 3


def spread_home(links, array, home_ref):
    x, y, z, c = links.here
    return [links.send(home_ref, array.at[c, z], dz=d) for d in (1, -1, 2)]


def experts(
    x_all, g_all, picked_all, own_grad, w_in_hbm, w_out_hbm, weights, others, hidden_ref,
    grad_out, grad_near_out, low_all, hidden_grad_out, gain_out, layer_out,
    w_in, w_out, gain_ref, x_ref, g_ref, picked_ref, gates_ref, gate_grad_ref, back_ref, pre_ref,
    gated_ref, give, keep, keep_layer, grad_far, grad_stage, q_buffer, q_layer, home_ref,
    core_in, p_one_in, p_two_in, p_three_in, q_one_in, q_two_in, q_three_in,
    core_layer, p_one_layer, p_two_layer, p_three_layer, q_one_layer, q_two_layer, q_three_layer,
    credits, send_sems, recv_sems, local_sems,
):
    links = Links(send_sems, recv_sems)
    x, y, z, c = links.here
    x_after, x_before, x_far = lax.rem(x + 1, 4), lax.rem(x + 3, 4), lax.rem(x + 2, 4)
    order = (lax.rem(y + 2, 4), lax.rem(y + 1, 4), lax.rem(y + 3, 4), y)
    loads = []

    def load(source, target):
        copy = pltpu.make_async_copy(source, target, local_sems.at[len(loads)])
        copy.start()
        loads.append(copy)
        return copy

    first = [load(g_all.at[order[0]], g_ref.at[0]), load(w_out_hbm, w_out)]
    first += [load(picked_all.at[place], picked_ref.at[k]) for k, place in enumerate(order)]
    first.append(load(others.at[:, :, :, pl.ds(0, 128)], w_in.at[:, :, :, pl.ds(1024, 128)]))
    first.append(load(weights.at[:, :, pl.ds(256, 16), pl.ds(0, 256)], gain_ref))
    first.append(load(x_all.at[order[0]], x_ref.at[0]))
    first += [
        load(w_in_hbm.at[e], w_in.at[:, :, :, pl.ds(e * 256, 256)]) for e in range(4)
    ]
    rest = [
        [
            load(g_all.at[order[k]] if k < 3 else own_grad, g_ref.at[k]),
            load(x_all.at[order[k]], x_ref.at[k]),
        ]
        for k in range(1, 4)
    ]
    links.greet(STEPS_X + STEPS_Y + STEPS_Z + STEPS_C)
    for copy in first:
        copy.wait()

    sums = TokenSum(
        links, give.at[0], keep,
        (core_in, p_one_in, p_two_in, p_three_in, q_one_in, q_two_in, q_three_in), credits.at[0],
    )
    layer_sums = TokenSum(
        links, give.at[1], keep_layer,
        (
            core_layer, p_one_layer, p_two_layer, p_three_layer, q_one_layer, q_two_layer, q_three_layer,
        ),
        credits.at[1],
    )
    lanes = lax.broadcasted_iota(jnp.int32, (ROWS, 128), 1)
    own_rows = at(c * HALF, HALF)
    other_rows = at((1 - c) * HALF, HALF)

    def in_block(first_column, size):
        return w_in[:, :, :, pl.ds(first_column, size)].reshape(WIDTH, size)

    for k in range(4):
        if k:
            for copy in rest[k - 1]:
                copy.wait()
        logits = dot(x_ref[k], in_block(1024, 128))
        marks = jnp.concatenate([picked_ref[k].astype(F32), jnp.zeros((112, ROWS), F32)], axis=0)
        logits = jnp.where(marks.T > 0.5, logits, MASKED_SCORE)
        exponents = jnp.exp(logits - jnp.max(logits, axis=-1, keepdims=True))
        gates_ref[...] = exponents / jnp.sum(exponents, axis=-1, keepdims=True)
        gate_grad_ref[...] = jnp.zeros_like(gate_grad_ref)
        back_ref[...] = dot_nt(g_ref[k], w_out[...].reshape(512, WIDTH))

        def two_experts(pair, carry, k=k):
            joined = dot(x_ref[k], in_block(pl.multiple_of(pair * 512, 512), 512))
            for n in range(2):
                one_expert(pair * 2 + n, joined[:, n * 256 : n * 256 + 256])
            return carry

        def one_expert(e, joined, k=k):
            gate_pre, up_pre = joined[:, :128], joined[:, 128:]
            logistic = 1.0 / (1.0 + jnp.exp(-gate_pre))
            silu_gate = gate_pre * logistic
            silu_slope = logistic * (1.0 + gate_pre * (1.0 - logistic))
            act = silu_gate * up_pre
            back = back_ref[:, at(e * 128, 128)]
            mine = lanes == y * 4 + e
            gate = jnp.sum(jnp.where(mine, gates_ref[...], 0.0), axis=-1, keepdims=True)
            term = jnp.sum(act.astype(BF).astype(F32) * back, axis=-1, keepdims=True)
            gate_grad_ref[...] += jnp.where(mine, term, 0.0)
            act_grad = back * gate
            pre_ref[k, :, pl.ds(pl.multiple_of(e * 256, 256), 128)] = (
                act_grad * up_pre * silu_slope
            ).astype(BF)
            pre_ref[k, :, pl.ds(pl.multiple_of(e * 256 + 128, 128), 128)] = (
                act_grad * silu_gate
            ).astype(BF)
            gated_ref[k, :, at(e * 128, 128)] = (act * gate).astype(BF)

        lax.fori_loop(0, 2, two_experts, 0)
        gates, gate_grad = gates_ref[...], gate_grad_ref[...]
        logit_grad = gates * (gate_grad - jnp.sum(gates * gate_grad, axis=-1, keepdims=True))
        pre_ref[k, :, 1024:1152] = logit_grad.astype(BF)

        def back_rows(rows, target, k=k):
            for s in range(0, 4, 2):
                block = w_in[s : s + 2].reshape(1024, 1152)
                target[:, s * 512 : s * 512 + 1024] = dot_nt(pre_ref[k, rows, :], block).astype(BF)

        def layer_rows(rows, target, k=k):
            for s in range(0, WIDTH, 1024):
                block = w_out[:, :, s : s + 1024].reshape(512, 1024)
                target[:, s : s + 1024] = dot(gated_ref[k, rows, :], block).astype(BF)

        sums.free(k)
        back_rows(other_rows, give.at[0])
        sums.give_core(k)
        layer_sums.free(k)
        layer_rows(other_rows, give.at[1])
        layer_sums.give_core(k)
        back_rows(own_rows, keep.at[k])
        layer_rows(own_rows, keep_layer.at[k])
        sums.add(k)
        if k in (1, 2):
            sums.p_step(k)
        layer_sums.add(k)
        if k > 0:
            sums.second(k - 1)
            layer_sums.second(k - 1)
        if k > 1:
            layer_sums.p_step(k - 1)
            sums.third(k - 2, q_buffer)
            layer_sums.third(k - 2, q_layer)
    sums.second(3)
    sums.third(2, q_buffer)
    sums.p_send()

    def weight_grad(slot, target):
        columns = at(slot * 256, 256)
        rows = x_ref[:, :, columns].reshape(4 * ROWS, 256)
        target[:, 0:1152] = dot_tn(rows, pre_ref[...].reshape(4 * ROWS, 1152)).astype(BF)
        rows = g_ref[:, :, columns].reshape(4 * ROWS, 256)
        target[:, 1152:MCOLS] = dot_tn(rows, gated_ref[...].reshape(4 * ROWS, 512)).astype(BF)

    def far_slot(i, carry):
        weight_grad(x_far * 2 + i, grad_far.at[i])
        return carry

    lax.fori_loop(0, 2, far_slot, 0)
    near = [
        links.send(grad_far.at[0], grad_near_out.at[0], dx=1),
        links.send(grad_far.at[1], grad_near_out.at[1], dx=-1),
    ]

    moe_gains = jnp.concatenate(
        [gain_ref[s // 2, s % 2].astype(F32)[1:2] for s in range(8)], axis=1
    )
    moe_grad = jnp.concatenate(sums.home(), axis=0)
    hidden = hidden_ref[...]
    home_grad = g_ref[3, at(c * HALF + z * HOME, HOME), :].astype(F32)
    back, gain_rows = norm_back(moe_grad, hidden, rms_scale(hidden), moe_gains)
    hidden_grad = home_grad + back
    hidden_grad_out[...] = hidden_grad
    gain_out[...] = jnp.broadcast_to(jnp.sum(gain_rows, axis=0, keepdims=True), (8, WIDTH))
    home_ref[...] = hidden_grad.astype(BF)
    place_home = load(home_ref, low_all.at[c, z])
    low_near = spread_home(links, low_all, home_ref)
    layer_sums.second(3)
    layer_sums.third(2, q_layer)
    layer_sums.p_send()

    first_sem = len(loads)

    def stage(i, n):
        slot = lax.rem(x_far * 2 + 2 + 2 * i + n, 8)
        return pltpu.make_async_copy(
            grad_stage.at[n], grad_out.at[slot], local_sems.at[first_sem + n]
        )

    def other_grads(i, carry):
        for n in range(2):

            @pl.when(i > 0)
            def _():
                stage(i - 1, n).wait()

            weight_grad(lax.rem(x_far * 2 + 2 + 2 * i + n, 8), grad_stage.at[n])
            stage(i, n).start()
        return carry

    lax.fori_loop(0, 2, other_grads, 0)
    arrived(low_near)
    place_home.wait()
    sibling = links.send(low_all.at[c], low_all.at[c], dc=1)
    layer_grad = jnp.concatenate(layer_sums.home(), axis=0)
    layer_out[...] = (hidden_ref[...] + layer_grad).astype(BF)
    other_grads(2, 0)
    for n in range(2):
        stage(2, n).wait()
    arrived(near)
    sibling.wait_recv()
    links.finish()


EXPERT_COPIES = 2 * TOKEN_SUM_COPIES + 2 + 3 + 1


def run_experts(moe_in_all, *rest):
    shape = jax.ShapeDtypeStruct
    outs = (
        (shape((8, 256, MCOLS), BF), ANY),
        (shape((2, 256, MCOLS), BF), ANY),
        (shape((2, 4, HOME, WIDTH), BF), ANY),
        (shape((HOME, WIDTH), F32), VMEM),
        (shape((8, WIDTH), F32), VMEM),
        (shape((HOME, WIDTH), BF), VMEM),
    )
    return pl.pallas_call(
        experts,
        out_shape=[o for o, _ in outs],
        in_specs=[ANY] * 8 + [VMEM],
        out_specs=[spec for _, spec in outs],
        scratch_shapes=[
            pltpu.VMEM((4, 2, 256, 1152), BF),
            pltpu.VMEM((4, 128, WIDTH), BF),
            pltpu.VMEM((4, 2, 16, 256), BF),
            pltpu.VMEM((4, ROWS, WIDTH), BF),
            pltpu.VMEM((4, ROWS, WIDTH), BF),
            pltpu.VMEM((4, 16, ROWS), BF),
            pltpu.VMEM((ROWS, 128), F32),
            pltpu.VMEM((ROWS, 128), F32),
            pltpu.VMEM((ROWS, 512), F32),
            pltpu.VMEM((4, ROWS, 1152), BF),
            pltpu.VMEM((4, ROWS, 512), BF),
            pltpu.VMEM((2, HALF, WIDTH), BF),
            pltpu.VMEM((4, HALF, WIDTH), BF),
            pltpu.VMEM((4, HALF, WIDTH), BF),
            pltpu.VMEM((2, 256, MCOLS), BF),
            pltpu.VMEM((2, 256, MCOLS), BF),
            pltpu.VMEM((3, 32, WIDTH), BF),
            pltpu.VMEM((3, 32, WIDTH), BF),
            pltpu.VMEM((HOME, WIDTH), BF),
            *scatter_buffers(),
            *scatter_buffers(),
            pltpu.SemaphoreType.REGULAR((2,)),
            pltpu.SemaphoreType.DMA((EXPERT_COPIES,)),
            pltpu.SemaphoreType.DMA((EXPERT_COPIES,)),
            pltpu.SemaphoreType.DMA((24,)),
        ],
        compiler_params=pltpu.CompilerParams(
            collective_id=2, has_side_effects=True, vmem_limit_bytes=62 * MIB
        ),
        name="experts",
    )(
        moe_in_all.reshape(4, ROWS, WIDTH),
        *rest,
    )


SMALL = 264


def back(
    grad_moe, grad_near, low_hbm, weights, others, mixed_hbm, rot_hbm, kv_hbm, kv_far_hbm, lse_hbm, pre_hbm,
    normed_hbm, tok_hbm,
    layer_ref, hidden_grad_ref, home_scale_ref, gain_ref, cosine_ref, sine_ref, segment_row,
    layer_all, input_all, groups_in, groups_out, moe_in,
    grad_q, grad_k, grad_v, grad_o, small_out, heads_out,
    w_ref, w_gains, low, mixed, rot, kv, kv_far, lse, pre, home_tok,
    bias, mixed_grad, dq, dkv, kv_give, kv_got, stacked,
    moe_after, moe_before, moe_near, pay_in, pay_out,
    attn_grad, attn_one, attn_two, attn_give, attn_keep, attn_y_one, attn_y_two,
    part, part_core, part_z, home_in,
    sums_ref, sums_x, sums_y, pair_ref, small_ref, small_z, small_c, routed,
    send_sems, recv_sems, local_sems,
):
    links = Links(send_sems, recv_sems)
    x, y, z, c = links.here
    ctx, y_low = y // 2, lax.rem(y, 2)
    x_after, x_before, x_far = lax.rem(x + 1, 4), lax.rem(x + 3, 4), lax.rem(x + 2, 4)
    own_rows, other_rows = at(c * HALF, HALF), at((1 - c) * HALF, HALF)
    loads = []

    def load(source, target):
        copy = pltpu.make_async_copy(source, target, local_sems.at[len(loads)])
        copy.start()
        loads.append(copy)
        return copy

    def pair_of(array, place):
        return array.at[at(place * 2, 2)]

    near_loads = [
        load(pair_of(grad_moe, x_after), moe_after),
        load(pair_of(grad_moe, x_before), moe_before),
        load(grad_near, moe_near),
    ]
    every = pl.ds(0, 256)
    out_loads = [
        load(low_hbm, low),
        load(others.at[:, :, :, pl.ds(128, 256)], w_ref.at[:, :, :, pl.ds(768, 256)]),
        load(mixed_hbm, mixed),
        load(rot_hbm, rot),
        load(kv_hbm, kv),
        load(kv_far_hbm, kv_far),
        load(lse_hbm, lse),
    ]
    next_loads = [
        load(pre_hbm, pre),
        load(weights.at[:, :, every, pl.ds(0, 768)], w_ref.at[:, :, :, pl.ds(0, 768)]),
        load(weights.at[:, :, pl.ds(256, 16), every], w_gains),
        load(tok_hbm.at[at(c * HALF + z * HOME, HOME)], home_tok),
    ]
    links.greet(STEPS_X + [(2, 0, 0, 0)] + STEPS_Y + STEPS_Z + STEPS_C)

    for copy in near_loads:
        copy.wait()
    moe_after[0] = (moe_after[0].astype(F32) + moe_near[0].astype(F32)).astype(BF)
    moe_two = [links.send(moe_after, moe_in.at[0], dx=1)]
    moe_before[1] = (moe_before[1].astype(F32) + moe_near[1].astype(F32)).astype(BF)
    moe_two.append(links.send(moe_before, moe_in.at[1], dx=-1))
    moe_own = moe_near
    own_load = load(pair_of(grad_moe, x), moe_own)

    place_layer = load(layer_ref, layer_all.at[c, z])
    layer_near = spread_home(links, layer_all, layer_ref)

    own_first = at(ctx * ROWS, ROWS)
    for copy in out_loads:
        copy.wait()
    total = jnp.zeros((ROWS, 256), F32)
    for s in range(8):
        total = total + dot_nt(low[:, s * 256 : s * 256 + 256], w_ref[s // 2, s % 2, :, 768:1024])
    mixed_grad[...] = total.astype(BF)

    score_scale = 128 ** (-0.5)
    deltas = []
    for h in range(2):
        lane = slice(h * 128, h * 128 + 128)
        deltas.append(
            jnp.sum(
                mixed_grad[:, lane].astype(F32) * mixed[:, lane].astype(F32), axis=-1, keepdims=True
            )
        )

    def scores_back(h, keys_values):
        lane = slice(h * 128, h * 128 + 128)
        keys, values = keys_values[:, lane], keys_values[:, 256 + h * 128 : 384 + h * 128]
        scores = dot_nt(rot[:, lane], keys) * score_scale + bias[...]
        probs = jnp.exp(scores - lse[h][:, 0:1])
        prob_grad = dot_nt(mixed_grad[:, lane], values)
        score_grad = (probs * (prob_grad - deltas[h])).astype(BF)
        query_part = dot(score_grad, keys) * score_scale
        key_part = dot_tn(score_grad, rot[:, lane]) * score_scale
        value_part = dot_tn(probs.astype(BF), mixed_grad[:, lane])
        return query_part, key_part, value_part

    earlier = links.send(kv_give, kv_got, dy=2, start=False)

    @pl.when(ctx == 1)
    def _():
        bias[...] = earlier_mask(segment_row, ctx * ROWS)
        for h in range(2):
            query_part, key_part, value_part = scores_back(h, kv_far)
            dq[:, h * 128 : h * 128 + 128] = query_part
            kv_give[:, h * 128 : h * 128 + 128] = key_part.astype(BF)
            kv_give[:, 256 + h * 128 : 384 + h * 128] = value_part.astype(BF)
        earlier.start()

    @pl.when(ctx == 0)
    def _():
        dq[...] = jnp.zeros_like(dq)

    bias[...] = own_mask(segment_row, ctx * ROWS)
    for h in range(2):
        query_part, key_part, value_part = scores_back(h, kv)
        dq[:, h * 128 : h * 128 + 128] += query_part
        dkv[:, h * 128 : h * 128 + 128] = key_part
        dkv[:, 256 + h * 128 : 384 + h * 128] = value_part

    def out_grad_block(s, carry):
        attn_grad[s, :, 768:1024] = dot_tn(mixed[...], low[:, at(s * 256, 256)]).astype(BF)
        return carry

    lax.fori_loop(0, 8, out_grad_block, 0)
    normed = low
    normed_load = load(normed_hbm, normed)
    for copy in next_loads:
        copy.wait()
    head_gains = jnp.zeros((16, 128), F32)
    for s in range(8):
        head_gains = head_gains + w_gains[s // 2, s % 2, :, 0:128].astype(F32)
    cosine, sine = cosine_ref[own_first, :], sine_ref[own_first, :]

    def head_back(grads, first, first_gain):
        for h in range(2):
            lane = slice(first + h * 128, first + h * 128 + 128)
            unit_grad = turned(
                grads[:, h * 128 : h * 128 + 128].astype(BF).astype(F32), cosine, -sine
            )
            source = pre[:, lane]
            gain = head_gains[first_gain + h : first_gain + h + 1]
            grad, gain_rows = norm_back(unit_grad, source, rms_scale(source), gain)
            stacked[:, lane] = grad.astype(BF)
            row = first_gain - 2 + h
            heads_row = jnp.sum(gain_rows, axis=0, keepdims=True)
            for s in range(8):
                sums_ref[s // 2, s % 2, row + 2 : row + 3, 0:128] = heads_row
                sums_ref[s // 2, s % 2, row + 2 : row + 3, 128:256] = jnp.zeros_like(heads_row)

    head_back(dq, 0, 2)

    @pl.when(ctx == 0)
    def _():
        earlier.wait_recv()
        dkv[...] += kv_got[...].astype(F32)

    head_back(dkv, 256, 4)
    stacked[:, 512:768] = dkv[:, 256:512].astype(BF)

    def input_rows(rows, target):
        def one_block(s, carry):
            block = w_ref[s // 2, lax.rem(s, 2), :, 0:768]
            part[target, :, at(s * 256, 256)] = dot_nt(stacked[rows, :], block).astype(BF)
            return carry

        lax.fori_loop(0, 8, one_block, 0)

    input_rows(other_rows, 1)
    core_sum = links.send(part.at[1], part_core, dc=1)
    input_rows(own_rows, 0)

    def weight_block(slot):
        attn_grad[slot, :, 0:768] = dot_tn(normed[:, at(slot * 256, 256)], stacked[...]).astype(BF)

    normed_load.wait()
    weight_block(x_far * 2)
    weight_block(x_far * 2 + 1)
    attn_first = [
        links.send(attn_grad.at[x_far * 2], attn_one.at[0], dx=1),
        links.send(attn_grad.at[x_far * 2 + 1], attn_one.at[1], dx=-1),
    ]
    core_sum.wait_recv()
    part[0] = (part[0].astype(F32) + part_core[...].astype(F32)).astype(BF)
    z_sum = [
        links.send(part.at[0, at(lax.rem(z + d + 4, 4) * HOME, HOME)], part_z.at[k], dz=d)
        for k, d in enumerate((1, -1, 2))
    ]

    def other_blocks(i, carry):
        weight_block(lax.rem(x_far * 2 + 2 + i, 8))
        return carry

    lax.fori_loop(0, 6, other_blocks, 0)
    arrived(layer_near)
    place_layer.wait()
    siblings = [links.send(layer_all.at[c], layer_all.at[c], dc=1)]

    arrived(z_sum)
    normed_grad = part[0, at(z * HOME, HOME), :].astype(F32)
    for k in range(3):
        normed_grad = normed_grad + part_z[k].astype(F32)
    gains = jnp.concatenate(
        [w_gains[s // 2, s % 2].astype(F32)[0:1] for s in range(8)], axis=1
    )
    input_back, gain_rows = norm_back(
        normed_grad, home_tok[...].astype(F32), home_scale_ref[:, 0:1], gains
    )
    home_in[...] = (hidden_grad_ref[...] + input_back).astype(BF)
    gain_row = jnp.sum(gain_rows, axis=0, keepdims=True)
    for s in range(8):
        columns = slice(s * 256, s * 256 + 256)
        sums_ref[s // 2, s % 2, 0:1, :] = gain_row[:, columns]
        sums_ref[s // 2, s % 2, 1:2, :] = gain_ref[0:1, columns]
        sums_ref[s // 2, s % 2, 6:16, :] = jnp.zeros((10, 256), F32)
    place_in = load(home_in, input_all.at[c, z])
    input_near = spread_home(links, input_all, home_in)
    sum_x = [
        links.send(sums_ref.at[lax.rem(x + d + 4, 4)], sums_x.at[k], dx=d)
        for k, d in enumerate((1, -1, 2))
    ]

    arrived(moe_two)
    arrivals = []
    for n, target in enumerate((moe_after, moe_before)):
        links.left(moe_two[n])
        arrivals.append(load(moe_in.at[n], target))
    own_load.wait()
    for copy in arrivals:
        copy.wait()
    for i in range(2):
        total = moe_own[i].astype(F32) + moe_after[i].astype(F32) + moe_before[i].astype(F32)
        for e in range(4):
            pay_in[i, e] = total[:, e * 256 : e * 256 + 128].astype(BF)
            pay_in[i, 4 + e] = total[:, e * 256 + 128 : e * 256 + 256].astype(BF)
            pay_out[i, e] = total[:, 1152 + e * 128 : 1280 + e * 128].T.astype(BF)
        pay_in[i, 8] = total[:, 1024:1152].astype(BF)
    groups = []
    for d, low_place in ((1, 1 - y_low), (-1, 1 - y_low), (2, y_low)):
        groups.append(links.send(pay_in.at[low_place], groups_in.at[y], dy=d))
        groups.append(links.send(pay_out.at[low_place], groups_out.at[y], dy=d))
    place_groups = [load(pay_in.at[y_low], groups_in.at[y]), load(pay_out.at[y_low], groups_out.at[y])]

    arrived(attn_first)
    slot = x_after * 2
    attn_grad[slot] = (attn_grad[slot].astype(F32) + attn_one[0].astype(F32)).astype(BF)
    attn_next = [links.send(pair_of(attn_grad, x_after), attn_two.at[0], dx=1)]
    slot = x_before * 2 + 1
    attn_grad[slot] = (attn_grad[slot].astype(F32) + attn_one[1].astype(F32)).astype(BF)
    attn_next.append(links.send(pair_of(attn_grad, x_before), attn_two.at[1], dx=-1))

    arrived(input_near)
    place_in.wait()
    siblings.append(links.send(input_all.at[c], input_all.at[c], dc=1))

    arrived(sum_x)
    pair_ref[...] = sums_ref[x] + sums_x[0] + sums_x[1] + sums_x[2]
    sum_y = [
        links.send(pair_ref.at[low_place], sums_y.at[k], dy=d)
        for k, (d, low_place) in enumerate(((1, 1 - y_low), (-1, 1 - y_low), (2, y_low)))
    ]
    arrived(groups)
    for copy in place_groups:
        copy.wait()
    get_routed = load(groups_in.at[:, 8], routed)
    arrived(sum_y)
    summed = pair_ref[y_low] + sums_y[0] + sums_y[1] + sums_y[2]
    heads_out[...] = jnp.concatenate([summed[2:6, 0:128], jnp.zeros((4, 128), F32)], axis=0)
    get_routed.wait()
    small_ref[0:256] = (
        routed[0].astype(F32) + routed[1].astype(F32) + routed[2].astype(F32) + routed[3].astype(F32)
    )
    small_ref[256:SMALL] = jnp.concatenate(
        [summed[0:2, 0:128], summed[0:2, 128:256], jnp.zeros((4, 128), F32)], axis=0
    )
    small_sums = [
        links.send(small_ref, small_z.at[k], dz=d) for k, d in enumerate((1, -1, 2))
    ]

    arrived(attn_next)
    def attn_total(low_place):
        slot = x * 2 + low_place
        return (
            attn_grad[slot].astype(F32)
            + attn_two[0, low_place].astype(F32)
            + attn_two[1, low_place].astype(F32)
        )

    attn_give[...] = attn_total(1 - y_low).astype(BF)
    top, bottom = pl.ds(0, 128), pl.ds(128, 128)
    y_first = [
        links.send(attn_give.at[top], attn_y_one.at[top], dy=1),
        links.send(attn_give.at[bottom], attn_y_one.at[bottom], dy=-1),
    ]
    kept = attn_total(y_low)
    arrived(small_sums)
    small_ref_total = small_ref[...] + small_z[0] + small_z[1] + small_z[2]
    small_out[...] = small_ref_total
    small_core = links.send(small_out, small_c, dc=1)
    arrived(y_first)
    attn_keep[...] = (kept + attn_y_one[...].astype(F32)).astype(BF)
    y_second = links.send(attn_keep, attn_y_two, dy=2)
    small_core.wait()
    small_out[...] = small_ref_total + small_c[...]
    arrived(siblings)
    y_second.wait_recv()
    for n, target in enumerate((grad_q, grad_k, grad_v, grad_o)):
        columns = slice(n * 256, n * 256 + 256)
        target[...] = attn_keep[:, columns].astype(F32) + attn_y_two[:, columns].astype(F32)

    for copy in links.made:
        if copy is not earlier and copy is not small_core:
            copy.wait_send()

    @pl.when(ctx == 1)
    def _():
        earlier.wait_send()


BACK_COPIES = 2 + 1 + 1 + 3 + 2 + 3 + 3 + 6 + 2 + 3 + 2 + 3 + 3 + 1 + 3


def run_back(hbm, vmem):
    shape = jax.ShapeDtypeStruct
    outs = (
        (shape((2, 4, HOME, WIDTH), BF), ANY),
        (shape((2, 4, HOME, WIDTH), BF), ANY),
        (shape((4, 9, 256, 128), BF), ANY),
        (shape((4, 4, 128, 256), BF), ANY),
        (shape((2, 2, 256, MCOLS), BF), ANY),
        (shape((256, 256), F32), VMEM),
        (shape((256, 256), F32), VMEM),
        (shape((256, 256), F32), VMEM),
        (shape((256, 256), F32), VMEM),
        (shape((SMALL, 128), F32), VMEM),
        (shape((8, 128), F32), VMEM),
    )

    def buffer(*dims, kind=BF):
        return pltpu.VMEM(dims, kind)

    return pl.pallas_call(
        back,
        out_shape=[o for o, _ in outs],
        in_specs=[ANY] * len(hbm) + [VMEM] * len(vmem),
        out_specs=[spec for _, spec in outs],
        scratch_shapes=[
            buffer(4, 2, 256, 1024),
            buffer(4, 2, 16, 256),
            buffer(ROWS, WIDTH),
            buffer(ROWS, 256),
            buffer(ROWS, 512),
            buffer(ROWS, 512),
            buffer(ROWS, 512),
            buffer(2, ROWS, 128, kind=F32),
            buffer(ROWS, 512, kind=F32),
            buffer(HOME, WIDTH),
            buffer(ROWS, ROWS, kind=F32),
            buffer(ROWS, 256),
            buffer(ROWS, 256, kind=F32),
            buffer(ROWS, 512, kind=F32),
            buffer(ROWS, 512),
            buffer(ROWS, 512),
            buffer(ROWS, 768),
            buffer(2, 256, MCOLS),
            buffer(2, 256, MCOLS),
            buffer(2, 256, MCOLS),
            buffer(2, 9, 256, 128),
            buffer(2, 4, 128, 256),
            buffer(8, 256, 1024),
            buffer(2, 256, 1024),
            buffer(2, 2, 256, 1024),
            buffer(256, 1024),
            buffer(256, 1024),
            buffer(256, 1024),
            buffer(256, 1024),
            buffer(2, HALF, WIDTH),
            buffer(HALF, WIDTH),
            buffer(3, HOME, WIDTH),
            buffer(HOME, WIDTH),
            buffer(4, 2, 16, 256, kind=F32),
            buffer(3, 2, 16, 256, kind=F32),
            buffer(3, 16, 256, kind=F32),
            buffer(2, 16, 256, kind=F32),
            buffer(SMALL, 128, kind=F32),
            buffer(3, SMALL, 128, kind=F32),
            buffer(SMALL, 128, kind=F32),
            buffer(4, 256, 128),
            pltpu.SemaphoreType.DMA((BACK_COPIES,)),
            pltpu.SemaphoreType.DMA((BACK_COPIES,)),
            pltpu.SemaphoreType.DMA((32,)),
        ],
        compiler_params=pltpu.CompilerParams(
            collective_id=3, has_side_effects=True, vmem_limit_bytes=62 * MIB
        ),
        name="back",
    )(*hbm, *vmem)


def turn_tables():
    frequency = ROPE_BASE ** (-(np.arange(0, 128, 2, dtype=np.float64) / 128))
    angles = np.arange(1024, dtype=np.float64)[:, None] * frequency[None, :]
    cosine, sine = np.cos(angles), np.sin(angles)
    return (
        np.concatenate([cosine, cosine], axis=1).astype(np.float32),
        np.concatenate([-sine, sine], axis=1).astype(np.float32),
    )


def body(
    tokens,
    out_grad,
    segments,
    routes,
    query_weight,
    key_weight,
    value_weight,
    out_weight,
    router_weight,
    attn_gain,
    moe_gain,
    query_gain,
    key_gain,
    gate_weight,
    up_weight,
    down_weight,
):
    rows, width = tokens.shape[1], tokens.shape[2]
    experts_count = gate_weight.shape[0]
    shard = lax.axis_index("shard")

    own_grad = out_grad.reshape(rows, width)
    own_tokens = tokens.reshape(rows, width)
    tables = [jnp.asarray(table) for table in turn_tables()]
    (
        weights, others, experts_in, experts_out, grad_all, picked_all, moe_in_all,
        normed, pre, rot, key_value, key_value_far, mixed, lse, hidden, home_scale,
    ) = run_front(
        [
            own_tokens, router_weight, jnp.stack([attn_gain, moe_gain]), query_gain, key_gain, *tables,
            segments, routes.reshape(rows, -1),
        ],
        [
            query_weight, key_weight, value_weight, out_weight, gate_weight, up_weight, down_weight,
            own_grad,
        ],
    )
    grad_moe, grad_near, hidden_low, hidden_grad, gain_sum, layer_rows = run_experts(
        moe_in_all, grad_all, picked_all, own_grad, experts_in, experts_out, weights, others, hidden
    )
    (
        layer_all, input_all, groups_in, groups_out, _, grad_q, grad_k, grad_v, grad_o, small, heads,
    ) = run_back(
        [
            grad_moe, grad_near, hidden_low.reshape(rows, width), weights, others, mixed, rot, key_value,
            key_value_far, lse, pre, normed, own_tokens,
        ],
        [layer_rows, hidden_grad, home_scale, gain_sum, *tables, segments],
    )
    head_grads = lax.dynamic_slice_in_dim(heads[:4], shard * 16, 16, 1)

    def grown(groups):
        return groups.reshape((experts_count,) + groups.shape[2:]).astype(F32)

    return (
        layer_all.reshape(tokens.shape),
        input_all.reshape(tokens.shape),
        grad_q,
        grad_k,
        grad_v,
        grad_o,
        small[:256, :experts_count],
        small[256::2][:2].reshape(-1),
        small[257::2][:2].reshape(-1),
        head_grads[:2],
        head_grads[2:],
        grown(groups_in[:, :4]),
        grown(groups_in[:, 4:8]),
        grown(groups_out),
    )


def solution(mesh):
    return jax.shard_map(
        body,
        mesh=mesh,
        in_specs=(
            P("shard", "ctx", None),
            P("shard", "ctx", None),
            P("shard", None),
            P("shard", "ctx", None),
            P("shard", "tp"),
            P("shard", "tp"),
            P("shard", "tp"),
            P("tp", "shard"),
            P("shard", None),
            P("shard"),
            P("shard"),
            P("tp", "shard"),
            P("tp", "shard"),
            P(None, "shard", "tp"),
            P(None, "shard", "tp"),
            P(None, "tp", "shard"),
        ),
        out_specs=(
            P("shard", "ctx", None),
            P("shard", "ctx", None),
            P("shard", "tp"),
            P("shard", "tp"),
            P("shard", "tp"),
            P("tp", "shard"),
            P("shard", None),
            P("shard"),
            P("shard"),
            P("tp", "shard"),
            P("tp", "shard"),
            P(None, "shard", "tp"),
            P(None, "shard", "tp"),
            P(None, "tp", "shard"),
        ),
        check_vma=False,
    )
```

```python
import jax
import jax.numpy as jnp
import numpy as np
from jax import lax
from jax.experimental import pallas as pl
from jax.experimental.pallas import tpu as pltpu
from jax.sharding import PartitionSpec as P

EPSILON = 1e-05
ROPE_BASE = 10000.0
MASKED_SCORE = -1e30
AXES = ("shard", "ctx", "tp")
BF = jnp.bfloat16
F32 = jnp.float32

def rms_scale(values):
    return lax.rsqrt(jnp.mean(values * values, axis=-1, keepdims=True) + EPSILON)


def norm_back(grad_normed, source, scale_row, gain_row):
    unit_values = source * scale_row
    grad_unit = grad_normed * gain_row
    grad_source = scale_row * (
        grad_unit - unit_values * jnp.mean(grad_unit * unit_values, axis=-1, keepdims=True)
    )
    return (grad_source, grad_normed * unit_values)


def dot(left, right):
    return jnp.dot(left, right, preferred_element_type=F32)


def dot_nt(left, right):
    return lax.dot_general(left, right, (((1,), (1,)), ((), ())), preferred_element_type=F32)


def dot_tn(left, right):
    return lax.dot_general(left, right, (((0,), (0,)), ((), ())), preferred_element_type=F32)


ANY = pl.BlockSpec(memory_space=pl.ANY)
VMEM = pl.BlockSpec(memory_space=pltpu.VMEM)
MIB = 1024 * 1024
ROWS, WIDTH, HOME, HALF = 512, 2048, 64, 256
WROWS = 272


def places():
    shard, ctx, tp = lax.axis_index("shard"), lax.axis_index("ctx"), lax.axis_index("tp")
    return shard // 2, ctx * 2 + shard % 2, tp // 2, tp % 2


def device(x, y, z, c):
    x, y, z, c = lax.rem(x + 4, 4), lax.rem(y + 4, 4), lax.rem(z + 4, 4), lax.rem(c + 2, 2)
    return {"shard": x * 2 + lax.rem(y, 2), "ctx": y // 2, "tp": z * 2 + c}


def at(first, size):
    return pl.ds(pl.multiple_of(first, size), size)


class Links:
    def __init__(self, send_sems, recv_sems):
        self.here = places()
        self.send_sems, self.recv_sems, self.made, self.count = send_sems, recv_sems, [], 0

    def send(self, source, target, dx=0, dy=0, dz=0, dc=0, start=True):
        x, y, z, c = self.here
        number = self.count
        self.count += 1
        copy = pltpu.make_async_remote_copy(
            src_ref=source,
            dst_ref=target,
            send_sem=self.send_sems.at[number],
            recv_sem=self.recv_sems.at[number],
            device_id=device(x + dx, y + dy, z + dz, c + dc),
            device_id_type=pl.DeviceIdType.MESH,
        )
        self.made.append(copy)
        if start:
            copy.start()
        return copy

    def left(self, copy):
        copy.wait_send()
        self.made = [other for other in self.made if other is not copy]

    def finish(self):
        for copy in self.made:
            copy.wait_send()

    def greet(self, steps):
        x, y, z, c = self.here
        barrier = pltpu.get_barrier_semaphore()
        for dx, dy, dz, dc in steps:
            pl.semaphore_signal(
                barrier,
                inc=1,
                device_id=device(x + dx, y + dy, z + dz, c + dc),
                device_id_type=pl.DeviceIdType.MESH,
            )
        pl.semaphore_wait(barrier, len(steps))


STEPS_X = [(1, 0, 0, 0), (-1, 0, 0, 0)]
STEPS_Y = [(0, 1, 0, 0), (0, -1, 0, 0), (0, 2, 0, 0)]
STEPS_Z = [(0, 0, 1, 0), (0, 0, -1, 0), (0, 0, 2, 0)]
STEPS_C = [(0, 0, 0, 1)]


def arrived(copies):
    for copy in copies:
        copy.wait_recv()


def turned(values, cosine, sine):
    return values * cosine + pltpu.roll(values, 64, 1) * sine


class Spread:
    def __init__(self, links, array, home_ref, first, start):
        self.links, self.first, self.second = links, first, "z" if first == "y" else "y"
        rows = pl.ds(start, 32)
        x, y, z, c = links.here
        self.source = home_ref.at[rows]
        if first == "z":
            self.block = lambda one, two: array.at[
                lax.rem(y + two + 4, 4), c, lax.rem(z + one + 4, 4), rows
            ]
            self.blocks = lambda two: array.at[lax.rem(y + two + 4, 4), c, :, rows]
        else:
            self.block = lambda one, two: array.at[
                lax.rem(y + one + 4, 4), c, lax.rem(z + two + 4, 4), rows
            ]
            self.blocks = lambda two: array.at[:, c, lax.rem(z + two + 4, 4), rows]
        self.near, self.siblings = {}, []

    def pass_on(self, one):
        block = self.block(one, 0)
        self.near[one] = {
            d: self.links.send(block, block, **{"d" + self.second: d}) for d in (1, -1)
        }

    def to_sibling(self, two):
        self.siblings.append(self.links.send(self.blocks(two), self.blocks(two), dc=1))

    def begin(self):
        self.coming = {
            -d if d != 2 else 2: self.links.send(
                self.source, self.block(0, 0), **{"d" + self.first: d}
            )
            for d in (1, -1, 2)
        }
        block = self.block(0, 0)
        self.near[0] = {
            d: self.links.send(self.source, block, **{"d" + self.second: d}) for d in (1, -1)
        }

    def neighbours(self):
        for one in (-1, 1):
            self.coming[one].wait_recv()
            self.pass_on(one)

    def opposite(self):
        self.coming[2].wait_recv()
        self.pass_on(2)
        self.to_sibling(0)

    def onward(self):
        self.far = []
        for one, d in ((0, 1), (1, -1), (-1, 1), (2, -1)):
            self.near[one][d].wait_recv()
            block = self.block(one, -d)
            self.far.append(self.links.send(block, block, **{"d" + self.second: d}))

    def rest(self):
        for one, d in ((0, -1), (1, 1), (-1, -1), (2, 1)):
            self.near[one][d].wait_recv()
        self.to_sibling(-1)
        self.to_sibling(1)

    def end(self):
        arrived(self.far)
        self.to_sibling(2)


def spread(links, array, home_ref, between):
    halves = (Spread(links, array, home_ref, "z", 0), Spread(links, array, home_ref, "y", 32))
    for step in ("begin", "neighbours", "opposite", "onward", "rest", "end"):
        for half in halves:
            getattr(half, step)()
        if step == "opposite":
            between()
    return halves[0].siblings + halves[1].siblings


class SlotGather:
    def __init__(self, links, array, first, size):
        x, y, z, c = links.here
        self.links, self.array, self.place, self.low = links, array, x, lax.rem(y, 2)
        self.all = pl.ds(first, size)
        self.halves = pl.ds(first, size // 2), pl.ds(first + size // 2, size // 2)
        self.along_y = []

    def part(self, d, rows):
        return self.array.at[lax.rem(self.place + d + 4, 4), self.low, rows]

    def to_pair(self, d):
        for rows, step in zip(self.halves, (1, -1)):
            block = self.part(d, rows)
            self.along_y.append(self.links.send(block, block, dy=step))

    def begin(self):
        block = self.part(0, self.all)
        self.near = {d: self.links.send(block, block, dx=d) for d in (1, -1)}
        self.to_pair(0)

    def onward(self):
        self.far = []
        for rows, d in zip(self.halves, (1, -1)):
            self.near[d].wait_recv()
            block = self.part(-d, rows)
            self.far.append(self.links.send(block, block, dx=d))
            self.to_pair(-d)

    def end(self):
        arrived(self.far)
        self.to_pair(2)


def wide_column(segment_row, first):
    blocks = []
    for n in range(4):
        row = segment_row[:, pl.ds(pl.multiple_of(first + n * 128, 128), 128)].astype(F32)
        block = jnp.broadcast_to(row, (128, 128)).T
        blocks.append(jnp.concatenate([block] * 4, axis=1))
    return jnp.concatenate(blocks, axis=0)


def own_mask(segment_row, first):
    rows_at = lax.broadcasted_iota(jnp.int32, (ROWS, ROWS), 0)
    cols_at = lax.broadcasted_iota(jnp.int32, (ROWS, ROWS), 1)
    same = wide_column(segment_row, first) == segment_row[:, at(first, ROWS)].astype(F32)
    return jnp.where(same & (rows_at >= cols_at), 0.0, MASKED_SCORE)


def earlier_mask(segment_row, first):
    same = wide_column(segment_row, first) == segment_row[:, pl.ds(0, ROWS)].astype(F32)
    return jnp.where(same, 0.0, MASKED_SCORE)


def front(
    tok, router, gain_pair, query_gain, key_gain, cosine_ref, sine_ref, segment_row, routes,
    query_weight, key_weight, value_weight, out_weight, gate, up, down, grad,
    weights_out, others_out, experts_in, experts_out, grad_all, picked_all, moe_in_all,
    normed_out, pre_out, rot_out, kv_out, kv_far, mixed_out, lse_out, hidden_out, home_scale_out,
    weights, others, picked, stage_in, stage_out, biases, accs, totals, part, part_core, part_z, home_ref,
    send_sems, recv_sems, local_sems,
):
    links = Links(send_sems, recv_sems)
    x, y, z, c = links.here
    ctx, y_low = y // 2, lax.rem(y, 2)
    x_after, x_before = lax.rem(x + 1, 4), lax.rem(x + 3, 4)
    y_after, y_before, y_far = lax.rem(y + 1, 4), lax.rem(y + 3, 4), lax.rem(y + 2, 4)
    own = c * HALF
    own_rows = pl.ds(pl.multiple_of(own, HALF), HALF)
    loads = []

    def load(source, target):
        copy = pltpu.make_async_copy(source, target, local_sems.at[len(loads)])
        copy.start()
        loads.append(copy)
        return copy

    slot, other_slot = weights.at[x, y_low], others.at[x, y_low]
    every = pl.ds(0, 256)
    slot_loads = [
        load(array, slot.at[every, pl.ds(n * 256, 256)])
        for n, array in enumerate((query_weight, key_weight, value_weight))
    ]
    other_load = load(out_weight, other_slot.at[:, pl.ds(128, 256)])

    def mine(array, group):
        return array.at[pl.ds(group * 4, 4)]

    def columns(place, low_place):
        return pl.ds(pl.multiple_of(place * 512 + low_place * 256, 256), 256)

    staged = [
        load(mine(gate, y), stage_in.at[:, :, pl.ds(0, 128)]),
        load(mine(up, y), stage_in.at[:, :, pl.ds(128, 128)]),
        load(mine(down, y), stage_out),
    ]
    lanes = lax.broadcasted_iota(jnp.int32, (16, 128), 1)
    rows_of = lax.broadcasted_iota(jnp.int32, (16, 128), 0)
    turned_to = (lanes == (x * 2 + y_low) * 16 + rows_of).astype(BF)
    head_rows = dot(jnp.concatenate([query_gain[...], key_gain[...]], axis=0), turned_to)
    gain_block = jnp.concatenate(
        [
            gain_pair[...].astype(F32),
            jnp.concatenate([head_rows, jnp.zeros((4, 128), F32)], axis=1),
            jnp.zeros((10, 256), F32),
        ],
        axis=0,
    )
    weights[x, y_low, 256:272, 0:256] = gain_block.astype(BF)
    weights[x, y_low, 256:272, 256:768] = jnp.zeros((16, 512), BF)
    others[x, y_low, :, 0:128] = jnp.concatenate(
        [router[...].astype(F32), jnp.zeros((112, 256), F32)], axis=0
    ).T.astype(BF)
    links.greet(STEPS_X + STEPS_Y + STEPS_Z + STEPS_C)
    for copy in slot_loads:
        copy.wait()

    first_rows = pl.ds(0, 80)
    pair = [
        links.send(slot.at[pl.ds(0, 48)], slot.at[pl.ds(0, 48)], dy=1),
        links.send(slot.at[pl.ds(48, 32)], slot.at[pl.ds(48, 32)], dy=-1),
    ]
    most = SlotGather(links, weights, 80, WROWS - 80)
    most.begin()
    other_load.wait()
    behind = SlotGather(links, others, 0, 256)

    def grad_block(dy, dz, first=0, size=HOME):
        start = own + lax.rem(z + dz + 4, 4) * HOME + first
        return grad_all.at[lax.rem(y + dy + 4, 4), pl.ds(pl.multiple_of(start, 32), size)]

    home_rows = pl.ds(pl.multiple_of(own + z * HOME, HOME), HOME)
    grad_near = {
        -d if d != 2 else 2: links.send(grad.at[home_rows], grad_block(0, 0), dy=d)
        for d in (1, -1, 2)
    }
    for copy in staged:
        copy.wait()
    place_staged = [
        load(stage_in, experts_in.at[:, x, y_low]),
        load(stage_out, experts_out.at[:, :, columns(x, y_low)]),
    ]
    arrived(pair)
    both = weights.at[x, :, first_rows]
    near = [links.send(both, both, dx=d) for d in (1, -1)]
    behind.begin()

    expert_rows = lax.broadcasted_iota(jnp.int32, (16, ROWS), 0)
    marked = jnp.zeros((16, ROWS), F32)
    for k in range(8):
        marked = marked + jnp.where(expert_rows == routes[k : k + 1, :], 1.0, 0.0)
    picked[...] = marked.astype(BF)
    place_picked = load(picked, picked_all.at[y])
    most.onward()
    first_row = ctx * ROWS
    own_first = at(first_row, ROWS)
    biases[0] = own_mask(segment_row, first_row)
    biases[1] = earlier_mask(segment_row, first_row)
    far = []
    for n, (d, place) in enumerate(((1, x_before), (-1, x_after))):
        near[n].wait_recv()
        block = weights.at[place, n, first_rows]
        far.append(links.send(block, block, dx=d))
    tokens = tok[...].astype(F32)
    scale_one = rms_scale(tokens)
    most.end()
    grad_next = {}
    for dy in (-1, 1, 2):
        grad_near[dy].wait_recv()
        block = grad_block(dy, 0)
        grad_next[dy] = {d: links.send(block, block, dz=d) for d in (1, -1)}
    behind.onward()

    def expert_block(place, low_place):
        return [
            experts_in.at[:, place, low_place],
            experts_out.at[:, :, columns(place, low_place)],
        ]

    for copy in place_staged:
        copy.wait()
    expert_near = {
        d: [links.send(block, block, dx=d) for block in expert_block(x, y_low)] for d in (1, -1)
    }
    expert_pair = []
    for group, start, step in ((y_after, 0, 1), (y_before, 2, -1)):
        some = pl.ds(group * 4 + start, 2)
        there = pl.ds(start, 2)
        expert_pair += [
            links.send(
                gate.at[some], experts_in.at[there, x, y_low, :, pl.ds(0, 128)], dy=step
            ),
            links.send(
                up.at[some], experts_in.at[there, x, y_low, :, pl.ds(128, 128)], dy=step
            ),
            links.send(down.at[some], experts_out.at[there, :, columns(x, y_low)], dy=step),
        ]
    arrived(most.along_y)
    arrived(far)

    gain_blocks = [weights[s // 2, s % 2, 256:272, 0:256].astype(F32) for s in range(8)]
    gains = jnp.concatenate([block[0:1] for block in gain_blocks], axis=1)
    moe_gains = jnp.concatenate([block[1:2] for block in gain_blocks], axis=1)
    head_gains = sum(block[:, 0:128] for block in gain_blocks)
    normed_out[...] = (tokens * scale_one * gains).astype(BF)

    def project(column):
        block = weights[:, :, 0:256, column * 256 : column * 256 + 256].reshape(WIDTH, 256)
        return jnp.dot(normed_out[...], block, preferred_element_type=F32)

    cosine, sine = cosine_ref[own_first, :], sine_ref[own_first, :]

    def heads(pre, first_gain, base):
        for h in range(2):
            part_h = pre[:, h * 128 : h * 128 + 128]
            unit = part_h * rms_scale(part_h) * head_gains[first_gain + h : first_gain + h + 1]
            rot_out[:, base + h * 128 : base + h * 128 + 128] = turned(unit, cosine, sine).astype(BF)

    key_pre = project(1)
    pre_out[:, 256:512] = key_pre
    heads(key_pre, 4, 256)
    kv_out[:, 0:256] = rot_out[:, 256:512]
    kv_out[:, 256:512] = project(2).astype(BF)
    later = links.send(kv_out, kv_far, dy=2, start=False)

    @pl.when(ctx == 0)
    def _():
        later.start()
        kv_far[...] = jnp.zeros_like(kv_far)

    picked_near = [links.send(picked, picked_all.at[y], dy=d) for d in (1, -1, 2)]
    query_pre = project(0)
    pre_out[:, 0:256] = query_pre
    heads(query_pre, 2, 0)
    score_scale = 128 ** (-0.5)
    for h in range(2):
        lane = slice(h * 128, h * 128 + 128)
        scores = dot_nt(rot_out[:, lane], kv_out[:, lane]) * score_scale + biases[0]
        peak = jnp.max(scores, axis=-1, keepdims=True)
        exponents = jnp.exp(scores - peak)
        lse_out[h] = jnp.broadcast_to(peak, (ROWS, 128))
        totals[h] = jnp.broadcast_to(jnp.sum(exponents, axis=-1, keepdims=True), (ROWS, 128))
        accs[h] = dot(exponents.astype(BF), kv_out[:, 256 + h * 128 : 384 + h * 128])

    behind.end()
    grad_far = []
    for dy in (-1, 1, 2):
        for d, first in ((1, 0), (-1, 32)):
            grad_next[dy][d].wait_recv()
            block = grad_block(dy, -d, first, 32)
            grad_far.append(links.send(block, block, dz=d))
    arrived(expert_pair)
    expert_pair_near = {
        d: [links.send(block, block, dx=d) for block in expert_block(x, 1 - y_low)] for d in (1, -1)
    }
    @pl.when(ctx == 1)
    def _():
        later.wait_recv()
        for h in range(2):
            lane = slice(h * 128, h * 128 + 128)
            scores = dot_nt(rot_out[:, lane], kv_far[:, lane]) * score_scale + biases[1]
            old_peak = lse_out[h][:, 0:1]
            peak = jnp.maximum(old_peak, jnp.max(scores, axis=-1, keepdims=True))
            exponents = jnp.exp(scores - peak)
            old = jnp.exp(old_peak - peak)
            lse_out[h] = jnp.broadcast_to(peak, (ROWS, 128))
            totals[h] = totals[h] * old + jnp.sum(exponents, axis=-1, keepdims=True)
            accs[h] = accs[h] * old + dot(
                exponents.astype(BF), kv_far[:, 256 + h * 128 : 384 + h * 128]
            )

    for h in range(2):
        total = totals[h]
        mixed_out[:, h * 128 : h * 128 + 128] = (accs[h] / total).astype(BF)
        lse_out[h] = lse_out[h] + jnp.log(total)

    quarter = pl.multiple_of(own, HALF)
    arrived(behind.along_y)
    other = pl.multiple_of((1 - c) * HALF, HALF)
    give_rows = mixed_out[pl.ds(other, HALF), :]
    for s in range(8):
        block = others[s // 2, s % 2, :, 128:384]
        part[1, :, s * 256 : s * 256 + 256] = dot(give_rows, block).astype(BF)
    core_sum = links.send(part.at[1], part_core, dc=1)
    keep_rows = mixed_out[pl.ds(quarter, HALF), :]
    for s in range(8):
        block = others[s // 2, s % 2, :, 128:384]
        part[0, :, s * 256 : s * 256 + 256] = dot(keep_rows, block).astype(BF)
    core_sum.wait_recv()
    part[0] = (part[0].astype(F32) + part_core[...].astype(F32)).astype(BF)
    z_sum = []
    for k, d in enumerate((1, -1, 2)):
        there = pl.multiple_of(lax.rem(z + d + 4, 4) * HOME, HOME)
        z_sum.append(links.send(part.at[0, pl.ds(there, HOME)], part_z.at[k], dz=d))

    arrived(grad_far)
    siblings = [
        links.send(grad_all.at[place, own_rows], grad_all.at[place, own_rows], dc=1)
        for place in (y_before, y_after, y_far)
    ]
    arrived(expert_near[1] + expert_near[-1])
    expert_far = [links.send(block, block, dx=1) for block in expert_block(x_before, y_low)]
    arrived(z_sum)
    summed = part[0, pl.ds(pl.multiple_of(z * HOME, HOME), HOME), :].astype(F32)
    for k in range(3):
        summed = summed + part_z[k].astype(F32)
    home_tokens = tok[home_rows, :].astype(F32)
    hidden = home_tokens + summed
    hidden_out[...] = hidden
    home_scale_out[...] = jnp.broadcast_to(rms_scale(home_tokens), (HOME, 128))
    home_ref[...] = (hidden * rms_scale(hidden) * moe_gains).astype(BF)
    place_home = load(home_ref, moe_in_all.at[y, c, z])
    keep_weights = [load(weights, weights_out), load(others, others_out)]
    place_home.wait()

    def onward():
        arrived(expert_pair_near[1] + expert_pair_near[-1])
        expert_far.extend(
            links.send(block, block, dx=-1) for block in expert_block(x_after, 1 - y_low)
        )

    siblings += spread(links, moe_in_all, home_ref, lambda: onward())
    arrived(expert_far)
    arrived(picked_near)
    arrived(siblings)
    place_picked.wait()
    for copy in keep_weights:
        copy.wait()

    for copy in links.made:
        if copy is not later:
            copy.wait_send()

    @pl.when(ctx == 0)
    def _():
        later.wait_send()


FRONT_COPIES = 6 + 12 + 12 + 18 + 18 + 3 + 1 + 4 + 38


def run_front(vmem, hbm):
    shape = jax.ShapeDtypeStruct
    outs = (
        (shape((4, 2, WROWS, 768), BF), ANY),
        (shape((4, 2, 256, 384), BF), ANY),
        (shape((4, 4, 2, 256, 256), BF), ANY),
        (shape((4, 128, WIDTH), BF), ANY),
        (shape((4, ROWS, WIDTH), BF), ANY),
        (shape((4, 16, ROWS), BF), ANY),
        (shape((4, 2, 4, HOME, WIDTH), BF), ANY),
        (shape((ROWS, WIDTH), BF), VMEM),
        (shape((ROWS, 512), F32), VMEM),
        (shape((ROWS, 512), BF), VMEM),
        (shape((ROWS, 512), BF), VMEM),
        (shape((ROWS, 512), BF), VMEM),
        (shape((ROWS, 256), BF), VMEM),
        (shape((2, ROWS, 128), F32), VMEM),
        (shape((HOME, WIDTH), F32), VMEM),
        (shape((HOME, 128), F32), VMEM),
    )
    return pl.pallas_call(
        front,
        out_shape=[o for o, _ in outs],
        in_specs=[VMEM] * len(vmem) + [ANY] * len(hbm),
        out_specs=[spec for _, spec in outs],
        scratch_shapes=[
            pltpu.VMEM((4, 2, WROWS, 768), BF),
            pltpu.VMEM((4, 2, 256, 384), BF),
            pltpu.VMEM((16, ROWS), BF),
            pltpu.VMEM((4, 256, 256), BF),
            pltpu.VMEM((4, 128, 256), BF),
            pltpu.VMEM((2, ROWS, ROWS), F32),
            pltpu.VMEM((2, ROWS, 128), F32),
            pltpu.VMEM((2, ROWS, 128), F32),
            pltpu.VMEM((2, HALF, WIDTH), BF),
            pltpu.VMEM((HALF, WIDTH), BF),
            pltpu.VMEM((3, HOME, WIDTH), BF),
            pltpu.VMEM((HOME, WIDTH), BF),
            pltpu.SemaphoreType.DMA((FRONT_COPIES,)),
            pltpu.SemaphoreType.DMA((FRONT_COPIES,)),
            pltpu.SemaphoreType.DMA((16,)),
        ],
        compiler_params=pltpu.CompilerParams(
            collective_id=1, has_side_effects=True, vmem_limit_bytes=56 * MIB
        ),
        name="front",
    )(*vmem, *hbm)


MCOLS = 1664


def scatter_buffers():
    return [
        pltpu.VMEM((2, HALF, WIDTH), BF),
        pltpu.VMEM((2, 2, 32, WIDTH), BF),
        pltpu.VMEM((2, 4, 32, WIDTH), BF),
        pltpu.VMEM((3, 32, WIDTH), BF),
        pltpu.VMEM((4, 2, 16, WIDTH), BF),
        pltpu.VMEM((4, 2, 32, WIDTH), BF),
        pltpu.VMEM((3, 32, WIDTH), BF),
    ]


class TokenSum:
    def __init__(self, links, give, keep, landings, credit):
        self.links, self.give, self.keep, self.credit = links, give, keep, credit
        (
            self.core_in, self.p_one_in, self.p_two_in, self.p_three_in,
            self.q_one_in, self.q_two_in, self.q_three_in,
        ) = landings
        self.core, self.p_one, self.p_two, self.q_one, self.q_two, self.q_three = {}, [], [], {}, {}, []

    def free(self, k):
        if k:
            self.links.left(self.core[k - 1])

    def give_core(self, k):
        if k >= 2:
            pl.semaphore_wait(self.credit, 1)
        self.core[k] = self.links.send(self.give, self.core_in.at[k % 2], dc=1)

    def q_rows(self, d, first=0, size=32):
        place = lax.rem(self.links.here[2] + d + 4, 4)
        return pl.ds(pl.multiple_of(place * HOME + 32 + first, 16), size)

    def add(self, k):
        links, keep = self.links, self.keep
        self.core[k].wait_recv()
        keep[k] = keep[k] + self.core_in[k % 2]
        if k < 2:
            x, y, z, c = links.here
            pl.semaphore_signal(
                self.credit,
                inc=1,
                device_id=device(x, y, z, c + 1),
                device_id_type=pl.DeviceIdType.MESH,
            )
        self.q_one[k] = [
            links.send(keep.at[k, self.q_rows(2, 16 * n, 16)], self.q_one_in.at[k, n], dz=d)
            for n, d in enumerate((1, -1))
        ]
        if k == 0:
            rows = keep.at[0].reshape(4, HOME, WIDTH)
            first = pl.ds(0, 32)
            self.p_one = [
                links.send(rows.at[pl.ds(0, 2), first], self.p_one_in.at[0], dy=1),
                links.send(rows.at[pl.ds(2, 2), first], self.p_one_in.at[1], dy=-1),
            ]

    def p_step(self, k):
        links, keep, n = self.links, self.keep, k - 1
        self.p_one[n].wait_recv()
        for i in range(2):
            row = (2 * n + i) * HOME
            keep[k, row : row + 32] = keep[k, row : row + 32] + self.p_one_in[n, i]
        rows = keep.at[k].reshape(4, HOME, WIDTH)
        self.p_two.append(
            links.send(rows.at[:, pl.ds(0, 32)], self.p_two_in.at[n], dy=(1, -1)[n])
        )

    def second(self, k):
        links, keep = self.links, self.keep
        self.q_two[k] = []
        for n, d in enumerate((1, -1)):
            self.q_one[k][n].wait_recv()
            rows = self.q_rows(d, 16 * n, 16)
            keep[k, rows, :] = keep[k, rows, :] + self.q_one_in[k, n]
            self.q_two[k].append(
                links.send(keep.at[k, self.q_rows(d)], self.q_two_in.at[k, n], dz=d)
            )

    def q_sum(self, k):
        arrived(self.q_two[k])
        part = self.keep[k, self.q_rows(0), :].astype(F32)
        for n in range(2):
            part = part + self.q_two_in[k, n].astype(F32)
        return part

    def third(self, k, buffer):
        buffer[k] = self.q_sum(k).astype(BF)
        self.q_three.append(
            self.links.send(buffer.at[k], self.q_three_in.at[k], dy=(2, 1, -1)[k])
        )

    def p_send(self):
        links, keep = self.links, self.keep
        z = links.here[2]
        arrived(self.p_two)
        for place in range(4):
            row = place * HOME
            keep[3, row : row + 32] = (
                keep[3, row : row + 32].astype(F32)
                + self.p_two_in[0, place].astype(F32)
                + self.p_two_in[1, place].astype(F32)
            ).astype(BF)
        self.p_three = [
            links.send(
                keep.at[3, at(lax.rem(z + d + 4, 4) * HOME, 32)], self.p_three_in.at[n], dz=d
            )
            for n, d in enumerate((1, -1, 2))
        ]

    def home(self):
        z = self.links.here[2]
        second = self.q_sum(3)
        arrived(self.q_three)
        for n in range(3):
            second = second + self.q_three_in[n].astype(F32)
        arrived(self.p_three)
        first = self.keep[3, at(z * HOME, 32), :].astype(F32)
        for n in range(3):
            first = first + self.p_three_in[n].astype(F32)
        return first, second


TOKEN_SUM_COPIES = 4 + 8 + 8 + 2 + 2 + 3 + 3


def spread_home(links, array, home_ref):
    x, y, z, c = links.here
    return [links.send(home_ref, array.at[c, z], dz=d) for d in (1, -1, 2)]


def experts(
    x_all, g_all, picked_all, own_grad, w_in_hbm, w_out_hbm, weights, others, hidden_ref,
    grad_out, grad_near_out, low_all, hidden_grad_out, gain_out, layer_out,
    w_in, w_out, gain_ref, x_ref, g_ref, picked_ref, gates_ref, gate_grad_ref, back_ref, pre_ref,
    gated_ref, give, keep, keep_layer, grad_far, grad_stage, q_buffer, q_layer, home_ref,
    core_in, p_one_in, p_two_in, p_three_in, q_one_in, q_two_in, q_three_in,
    core_layer, p_one_layer, p_two_layer, p_three_layer, q_one_layer, q_two_layer, q_three_layer,
    credits, send_sems, recv_sems, local_sems,
):
    links = Links(send_sems, recv_sems)
    x, y, z, c = links.here
    x_after, x_before, x_far = lax.rem(x + 1, 4), lax.rem(x + 3, 4), lax.rem(x + 2, 4)
    order = (lax.rem(y + 2, 4), lax.rem(y + 1, 4), lax.rem(y + 3, 4), y)
    loads = []

    def load(source, target):
        copy = pltpu.make_async_copy(source, target, local_sems.at[len(loads)])
        copy.start()
        loads.append(copy)
        return copy

    first = [load(g_all.at[order[0]], g_ref.at[0]), load(w_out_hbm, w_out)]
    first += [load(picked_all.at[place], picked_ref.at[k]) for k, place in enumerate(order)]
    first.append(load(others.at[:, :, :, pl.ds(0, 128)], w_in.at[:, :, :, pl.ds(1024, 128)]))
    first.append(load(weights.at[:, :, pl.ds(256, 16), pl.ds(0, 256)], gain_ref))
    first.append(load(x_all.at[order[0]], x_ref.at[0]))
    first += [
        load(w_in_hbm.at[e], w_in.at[:, :, :, pl.ds(e * 256, 256)]) for e in range(4)
    ]
    rest = [
        [
            load(g_all.at[order[k]] if k < 3 else own_grad, g_ref.at[k]),
            load(x_all.at[order[k]], x_ref.at[k]),
        ]
        for k in range(1, 4)
    ]
    links.greet(STEPS_X + STEPS_Y + STEPS_Z + STEPS_C)
    for copy in first:
        copy.wait()

    sums = TokenSum(
        links, give.at[0], keep,
        (core_in, p_one_in, p_two_in, p_three_in, q_one_in, q_two_in, q_three_in), credits.at[0],
    )
    layer_sums = TokenSum(
        links, give.at[1], keep_layer,
        (
            core_layer, p_one_layer, p_two_layer, p_three_layer, q_one_layer, q_two_layer, q_three_layer,
        ),
        credits.at[1],
    )
    lanes = lax.broadcasted_iota(jnp.int32, (ROWS, 128), 1)
    own_rows = at(c * HALF, HALF)
    other_rows = at((1 - c) * HALF, HALF)

    def in_block(first_column, size):
        return w_in[:, :, :, pl.ds(first_column, size)].reshape(WIDTH, size)

    for k in range(4):
        if k:
            for copy in rest[k - 1]:
                copy.wait()
        logits = dot(x_ref[k], in_block(1024, 128))
        marks = jnp.concatenate([picked_ref[k].astype(F32), jnp.zeros((112, ROWS), F32)], axis=0)
        logits = jnp.where(marks.T > 0.5, logits, MASKED_SCORE)
        exponents = jnp.exp(logits - jnp.max(logits, axis=-1, keepdims=True))
        gates_ref[...] = exponents / jnp.sum(exponents, axis=-1, keepdims=True)
        gate_grad_ref[...] = jnp.zeros_like(gate_grad_ref)
        back_ref[...] = dot_nt(g_ref[k], w_out[...].reshape(512, WIDTH))

        def two_experts(pair, carry, k=k):
            joined = dot(x_ref[k], in_block(pl.multiple_of(pair * 512, 512), 512))
            for n in range(2):
                one_expert(pair * 2 + n, joined[:, n * 256 : n * 256 + 256])
            return carry

        def one_expert(e, joined, k=k):
            gate_pre, up_pre = joined[:, :128], joined[:, 128:]
            logistic = 1.0 / (1.0 + jnp.exp(-gate_pre))
            silu_gate = gate_pre * logistic
            silu_slope = logistic * (1.0 + gate_pre * (1.0 - logistic))
            act = silu_gate * up_pre
            back = back_ref[:, at(e * 128, 128)]
            mine = lanes == y * 4 + e
            gate = jnp.sum(jnp.where(mine, gates_ref[...], 0.0), axis=-1, keepdims=True)
            term = jnp.sum(act.astype(BF).astype(F32) * back, axis=-1, keepdims=True)
            gate_grad_ref[...] += jnp.where(mine, term, 0.0)
            act_grad = back * gate
            pre_ref[k, :, pl.ds(pl.multiple_of(e * 256, 256), 128)] = (
                act_grad * up_pre * silu_slope
            ).astype(BF)
            pre_ref[k, :, pl.ds(pl.multiple_of(e * 256 + 128, 128), 128)] = (
                act_grad * silu_gate
            ).astype(BF)
            gated_ref[k, :, at(e * 128, 128)] = (act * gate).astype(BF)

        lax.fori_loop(0, 2, two_experts, 0)
        gates, gate_grad = gates_ref[...], gate_grad_ref[...]
        logit_grad = gates * (gate_grad - jnp.sum(gates * gate_grad, axis=-1, keepdims=True))
        pre_ref[k, :, 1024:1152] = logit_grad.astype(BF)

        def back_rows(rows, target, k=k):
            for s in range(0, 4, 2):
                block = w_in[s : s + 2].reshape(1024, 1152)
                target[:, s * 512 : s * 512 + 1024] = dot_nt(pre_ref[k, rows, :], block).astype(BF)

        def layer_rows(rows, target, k=k):
            for s in range(0, WIDTH, 1024):
                block = w_out[:, :, s : s + 1024].reshape(512, 1024)
                target[:, s : s + 1024] = dot(gated_ref[k, rows, :], block).astype(BF)

        sums.free(k)
        back_rows(other_rows, give.at[0])
        sums.give_core(k)
        layer_sums.free(k)
        layer_rows(other_rows, give.at[1])
        layer_sums.give_core(k)
        back_rows(own_rows, keep.at[k])
        layer_rows(own_rows, keep_layer.at[k])
        sums.add(k)
        if k in (1, 2):
            sums.p_step(k)
        layer_sums.add(k)
        if k > 0:
            sums.second(k - 1)
            layer_sums.second(k - 1)
        if k > 1:
            layer_sums.p_step(k - 1)
            sums.third(k - 2, q_buffer)
            layer_sums.third(k - 2, q_layer)
    sums.second(3)
    sums.third(2, q_buffer)
    sums.p_send()

    def weight_grad(slot, target):
        columns = at(slot * 256, 256)
        rows = x_ref[:, :, columns].reshape(4 * ROWS, 256)
        target[:, 0:1152] = dot_tn(rows, pre_ref[...].reshape(4 * ROWS, 1152)).astype(BF)
        rows = g_ref[:, :, columns].reshape(4 * ROWS, 256)
        target[:, 1152:MCOLS] = dot_tn(rows, gated_ref[...].reshape(4 * ROWS, 512)).astype(BF)

    def far_slot(i, carry):
        weight_grad(x_far * 2 + i, grad_far.at[i])
        return carry

    lax.fori_loop(0, 2, far_slot, 0)
    near = [
        links.send(grad_far.at[0], grad_near_out.at[0], dx=1),
        links.send(grad_far.at[1], grad_near_out.at[1], dx=-1),
    ]

    moe_gains = jnp.concatenate(
        [gain_ref[s // 2, s % 2].astype(F32)[1:2] for s in range(8)], axis=1
    )
    moe_grad = jnp.concatenate(sums.home(), axis=0)
    hidden = hidden_ref[...]
    home_grad = g_ref[3, at(c * HALF + z * HOME, HOME), :].astype(F32)
    back, gain_rows = norm_back(moe_grad, hidden, rms_scale(hidden), moe_gains)
    hidden_grad = home_grad + back
    hidden_grad_out[...] = hidden_grad
    gain_out[...] = jnp.broadcast_to(jnp.sum(gain_rows, axis=0, keepdims=True), (8, WIDTH))
    home_ref[...] = hidden_grad.astype(BF)
    place_home = load(home_ref, low_all.at[c, z])
    low_near = spread_home(links, low_all, home_ref)
    layer_sums.second(3)
    layer_sums.third(2, q_layer)
    layer_sums.p_send()

    first_sem = len(loads)

    def stage(i, n):
        slot = lax.rem(x_far * 2 + 2 + 2 * i + n, 8)
        return pltpu.make_async_copy(
            grad_stage.at[n], grad_out.at[slot], local_sems.at[first_sem + n]
        )

    def other_grads(i, carry):
        for n in range(2):

            @pl.when(i > 0)
            def _():
                stage(i - 1, n).wait()

            weight_grad(lax.rem(x_far * 2 + 2 + 2 * i + n, 8), grad_stage.at[n])
            stage(i, n).start()
        return carry

    lax.fori_loop(0, 2, other_grads, 0)
    arrived(low_near)
    place_home.wait()
    sibling = links.send(low_all.at[c], low_all.at[c], dc=1)
    layer_grad = jnp.concatenate(layer_sums.home(), axis=0)
    layer_out[...] = (hidden_ref[...] + layer_grad).astype(BF)
    other_grads(2, 0)
    for n in range(2):
        stage(2, n).wait()
    arrived(near)
    sibling.wait_recv()
    links.finish()


EXPERT_COPIES = 2 * TOKEN_SUM_COPIES + 2 + 3 + 1


def run_experts(moe_in_all, *rest):
    shape = jax.ShapeDtypeStruct
    outs = (
        (shape((8, 256, MCOLS), BF), ANY),
        (shape((2, 256, MCOLS), BF), ANY),
        (shape((2, 4, HOME, WIDTH), BF), ANY),
        (shape((HOME, WIDTH), F32), VMEM),
        (shape((8, WIDTH), F32), VMEM),
        (shape((HOME, WIDTH), BF), VMEM),
    )
    return pl.pallas_call(
        experts,
        out_shape=[o for o, _ in outs],
        in_specs=[ANY] * 8 + [VMEM],
        out_specs=[spec for _, spec in outs],
        scratch_shapes=[
            pltpu.VMEM((4, 2, 256, 1152), BF),
            pltpu.VMEM((4, 128, WIDTH), BF),
            pltpu.VMEM((4, 2, 16, 256), BF),
            pltpu.VMEM((4, ROWS, WIDTH), BF),
            pltpu.VMEM((4, ROWS, WIDTH), BF),
            pltpu.VMEM((4, 16, ROWS), BF),
            pltpu.VMEM((ROWS, 128), F32),
            pltpu.VMEM((ROWS, 128), F32),
            pltpu.VMEM((ROWS, 512), F32),
            pltpu.VMEM((4, ROWS, 1152), BF),
            pltpu.VMEM((4, ROWS, 512), BF),
            pltpu.VMEM((2, HALF, WIDTH), BF),
            pltpu.VMEM((4, HALF, WIDTH), BF),
            pltpu.VMEM((4, HALF, WIDTH), BF),
            pltpu.VMEM((2, 256, MCOLS), BF),
            pltpu.VMEM((2, 256, MCOLS), BF),
            pltpu.VMEM((3, 32, WIDTH), BF),
            pltpu.VMEM((3, 32, WIDTH), BF),
            pltpu.VMEM((HOME, WIDTH), BF),
            *scatter_buffers(),
            *scatter_buffers(),
            pltpu.SemaphoreType.REGULAR((2,)),
            pltpu.SemaphoreType.DMA((EXPERT_COPIES,)),
            pltpu.SemaphoreType.DMA((EXPERT_COPIES,)),
            pltpu.SemaphoreType.DMA((24,)),
        ],
        compiler_params=pltpu.CompilerParams(
            collective_id=2, has_side_effects=True, vmem_limit_bytes=62 * MIB
        ),
        name="experts",
    )(
        moe_in_all.reshape(4, ROWS, WIDTH),
        *rest,
    )


SMALL = 264


def back(
    grad_moe, grad_near, low_hbm, weights, others, mixed_hbm, rot_hbm, kv_hbm, kv_far_hbm, lse_hbm, pre_hbm,
    normed_hbm, tok_hbm,
    layer_ref, hidden_grad_ref, home_scale_ref, gain_ref, cosine_ref, sine_ref, segment_row,
    layer_all, input_all, groups_in, groups_out, moe_in,
    grad_q, grad_k, grad_v, grad_o, small_out, heads_out,
    w_ref, w_gains, low, mixed, rot, kv, kv_far, lse, pre, home_tok,
    bias, mixed_grad, dq, dkv, kv_give, kv_got, stacked,
    moe_after, moe_before, moe_near, pay_in, pay_out,
    attn_grad, attn_one, attn_two, attn_give, attn_keep, attn_y_one, attn_y_two,
    part, part_core, part_z, home_in,
    sums_ref, sums_x, sums_y, pair_ref, small_ref, small_z, small_c, routed,
    send_sems, recv_sems, local_sems,
):
    links = Links(send_sems, recv_sems)
    x, y, z, c = links.here
    ctx, y_low = y // 2, lax.rem(y, 2)
    x_after, x_before, x_far = lax.rem(x + 1, 4), lax.rem(x + 3, 4), lax.rem(x + 2, 4)
    own_rows, other_rows = at(c * HALF, HALF), at((1 - c) * HALF, HALF)
    loads = []

    def load(source, target):
        copy = pltpu.make_async_copy(source, target, local_sems.at[len(loads)])
        copy.start()
        loads.append(copy)
        return copy

    def pair_of(array, place):
        return array.at[at(place * 2, 2)]

    near_loads = [
        load(pair_of(grad_moe, x_after), moe_after),
        load(pair_of(grad_moe, x_before), moe_before),
        load(grad_near, moe_near),
    ]
    every = pl.ds(0, 256)
    out_loads = [
        load(low_hbm, low),
        load(others.at[:, :, :, pl.ds(128, 256)], w_ref.at[:, :, :, pl.ds(768, 256)]),
        load(mixed_hbm, mixed),
        load(rot_hbm, rot),
        load(kv_hbm, kv),
        load(kv_far_hbm, kv_far),
        load(lse_hbm, lse),
    ]
    next_loads = [
        load(pre_hbm, pre),
        load(weights.at[:, :, every, pl.ds(0, 768)], w_ref.at[:, :, :, pl.ds(0, 768)]),
        load(weights.at[:, :, pl.ds(256, 16), every], w_gains),
        load(tok_hbm.at[at(c * HALF + z * HOME, HOME)], home_tok),
    ]
    links.greet(STEPS_X + [(2, 0, 0, 0)] + STEPS_Y + STEPS_Z + STEPS_C)

    for copy in near_loads:
        copy.wait()
    moe_after[0] = (moe_after[0].astype(F32) + moe_near[0].astype(F32)).astype(BF)
    moe_before[1] = (moe_before[1].astype(F32) + moe_near[1].astype(F32)).astype(BF)
    moe_parts = pl.ds(0, 1152), pl.ds(1152, 512)
    moe_two = [
        [
            links.send(source.at[:, :, cols], moe_in.at[n, :, :, cols], dx=d)
            for n, (source, d) in enumerate(((moe_after, 1), (moe_before, -1)))
        ]
        for cols in moe_parts
    ]
    moe_own = moe_near
    own_load = load(pair_of(grad_moe, x), moe_own)

    place_layer = load(layer_ref, layer_all.at[c, z])
    layer_near = spread_home(links, layer_all, layer_ref)

    own_first = at(ctx * ROWS, ROWS)
    for copy in out_loads:
        copy.wait()
    total = jnp.zeros((ROWS, 256), F32)
    for s in range(8):
        total = total + dot_nt(low[:, s * 256 : s * 256 + 256], w_ref[s // 2, s % 2, :, 768:1024])
    mixed_grad[...] = total.astype(BF)

    score_scale = 128 ** (-0.5)
    deltas = []
    for h in range(2):
        lane = slice(h * 128, h * 128 + 128)
        deltas.append(
            jnp.sum(
                mixed_grad[:, lane].astype(F32) * mixed[:, lane].astype(F32), axis=-1, keepdims=True
            )
        )

    def scores_back(h, keys_values):
        lane = slice(h * 128, h * 128 + 128)
        keys, values = keys_values[:, lane], keys_values[:, 256 + h * 128 : 384 + h * 128]
        scores = dot_nt(rot[:, lane], keys) * score_scale + bias[...]
        probs = jnp.exp(scores - lse[h][:, 0:1])
        prob_grad = dot_nt(mixed_grad[:, lane], values)
        score_grad = (probs * (prob_grad - deltas[h])).astype(BF)
        query_part = dot(score_grad, keys) * score_scale
        key_part = dot_tn(score_grad, rot[:, lane]) * score_scale
        value_part = dot_tn(probs.astype(BF), mixed_grad[:, lane])
        return query_part, key_part, value_part

    earlier = links.send(kv_give, kv_got, dy=2, start=False)

    @pl.when(ctx == 1)
    def _():
        bias[...] = earlier_mask(segment_row, ctx * ROWS)
        for h in range(2):
            query_part, key_part, value_part = scores_back(h, kv_far)
            dq[:, h * 128 : h * 128 + 128] = query_part
            kv_give[:, h * 128 : h * 128 + 128] = key_part.astype(BF)
            kv_give[:, 256 + h * 128 : 384 + h * 128] = value_part.astype(BF)
        earlier.start()

    @pl.when(ctx == 0)
    def _():
        dq[...] = jnp.zeros_like(dq)

    bias[...] = own_mask(segment_row, ctx * ROWS)
    for h in range(2):
        query_part, key_part, value_part = scores_back(h, kv)
        dq[:, h * 128 : h * 128 + 128] += query_part
        dkv[:, h * 128 : h * 128 + 128] = key_part
        dkv[:, 256 + h * 128 : 384 + h * 128] = value_part

    def out_grad_block(s, carry):
        attn_grad[s, :, 768:1024] = dot_tn(mixed[...], low[:, at(s * 256, 256)]).astype(BF)
        return carry

    lax.fori_loop(0, 8, out_grad_block, 0)
    normed = low
    normed_load = load(normed_hbm, normed)
    for copy in next_loads:
        copy.wait()
    head_gains = jnp.zeros((16, 128), F32)
    for s in range(8):
        head_gains = head_gains + w_gains[s // 2, s % 2, :, 0:128].astype(F32)
    cosine, sine = cosine_ref[own_first, :], sine_ref[own_first, :]

    def head_back(grads, first, first_gain):
        for h in range(2):
            lane = slice(first + h * 128, first + h * 128 + 128)
            unit_grad = turned(
                grads[:, h * 128 : h * 128 + 128].astype(BF).astype(F32), cosine, -sine
            )
            source = pre[:, lane]
            gain = head_gains[first_gain + h : first_gain + h + 1]
            grad, gain_rows = norm_back(unit_grad, source, rms_scale(source), gain)
            stacked[:, lane] = grad.astype(BF)
            row = first_gain - 2 + h
            heads_row = jnp.sum(gain_rows, axis=0, keepdims=True)
            for s in range(8):
                sums_ref[s // 2, s % 2, row + 2 : row + 3, 0:128] = heads_row
                sums_ref[s // 2, s % 2, row + 2 : row + 3, 128:256] = jnp.zeros_like(heads_row)

    head_back(dq, 0, 2)

    @pl.when(ctx == 0)
    def _():
        earlier.wait_recv()
        dkv[...] += kv_got[...].astype(F32)

    head_back(dkv, 256, 4)
    stacked[:, 512:768] = dkv[:, 256:512].astype(BF)

    def input_rows(rows, target):
        def one_block(s, carry):
            block = w_ref[s // 2, lax.rem(s, 2), :, 0:768]
            part[target, :, at(s * 256, 256)] = dot_nt(stacked[rows, :], block).astype(BF)
            return carry

        lax.fori_loop(0, 8, one_block, 0)

    input_rows(other_rows, 1)
    core_sum = links.send(part.at[1], part_core, dc=1)
    input_rows(own_rows, 0)

    def weight_block(slot):
        attn_grad[slot, :, 0:768] = dot_tn(normed[:, at(slot * 256, 256)], stacked[...]).astype(BF)

    normed_load.wait()
    weight_block(x_far * 2)
    weight_block(x_far * 2 + 1)
    attn_first = [
        links.send(attn_grad.at[x_far * 2], attn_one.at[0], dx=1),
        links.send(attn_grad.at[x_far * 2 + 1], attn_one.at[1], dx=-1),
    ]
    core_sum.wait_recv()
    part[0] = (part[0].astype(F32) + part_core[...].astype(F32)).astype(BF)
    z_sum = [
        links.send(part.at[0, at(lax.rem(z + d + 4, 4) * HOME, HOME)], part_z.at[k], dz=d)
        for k, d in enumerate((1, -1, 2))
    ]

    def other_blocks(i, carry):
        weight_block(lax.rem(x_far * 2 + 2 + i, 8))
        return carry

    lax.fori_loop(0, 6, other_blocks, 0)
    own_load.wait()

    def moe_total(part):
        cols, arrivals = moe_parts[part], []
        arrived(moe_two[part])
        for n, target in enumerate((moe_after, moe_before)):
            links.left(moe_two[part][n])
            arrivals.append(load(moe_in.at[n, :, :, cols], target.at[:, :, cols]))
        for copy in arrivals:
            copy.wait()

        def total(i):
            return (
                moe_own[i, :, cols].astype(F32)
                + moe_after[i, :, cols].astype(F32)
                + moe_before[i, :, cols].astype(F32)
            )

        return total

    def to_groups(source, target):
        copies = [
            links.send(source.at[low_place], target.at[y], dy=d)
            for d, low_place in ((1, 1 - y_low), (-1, 1 - y_low), (2, y_low))
        ]
        return copies, load(source.at[y_low], target.at[y])

    moe_sum = moe_total(0)
    for i in range(2):
        total = moe_sum(i)
        for e in range(4):
            pay_in[i, e] = total[:, e * 256 : e * 256 + 128].astype(BF)
            pay_in[i, 4 + e] = total[:, e * 256 + 128 : e * 256 + 256].astype(BF)
        pay_in[i, 8] = total[:, 1024:1152].astype(BF)
    groups, place_in_groups = to_groups(pay_in, groups_in)
    arrived(layer_near)
    place_layer.wait()
    siblings = [links.send(layer_all.at[c], layer_all.at[c], dc=1)]

    arrived(z_sum)
    normed_grad = part[0, at(z * HOME, HOME), :].astype(F32)
    for k in range(3):
        normed_grad = normed_grad + part_z[k].astype(F32)
    gains = jnp.concatenate(
        [w_gains[s // 2, s % 2].astype(F32)[0:1] for s in range(8)], axis=1
    )
    input_back, gain_rows = norm_back(
        normed_grad, home_tok[...].astype(F32), home_scale_ref[:, 0:1], gains
    )
    home_in[...] = (hidden_grad_ref[...] + input_back).astype(BF)
    gain_row = jnp.sum(gain_rows, axis=0, keepdims=True)
    for s in range(8):
        columns = slice(s * 256, s * 256 + 256)
        sums_ref[s // 2, s % 2, 0:1, :] = gain_row[:, columns]
        sums_ref[s // 2, s % 2, 1:2, :] = gain_ref[0:1, columns]
        sums_ref[s // 2, s % 2, 6:16, :] = jnp.zeros((10, 256), F32)
    place_in = load(home_in, input_all.at[c, z])
    input_near = spread_home(links, input_all, home_in)
    sum_x = [
        links.send(sums_ref.at[lax.rem(x + d + 4, 4)], sums_x.at[k], dx=d)
        for k, d in enumerate((1, -1, 2))
    ]

    moe_sum = moe_total(1)
    for i in range(2):
        total = moe_sum(i)
        for e in range(4):
            pay_out[i, e] = total[:, e * 128 : e * 128 + 128].T.astype(BF)
    out_groups, place_out_groups = to_groups(pay_out, groups_out)

    arrived(attn_first)
    slot = x_after * 2
    attn_grad[slot] = (attn_grad[slot].astype(F32) + attn_one[0].astype(F32)).astype(BF)
    attn_next = [links.send(pair_of(attn_grad, x_after), attn_two.at[0], dx=1)]
    slot = x_before * 2 + 1
    attn_grad[slot] = (attn_grad[slot].astype(F32) + attn_one[1].astype(F32)).astype(BF)
    attn_next.append(links.send(pair_of(attn_grad, x_before), attn_two.at[1], dx=-1))

    arrived(input_near)
    place_in.wait()
    siblings.append(links.send(input_all.at[c], input_all.at[c], dc=1))

    arrived(sum_x)
    pair_ref[...] = sums_ref[x] + sums_x[0] + sums_x[1] + sums_x[2]
    sum_y = [
        links.send(pair_ref.at[low_place], sums_y.at[k], dy=d)
        for k, (d, low_place) in enumerate(((1, 1 - y_low), (-1, 1 - y_low), (2, y_low)))
    ]
    arrived(groups)
    place_in_groups.wait()
    get_routed = load(groups_in.at[:, 8], routed)
    arrived(sum_y)
    summed = pair_ref[y_low] + sums_y[0] + sums_y[1] + sums_y[2]
    heads_out[...] = jnp.concatenate([summed[2:6, 0:128], jnp.zeros((4, 128), F32)], axis=0)
    get_routed.wait()
    small_ref[0:256] = (
        routed[0].astype(F32) + routed[1].astype(F32) + routed[2].astype(F32) + routed[3].astype(F32)
    )
    small_ref[256:SMALL] = jnp.concatenate(
        [summed[0:2, 0:128], summed[0:2, 128:256], jnp.zeros((4, 128), F32)], axis=0
    )
    small_sums = [
        links.send(small_ref, small_z.at[k], dz=d) for k, d in enumerate((1, -1, 2))
    ]

    arrived(attn_next)
    def attn_total(low_place):
        slot = x * 2 + low_place
        return (
            attn_grad[slot].astype(F32)
            + attn_two[0, low_place].astype(F32)
            + attn_two[1, low_place].astype(F32)
        )

    attn_give[...] = attn_total(1 - y_low).astype(BF)
    top, bottom = pl.ds(0, 128), pl.ds(128, 128)
    y_first = [
        links.send(attn_give.at[top], attn_y_one.at[top], dy=1),
        links.send(attn_give.at[bottom], attn_y_one.at[bottom], dy=-1),
    ]
    kept = attn_total(y_low)
    arrived(small_sums)
    small_ref_total = small_ref[...] + small_z[0] + small_z[1] + small_z[2]
    small_out[...] = small_ref_total
    small_core = links.send(small_out, small_c, dc=1)
    arrived(y_first)
    attn_keep[...] = (kept + attn_y_one[...].astype(F32)).astype(BF)
    y_second = links.send(attn_keep, attn_y_two, dy=2)
    small_core.wait()
    small_out[...] = small_ref_total + small_c[...]
    arrived(siblings + out_groups)
    place_out_groups.wait()
    y_second.wait_recv()
    for n, target in enumerate((grad_q, grad_k, grad_v, grad_o)):
        columns = slice(n * 256, n * 256 + 256)
        target[...] = attn_keep[:, columns].astype(F32) + attn_y_two[:, columns].astype(F32)

    for copy in links.made:
        if copy is not earlier and copy is not small_core:
            copy.wait_send()

    @pl.when(ctx == 1)
    def _():
        earlier.wait_send()


BACK_COPIES = 4 + 1 + 1 + 3 + 2 + 3 + 3 + 6 + 2 + 3 + 2 + 3 + 3 + 1 + 3


def run_back(hbm, vmem):
    shape = jax.ShapeDtypeStruct
    outs = (
        (shape((2, 4, HOME, WIDTH), BF), ANY),
        (shape((2, 4, HOME, WIDTH), BF), ANY),
        (shape((4, 9, 256, 128), BF), ANY),
        (shape((4, 4, 128, 256), BF), ANY),
        (shape((2, 2, 256, MCOLS), BF), ANY),
        (shape((256, 256), F32), VMEM),
        (shape((256, 256), F32), VMEM),
        (shape((256, 256), F32), VMEM),
        (shape((256, 256), F32), VMEM),
        (shape((SMALL, 128), F32), VMEM),
        (shape((8, 128), F32), VMEM),
    )

    def buffer(*dims, kind=BF):
        return pltpu.VMEM(dims, kind)

    return pl.pallas_call(
        back,
        out_shape=[o for o, _ in outs],
        in_specs=[ANY] * len(hbm) + [VMEM] * len(vmem),
        out_specs=[spec for _, spec in outs],
        scratch_shapes=[
            buffer(4, 2, 256, 1024),
            buffer(4, 2, 16, 256),
            buffer(ROWS, WIDTH),
            buffer(ROWS, 256),
            buffer(ROWS, 512),
            buffer(ROWS, 512),
            buffer(ROWS, 512),
            buffer(2, ROWS, 128, kind=F32),
            buffer(ROWS, 512, kind=F32),
            buffer(HOME, WIDTH),
            buffer(ROWS, ROWS, kind=F32),
            buffer(ROWS, 256),
            buffer(ROWS, 256, kind=F32),
            buffer(ROWS, 512, kind=F32),
            buffer(ROWS, 512),
            buffer(ROWS, 512),
            buffer(ROWS, 768),
            buffer(2, 256, MCOLS),
            buffer(2, 256, MCOLS),
            buffer(2, 256, MCOLS),
            buffer(2, 9, 256, 128),
            buffer(2, 4, 128, 256),
            buffer(8, 256, 1024),
            buffer(2, 256, 1024),
            buffer(2, 2, 256, 1024),
            buffer(256, 1024),
            buffer(256, 1024),
            buffer(256, 1024),
            buffer(256, 1024),
            buffer(2, HALF, WIDTH),
            buffer(HALF, WIDTH),
            buffer(3, HOME, WIDTH),
            buffer(HOME, WIDTH),
            buffer(4, 2, 16, 256, kind=F32),
            buffer(3, 2, 16, 256, kind=F32),
            buffer(3, 16, 256, kind=F32),
            buffer(2, 16, 256, kind=F32),
            buffer(SMALL, 128, kind=F32),
            buffer(3, SMALL, 128, kind=F32),
            buffer(SMALL, 128, kind=F32),
            buffer(4, 256, 128),
            pltpu.SemaphoreType.DMA((BACK_COPIES,)),
            pltpu.SemaphoreType.DMA((BACK_COPIES,)),
            pltpu.SemaphoreType.DMA((32,)),
        ],
        compiler_params=pltpu.CompilerParams(
            collective_id=3, has_side_effects=True, vmem_limit_bytes=62 * MIB
        ),
        name="back",
    )(*hbm, *vmem)


def results(
    layer, grad, groups_in, groups_out, grad_q, grad_k, grad_v, grad_o,
    layer_out, grad_out, gate_out, up_out, down_out, q_out, k_out, v_out, o_out,
):
    layer_out[...] = layer[...]
    grad_out[...] = grad[...]
    gate_out[...] = groups_in[0, 0:4].astype(F32)
    up_out[...] = groups_in[0, 4:8].astype(F32)
    down_out[...] = groups_out[0].astype(F32)
    for source, target in ((grad_q, q_out), (grad_k, k_out), (grad_v, v_out), (grad_o, o_out)):
        target[...] = source[...]


def run_results(layer_all, input_all, groups_in, groups_out, *grads):
    shape = jax.ShapeDtypeStruct
    rows = pl.BlockSpec((ROWS // 4, WIDTH), lambda i: (i, 0))
    some = pl.BlockSpec((64, 256), lambda i: (i, 0))
    wide = pl.BlockSpec((4, 256, 128), lambda i: (i, 0, 0))
    return pl.pallas_call(
        results,
        grid=(4,),
        out_shape=[shape((ROWS, WIDTH), BF)] * 2
        + [shape((16, 256, 128), F32)] * 2
        + [shape((16, 128, 256), F32)]
        + [shape((256, 256), F32)] * 4,
        in_specs=[rows] * 2
        + [
            pl.BlockSpec((1, 9, 256, 128), lambda i: (i, 0, 0, 0)),
            pl.BlockSpec((1, 4, 128, 256), lambda i: (i, 0, 0, 0)),
        ]
        + [some] * 4,
        out_specs=[rows] * 2
        + [wide] * 2
        + [pl.BlockSpec((4, 128, 256), lambda i: (i, 0, 0))]
        + [some] * 4,
        compiler_params=pltpu.CompilerParams(vmem_limit_bytes=62 * MIB),
        name="results",
    )(
        layer_all.reshape(ROWS, WIDTH),
        input_all.reshape(ROWS, WIDTH),
        groups_in,
        groups_out,
        *grads,
    )


def turn_tables():
    frequency = ROPE_BASE ** (-(np.arange(0, 128, 2, dtype=np.float64) / 128))
    angles = np.arange(1024, dtype=np.float64)[:, None] * frequency[None, :]
    cosine, sine = np.cos(angles), np.sin(angles)
    return (
        np.concatenate([cosine, cosine], axis=1).astype(np.float32),
        np.concatenate([-sine, sine], axis=1).astype(np.float32),
    )


def body(
    tokens,
    out_grad,
    segments,
    routes,
    query_weight,
    key_weight,
    value_weight,
    out_weight,
    router_weight,
    attn_gain,
    moe_gain,
    query_gain,
    key_gain,
    gate_weight,
    up_weight,
    down_weight,
):
    rows, width = tokens.shape[1], tokens.shape[2]
    experts_count = gate_weight.shape[0]
    shard = lax.axis_index("shard")

    own_grad = out_grad.reshape(rows, width)
    own_tokens = tokens.reshape(rows, width)
    tables = [jnp.asarray(table) for table in turn_tables()]
    (
        weights, others, experts_in, experts_out, grad_all, picked_all, moe_in_all,
        normed, pre, rot, key_value, key_value_far, mixed, lse, hidden, home_scale,
    ) = run_front(
        [
            own_tokens, router_weight.T, jnp.stack([attn_gain, moe_gain]), query_gain, key_gain, *tables,
            segments, routes.reshape(rows, -1).T,
        ],
        [
            query_weight, key_weight, value_weight, out_weight, gate_weight, up_weight, down_weight,
            own_grad,
        ],
    )
    grad_moe, grad_near, hidden_low, hidden_grad, gain_sum, layer_rows = run_experts(
        moe_in_all, grad_all, picked_all, own_grad, experts_in, experts_out, weights, others, hidden
    )
    (
        layer_all, input_all, groups_in, groups_out, _, grad_q, grad_k, grad_v, grad_o, small, heads,
    ) = run_back(
        [
            grad_moe, grad_near, hidden_low.reshape(rows, width), weights, others, mixed, rot, key_value,
            key_value_far, lse, pre, normed, own_tokens,
        ],
        [layer_rows, hidden_grad, home_scale, gain_sum, *tables, segments],
    )
    head_grads = lax.dynamic_slice_in_dim(heads[:4], shard * 16, 16, 1)

    layer_out, input_grad, gate_grad, up_grad, down_grad, grad_q, grad_k, grad_v, grad_o = run_results(
        layer_all, input_all, groups_in, groups_out, grad_q, grad_k, grad_v, grad_o
    )
    return (
        layer_out.reshape(tokens.shape),
        input_grad.reshape(tokens.shape),
        grad_q,
        grad_k,
        grad_v,
        grad_o,
        small[:256, :experts_count],
        small[256::2][:2].reshape(-1),
        small[257::2][:2].reshape(-1),
        head_grads[:2],
        head_grads[2:],
        gate_grad,
        up_grad,
        down_grad,
    )


def solution(mesh):
    return jax.shard_map(
        body,
        mesh=mesh,
        in_specs=(
            P("shard", "ctx", None),
            P("shard", "ctx", None),
            P("shard", None),
            P("shard", "ctx", None),
            P("shard", "tp"),
            P("shard", "tp"),
            P("shard", "tp"),
            P("tp", "shard"),
            P("shard", None),
            P("shard"),
            P("shard"),
            P("tp", "shard"),
            P("tp", "shard"),
            P(None, "shard", "tp"),
            P(None, "shard", "tp"),
            P(None, "tp", "shard"),
        ),
        out_specs=(
            P("shard", "ctx", None),
            P("shard", "ctx", None),
            P("shard", "tp"),
            P("shard", "tp"),
            P("shard", "tp"),
            P("tp", "shard"),
            P("shard", None),
            P("shard"),
            P("shard"),
            P("tp", "shard"),
            P("tp", "shard"),
            P(None, "shard", "tp"),
            P(None, "shard", "tp"),
            P(None, "tp", "shard"),
        ),
        check_vma=False,
    )
```

```python
import jax
import jax.numpy as jnp
import numpy as np
from jax import lax
from jax.experimental import pallas as pl
from jax.experimental.pallas import tpu as pltpu
from jax.sharding import PartitionSpec as P

EPSILON = 1e-05
ROPE_BASE = 10000.0
MASKED_SCORE = -1e30
AXES = ("shard", "ctx", "tp")
BF = jnp.bfloat16
F32 = jnp.float32

def rms_scale(values):
    return lax.rsqrt(jnp.mean(values * values, axis=-1, keepdims=True) + EPSILON)


def norm_back(grad_normed, source, scale_row, gain_row):
    unit_values = source * scale_row
    grad_unit = grad_normed * gain_row
    grad_source = scale_row * (
        grad_unit - unit_values * jnp.mean(grad_unit * unit_values, axis=-1, keepdims=True)
    )
    return (grad_source, grad_normed * unit_values)


def dot(left, right):
    return jnp.dot(left, right, preferred_element_type=F32)


def dot_nt(left, right):
    return lax.dot_general(left, right, (((1,), (1,)), ((), ())), preferred_element_type=F32)


def dot_tn(left, right):
    return lax.dot_general(left, right, (((0,), (0,)), ((), ())), preferred_element_type=F32)


ANY = pl.BlockSpec(memory_space=pl.ANY)
VMEM = pl.BlockSpec(memory_space=pltpu.VMEM)
MIB = 1024 * 1024
ROWS, WIDTH, HOME, HALF = 512, 2048, 64, 256
WROWS = 272


def places():
    shard, ctx, tp = lax.axis_index("shard"), lax.axis_index("ctx"), lax.axis_index("tp")
    return shard // 2, ctx * 2 + shard % 2, tp // 2, tp % 2


def device(x, y, z, c):
    x, y, z, c = lax.rem(x + 4, 4), lax.rem(y + 4, 4), lax.rem(z + 4, 4), lax.rem(c + 2, 2)
    return {"shard": x * 2 + lax.rem(y, 2), "ctx": y // 2, "tp": z * 2 + c}


def at(first, size):
    return pl.ds(pl.multiple_of(first, size), size)


class Links:
    def __init__(self, send_sems, recv_sems):
        self.here = places()
        self.send_sems, self.recv_sems, self.made, self.count = send_sems, recv_sems, [], 0

    def send(self, source, target, dx=0, dy=0, dz=0, dc=0, start=True):
        x, y, z, c = self.here
        number = self.count
        self.count += 1
        copy = pltpu.make_async_remote_copy(
            src_ref=source,
            dst_ref=target,
            send_sem=self.send_sems.at[number],
            recv_sem=self.recv_sems.at[number],
            device_id=device(x + dx, y + dy, z + dz, c + dc),
            device_id_type=pl.DeviceIdType.MESH,
        )
        self.made.append(copy)
        if start:
            copy.start()
        return copy

    def left(self, copy):
        copy.wait_send()
        self.made = [other for other in self.made if other is not copy]

    def finish(self):
        for copy in self.made:
            copy.wait_send()

    def greet(self, steps):
        x, y, z, c = self.here
        barrier = pltpu.get_barrier_semaphore()
        for dx, dy, dz, dc in steps:
            pl.semaphore_signal(
                barrier,
                inc=1,
                device_id=device(x + dx, y + dy, z + dz, c + dc),
                device_id_type=pl.DeviceIdType.MESH,
            )
        pl.semaphore_wait(barrier, len(steps))


STEPS_X = [(1, 0, 0, 0), (-1, 0, 0, 0)]
STEPS_Y = [(0, 1, 0, 0), (0, -1, 0, 0), (0, 2, 0, 0)]
STEPS_Z = [(0, 0, 1, 0), (0, 0, -1, 0), (0, 0, 2, 0)]
STEPS_C = [(0, 0, 0, 1)]


def arrived(copies):
    for copy in copies:
        copy.wait_recv()


def turned(values, cosine, sine):
    return values * cosine + pltpu.roll(values, 64, 1) * sine


class Spread:
    def __init__(self, links, array, home_ref, first, start):
        self.links, self.first, self.second = links, first, "z" if first == "y" else "y"
        rows = pl.ds(start, 32)
        x, y, z, c = links.here
        self.source = home_ref.at[rows]
        if first == "z":
            self.block = lambda one, two: array.at[
                lax.rem(y + two + 4, 4), c, lax.rem(z + one + 4, 4), rows
            ]
            self.blocks = lambda two: array.at[lax.rem(y + two + 4, 4), c, :, rows]
        else:
            self.block = lambda one, two: array.at[
                lax.rem(y + one + 4, 4), c, lax.rem(z + two + 4, 4), rows
            ]
            self.blocks = lambda two: array.at[:, c, lax.rem(z + two + 4, 4), rows]
        self.near, self.siblings = {}, []

    def pass_on(self, one):
        block = self.block(one, 0)
        self.near[one] = {
            d: self.links.send(block, block, **{"d" + self.second: d}) for d in (1, -1)
        }

    def to_sibling(self, two):
        self.siblings.append(self.links.send(self.blocks(two), self.blocks(two), dc=1))

    def begin(self):
        self.coming = {
            -d if d != 2 else 2: self.links.send(
                self.source, self.block(0, 0), **{"d" + self.first: d}
            )
            for d in (1, -1, 2)
        }
        block = self.block(0, 0)
        self.near[0] = {
            d: self.links.send(self.source, block, **{"d" + self.second: d}) for d in (1, -1)
        }

    def neighbours(self):
        for one in (-1, 1):
            self.coming[one].wait_recv()
            self.pass_on(one)

    def opposite(self):
        self.coming[2].wait_recv()
        self.pass_on(2)
        self.to_sibling(0)

    def onward(self):
        self.far = []
        for one, d in ((0, 1), (1, -1), (-1, 1), (2, -1)):
            self.near[one][d].wait_recv()
            block = self.block(one, -d)
            self.far.append(self.links.send(block, block, **{"d" + self.second: d}))

    def rest(self):
        for one, d in ((0, -1), (1, 1), (-1, -1), (2, 1)):
            self.near[one][d].wait_recv()
        self.to_sibling(-1)
        self.to_sibling(1)

    def end(self):
        arrived(self.far)
        self.to_sibling(2)


def spread(links, array, home_ref):
    halves = (Spread(links, array, home_ref, "z", 0), Spread(links, array, home_ref, "y", 32))
    for step in ("begin", "neighbours", "opposite", "onward", "rest", "end"):
        for half in halves:
            getattr(half, step)()
    return halves[0].siblings + halves[1].siblings


class SlotGather:
    def __init__(self, links, array, first, size):
        x, y, z, c = links.here
        self.links, self.array, self.place, self.low = links, array, x, lax.rem(y, 2)
        self.all = pl.ds(first, size)
        self.halves = pl.ds(first, size // 2), pl.ds(first + size // 2, size // 2)
        self.along_y = []

    def part(self, d, rows):
        return self.array.at[lax.rem(self.place + d + 4, 4), self.low, rows]

    def to_pair(self, d):
        for rows, step in zip(self.halves, (1, -1)):
            block = self.part(d, rows)
            self.along_y.append(self.links.send(block, block, dy=step))

    def begin(self):
        block = self.part(0, self.all)
        self.near = {d: self.links.send(block, block, dx=d) for d in (1, -1)}
        self.to_pair(0)

    def onward(self):
        self.far = []
        for rows, d in zip(self.halves, (1, -1)):
            self.near[d].wait_recv()
            block = self.part(-d, rows)
            self.far.append(self.links.send(block, block, dx=d))
            self.to_pair(-d)

    def end(self):
        arrived(self.far)
        self.to_pair(2)


def wide_column(segment_row, first):
    blocks = []
    for n in range(4):
        row = segment_row[:, pl.ds(pl.multiple_of(first + n * 128, 128), 128)].astype(F32)
        block = jnp.broadcast_to(row, (128, 128)).T
        blocks.append(jnp.concatenate([block] * 4, axis=1))
    return jnp.concatenate(blocks, axis=0)


def own_mask(segment_row, first):
    rows_at = lax.broadcasted_iota(jnp.int32, (ROWS, ROWS), 0)
    cols_at = lax.broadcasted_iota(jnp.int32, (ROWS, ROWS), 1)
    same = wide_column(segment_row, first) == segment_row[:, at(first, ROWS)].astype(F32)
    return jnp.where(same & (rows_at >= cols_at), 0.0, MASKED_SCORE)


def earlier_mask(segment_row, first):
    same = wide_column(segment_row, first) == segment_row[:, pl.ds(0, ROWS)].astype(F32)
    return jnp.where(same, 0.0, MASKED_SCORE)


def front(
    tok, router, gain_pair, query_gain, key_gain, cosine_ref, sine_ref, segment_row, routes,
    query_weight, key_weight, value_weight, out_weight, gate, up, down, grad,
    weights_out, others_out, experts_in, experts_out, grad_all, picked_all, moe_in_all,
    normed_out, pre_out, rot_out, kv_out, kv_far, mixed_out, lse_out, hidden_out, home_scale_out,
    weights, others, picked, stage_in, stage_out, biases, accs, totals, part, part_core, part_z, home_ref,
    send_sems, recv_sems, local_sems,
):
    links = Links(send_sems, recv_sems)
    x, y, z, c = links.here
    ctx, y_low = y // 2, lax.rem(y, 2)
    x_after, x_before = lax.rem(x + 1, 4), lax.rem(x + 3, 4)
    y_after, y_before, y_far = lax.rem(y + 1, 4), lax.rem(y + 3, 4), lax.rem(y + 2, 4)
    own = c * HALF
    own_rows = pl.ds(pl.multiple_of(own, HALF), HALF)
    loads = []

    def load(source, target):
        copy = pltpu.make_async_copy(source, target, local_sems.at[len(loads)])
        copy.start()
        loads.append(copy)
        return copy

    slot, other_slot = weights.at[x, y_low], others.at[x, y_low]
    every = pl.ds(0, 256)
    slot_loads = [
        load(array, slot.at[every, pl.ds(n * 256, 256)])
        for n, array in enumerate((query_weight, key_weight, value_weight))
    ]
    other_load = load(out_weight, other_slot.at[:, pl.ds(128, 256)])

    def mine(array, group):
        return array.at[pl.ds(group * 4, 4)]

    def columns(place, low_place):
        return pl.ds(pl.multiple_of(place * 512 + low_place * 256, 256), 256)

    staged = [
        load(mine(gate, y), stage_in.at[:, :, pl.ds(0, 128)]),
        load(mine(up, y), stage_in.at[:, :, pl.ds(128, 128)]),
        load(mine(down, y), stage_out),
    ]
    lanes = lax.broadcasted_iota(jnp.int32, (16, 128), 1)
    rows_of = lax.broadcasted_iota(jnp.int32, (16, 128), 0)
    turned_to = (lanes == (x * 2 + y_low) * 16 + rows_of).astype(BF)
    head_rows = dot(jnp.concatenate([query_gain[...], key_gain[...]], axis=0), turned_to)
    gain_block = jnp.concatenate(
        [
            gain_pair[...].astype(F32),
            jnp.concatenate([head_rows, jnp.zeros((4, 128), F32)], axis=1),
            jnp.zeros((10, 256), F32),
        ],
        axis=0,
    )
    weights[x, y_low, 256:272, 0:256] = gain_block.astype(BF)
    weights[x, y_low, 256:272, 256:768] = jnp.zeros((16, 512), BF)
    others[x, y_low, :, 0:128] = jnp.concatenate(
        [router[...].astype(F32), jnp.zeros((112, 256), F32)], axis=0
    ).T.astype(BF)
    links.greet(STEPS_X + STEPS_Y + STEPS_Z + STEPS_C)
    for copy in slot_loads:
        copy.wait()

    first_rows = pl.ds(0, 144)
    pair = [
        links.send(slot.at[pl.ds(0, 80)], slot.at[pl.ds(0, 80)], dy=1),
        links.send(slot.at[pl.ds(80, 64)], slot.at[pl.ds(80, 64)], dy=-1),
    ]
    most = SlotGather(links, weights, 144, WROWS - 144)
    most.begin()
    other_load.wait()
    behind = SlotGather(links, others, 0, 256)

    def grad_block(dy, dz, first=0, size=HOME):
        start = own + lax.rem(z + dz + 4, 4) * HOME + first
        return grad_all.at[lax.rem(y + dy + 4, 4), pl.ds(pl.multiple_of(start, 32), size)]

    home_rows = pl.ds(pl.multiple_of(own + z * HOME, HOME), HOME)
    grad_near = {
        -d if d != 2 else 2: links.send(grad.at[home_rows], grad_block(0, 0), dy=d)
        for d in (1, -1, 2)
    }
    for copy in staged:
        copy.wait()
    place_staged = [
        load(stage_in, experts_in.at[:, x, y_low]),
        load(stage_out, experts_out.at[:, :, columns(x, y_low)]),
    ]
    arrived(pair)
    both = weights.at[x, :, first_rows]
    near = [links.send(both, both, dx=d) for d in (1, -1)]
    behind.begin()

    expert_rows = lax.broadcasted_iota(jnp.int32, (16, ROWS), 0)
    marked = jnp.zeros((16, ROWS), F32)
    for k in range(8):
        marked = marked + jnp.where(expert_rows == routes[k : k + 1, :], 1.0, 0.0)
    picked[...] = marked.astype(BF)
    place_picked = load(picked, picked_all.at[y])
    most.onward()
    first_row = ctx * ROWS
    own_first = at(first_row, ROWS)
    biases[0] = own_mask(segment_row, first_row)
    biases[1] = earlier_mask(segment_row, first_row)
    far = []
    for n, (d, place) in enumerate(((1, x_before), (-1, x_after))):
        near[n].wait_recv()
        block = weights.at[place, n, first_rows]
        far.append(links.send(block, block, dx=d))
    tokens = tok[...].astype(F32)
    scale_one = rms_scale(tokens)
    most.end()
    grad_next = {}
    for dy in (-1, 1, 2):
        grad_near[dy].wait_recv()
        block = grad_block(dy, 0)
        grad_next[dy] = {d: links.send(block, block, dz=d) for d in (1, -1)}
    behind.onward()

    def expert_block(place, low_place):
        return [
            experts_in.at[:, place, low_place],
            experts_out.at[:, :, columns(place, low_place)],
        ]

    for copy in place_staged:
        copy.wait()
    expert_near = {
        d: [links.send(block, block, dx=d) for block in expert_block(x, y_low)] for d in (1, -1)
    }
    expert_pair = []
    for group, start, step in ((y_after, 0, 1), (y_before, 2, -1)):
        some = pl.ds(group * 4 + start, 2)
        there = pl.ds(start, 2)
        expert_pair += [
            links.send(
                gate.at[some], experts_in.at[there, x, y_low, :, pl.ds(0, 128)], dy=step
            ),
            links.send(
                up.at[some], experts_in.at[there, x, y_low, :, pl.ds(128, 128)], dy=step
            ),
            links.send(down.at[some], experts_out.at[there, :, columns(x, y_low)], dy=step),
        ]
    arrived(most.along_y)
    arrived(far)

    gain_blocks = [weights[s // 2, s % 2, 256:272, 0:256].astype(F32) for s in range(8)]
    gains = jnp.concatenate([block[0:1] for block in gain_blocks], axis=1)
    moe_gains = jnp.concatenate([block[1:2] for block in gain_blocks], axis=1)
    head_gains = sum(block[:, 0:128] for block in gain_blocks)
    normed_out[...] = (tokens * scale_one * gains).astype(BF)

    def project(column):
        block = weights[:, :, 0:256, column * 256 : column * 256 + 256].reshape(WIDTH, 256)
        return jnp.dot(normed_out[...], block, preferred_element_type=F32)

    cosine, sine = cosine_ref[own_first, :], sine_ref[own_first, :]

    def heads(pre, first_gain, base):
        for h in range(2):
            part_h = pre[:, h * 128 : h * 128 + 128]
            unit = part_h * rms_scale(part_h) * head_gains[first_gain + h : first_gain + h + 1]
            rot_out[:, base + h * 128 : base + h * 128 + 128] = turned(unit, cosine, sine).astype(BF)

    key_pre = project(1)
    pre_out[:, 256:512] = key_pre
    heads(key_pre, 4, 256)
    kv_out[:, 0:256] = rot_out[:, 256:512]
    kv_out[:, 256:512] = project(2).astype(BF)
    later = links.send(kv_out, kv_far, dy=2, start=False)

    @pl.when(ctx == 0)
    def _():
        later.start()
        kv_far[...] = jnp.zeros_like(kv_far)

    picked_near = [links.send(picked, picked_all.at[y], dy=d) for d in (1, -1, 2)]
    query_pre = project(0)
    pre_out[:, 0:256] = query_pre
    heads(query_pre, 2, 0)
    score_scale = 128 ** (-0.5)
    for h in range(2):
        lane = slice(h * 128, h * 128 + 128)
        scores = dot_nt(rot_out[:, lane], kv_out[:, lane]) * score_scale + biases[0]
        peak = jnp.max(scores, axis=-1, keepdims=True)
        exponents = jnp.exp(scores - peak)
        lse_out[h] = jnp.broadcast_to(peak, (ROWS, 128))
        totals[h] = jnp.broadcast_to(jnp.sum(exponents, axis=-1, keepdims=True), (ROWS, 128))
        accs[h] = dot(exponents.astype(BF), kv_out[:, 256 + h * 128 : 384 + h * 128])

    behind.end()
    grad_far = []
    for dy in (-1, 1, 2):
        for d, first in ((1, 0), (-1, 32)):
            grad_next[dy][d].wait_recv()
            block = grad_block(dy, -d, first, 32)
            grad_far.append(links.send(block, block, dz=d))
    arrived(expert_near[1])
    expert_far = [links.send(block, block, dx=1) for block in expert_block(x_before, y_low)]
    arrived(expert_pair)
    expert_pair_near = {
        d: [links.send(block, block, dx=d) for block in expert_block(x, 1 - y_low)] for d in (1, -1)
    }
    @pl.when(ctx == 1)
    def _():
        later.wait_recv()
        for h in range(2):
            lane = slice(h * 128, h * 128 + 128)
            scores = dot_nt(rot_out[:, lane], kv_far[:, lane]) * score_scale + biases[1]
            old_peak = lse_out[h][:, 0:1]
            peak = jnp.maximum(old_peak, jnp.max(scores, axis=-1, keepdims=True))
            exponents = jnp.exp(scores - peak)
            old = jnp.exp(old_peak - peak)
            lse_out[h] = jnp.broadcast_to(peak, (ROWS, 128))
            totals[h] = totals[h] * old + jnp.sum(exponents, axis=-1, keepdims=True)
            accs[h] = accs[h] * old + dot(
                exponents.astype(BF), kv_far[:, 256 + h * 128 : 384 + h * 128]
            )

    for h in range(2):
        total = totals[h]
        mixed_out[:, h * 128 : h * 128 + 128] = (accs[h] / total).astype(BF)
        lse_out[h] = lse_out[h] + jnp.log(total)

    quarter = pl.multiple_of(own, HALF)
    arrived(behind.along_y)
    other = pl.multiple_of((1 - c) * HALF, HALF)
    give_rows = mixed_out[pl.ds(other, HALF), :]
    for s in range(8):
        block = others[s // 2, s % 2, :, 128:384]
        part[1, :, s * 256 : s * 256 + 256] = dot(give_rows, block).astype(BF)
    core_sum = links.send(part.at[1], part_core, dc=1)
    keep_rows = mixed_out[pl.ds(quarter, HALF), :]
    for s in range(8):
        block = others[s // 2, s % 2, :, 128:384]
        part[0, :, s * 256 : s * 256 + 256] = dot(keep_rows, block).astype(BF)
    core_sum.wait_recv()
    part[0] = (part[0].astype(F32) + part_core[...].astype(F32)).astype(BF)
    z_sum = []
    for k, d in enumerate((1, -1, 2)):
        there = pl.multiple_of(lax.rem(z + d + 4, 4) * HOME, HOME)
        z_sum.append(links.send(part.at[0, pl.ds(there, HOME)], part_z.at[k], dz=d))

    arrived(grad_far)
    siblings = [
        links.send(grad_all.at[place, own_rows], grad_all.at[place, own_rows], dc=1)
        for place in (y_before, y_after, y_far)
    ]
    arrived(expert_pair_near[-1])
    expert_far += [links.send(block, block, dx=-1) for block in expert_block(x_after, 1 - y_low)]
    arrived(z_sum)
    summed = part[0, pl.ds(pl.multiple_of(z * HOME, HOME), HOME), :].astype(F32)
    for k in range(3):
        summed = summed + part_z[k].astype(F32)
    home_tokens = tok[home_rows, :].astype(F32)
    hidden = home_tokens + summed
    hidden_out[...] = hidden
    home_scale_out[...] = jnp.broadcast_to(rms_scale(home_tokens), (HOME, 128))
    home_ref[...] = (hidden * rms_scale(hidden) * moe_gains).astype(BF)
    place_home = load(home_ref, moe_in_all.at[y, c, z])
    keep_weights = [load(weights, weights_out), load(others, others_out)]
    place_home.wait()

    siblings += spread(links, moe_in_all, home_ref)
    arrived(expert_near[-1] + expert_pair_near[1] + expert_far)
    arrived(picked_near)
    arrived(siblings)
    place_picked.wait()
    for copy in keep_weights:
        copy.wait()

    for copy in links.made:
        if copy is not later:
            copy.wait_send()

    @pl.when(ctx == 0)
    def _():
        later.wait_send()


FRONT_COPIES = 6 + 12 + 12 + 18 + 18 + 3 + 1 + 4 + 38


def run_front(vmem, hbm):
    shape = jax.ShapeDtypeStruct
    outs = (
        (shape((4, 2, WROWS, 768), BF), ANY),
        (shape((4, 2, 256, 384), BF), ANY),
        (shape((4, 4, 2, 256, 256), BF), ANY),
        (shape((4, 128, WIDTH), BF), ANY),
        (shape((4, ROWS, WIDTH), BF), ANY),
        (shape((4, 16, ROWS), BF), ANY),
        (shape((4, 2, 4, HOME, WIDTH), BF), ANY),
        (shape((ROWS, WIDTH), BF), VMEM),
        (shape((ROWS, 512), F32), VMEM),
        (shape((ROWS, 512), BF), VMEM),
        (shape((ROWS, 512), BF), VMEM),
        (shape((ROWS, 512), BF), VMEM),
        (shape((ROWS, 256), BF), VMEM),
        (shape((2, ROWS, 128), F32), VMEM),
        (shape((HOME, WIDTH), F32), VMEM),
        (shape((HOME, 128), F32), VMEM),
    )
    return pl.pallas_call(
        front,
        out_shape=[o for o, _ in outs],
        in_specs=[VMEM] * len(vmem) + [ANY] * len(hbm),
        out_specs=[spec for _, spec in outs],
        scratch_shapes=[
            pltpu.VMEM((4, 2, WROWS, 768), BF),
            pltpu.VMEM((4, 2, 256, 384), BF),
            pltpu.VMEM((16, ROWS), BF),
            pltpu.VMEM((4, 256, 256), BF),
            pltpu.VMEM((4, 128, 256), BF),
            pltpu.VMEM((2, ROWS, ROWS), F32),
            pltpu.VMEM((2, ROWS, 128), F32),
            pltpu.VMEM((2, ROWS, 128), F32),
            pltpu.VMEM((2, HALF, WIDTH), BF),
            pltpu.VMEM((HALF, WIDTH), BF),
            pltpu.VMEM((3, HOME, WIDTH), BF),
            pltpu.VMEM((HOME, WIDTH), BF),
            pltpu.SemaphoreType.DMA((FRONT_COPIES,)),
            pltpu.SemaphoreType.DMA((FRONT_COPIES,)),
            pltpu.SemaphoreType.DMA((16,)),
        ],
        compiler_params=pltpu.CompilerParams(
            collective_id=1, has_side_effects=True, vmem_limit_bytes=56 * MIB
        ),
        name="front",
    )(*vmem, *hbm)


MCOLS = 1664


def scatter_buffers():
    return [
        pltpu.VMEM((2, HALF, WIDTH), BF),
        pltpu.VMEM((2, 2, 32, WIDTH), BF),
        pltpu.VMEM((2, 4, 32, WIDTH), BF),
        pltpu.VMEM((3, 32, WIDTH), BF),
        pltpu.VMEM((4, 2, 16, WIDTH), BF),
        pltpu.VMEM((4, 2, 32, WIDTH), BF),
        pltpu.VMEM((3, 32, WIDTH), BF),
    ]


class TokenSum:
    def __init__(self, links, give, keep, landings, credit):
        self.links, self.give, self.keep, self.credit = links, give, keep, credit
        (
            self.core_in, self.p_one_in, self.p_two_in, self.p_three_in,
            self.q_one_in, self.q_two_in, self.q_three_in,
        ) = landings
        self.core, self.p_one, self.p_two, self.q_one, self.q_two, self.q_three = {}, [], [], {}, {}, []

    def free(self, k):
        if k:
            self.links.left(self.core[k - 1])

    def give_core(self, k):
        if k >= 2:
            pl.semaphore_wait(self.credit, 1)
        self.core[k] = self.links.send(self.give, self.core_in.at[k % 2], dc=1)

    def q_rows(self, d, first=0, size=32):
        place = lax.rem(self.links.here[2] + d + 4, 4)
        return pl.ds(pl.multiple_of(place * HOME + 32 + first, 16), size)

    def add(self, k):
        links, keep = self.links, self.keep
        self.core[k].wait_recv()
        keep[k] = keep[k] + self.core_in[k % 2]
        if k < 2:
            x, y, z, c = links.here
            pl.semaphore_signal(
                self.credit,
                inc=1,
                device_id=device(x, y, z, c + 1),
                device_id_type=pl.DeviceIdType.MESH,
            )
        self.q_one[k] = [
            links.send(keep.at[k, self.q_rows(2, 16 * n, 16)], self.q_one_in.at[k, n], dz=d)
            for n, d in enumerate((1, -1))
        ]
        if k == 0:
            rows = keep.at[0].reshape(4, HOME, WIDTH)
            first = pl.ds(0, 32)
            self.p_one = [
                links.send(rows.at[pl.ds(0, 2), first], self.p_one_in.at[0], dy=1),
                links.send(rows.at[pl.ds(2, 2), first], self.p_one_in.at[1], dy=-1),
            ]

    def p_step(self, k):
        links, keep, n = self.links, self.keep, k - 1
        self.p_one[n].wait_recv()
        for i in range(2):
            row = (2 * n + i) * HOME
            keep[k, row : row + 32] = keep[k, row : row + 32] + self.p_one_in[n, i]
        rows = keep.at[k].reshape(4, HOME, WIDTH)
        self.p_two.append(
            links.send(rows.at[:, pl.ds(0, 32)], self.p_two_in.at[n], dy=(1, -1)[n])
        )

    def second(self, k):
        links, keep = self.links, self.keep
        self.q_two[k] = []
        for n, d in enumerate((1, -1)):
            self.q_one[k][n].wait_recv()
            rows = self.q_rows(d, 16 * n, 16)
            keep[k, rows, :] = keep[k, rows, :] + self.q_one_in[k, n]
            self.q_two[k].append(
                links.send(keep.at[k, self.q_rows(d)], self.q_two_in.at[k, n], dz=d)
            )

    def q_sum(self, k):
        arrived(self.q_two[k])
        part = self.keep[k, self.q_rows(0), :].astype(F32)
        for n in range(2):
            part = part + self.q_two_in[k, n].astype(F32)
        return part

    def third(self, k, buffer):
        buffer[k] = self.q_sum(k).astype(BF)
        self.q_three.append(
            self.links.send(buffer.at[k], self.q_three_in.at[k], dy=(2, 1, -1)[k])
        )

    def p_send(self):
        links, keep = self.links, self.keep
        z = links.here[2]
        arrived(self.p_two)
        for place in range(4):
            row = place * HOME
            keep[3, row : row + 32] = (
                keep[3, row : row + 32].astype(F32)
                + self.p_two_in[0, place].astype(F32)
                + self.p_two_in[1, place].astype(F32)
            ).astype(BF)
        self.p_three = [
            links.send(
                keep.at[3, at(lax.rem(z + d + 4, 4) * HOME, 32)], self.p_three_in.at[n], dz=d
            )
            for n, d in enumerate((1, -1, 2))
        ]

    def home(self):
        z = self.links.here[2]
        second = self.q_sum(3)
        arrived(self.q_three)
        for n in range(3):
            second = second + self.q_three_in[n].astype(F32)
        arrived(self.p_three)
        first = self.keep[3, at(z * HOME, 32), :].astype(F32)
        for n in range(3):
            first = first + self.p_three_in[n].astype(F32)
        return first, second


TOKEN_SUM_COPIES = 4 + 8 + 8 + 2 + 2 + 3 + 3


def spread_home(links, array, home_ref):
    x, y, z, c = links.here
    return [links.send(home_ref, array.at[c, z], dz=d) for d in (1, -1, 2)]


def experts(
    x_all, g_all, picked_all, own_grad, w_in_hbm, w_out_hbm, weights, others, hidden_ref,
    grad_out, grad_near_out, low_all, hidden_grad_out, gain_out, layer_out,
    w_in, w_out, gain_ref, x_ref, g_ref, picked_ref, gates_ref, gate_grad_ref, back_ref, pre_ref,
    gated_ref, give, keep, keep_layer, grad_far, grad_stage, q_buffer, q_layer, home_ref,
    core_in, p_one_in, p_two_in, p_three_in, q_one_in, q_two_in, q_three_in,
    core_layer, p_one_layer, p_two_layer, p_three_layer, q_one_layer, q_two_layer, q_three_layer,
    credits, send_sems, recv_sems, local_sems,
):
    links = Links(send_sems, recv_sems)
    x, y, z, c = links.here
    x_after, x_before, x_far = lax.rem(x + 1, 4), lax.rem(x + 3, 4), lax.rem(x + 2, 4)
    order = (lax.rem(y + 2, 4), lax.rem(y + 1, 4), lax.rem(y + 3, 4), y)
    loads = []

    def load(source, target):
        copy = pltpu.make_async_copy(source, target, local_sems.at[len(loads)])
        copy.start()
        loads.append(copy)
        return copy

    first = [load(g_all.at[order[0]], g_ref.at[0]), load(w_out_hbm, w_out)]
    first += [load(picked_all.at[place], picked_ref.at[k]) for k, place in enumerate(order)]
    first.append(load(others.at[:, :, :, pl.ds(0, 128)], w_in.at[:, :, :, pl.ds(1024, 128)]))
    first.append(load(weights.at[:, :, pl.ds(256, 16), pl.ds(0, 256)], gain_ref))
    first.append(load(x_all.at[order[0]], x_ref.at[0]))
    first += [
        load(w_in_hbm.at[e], w_in.at[:, :, :, pl.ds(e * 256, 256)]) for e in range(4)
    ]
    rest = [
        [
            load(g_all.at[order[k]] if k < 3 else own_grad, g_ref.at[k]),
            load(x_all.at[order[k]], x_ref.at[k]),
        ]
        for k in range(1, 4)
    ]
    links.greet(STEPS_X + STEPS_Y + STEPS_Z + STEPS_C)
    for copy in first[:2]:
        copy.wait()

    sums = TokenSum(
        links, give.at[0], keep,
        (core_in, p_one_in, p_two_in, p_three_in, q_one_in, q_two_in, q_three_in), credits.at[0],
    )
    layer_sums = TokenSum(
        links, give.at[1], keep_layer,
        (
            core_layer, p_one_layer, p_two_layer, p_three_layer, q_one_layer, q_two_layer, q_three_layer,
        ),
        credits.at[1],
    )
    lanes = lax.broadcasted_iota(jnp.int32, (ROWS, 128), 1)
    own_rows = at(c * HALF, HALF)
    other_rows = at((1 - c) * HALF, HALF)

    def in_block(first_column, size):
        return w_in[:, :, :, pl.ds(first_column, size)].reshape(WIDTH, size)

    for k in range(4):
        if k:
            for copy in rest[k - 1]:
                copy.wait()
        back_ref[...] = dot_nt(g_ref[k], w_out[...].reshape(512, WIDTH))
        if k == 0:
            for copy in first[2:]:
                copy.wait()
        logits = dot(x_ref[k], in_block(1024, 128))
        marks = jnp.concatenate([picked_ref[k].astype(F32), jnp.zeros((112, ROWS), F32)], axis=0)
        logits = jnp.where(marks.T > 0.5, logits, MASKED_SCORE)
        exponents = jnp.exp(logits - jnp.max(logits, axis=-1, keepdims=True))
        gates_ref[...] = exponents / jnp.sum(exponents, axis=-1, keepdims=True)
        gate_grad_ref[...] = jnp.zeros_like(gate_grad_ref)

        def two_experts(pair, carry, k=k):
            joined = dot(x_ref[k], in_block(pl.multiple_of(pair * 512, 512), 512))
            for n in range(2):
                one_expert(pair * 2 + n, joined[:, n * 256 : n * 256 + 256])
            return carry

        def one_expert(e, joined, k=k):
            gate_pre, up_pre = joined[:, :128], joined[:, 128:]
            logistic = 1.0 / (1.0 + jnp.exp(-gate_pre))
            silu_gate = gate_pre * logistic
            silu_slope = logistic * (1.0 + gate_pre * (1.0 - logistic))
            act = silu_gate * up_pre
            back = back_ref[:, at(e * 128, 128)]
            mine = lanes == y * 4 + e
            gate = jnp.sum(jnp.where(mine, gates_ref[...], 0.0), axis=-1, keepdims=True)
            term = jnp.sum(act.astype(BF).astype(F32) * back, axis=-1, keepdims=True)
            gate_grad_ref[...] += jnp.where(mine, term, 0.0)
            act_grad = back * gate
            pre_ref[k, :, pl.ds(pl.multiple_of(e * 256, 256), 128)] = (
                act_grad * up_pre * silu_slope
            ).astype(BF)
            pre_ref[k, :, pl.ds(pl.multiple_of(e * 256 + 128, 128), 128)] = (
                act_grad * silu_gate
            ).astype(BF)
            gated_ref[k, :, at(e * 128, 128)] = (act * gate).astype(BF)

        lax.fori_loop(0, 2, two_experts, 0)
        gates, gate_grad = gates_ref[...], gate_grad_ref[...]
        logit_grad = gates * (gate_grad - jnp.sum(gates * gate_grad, axis=-1, keepdims=True))
        pre_ref[k, :, 1024:1152] = logit_grad.astype(BF)

        def back_rows(rows, target, k=k):
            for s in range(0, 4, 2):
                block = w_in[s : s + 2].reshape(1024, 1152)
                target[:, s * 512 : s * 512 + 1024] = dot_nt(pre_ref[k, rows, :], block).astype(BF)

        def layer_rows(rows, target, k=k):
            for s in range(0, WIDTH, 1024):
                block = w_out[:, :, s : s + 1024].reshape(512, 1024)
                target[:, s : s + 1024] = dot(gated_ref[k, rows, :], block).astype(BF)

        sums.free(k)
        back_rows(other_rows, give.at[0])
        sums.give_core(k)
        layer_sums.free(k)
        layer_rows(other_rows, give.at[1])
        layer_sums.give_core(k)
        back_rows(own_rows, keep.at[k])
        layer_rows(own_rows, keep_layer.at[k])
        sums.add(k)
        if k in (1, 2):
            sums.p_step(k)
        layer_sums.add(k)
        if k > 0:
            sums.second(k - 1)
            layer_sums.second(k - 1)
        if k > 1:
            layer_sums.p_step(k - 1)
            sums.third(k - 2, q_buffer)
            layer_sums.third(k - 2, q_layer)
    sums.second(3)
    layer_sums.second(3)
    sums.third(2, q_buffer)
    sums.p_send()
    layer_sums.third(2, q_layer)

    def weight_grad(slot, target):
        columns = at(slot * 256, 256)
        rows = x_ref[:, :, columns].reshape(4 * ROWS, 256)
        target[:, 0:1152] = dot_tn(rows, pre_ref[...].reshape(4 * ROWS, 1152)).astype(BF)
        rows = g_ref[:, :, columns].reshape(4 * ROWS, 256)
        target[:, 1152:MCOLS] = dot_tn(rows, gated_ref[...].reshape(4 * ROWS, 512)).astype(BF)

    def far_slot(i, carry):
        weight_grad(x_far * 2 + i, grad_far.at[i])
        return carry

    lax.fori_loop(0, 2, far_slot, 0)
    layer_sums.p_send()
    near = [
        links.send(grad_far.at[0], grad_near_out.at[0], dx=1),
        links.send(grad_far.at[1], grad_near_out.at[1], dx=-1),
    ]

    moe_gains = jnp.concatenate(
        [gain_ref[s // 2, s % 2].astype(F32)[1:2] for s in range(8)], axis=1
    )
    moe_grad = jnp.concatenate(sums.home(), axis=0)
    hidden = hidden_ref[...]
    home_grad = g_ref[3, at(c * HALF + z * HOME, HOME), :].astype(F32)
    back, gain_rows = norm_back(moe_grad, hidden, rms_scale(hidden), moe_gains)
    hidden_grad = home_grad + back
    hidden_grad_out[...] = hidden_grad
    gain_out[...] = jnp.broadcast_to(jnp.sum(gain_rows, axis=0, keepdims=True), (8, WIDTH))
    home_ref[...] = hidden_grad.astype(BF)
    place_home = load(home_ref, low_all.at[c, z])
    low_near = spread_home(links, low_all, home_ref)

    first_sem = len(loads)

    def stage(i, n):
        slot = lax.rem(x_far * 2 + 2 + 2 * i + n, 8)
        return pltpu.make_async_copy(
            grad_stage.at[n], grad_out.at[slot], local_sems.at[first_sem + n]
        )

    def other_grads(i, carry):
        for n in range(2):

            @pl.when(i > 0)
            def _():
                stage(i - 1, n).wait()

            weight_grad(lax.rem(x_far * 2 + 2 + 2 * i + n, 8), grad_stage.at[n])
            stage(i, n).start()
        return carry

    lax.fori_loop(0, 2, other_grads, 0)
    arrived(low_near)
    place_home.wait()
    sibling = links.send(low_all.at[c], low_all.at[c], dc=1)
    layer_grad = jnp.concatenate(layer_sums.home(), axis=0)
    layer_out[...] = (hidden_ref[...] + layer_grad).astype(BF)
    other_grads(2, 0)
    for n in range(2):
        stage(2, n).wait()
    arrived(near)
    sibling.wait_recv()
    links.finish()


EXPERT_COPIES = 2 * TOKEN_SUM_COPIES + 2 + 3 + 1


def run_experts(moe_in_all, *rest):
    shape = jax.ShapeDtypeStruct
    outs = (
        (shape((8, 256, MCOLS), BF), ANY),
        (shape((2, 256, MCOLS), BF), ANY),
        (shape((2, 4, HOME, WIDTH), BF), ANY),
        (shape((HOME, WIDTH), F32), VMEM),
        (shape((8, WIDTH), F32), VMEM),
        (shape((HOME, WIDTH), BF), VMEM),
    )
    return pl.pallas_call(
        experts,
        out_shape=[o for o, _ in outs],
        in_specs=[ANY] * 8 + [VMEM],
        out_specs=[spec for _, spec in outs],
        scratch_shapes=[
            pltpu.VMEM((4, 2, 256, 1152), BF),
            pltpu.VMEM((4, 128, WIDTH), BF),
            pltpu.VMEM((4, 2, 16, 256), BF),
            pltpu.VMEM((4, ROWS, WIDTH), BF),
            pltpu.VMEM((4, ROWS, WIDTH), BF),
            pltpu.VMEM((4, 16, ROWS), BF),
            pltpu.VMEM((ROWS, 128), F32),
            pltpu.VMEM((ROWS, 128), F32),
            pltpu.VMEM((ROWS, 512), F32),
            pltpu.VMEM((4, ROWS, 1152), BF),
            pltpu.VMEM((4, ROWS, 512), BF),
            pltpu.VMEM((2, HALF, WIDTH), BF),
            pltpu.VMEM((4, HALF, WIDTH), BF),
            pltpu.VMEM((4, HALF, WIDTH), BF),
            pltpu.VMEM((2, 256, MCOLS), BF),
            pltpu.VMEM((2, 256, MCOLS), BF),
            pltpu.VMEM((3, 32, WIDTH), BF),
            pltpu.VMEM((3, 32, WIDTH), BF),
            pltpu.VMEM((HOME, WIDTH), BF),
            *scatter_buffers(),
            *scatter_buffers(),
            pltpu.SemaphoreType.REGULAR((2,)),
            pltpu.SemaphoreType.DMA((EXPERT_COPIES,)),
            pltpu.SemaphoreType.DMA((EXPERT_COPIES,)),
            pltpu.SemaphoreType.DMA((24,)),
        ],
        compiler_params=pltpu.CompilerParams(
            collective_id=2, has_side_effects=True, vmem_limit_bytes=62 * MIB
        ),
        name="experts",
    )(
        moe_in_all.reshape(4, ROWS, WIDTH),
        *rest,
    )


SMALL = 264


def back(
    grad_moe, grad_near, low_hbm, weights, others, mixed_hbm, rot_hbm, kv_hbm, kv_far_hbm, lse_hbm, pre_hbm,
    normed_hbm, tok_hbm,
    layer_ref, hidden_grad_ref, home_scale_ref, gain_ref, cosine_ref, sine_ref, segment_row,
    layer_all, input_all, groups_in, groups_out, moe_in,
    grad_q, grad_k, grad_v, grad_o, small_out, heads_out,
    w_ref, w_gains, low, mixed, rot, kv, kv_far, lse, pre, home_tok,
    bias, mixed_grad, dq, dkv, kv_give, kv_got, stacked,
    moe_after, moe_before, moe_near, pay_in, pay_out,
    attn_grad, attn_one, attn_two, attn_give, attn_keep, attn_y_one, attn_y_two,
    part, part_core, part_z, home_in,
    sums_ref, sums_x, sums_y, pair_ref, small_ref, small_z, small_c, routed,
    send_sems, recv_sems, local_sems,
):
    links = Links(send_sems, recv_sems)
    x, y, z, c = links.here
    ctx, y_low = y // 2, lax.rem(y, 2)
    x_after, x_before, x_far = lax.rem(x + 1, 4), lax.rem(x + 3, 4), lax.rem(x + 2, 4)
    own_rows, other_rows = at(c * HALF, HALF), at((1 - c) * HALF, HALF)
    loads = []

    def load(source, target):
        copy = pltpu.make_async_copy(source, target, local_sems.at[len(loads)])
        copy.start()
        loads.append(copy)
        return copy

    def pair_of(array, place):
        return array.at[at(place * 2, 2)]

    near_loads = [
        load(pair_of(grad_moe, x_after), moe_after),
        load(pair_of(grad_moe, x_before), moe_before),
        load(grad_near, moe_near),
    ]
    every = pl.ds(0, 256)
    out_loads = [
        load(low_hbm, low),
        load(others.at[:, :, :, pl.ds(128, 256)], w_ref.at[:, :, :, pl.ds(768, 256)]),
        load(mixed_hbm, mixed),
        load(rot_hbm, rot),
        load(kv_hbm, kv),
        load(kv_far_hbm, kv_far),
        load(lse_hbm, lse),
    ]
    next_loads = [
        load(pre_hbm, pre),
        load(weights.at[:, :, every, pl.ds(0, 768)], w_ref.at[:, :, :, pl.ds(0, 768)]),
        load(weights.at[:, :, pl.ds(256, 16), every], w_gains),
        load(tok_hbm.at[at(c * HALF + z * HOME, HOME)], home_tok),
    ]
    links.greet(STEPS_X + [(2, 0, 0, 0)] + STEPS_Y + STEPS_Z + STEPS_C)

    for copy in near_loads:
        copy.wait()
    moe_after[0] = (moe_after[0].astype(F32) + moe_near[0].astype(F32)).astype(BF)
    moe_before[1] = (moe_before[1].astype(F32) + moe_near[1].astype(F32)).astype(BF)
    moe_parts = pl.ds(0, 1152), pl.ds(1152, 512)
    moe_two = [
        [
            links.send(source.at[:, :, cols], moe_in.at[n, :, :, cols], dx=d)
            for n, (source, d) in enumerate(((moe_after, 1), (moe_before, -1)))
        ]
        for cols in moe_parts
    ]
    moe_own = moe_near
    own_load = load(pair_of(grad_moe, x), moe_own)

    place_layer = load(layer_ref, layer_all.at[c, z])
    layer_near = spread_home(links, layer_all, layer_ref)

    own_first = at(ctx * ROWS, ROWS)
    for copy in out_loads:
        copy.wait()
    total = jnp.zeros((ROWS, 256), F32)
    for s in range(8):
        total = total + dot_nt(low[:, s * 256 : s * 256 + 256], w_ref[s // 2, s % 2, :, 768:1024])
    mixed_grad[...] = total.astype(BF)

    score_scale = 128 ** (-0.5)
    deltas = []
    for h in range(2):
        lane = slice(h * 128, h * 128 + 128)
        deltas.append(
            jnp.sum(
                mixed_grad[:, lane].astype(F32) * mixed[:, lane].astype(F32), axis=-1, keepdims=True
            )
        )

    def scores_back(h, keys_values):
        lane = slice(h * 128, h * 128 + 128)
        keys, values = keys_values[:, lane], keys_values[:, 256 + h * 128 : 384 + h * 128]
        scores = dot_nt(rot[:, lane], keys) * score_scale + bias[...]
        probs = jnp.exp(scores - lse[h][:, 0:1])
        prob_grad = dot_nt(mixed_grad[:, lane], values)
        score_grad = (probs * (prob_grad - deltas[h])).astype(BF)
        query_part = dot(score_grad, keys) * score_scale
        key_part = dot_tn(score_grad, rot[:, lane]) * score_scale
        value_part = dot_tn(probs.astype(BF), mixed_grad[:, lane])
        return query_part, key_part, value_part

    earlier = links.send(kv_give, kv_got, dy=2, start=False)

    @pl.when(ctx == 1)
    def _():
        bias[...] = earlier_mask(segment_row, ctx * ROWS)
        for h in range(2):
            query_part, key_part, value_part = scores_back(h, kv_far)
            dq[:, h * 128 : h * 128 + 128] = query_part
            kv_give[:, h * 128 : h * 128 + 128] = key_part.astype(BF)
            kv_give[:, 256 + h * 128 : 384 + h * 128] = value_part.astype(BF)
        earlier.start()

    @pl.when(ctx == 0)
    def _():
        dq[...] = jnp.zeros_like(dq)

    bias[...] = own_mask(segment_row, ctx * ROWS)
    for h in range(2):
        query_part, key_part, value_part = scores_back(h, kv)
        dq[:, h * 128 : h * 128 + 128] += query_part
        dkv[:, h * 128 : h * 128 + 128] = key_part
        dkv[:, 256 + h * 128 : 384 + h * 128] = value_part

    def out_grad_block(s, carry):
        attn_grad[s, :, 0:256] = dot_tn(mixed[...], low[:, at(s * 256, 256)]).astype(BF)
        return carry

    lax.fori_loop(0, 8, out_grad_block, 0)
    normed = low
    normed_load = load(normed_hbm, normed)
    for copy in next_loads:
        copy.wait()
    head_gains = jnp.zeros((16, 128), F32)
    for s in range(8):
        head_gains = head_gains + w_gains[s // 2, s % 2, :, 0:128].astype(F32)
    cosine, sine = cosine_ref[own_first, :], sine_ref[own_first, :]

    def head_back(grads, first, first_gain):
        for h in range(2):
            lane = slice(first + h * 128, first + h * 128 + 128)
            unit_grad = turned(
                grads[:, h * 128 : h * 128 + 128].astype(BF).astype(F32), cosine, -sine
            )
            source = pre[:, lane]
            gain = head_gains[first_gain + h : first_gain + h + 1]
            grad, gain_rows = norm_back(unit_grad, source, rms_scale(source), gain)
            stacked[:, lane] = grad.astype(BF)
            row = first_gain - 2 + h
            heads_row = jnp.sum(gain_rows, axis=0, keepdims=True)
            for s in range(8):
                sums_ref[s // 2, s % 2, row + 2 : row + 3, 0:128] = heads_row
                sums_ref[s // 2, s % 2, row + 2 : row + 3, 128:256] = jnp.zeros_like(heads_row)

    head_back(dq, 0, 2)
    normed_load.wait()

    def query_block(s, carry):
        attn_grad[s, :, 256:512] = dot_tn(normed[:, at(s * 256, 256)], stacked[:, 0:256]).astype(BF)
        return carry

    lax.fori_loop(0, 8, query_block, 0)
    attn_parts = pl.ds(0, 512), pl.ds(512, 512)

    def attn_begin(part):
        cols = attn_parts[part]
        return [
            links.send(attn_grad.at[x_far * 2, :, cols], attn_one.at[0, :, cols], dx=1),
            links.send(attn_grad.at[x_far * 2 + 1, :, cols], attn_one.at[1, :, cols], dx=-1),
        ]

    attn_first = [attn_begin(0)]

    @pl.when(ctx == 0)
    def _():
        earlier.wait_recv()
        dkv[...] += kv_got[...].astype(F32)

    head_back(dkv, 256, 4)
    stacked[:, 512:768] = dkv[:, 256:512].astype(BF)

    def input_rows(rows, target):
        def one_block(s, carry):
            block = w_ref[s // 2, lax.rem(s, 2), :, 0:768]
            part[target, :, at(s * 256, 256)] = dot_nt(stacked[rows, :], block).astype(BF)
            return carry

        lax.fori_loop(0, 8, one_block, 0)

    input_rows(other_rows, 1)
    core_sum = links.send(part.at[1], part_core, dc=1)
    input_rows(own_rows, 0)

    def weight_block(slot):
        attn_grad[slot, :, 512:1024] = dot_tn(
            normed[:, at(slot * 256, 256)], stacked[:, 256:768]
        ).astype(BF)

    weight_block(x_far * 2)
    weight_block(x_far * 2 + 1)
    attn_first.append(attn_begin(1))
    core_sum.wait_recv()
    part[0] = (part[0].astype(F32) + part_core[...].astype(F32)).astype(BF)
    z_sum = [
        links.send(part.at[0, at(lax.rem(z + d + 4, 4) * HOME, HOME)], part_z.at[k], dz=d)
        for k, d in enumerate((1, -1, 2))
    ]

    def other_blocks(i, carry):
        weight_block(lax.rem(x_far * 2 + 2 + i, 8))
        return carry

    lax.fori_loop(0, 6, other_blocks, 0)
    own_load.wait()

    def moe_total(part):
        cols, arrivals = moe_parts[part], []
        arrived(moe_two[part])
        for n, target in enumerate((moe_after, moe_before)):
            links.left(moe_two[part][n])
            arrivals.append(load(moe_in.at[n, :, :, cols], target.at[:, :, cols]))
        for copy in arrivals:
            copy.wait()

        def total(i):
            return (
                moe_own[i, :, cols].astype(F32)
                + moe_after[i, :, cols].astype(F32)
                + moe_before[i, :, cols].astype(F32)
            )

        return total

    def to_groups(source, target):
        copies = [
            links.send(source.at[low_place], target.at[y], dy=d)
            for d, low_place in ((1, 1 - y_low), (-1, 1 - y_low), (2, y_low))
        ]
        return copies, load(source.at[y_low], target.at[y])

    moe_sum = moe_total(0)
    for i in range(2):
        total = moe_sum(i)
        for e in range(4):
            pay_in[i, e] = total[:, e * 256 : e * 256 + 128].astype(BF)
            pay_in[i, 4 + e] = total[:, e * 256 + 128 : e * 256 + 256].astype(BF)
        pay_in[i, 8] = total[:, 1024:1152].astype(BF)
    groups, place_in_groups = to_groups(pay_in, groups_in)
    arrived(layer_near)
    place_layer.wait()
    siblings = [links.send(layer_all.at[c], layer_all.at[c], dc=1)]

    arrived(z_sum)
    normed_grad = part[0, at(z * HOME, HOME), :].astype(F32)
    for k in range(3):
        normed_grad = normed_grad + part_z[k].astype(F32)
    gains = jnp.concatenate(
        [w_gains[s // 2, s % 2].astype(F32)[0:1] for s in range(8)], axis=1
    )
    input_back, gain_rows = norm_back(
        normed_grad, home_tok[...].astype(F32), home_scale_ref[:, 0:1], gains
    )
    home_in[...] = (hidden_grad_ref[...] + input_back).astype(BF)
    gain_row = jnp.sum(gain_rows, axis=0, keepdims=True)
    for s in range(8):
        columns = slice(s * 256, s * 256 + 256)
        sums_ref[s // 2, s % 2, 0:1, :] = gain_row[:, columns]
        sums_ref[s // 2, s % 2, 1:2, :] = gain_ref[0:1, columns]
        sums_ref[s // 2, s % 2, 6:16, :] = jnp.zeros((10, 256), F32)
    place_in = load(home_in, input_all.at[c, z])
    input_near = spread_home(links, input_all, home_in)
    sum_x = [
        links.send(sums_ref.at[lax.rem(x + d + 4, 4)], sums_x.at[k], dx=d)
        for k, d in enumerate((1, -1, 2))
    ]

    moe_sum = moe_total(1)
    for i in range(2):
        total = moe_sum(i)
        for e in range(4):
            pay_out[i, e] = total[:, e * 128 : e * 128 + 128].T.astype(BF)
    out_groups, place_out_groups = to_groups(pay_out, groups_out)

    def attn_onward(part):
        cols = attn_parts[part]
        arrived(attn_first[part])
        copies = []
        for n, (place, d) in enumerate(((x_after, 1), (x_before, -1))):
            slot = place * 2 + n
            attn_grad[slot, :, cols] = (
                attn_grad[slot, :, cols].astype(F32) + attn_one[n, :, cols].astype(F32)
            ).astype(BF)
            copies.append(
                links.send(
                    attn_grad.at[at(place * 2, 2), :, cols], attn_two.at[n, :, :, cols], dx=d
                )
            )
        return copies

    attn_next = [attn_onward(0), attn_onward(1)]

    arrived(input_near)
    place_in.wait()
    siblings.append(links.send(input_all.at[c], input_all.at[c], dc=1))

    arrived(sum_x)
    pair_ref[...] = sums_ref[x] + sums_x[0] + sums_x[1] + sums_x[2]
    sum_y = [
        links.send(pair_ref.at[low_place], sums_y.at[k], dy=d)
        for k, (d, low_place) in enumerate(((1, 1 - y_low), (-1, 1 - y_low), (2, y_low)))
    ]
    arrived(groups)
    place_in_groups.wait()
    get_routed = load(groups_in.at[:, 8], routed)
    arrived(sum_y)
    summed = pair_ref[y_low] + sums_y[0] + sums_y[1] + sums_y[2]
    heads_out[...] = jnp.concatenate([summed[2:6, 0:128], jnp.zeros((4, 128), F32)], axis=0)
    get_routed.wait()
    small_ref[0:256] = (
        routed[0].astype(F32) + routed[1].astype(F32) + routed[2].astype(F32) + routed[3].astype(F32)
    )
    small_ref[256:SMALL] = jnp.concatenate(
        [summed[0:2, 0:128], summed[0:2, 128:256], jnp.zeros((4, 128), F32)], axis=0
    )
    small_sums = [
        links.send(small_ref, small_z.at[k], dz=d) for k, d in enumerate((1, -1, 2))
    ]

    top, bottom = pl.ds(0, 128), pl.ds(128, 128)

    def attn_total(low_place, cols):
        slot = x * 2 + low_place
        return (
            attn_grad[slot, :, cols].astype(F32)
            + attn_two[0, low_place, :, cols].astype(F32)
            + attn_two[1, low_place, :, cols].astype(F32)
        )

    def attn_to_pair(part):
        cols = attn_parts[part]
        arrived(attn_next[part])
        attn_give[:, cols] = attn_total(1 - y_low, cols).astype(BF)
        return [
            links.send(attn_give.at[rows, cols], attn_y_one.at[rows, cols], dy=d)
            for rows, d in ((top, 1), (bottom, -1))
        ]

    def attn_to_far(part, copies):
        cols = attn_parts[part]
        kept = attn_total(y_low, cols)
        arrived(copies)
        attn_keep[:, cols] = (kept + attn_y_one[:, cols].astype(F32)).astype(BF)
        return links.send(attn_keep.at[:, cols], attn_y_two.at[:, cols], dy=2)

    to_pair = attn_to_pair(0)
    arrived(small_sums)
    small_ref_total = small_ref[...] + small_z[0] + small_z[1] + small_z[2]
    small_out[...] = small_ref_total
    small_core = links.send(small_out, small_c, dc=1)
    to_far = [attn_to_far(0, to_pair)]
    to_pair = attn_to_pair(1)
    small_core.wait()
    small_out[...] = small_ref_total + small_c[...]
    to_far.append(attn_to_far(1, to_pair))
    arrived(siblings + out_groups)
    place_out_groups.wait()
    arrived(to_far)
    for n, target in enumerate((grad_o, grad_q, grad_k, grad_v)):
        columns = slice(n * 256, n * 256 + 256)
        target[...] = attn_keep[:, columns].astype(F32) + attn_y_two[:, columns].astype(F32)

    for copy in links.made:
        if copy is not earlier and copy is not small_core:
            copy.wait_send()

    @pl.when(ctx == 1)
    def _():
        earlier.wait_send()


BACK_COPIES = 7 + 4 + 1 + 1 + 3 + 2 + 3 + 3 + 6 + 2 + 3 + 2 + 3 + 3 + 1 + 3


def run_back(hbm, vmem):
    shape = jax.ShapeDtypeStruct
    outs = (
        (shape((2, 4, HOME, WIDTH), BF), ANY),
        (shape((2, 4, HOME, WIDTH), BF), ANY),
        (shape((4, 9, 256, 128), BF), ANY),
        (shape((4, 4, 128, 256), BF), ANY),
        (shape((2, 2, 256, MCOLS), BF), ANY),
        (shape((256, 256), F32), VMEM),
        (shape((256, 256), F32), VMEM),
        (shape((256, 256), F32), VMEM),
        (shape((256, 256), F32), VMEM),
        (shape((SMALL, 128), F32), VMEM),
        (shape((8, 128), F32), VMEM),
    )

    def buffer(*dims, kind=BF):
        return pltpu.VMEM(dims, kind)

    return pl.pallas_call(
        back,
        out_shape=[o for o, _ in outs],
        in_specs=[ANY] * len(hbm) + [VMEM] * len(vmem),
        out_specs=[spec for _, spec in outs],
        scratch_shapes=[
            buffer(4, 2, 256, 1024),
            buffer(4, 2, 16, 256),
            buffer(ROWS, WIDTH),
            buffer(ROWS, 256),
            buffer(ROWS, 512),
            buffer(ROWS, 512),
            buffer(ROWS, 512),
            buffer(2, ROWS, 128, kind=F32),
            buffer(ROWS, 512, kind=F32),
            buffer(HOME, WIDTH),
            buffer(ROWS, ROWS, kind=F32),
            buffer(ROWS, 256),
            buffer(ROWS, 256, kind=F32),
            buffer(ROWS, 512, kind=F32),
            buffer(ROWS, 512),
            buffer(ROWS, 512),
            buffer(ROWS, 768),
            buffer(2, 256, MCOLS),
            buffer(2, 256, MCOLS),
            buffer(2, 256, MCOLS),
            buffer(2, 9, 256, 128),
            buffer(2, 4, 128, 256),
            buffer(8, 256, 1024),
            buffer(2, 256, 1024),
            buffer(2, 2, 256, 1024),
            buffer(256, 1024),
            buffer(256, 1024),
            buffer(256, 1024),
            buffer(256, 1024),
            buffer(2, HALF, WIDTH),
            buffer(HALF, WIDTH),
            buffer(3, HOME, WIDTH),
            buffer(HOME, WIDTH),
            buffer(4, 2, 16, 256, kind=F32),
            buffer(3, 2, 16, 256, kind=F32),
            buffer(3, 16, 256, kind=F32),
            buffer(2, 16, 256, kind=F32),
            buffer(SMALL, 128, kind=F32),
            buffer(3, SMALL, 128, kind=F32),
            buffer(SMALL, 128, kind=F32),
            buffer(4, 256, 128),
            pltpu.SemaphoreType.DMA((BACK_COPIES,)),
            pltpu.SemaphoreType.DMA((BACK_COPIES,)),
            pltpu.SemaphoreType.DMA((32,)),
        ],
        compiler_params=pltpu.CompilerParams(
            collective_id=3, has_side_effects=True, vmem_limit_bytes=62 * MIB
        ),
        name="back",
    )(*hbm, *vmem)


def results(
    layer, grad, groups_in, groups_out, grad_q, grad_k, grad_v, grad_o,
    layer_out, grad_out, gate_out, up_out, down_out, q_out, k_out, v_out, o_out,
):
    layer_out[...] = layer[...]
    grad_out[...] = grad[...]
    gate_out[...] = groups_in[0, 0:4].astype(F32)
    up_out[...] = groups_in[0, 4:8].astype(F32)
    down_out[...] = groups_out[0].astype(F32)
    for source, target in ((grad_q, q_out), (grad_k, k_out), (grad_v, v_out), (grad_o, o_out)):
        target[...] = source[...]


def run_results(layer_all, input_all, groups_in, groups_out, *grads):
    shape = jax.ShapeDtypeStruct
    rows = pl.BlockSpec((ROWS // 4, WIDTH), lambda i: (i, 0))
    some = pl.BlockSpec((64, 256), lambda i: (i, 0))
    wide = pl.BlockSpec((4, 256, 128), lambda i: (i, 0, 0))
    return pl.pallas_call(
        results,
        grid=(4,),
        out_shape=[shape((ROWS, WIDTH), BF)] * 2
        + [shape((16, 256, 128), F32)] * 2
        + [shape((16, 128, 256), F32)]
        + [shape((256, 256), F32)] * 4,
        in_specs=[rows] * 2
        + [
            pl.BlockSpec((1, 9, 256, 128), lambda i: (i, 0, 0, 0)),
            pl.BlockSpec((1, 4, 128, 256), lambda i: (i, 0, 0, 0)),
        ]
        + [some] * 4,
        out_specs=[rows] * 2
        + [wide] * 2
        + [pl.BlockSpec((4, 128, 256), lambda i: (i, 0, 0))]
        + [some] * 4,
        compiler_params=pltpu.CompilerParams(vmem_limit_bytes=62 * MIB),
        name="results",
    )(
        layer_all.reshape(ROWS, WIDTH),
        input_all.reshape(ROWS, WIDTH),
        groups_in,
        groups_out,
        *grads,
    )


def turn_tables():
    frequency = ROPE_BASE ** (-(np.arange(0, 128, 2, dtype=np.float64) / 128))
    angles = np.arange(1024, dtype=np.float64)[:, None] * frequency[None, :]
    cosine, sine = np.cos(angles), np.sin(angles)
    return (
        np.concatenate([cosine, cosine], axis=1).astype(np.float32),
        np.concatenate([-sine, sine], axis=1).astype(np.float32),
    )


def body(
    tokens,
    out_grad,
    segments,
    routes,
    query_weight,
    key_weight,
    value_weight,
    out_weight,
    router_weight,
    attn_gain,
    moe_gain,
    query_gain,
    key_gain,
    gate_weight,
    up_weight,
    down_weight,
):
    rows, width = tokens.shape[1], tokens.shape[2]
    experts_count = gate_weight.shape[0]
    shard = lax.axis_index("shard")

    own_grad = out_grad.reshape(rows, width)
    own_tokens = tokens.reshape(rows, width)
    tables = [jnp.asarray(table) for table in turn_tables()]
    (
        weights, others, experts_in, experts_out, grad_all, picked_all, moe_in_all,
        normed, pre, rot, key_value, key_value_far, mixed, lse, hidden, home_scale,
    ) = run_front(
        [
            own_tokens, router_weight.T, jnp.stack([attn_gain, moe_gain]), query_gain, key_gain, *tables,
            segments, routes.reshape(rows, -1).T,
        ],
        [
            query_weight, key_weight, value_weight, out_weight, gate_weight, up_weight, down_weight,
            own_grad,
        ],
    )
    grad_moe, grad_near, hidden_low, hidden_grad, gain_sum, layer_rows = run_experts(
        moe_in_all, grad_all, picked_all, own_grad, experts_in, experts_out, weights, others, hidden
    )
    (
        layer_all, input_all, groups_in, groups_out, _, grad_q, grad_k, grad_v, grad_o, small, heads,
    ) = run_back(
        [
            grad_moe, grad_near, hidden_low.reshape(rows, width), weights, others, mixed, rot, key_value,
            key_value_far, lse, pre, normed, own_tokens,
        ],
        [layer_rows, hidden_grad, home_scale, gain_sum, *tables, segments],
    )
    head_grads = lax.dynamic_slice_in_dim(heads[:4], shard * 16, 16, 1)

    layer_out, input_grad, gate_grad, up_grad, down_grad, grad_q, grad_k, grad_v, grad_o = run_results(
        layer_all, input_all, groups_in, groups_out, grad_q, grad_k, grad_v, grad_o
    )
    return (
        layer_out.reshape(tokens.shape),
        input_grad.reshape(tokens.shape),
        grad_q,
        grad_k,
        grad_v,
        grad_o,
        small[:256, :experts_count],
        small[256::2][:2].reshape(-1),
        small[257::2][:2].reshape(-1),
        head_grads[:2],
        head_grads[2:],
        gate_grad,
        up_grad,
        down_grad,
    )


def solution(mesh):
    return jax.shard_map(
        body,
        mesh=mesh,
        in_specs=(
            P("shard", "ctx", None),
            P("shard", "ctx", None),
            P("shard", None),
            P("shard", "ctx", None),
            P("shard", "tp"),
            P("shard", "tp"),
            P("shard", "tp"),
            P("tp", "shard"),
            P("shard", None),
            P("shard"),
            P("shard"),
            P("tp", "shard"),
            P("tp", "shard"),
            P(None, "shard", "tp"),
            P(None, "shard", "tp"),
            P(None, "tp", "shard"),
        ),
        out_specs=(
            P("shard", "ctx", None),
            P("shard", "ctx", None),
            P("shard", "tp"),
            P("shard", "tp"),
            P("shard", "tp"),
            P("tp", "shard"),
            P("shard", None),
            P("shard"),
            P("shard"),
            P("tp", "shard"),
            P("tp", "shard"),
            P(None, "shard", "tp"),
            P(None, "shard", "tp"),
            P(None, "tp", "shard"),
        ),
        check_vma=False,
    )
```

```python
import jax
import jax.numpy as jnp
import numpy as np
from jax import lax
from jax.experimental import pallas as pl
from jax.experimental.pallas import tpu as pltpu
from jax.sharding import PartitionSpec as P

EPSILON = 1e-05
ROPE_BASE = 10000.0
MASKED_SCORE = -1e30
AXES = ("shard", "ctx", "tp")
BF = jnp.bfloat16
F32 = jnp.float32

def rms_scale(values):
    return lax.rsqrt(jnp.mean(values * values, axis=-1, keepdims=True) + EPSILON)


def norm_back(grad_normed, source, scale_row, gain_row):
    unit_values = source * scale_row
    grad_unit = grad_normed * gain_row
    grad_source = scale_row * (
        grad_unit - unit_values * jnp.mean(grad_unit * unit_values, axis=-1, keepdims=True)
    )
    return (grad_source, grad_normed * unit_values)


def dot(left, right):
    return jnp.dot(left, right, preferred_element_type=F32)


def dot_nt(left, right):
    return lax.dot_general(left, right, (((1,), (1,)), ((), ())), preferred_element_type=F32)


def dot_tn(left, right):
    return lax.dot_general(left, right, (((0,), (0,)), ((), ())), preferred_element_type=F32)


ANY = pl.BlockSpec(memory_space=pl.ANY)
VMEM = pl.BlockSpec(memory_space=pltpu.VMEM)
MIB = 1024 * 1024
ROWS, WIDTH, HOME, HALF = 512, 2048, 64, 256
WROWS = 272


def places():
    shard, ctx, tp = lax.axis_index("shard"), lax.axis_index("ctx"), lax.axis_index("tp")
    return shard // 2, ctx * 2 + shard % 2, tp // 2, tp % 2


def device(x, y, z, c):
    x, y, z, c = lax.rem(x + 4, 4), lax.rem(y + 4, 4), lax.rem(z + 4, 4), lax.rem(c + 2, 2)
    return {"shard": x * 2 + lax.rem(y, 2), "ctx": y // 2, "tp": z * 2 + c}


def at(first, size):
    return pl.ds(pl.multiple_of(first, size), size)


class Links:
    def __init__(self, send_sems, recv_sems):
        self.here = places()
        self.send_sems, self.recv_sems, self.made, self.count = send_sems, recv_sems, [], 0

    def send(self, source, target, dx=0, dy=0, dz=0, dc=0, start=True):
        x, y, z, c = self.here
        number = self.count
        self.count += 1
        copy = pltpu.make_async_remote_copy(
            src_ref=source,
            dst_ref=target,
            send_sem=self.send_sems.at[number],
            recv_sem=self.recv_sems.at[number],
            device_id=device(x + dx, y + dy, z + dz, c + dc),
            device_id_type=pl.DeviceIdType.MESH,
        )
        self.made.append(copy)
        if start:
            copy.start()
        return copy

    def left(self, copy):
        copy.wait_send()
        self.made = [other for other in self.made if other is not copy]

    def finish(self):
        for copy in self.made:
            copy.wait_send()

    def greet(self, steps):
        x, y, z, c = self.here
        barrier = pltpu.get_barrier_semaphore()
        for dx, dy, dz, dc in steps:
            pl.semaphore_signal(
                barrier,
                inc=1,
                device_id=device(x + dx, y + dy, z + dz, c + dc),
                device_id_type=pl.DeviceIdType.MESH,
            )
        pl.semaphore_wait(barrier, len(steps))


STEPS_X = [(1, 0, 0, 0), (-1, 0, 0, 0)]
STEPS_Y = [(0, 1, 0, 0), (0, -1, 0, 0), (0, 2, 0, 0)]
STEPS_Z = [(0, 0, 1, 0), (0, 0, -1, 0), (0, 0, 2, 0)]
STEPS_C = [(0, 0, 0, 1)]


def arrived(copies):
    for copy in copies:
        copy.wait_recv()


def turned(values, cosine, sine):
    return values * cosine + pltpu.roll(values, 64, 1) * sine


class Spread:
    def __init__(self, links, array, home_ref, first, start):
        self.links, self.first, self.second = links, first, "z" if first == "y" else "y"
        rows = pl.ds(start, 32)
        x, y, z, c = links.here
        self.source = home_ref.at[rows]
        if first == "z":
            self.block = lambda one, two: array.at[
                lax.rem(y + two + 4, 4), c, lax.rem(z + one + 4, 4), rows
            ]
            self.blocks = lambda two: array.at[lax.rem(y + two + 4, 4), c, :, rows]
        else:
            self.block = lambda one, two: array.at[
                lax.rem(y + one + 4, 4), c, lax.rem(z + two + 4, 4), rows
            ]
            self.blocks = lambda two: array.at[:, c, lax.rem(z + two + 4, 4), rows]
        self.near, self.siblings = {}, []

    def pass_on(self, one):
        block = self.block(one, 0)
        self.near[one] = {
            d: self.links.send(block, block, **{"d" + self.second: d}) for d in (1, -1)
        }

    def to_sibling(self, two):
        self.siblings.append(self.links.send(self.blocks(two), self.blocks(two), dc=1))

    def begin(self):
        self.coming = {
            -d if d != 2 else 2: self.links.send(
                self.source, self.block(0, 0), **{"d" + self.first: d}
            )
            for d in (1, -1, 2)
        }
        block = self.block(0, 0)
        self.near[0] = {
            d: self.links.send(self.source, block, **{"d" + self.second: d}) for d in (1, -1)
        }

    def neighbours(self):
        for one in (-1, 1):
            self.coming[one].wait_recv()
            self.pass_on(one)

    def opposite(self):
        self.coming[2].wait_recv()
        self.pass_on(2)
        self.to_sibling(0)

    def onward(self):
        self.far = []
        for one, d in ((0, 1), (1, -1), (-1, 1), (2, -1)):
            self.near[one][d].wait_recv()
            block = self.block(one, -d)
            self.far.append(self.links.send(block, block, **{"d" + self.second: d}))

    def rest(self):
        for one, d in ((0, -1), (1, 1), (-1, -1), (2, 1)):
            self.near[one][d].wait_recv()
        self.to_sibling(-1)
        self.to_sibling(1)

    def end(self):
        arrived(self.far)
        self.to_sibling(2)


def spread(links, array, home_ref):
    halves = (Spread(links, array, home_ref, "z", 0), Spread(links, array, home_ref, "y", 32))
    for step in ("begin", "neighbours", "opposite", "onward", "rest", "end"):
        for half in halves:
            getattr(half, step)()
    return halves[0].siblings + halves[1].siblings


class SlotGather:
    def __init__(self, links, array, first, size):
        x, y, z, c = links.here
        self.links, self.array, self.place, self.low = links, array, x, lax.rem(y, 2)
        self.all = pl.ds(first, size)
        self.halves = pl.ds(first, size // 2), pl.ds(first + size // 2, size // 2)
        self.along_y = []

    def part(self, d, rows):
        return self.array.at[lax.rem(self.place + d + 4, 4), self.low, rows]

    def to_pair(self, d):
        for rows, step in zip(self.halves, (1, -1)):
            block = self.part(d, rows)
            self.along_y.append(self.links.send(block, block, dy=step))

    def begin(self):
        block = self.part(0, self.all)
        self.near = {d: self.links.send(block, block, dx=d) for d in (1, -1)}
        self.to_pair(0)

    def onward(self):
        self.far = []
        for rows, d in zip(self.halves, (1, -1)):
            self.near[d].wait_recv()
            block = self.part(-d, rows)
            self.far.append(self.links.send(block, block, dx=d))
            self.to_pair(-d)

    def end(self):
        arrived(self.far)
        self.to_pair(2)


def wide_column(segment_row, first):
    blocks = []
    for n in range(4):
        row = segment_row[:, pl.ds(pl.multiple_of(first + n * 128, 128), 128)].astype(F32)
        block = jnp.broadcast_to(row, (128, 128)).T
        blocks.append(jnp.concatenate([block] * 4, axis=1))
    return jnp.concatenate(blocks, axis=0)


def own_mask(segment_row, first):
    rows_at = lax.broadcasted_iota(jnp.int32, (ROWS, ROWS), 0)
    cols_at = lax.broadcasted_iota(jnp.int32, (ROWS, ROWS), 1)
    same = wide_column(segment_row, first) == segment_row[:, at(first, ROWS)].astype(F32)
    return jnp.where(same & (rows_at >= cols_at), 0.0, MASKED_SCORE)


def earlier_mask(segment_row, first):
    same = wide_column(segment_row, first) == segment_row[:, pl.ds(0, ROWS)].astype(F32)
    return jnp.where(same, 0.0, MASKED_SCORE)


def front(
    tok, router, gain_pair, query_gain, key_gain, cosine_ref, sine_ref, segment_row, routes,
    query_weight, key_weight, value_weight, out_weight, gate, up, down, grad,
    weights_out, others_out, experts_in, experts_out, grad_all, picked_all, moe_in_all,
    normed_kept, pre_kept, rot_kept, kv_kept, far_kept, mixed_kept, lse_kept, hidden_out, home_scale_out,
    normed_out, pre_out, rot_out, kv_out, kv_far, mixed_out, lse_out,
    weights, others, picked, stage_in, stage_out, biases, accs, totals, part, part_core, part_z, home_ref,
    send_sems, recv_sems, local_sems,
):
    links = Links(send_sems, recv_sems)
    x, y, z, c = links.here
    ctx, y_low = y // 2, lax.rem(y, 2)
    x_after, x_before = lax.rem(x + 1, 4), lax.rem(x + 3, 4)
    y_after, y_before, y_far = lax.rem(y + 1, 4), lax.rem(y + 3, 4), lax.rem(y + 2, 4)
    own = c * HALF
    own_rows = pl.ds(pl.multiple_of(own, HALF), HALF)
    loads = []

    def load(source, target):
        copy = pltpu.make_async_copy(source, target, local_sems.at[len(loads)])
        copy.start()
        loads.append(copy)
        return copy

    slot, other_slot = weights.at[x, y_low], others.at[x, y_low]
    every = pl.ds(0, 256)
    slot_loads = [
        load(array, slot.at[every, pl.ds(n * 256, 256)])
        for n, array in enumerate((query_weight, key_weight, value_weight))
    ]
    other_load = load(out_weight, other_slot.at[:, pl.ds(128, 256)])

    def mine(array, group):
        return array.at[pl.ds(group * 4, 4)]

    def columns(place, low_place):
        return pl.ds(pl.multiple_of(place * 512 + low_place * 256, 256), 256)

    staged = [
        load(mine(gate, y), stage_in.at[:, :, pl.ds(0, 128)]),
        load(mine(up, y), stage_in.at[:, :, pl.ds(128, 128)]),
        load(mine(down, y), stage_out),
    ]
    lanes = lax.broadcasted_iota(jnp.int32, (16, 128), 1)
    rows_of = lax.broadcasted_iota(jnp.int32, (16, 128), 0)
    turned_to = (lanes == (x * 2 + y_low) * 16 + rows_of).astype(BF)
    head_rows = dot(jnp.concatenate([query_gain[...], key_gain[...]], axis=0), turned_to)
    gain_block = jnp.concatenate(
        [
            gain_pair[...].astype(F32),
            jnp.concatenate([head_rows, jnp.zeros((4, 128), F32)], axis=1),
            jnp.zeros((10, 256), F32),
        ],
        axis=0,
    )
    weights[x, y_low, 256:272, 0:256] = gain_block.astype(BF)
    weights[x, y_low, 256:272, 256:768] = jnp.zeros((16, 512), BF)
    others[x, y_low, :, 0:128] = jnp.concatenate(
        [router[...].astype(F32), jnp.zeros((112, 256), F32)], axis=0
    ).T.astype(BF)
    links.greet(STEPS_X + STEPS_Y + STEPS_Z + STEPS_C)
    for copy in slot_loads:
        copy.wait()

    first_rows = pl.ds(0, 144)
    pair = [
        links.send(slot.at[pl.ds(0, 80)], slot.at[pl.ds(0, 80)], dy=1),
        links.send(slot.at[pl.ds(80, 64)], slot.at[pl.ds(80, 64)], dy=-1),
    ]
    most = SlotGather(links, weights, 144, WROWS - 144)
    most.begin()
    other_load.wait()
    behind = SlotGather(links, others, 0, 256)

    def grad_block(dy, dz, first=0, size=HOME):
        start = own + lax.rem(z + dz + 4, 4) * HOME + first
        return grad_all.at[lax.rem(y + dy + 4, 4), pl.ds(pl.multiple_of(start, 32), size)]

    home_rows = pl.ds(pl.multiple_of(own + z * HOME, HOME), HOME)
    grad_near = {
        -d if d != 2 else 2: links.send(grad.at[home_rows], grad_block(0, 0), dy=d)
        for d in (1, -1, 2)
    }
    for copy in staged:
        copy.wait()
    place_staged = [
        load(stage_in, experts_in.at[:, x, y_low]),
        load(stage_out, experts_out.at[:, :, columns(x, y_low)]),
    ]
    arrived(pair)
    both = weights.at[x, :, first_rows]
    near = [links.send(both, both, dx=d) for d in (1, -1)]
    behind.begin()

    expert_rows = lax.broadcasted_iota(jnp.int32, (16, ROWS), 0)
    marked = jnp.zeros((16, ROWS), F32)
    for k in range(8):
        marked = marked + jnp.where(expert_rows == routes[k : k + 1, :], 1.0, 0.0)
    picked[...] = marked.astype(BF)
    place_picked = load(picked, picked_all.at[y])
    most.onward()
    first_row = ctx * ROWS
    own_first = at(first_row, ROWS)
    biases[0] = own_mask(segment_row, first_row)
    biases[1] = earlier_mask(segment_row, first_row)
    far = []
    for n, (d, place) in enumerate(((1, x_before), (-1, x_after))):
        near[n].wait_recv()
        block = weights.at[place, n, first_rows]
        far.append(links.send(block, block, dx=d))
    tokens = tok[...].astype(F32)
    scale_one = rms_scale(tokens)
    most.end()
    grad_next = {}
    for dy in (-1, 1, 2):
        grad_near[dy].wait_recv()
        block = grad_block(dy, 0)
        grad_next[dy] = {d: links.send(block, block, dz=d) for d in (1, -1)}
    behind.onward()

    def expert_block(place, low_place):
        return [
            experts_in.at[:, place, low_place],
            experts_out.at[:, :, columns(place, low_place)],
        ]

    for copy in place_staged:
        copy.wait()
    expert_near = {
        d: [links.send(block, block, dx=d) for block in expert_block(x, y_low)] for d in (1, -1)
    }
    expert_pair = []
    for group, start, step in ((y_after, 0, 1), (y_before, 2, -1)):
        some = pl.ds(group * 4 + start, 2)
        there = pl.ds(start, 2)
        expert_pair += [
            links.send(
                gate.at[some], experts_in.at[there, x, y_low, :, pl.ds(0, 128)], dy=step
            ),
            links.send(
                up.at[some], experts_in.at[there, x, y_low, :, pl.ds(128, 128)], dy=step
            ),
            links.send(down.at[some], experts_out.at[there, :, columns(x, y_low)], dy=step),
        ]
    arrived(most.along_y)
    arrived(far)

    gain_blocks = [weights[s // 2, s % 2, 256:272, 0:256].astype(F32) for s in range(8)]
    gains = jnp.concatenate([block[0:1] for block in gain_blocks], axis=1)
    moe_gains = jnp.concatenate([block[1:2] for block in gain_blocks], axis=1)
    head_gains = sum(block[:, 0:128] for block in gain_blocks)
    normed_out[...] = (tokens * scale_one * gains).astype(BF)

    def project(column):
        block = weights[:, :, 0:256, column * 256 : column * 256 + 256].reshape(WIDTH, 256)
        return jnp.dot(normed_out[...], block, preferred_element_type=F32)

    cosine, sine = cosine_ref[own_first, :], sine_ref[own_first, :]

    def heads(pre, first_gain, base):
        for h in range(2):
            part_h = pre[:, h * 128 : h * 128 + 128]
            unit = part_h * rms_scale(part_h) * head_gains[first_gain + h : first_gain + h + 1]
            rot_out[:, base + h * 128 : base + h * 128 + 128] = turned(unit, cosine, sine).astype(BF)

    key_pre = project(1)
    pre_out[:, 256:512] = key_pre
    heads(key_pre, 4, 256)
    kv_out[:, 0:256] = rot_out[:, 256:512]
    kv_out[:, 256:512] = project(2).astype(BF)
    later = links.send(kv_out, kv_far, dy=2, start=False)

    @pl.when(ctx == 0)
    def _():
        later.start()
        kv_far[...] = jnp.zeros_like(kv_far)

    picked_near = [links.send(picked, picked_all.at[y], dy=d) for d in (1, -1, 2)]
    query_pre = project(0)
    pre_out[:, 0:256] = query_pre
    heads(query_pre, 2, 0)
    score_scale = 128 ** (-0.5)
    for h in range(2):
        lane = slice(h * 128, h * 128 + 128)
        scores = dot_nt(rot_out[:, lane], kv_out[:, lane]) * score_scale + biases[0]
        peak = jnp.max(scores, axis=-1, keepdims=True)
        exponents = jnp.exp(scores - peak)
        lse_out[h] = jnp.broadcast_to(peak, (ROWS, 128))
        totals[h] = jnp.broadcast_to(jnp.sum(exponents, axis=-1, keepdims=True), (ROWS, 128))
        accs[h] = dot(exponents.astype(BF), kv_out[:, 256 + h * 128 : 384 + h * 128])

    behind.end()
    grad_far = []
    for dy in (-1, 1, 2):
        for d, first in ((1, 0), (-1, 32)):
            grad_next[dy][d].wait_recv()
            block = grad_block(dy, -d, first, 32)
            grad_far.append(links.send(block, block, dz=d))
    arrived(expert_near[1])
    expert_far = [links.send(block, block, dx=1) for block in expert_block(x_before, y_low)]
    arrived(expert_pair)
    expert_pair_near = {
        d: [links.send(block, block, dx=d) for block in expert_block(x, 1 - y_low)] for d in (1, -1)
    }
    @pl.when(ctx == 1)
    def _():
        later.wait_recv()
        for h in range(2):
            lane = slice(h * 128, h * 128 + 128)
            scores = dot_nt(rot_out[:, lane], kv_far[:, lane]) * score_scale + biases[1]
            old_peak = lse_out[h][:, 0:1]
            peak = jnp.maximum(old_peak, jnp.max(scores, axis=-1, keepdims=True))
            exponents = jnp.exp(scores - peak)
            old = jnp.exp(old_peak - peak)
            lse_out[h] = jnp.broadcast_to(peak, (ROWS, 128))
            totals[h] = totals[h] * old + jnp.sum(exponents, axis=-1, keepdims=True)
            accs[h] = accs[h] * old + dot(
                exponents.astype(BF), kv_far[:, 256 + h * 128 : 384 + h * 128]
            )

    for h in range(2):
        total = totals[h]
        mixed_out[:, h * 128 : h * 128 + 128] = (accs[h] / total).astype(BF)
        lse_out[h] = lse_out[h] + jnp.log(total)

    quarter = pl.multiple_of(own, HALF)
    arrived(behind.along_y)
    other = pl.multiple_of((1 - c) * HALF, HALF)
    give_rows = mixed_out[pl.ds(other, HALF), :]
    for s in range(8):
        block = others[s // 2, s % 2, :, 128:384]
        part[1, :, s * 256 : s * 256 + 256] = dot(give_rows, block).astype(BF)
    core_sum = links.send(part.at[1], part_core, dc=1)
    keep_rows = mixed_out[pl.ds(quarter, HALF), :]
    for s in range(8):
        block = others[s // 2, s % 2, :, 128:384]
        part[0, :, s * 256 : s * 256 + 256] = dot(keep_rows, block).astype(BF)
    core_sum.wait_recv()
    part[0] = (part[0].astype(F32) + part_core[...].astype(F32)).astype(BF)
    z_sum = []
    for k, d in enumerate((1, -1, 2)):
        there = pl.multiple_of(lax.rem(z + d + 4, 4) * HOME, HOME)
        z_sum.append(links.send(part.at[0, pl.ds(there, HOME)], part_z.at[k], dz=d))

    arrived(grad_far)
    siblings = [
        links.send(grad_all.at[place, own_rows], grad_all.at[place, own_rows], dc=1)
        for place in (y_before, y_after, y_far)
    ]
    arrived(expert_pair_near[-1])
    expert_far += [links.send(block, block, dx=-1) for block in expert_block(x_after, 1 - y_low)]
    arrived(z_sum)
    summed = part[0, pl.ds(pl.multiple_of(z * HOME, HOME), HOME), :].astype(F32)
    for k in range(3):
        summed = summed + part_z[k].astype(F32)
    home_tokens = tok[home_rows, :].astype(F32)
    hidden = home_tokens + summed
    hidden_out[...] = hidden
    home_scale_out[...] = jnp.broadcast_to(rms_scale(home_tokens), (HOME, 128))
    home_ref[...] = (hidden * rms_scale(hidden) * moe_gains).astype(BF)
    place_home = load(home_ref, moe_in_all.at[y, c, z])
    keep_weights = [load(weights, weights_out), load(others, others_out)]
    keep_weights += [
        load(source, target)
        for source, target in (
            (normed_out, normed_kept),
            (pre_out, pre_kept),
            (rot_out, rot_kept),
            (kv_out, kv_kept),
            (kv_far, far_kept),
            (mixed_out, mixed_kept),
            (lse_out, lse_kept),
        )
    ]
    place_home.wait()

    siblings += spread(links, moe_in_all, home_ref)
    arrived(expert_near[-1] + expert_pair_near[1] + expert_far)
    arrived(picked_near)
    arrived(siblings)
    place_picked.wait()
    for copy in keep_weights:
        copy.wait()

    for copy in links.made:
        if copy is not later:
            copy.wait_send()

    @pl.when(ctx == 0)
    def _():
        later.wait_send()


FRONT_COPIES = 6 + 12 + 12 + 18 + 18 + 3 + 1 + 4 + 38


def run_front(vmem, hbm):
    shape = jax.ShapeDtypeStruct
    outs = (
        (shape((4, 2, WROWS, 768), BF), ANY),
        (shape((4, 2, 256, 384), BF), ANY),
        (shape((4, 4, 2, 256, 256), BF), ANY),
        (shape((4, 128, WIDTH), BF), ANY),
        (shape((4, ROWS, WIDTH), BF), ANY),
        (shape((4, 16, ROWS), BF), ANY),
        (shape((4, 2, 4, HOME, WIDTH), BF), ANY),
        (shape((ROWS, WIDTH), BF), ANY),
        (shape((ROWS, 512), F32), ANY),
        (shape((ROWS, 512), BF), ANY),
        (shape((ROWS, 512), BF), ANY),
        (shape((ROWS, 512), BF), ANY),
        (shape((ROWS, 256), BF), ANY),
        (shape((2, ROWS, 128), F32), ANY),
        (shape((HOME, WIDTH), F32), VMEM),
        (shape((HOME, 128), F32), VMEM),
    )
    return pl.pallas_call(
        front,
        out_shape=[o for o, _ in outs],
        in_specs=[VMEM] * len(vmem) + [ANY] * len(hbm),
        out_specs=[spec for _, spec in outs],
        scratch_shapes=[
            pltpu.VMEM((ROWS, WIDTH), BF),
            pltpu.VMEM((ROWS, 512), F32),
            pltpu.VMEM((ROWS, 512), BF),
            pltpu.VMEM((ROWS, 512), BF),
            pltpu.VMEM((ROWS, 512), BF),
            pltpu.VMEM((ROWS, 256), BF),
            pltpu.VMEM((2, ROWS, 128), F32),
            pltpu.VMEM((4, 2, WROWS, 768), BF),
            pltpu.VMEM((4, 2, 256, 384), BF),
            pltpu.VMEM((16, ROWS), BF),
            pltpu.VMEM((4, 256, 256), BF),
            pltpu.VMEM((4, 128, 256), BF),
            pltpu.VMEM((2, ROWS, ROWS), F32),
            pltpu.VMEM((2, ROWS, 128), F32),
            pltpu.VMEM((2, ROWS, 128), F32),
            pltpu.VMEM((2, HALF, WIDTH), BF),
            pltpu.VMEM((HALF, WIDTH), BF),
            pltpu.VMEM((3, HOME, WIDTH), BF),
            pltpu.VMEM((HOME, WIDTH), BF),
            pltpu.SemaphoreType.DMA((FRONT_COPIES,)),
            pltpu.SemaphoreType.DMA((FRONT_COPIES,)),
            pltpu.SemaphoreType.DMA((32,)),
        ],
        compiler_params=pltpu.CompilerParams(
            collective_id=1, has_side_effects=True, vmem_limit_bytes=56 * MIB
        ),
        name="front",
    )(*vmem, *hbm)


MCOLS = 1664


def scatter_buffers():
    return [
        pltpu.VMEM((2, HALF, WIDTH), BF),
        pltpu.VMEM((2, 2, 32, WIDTH), BF),
        pltpu.VMEM((2, 4, 32, WIDTH), BF),
        pltpu.VMEM((3, 32, WIDTH), BF),
        pltpu.VMEM((4, 2, 16, WIDTH), BF),
        pltpu.VMEM((4, 2, 32, WIDTH), BF),
        pltpu.VMEM((3, 32, WIDTH), BF),
    ]


class TokenSum:
    def __init__(self, links, give, keep, landings, credit):
        self.links, self.give, self.keep, self.credit = links, give, keep, credit
        (
            self.core_in, self.p_one_in, self.p_two_in, self.p_three_in,
            self.q_one_in, self.q_two_in, self.q_three_in,
        ) = landings
        self.core, self.p_one, self.p_two, self.q_one, self.q_two, self.q_three = {}, [], [], {}, {}, []

    def free(self, k):
        if k:
            self.links.left(self.core[k - 1])

    def give_core(self, k):
        if k >= 2:
            pl.semaphore_wait(self.credit, 1)
        self.core[k] = self.links.send(self.give, self.core_in.at[k % 2], dc=1)

    def q_rows(self, d, first=0, size=32):
        place = lax.rem(self.links.here[2] + d + 4, 4)
        return pl.ds(pl.multiple_of(place * HOME + 32 + first, 16), size)

    def add(self, k):
        links, keep = self.links, self.keep
        self.core[k].wait_recv()
        keep[k] = keep[k] + self.core_in[k % 2]
        if k < 2:
            x, y, z, c = links.here
            pl.semaphore_signal(
                self.credit,
                inc=1,
                device_id=device(x, y, z, c + 1),
                device_id_type=pl.DeviceIdType.MESH,
            )
        self.q_one[k] = [
            links.send(keep.at[k, self.q_rows(2, 16 * n, 16)], self.q_one_in.at[k, n], dz=d)
            for n, d in enumerate((1, -1))
        ]
        if k == 0:
            rows = keep.at[0].reshape(4, HOME, WIDTH)
            first = pl.ds(0, 32)
            self.p_one = [
                links.send(rows.at[pl.ds(0, 2), first], self.p_one_in.at[0], dy=1),
                links.send(rows.at[pl.ds(2, 2), first], self.p_one_in.at[1], dy=-1),
            ]

    def p_step(self, k):
        links, keep, n = self.links, self.keep, k - 1
        self.p_one[n].wait_recv()
        for i in range(2):
            row = (2 * n + i) * HOME
            keep[k, row : row + 32] = keep[k, row : row + 32] + self.p_one_in[n, i]
        rows = keep.at[k].reshape(4, HOME, WIDTH)
        self.p_two.append(
            links.send(rows.at[:, pl.ds(0, 32)], self.p_two_in.at[n], dy=(1, -1)[n])
        )

    def second(self, k):
        links, keep = self.links, self.keep
        self.q_two[k] = []
        for n, d in enumerate((1, -1)):
            self.q_one[k][n].wait_recv()
            rows = self.q_rows(d, 16 * n, 16)
            keep[k, rows, :] = keep[k, rows, :] + self.q_one_in[k, n]
            self.q_two[k].append(
                links.send(keep.at[k, self.q_rows(d)], self.q_two_in.at[k, n], dz=d)
            )

    def q_sum(self, k):
        arrived(self.q_two[k])
        part = self.keep[k, self.q_rows(0), :].astype(F32)
        for n in range(2):
            part = part + self.q_two_in[k, n].astype(F32)
        return part

    def third(self, k, buffer):
        buffer[k] = self.q_sum(k).astype(BF)
        self.q_three.append(
            self.links.send(buffer.at[k], self.q_three_in.at[k], dy=(2, 1, -1)[k])
        )

    def p_send(self):
        links, keep = self.links, self.keep
        z = links.here[2]
        arrived(self.p_two)
        for place in range(4):
            row = place * HOME
            keep[3, row : row + 32] = (
                keep[3, row : row + 32].astype(F32)
                + self.p_two_in[0, place].astype(F32)
                + self.p_two_in[1, place].astype(F32)
            ).astype(BF)
        self.p_three = [
            links.send(
                keep.at[3, at(lax.rem(z + d + 4, 4) * HOME, 32)], self.p_three_in.at[n], dz=d
            )
            for n, d in enumerate((1, -1, 2))
        ]

    def home(self):
        z = self.links.here[2]
        second = self.q_sum(3)
        arrived(self.q_three)
        for n in range(3):
            second = second + self.q_three_in[n].astype(F32)
        arrived(self.p_three)
        first = self.keep[3, at(z * HOME, 32), :].astype(F32)
        for n in range(3):
            first = first + self.p_three_in[n].astype(F32)
        return first, second


TOKEN_SUM_COPIES = 4 + 8 + 8 + 2 + 2 + 3 + 3


def spread_home(links, array, home_ref):
    x, y, z, c = links.here
    return [links.send(home_ref, array.at[c, z], dz=d) for d in (1, -1, 2)]


def experts(
    x_all, g_all, picked_all, own_grad, w_in_hbm, w_out_hbm, weights, others, hidden_ref,
    grad_out, grad_near_out, low_all, hidden_grad_out, gain_out, layer_out,
    w_in, w_out, gain_ref, x_ref, g_ref, picked_ref, gates_ref, gate_grad_ref, back_ref, pre_ref,
    gated_ref, give, keep, keep_layer, grad_far, grad_stage, q_buffer, q_layer, home_ref,
    core_in, p_one_in, p_two_in, p_three_in, q_one_in, q_two_in, q_three_in,
    core_layer, p_one_layer, p_two_layer, p_three_layer, q_one_layer, q_two_layer, q_three_layer,
    credits, send_sems, recv_sems, local_sems,
):
    links = Links(send_sems, recv_sems)
    x, y, z, c = links.here
    x_after, x_before, x_far = lax.rem(x + 1, 4), lax.rem(x + 3, 4), lax.rem(x + 2, 4)
    order = (lax.rem(y + 2, 4), lax.rem(y + 1, 4), lax.rem(y + 3, 4), y)
    loads = []

    def load(source, target):
        copy = pltpu.make_async_copy(source, target, local_sems.at[len(loads)])
        copy.start()
        loads.append(copy)
        return copy

    first = [load(g_all.at[order[0]], g_ref.at[0]), load(w_out_hbm, w_out)]
    first += [load(picked_all.at[place], picked_ref.at[k]) for k, place in enumerate(order)]
    first.append(load(others.at[:, :, :, pl.ds(0, 128)], w_in.at[:, :, :, pl.ds(1024, 128)]))
    first.append(load(weights.at[:, :, pl.ds(256, 16), pl.ds(0, 256)], gain_ref))
    first.append(load(x_all.at[order[0]], x_ref.at[0]))
    first += [
        load(w_in_hbm.at[e], w_in.at[:, :, :, pl.ds(e * 256, 256)]) for e in range(4)
    ]
    rest = [
        [
            load(g_all.at[order[k]] if k < 3 else own_grad, g_ref.at[k]),
            load(x_all.at[order[k]], x_ref.at[k]),
        ]
        for k in range(1, 4)
    ]
    links.greet(STEPS_X + STEPS_Y + STEPS_Z + STEPS_C)
    for copy in first[:2]:
        copy.wait()

    sums = TokenSum(
        links, give.at[0], keep,
        (core_in, p_one_in, p_two_in, p_three_in, q_one_in, q_two_in, q_three_in), credits.at[0],
    )
    layer_sums = TokenSum(
        links, give.at[1], keep_layer,
        (
            core_layer, p_one_layer, p_two_layer, p_three_layer, q_one_layer, q_two_layer, q_three_layer,
        ),
        credits.at[1],
    )
    lanes = lax.broadcasted_iota(jnp.int32, (ROWS, 128), 1)
    own_rows = at(c * HALF, HALF)
    other_rows = at((1 - c) * HALF, HALF)

    def in_block(first_column, size):
        return w_in[:, :, :, pl.ds(first_column, size)].reshape(WIDTH, size)

    for k in range(4):
        if k:
            for copy in rest[k - 1]:
                copy.wait()
        back_ref[...] = dot_nt(g_ref[k], w_out[...].reshape(512, WIDTH))
        if k == 0:
            for copy in first[2:]:
                copy.wait()
        logits = dot(x_ref[k], in_block(1024, 128))
        marks = jnp.concatenate([picked_ref[k].astype(F32), jnp.zeros((112, ROWS), F32)], axis=0)
        logits = jnp.where(marks.T > 0.5, logits, MASKED_SCORE)
        exponents = jnp.exp(logits - jnp.max(logits, axis=-1, keepdims=True))
        gates_ref[...] = exponents / jnp.sum(exponents, axis=-1, keepdims=True)
        gate_grad_ref[...] = jnp.zeros_like(gate_grad_ref)

        def two_experts(pair, carry, k=k):
            joined = dot(x_ref[k], in_block(pl.multiple_of(pair * 512, 512), 512))
            for n in range(2):
                one_expert(pair * 2 + n, joined[:, n * 256 : n * 256 + 256])
            return carry

        def one_expert(e, joined, k=k):
            gate_pre, up_pre = joined[:, :128], joined[:, 128:]
            logistic = 1.0 / (1.0 + jnp.exp(-gate_pre))
            silu_gate = gate_pre * logistic
            silu_slope = logistic * (1.0 + gate_pre * (1.0 - logistic))
            act = silu_gate * up_pre
            back = back_ref[:, at(e * 128, 128)]
            mine = lanes == y * 4 + e
            gate = jnp.sum(jnp.where(mine, gates_ref[...], 0.0), axis=-1, keepdims=True)
            term = jnp.sum(act.astype(BF).astype(F32) * back, axis=-1, keepdims=True)
            gate_grad_ref[...] += jnp.where(mine, term, 0.0)
            act_grad = back * gate
            pre_ref[k, :, pl.ds(pl.multiple_of(e * 256, 256), 128)] = (
                act_grad * up_pre * silu_slope
            ).astype(BF)
            pre_ref[k, :, pl.ds(pl.multiple_of(e * 256 + 128, 128), 128)] = (
                act_grad * silu_gate
            ).astype(BF)
            gated_ref[k, :, at(e * 128, 128)] = (act * gate).astype(BF)

        lax.fori_loop(0, 2, two_experts, 0)
        gates, gate_grad = gates_ref[...], gate_grad_ref[...]
        logit_grad = gates * (gate_grad - jnp.sum(gates * gate_grad, axis=-1, keepdims=True))
        pre_ref[k, :, 1024:1152] = logit_grad.astype(BF)

        def back_rows(rows, target, k=k):
            for s in range(0, 4, 2):
                block = w_in[s : s + 2].reshape(1024, 1152)
                target[:, s * 512 : s * 512 + 1024] = dot_nt(pre_ref[k, rows, :], block).astype(BF)

        def layer_rows(rows, target, k=k):
            for s in range(0, WIDTH, 1024):
                block = w_out[:, :, s : s + 1024].reshape(512, 1024)
                target[:, s : s + 1024] = dot(gated_ref[k, rows, :], block).astype(BF)

        sums.free(k)
        back_rows(other_rows, give.at[0])
        sums.give_core(k)
        layer_sums.free(k)
        layer_rows(other_rows, give.at[1])
        layer_sums.give_core(k)
        back_rows(own_rows, keep.at[k])
        layer_rows(own_rows, keep_layer.at[k])
        sums.add(k)
        if k in (1, 2):
            sums.p_step(k)
        layer_sums.add(k)
        if k > 0:
            sums.second(k - 1)
            layer_sums.second(k - 1)
        if k > 1:
            layer_sums.p_step(k - 1)
            sums.third(k - 2, q_buffer)
            layer_sums.third(k - 2, q_layer)
    sums.second(3)
    layer_sums.second(3)
    sums.third(2, q_buffer)
    sums.p_send()
    layer_sums.third(2, q_layer)

    def weight_grad(slot, target):
        columns = at(slot * 256, 256)
        rows = x_ref[:, :, columns].reshape(4 * ROWS, 256)
        target[:, 0:1152] = dot_tn(rows, pre_ref[...].reshape(4 * ROWS, 1152)).astype(BF)
        rows = g_ref[:, :, columns].reshape(4 * ROWS, 256)
        target[:, 1152:MCOLS] = dot_tn(rows, gated_ref[...].reshape(4 * ROWS, 512)).astype(BF)

    def far_slot(i, carry):
        weight_grad(x_far * 2 + i, grad_far.at[i])
        return carry

    lax.fori_loop(0, 2, far_slot, 0)
    layer_sums.p_send()
    near = [
        links.send(grad_far.at[0], grad_near_out.at[0], dx=1),
        links.send(grad_far.at[1], grad_near_out.at[1], dx=-1),
    ]

    moe_gains = jnp.concatenate(
        [gain_ref[s // 2, s % 2].astype(F32)[1:2] for s in range(8)], axis=1
    )
    moe_grad = jnp.concatenate(sums.home(), axis=0)
    hidden = hidden_ref[...]
    home_grad = g_ref[3, at(c * HALF + z * HOME, HOME), :].astype(F32)
    back, gain_rows = norm_back(moe_grad, hidden, rms_scale(hidden), moe_gains)
    hidden_grad = home_grad + back
    hidden_grad_out[...] = hidden_grad
    gain_out[...] = jnp.broadcast_to(jnp.sum(gain_rows, axis=0, keepdims=True), (8, WIDTH))
    home_ref[...] = hidden_grad.astype(BF)
    place_home = load(home_ref, low_all.at[c, z])
    low_near = spread_home(links, low_all, home_ref)

    first_sem = len(loads)

    def stage(i, n):
        slot = lax.rem(x_far * 2 + 2 + 2 * i + n, 8)
        return pltpu.make_async_copy(
            grad_stage.at[n], grad_out.at[slot], local_sems.at[first_sem + n]
        )

    def other_grads(i, carry):
        for n in range(2):

            @pl.when(i > 0)
            def _():
                stage(i - 1, n).wait()

            weight_grad(lax.rem(x_far * 2 + 2 + 2 * i + n, 8), grad_stage.at[n])
            stage(i, n).start()
        return carry

    lax.fori_loop(0, 2, other_grads, 0)
    arrived(low_near)
    place_home.wait()
    sibling = links.send(low_all.at[c], low_all.at[c], dc=1)
    layer_grad = jnp.concatenate(layer_sums.home(), axis=0)
    layer_out[...] = (hidden_ref[...] + layer_grad).astype(BF)
    other_grads(2, 0)
    for n in range(2):
        stage(2, n).wait()
    arrived(near)
    sibling.wait_recv()
    links.finish()


EXPERT_COPIES = 2 * TOKEN_SUM_COPIES + 2 + 3 + 1


def run_experts(moe_in_all, *rest):
    shape = jax.ShapeDtypeStruct
    outs = (
        (shape((8, 256, MCOLS), BF), ANY),
        (shape((2, 256, MCOLS), BF), ANY),
        (shape((2, 4, HOME, WIDTH), BF), ANY),
        (shape((HOME, WIDTH), F32), VMEM),
        (shape((8, WIDTH), F32), VMEM),
        (shape((HOME, WIDTH), BF), VMEM),
    )
    return pl.pallas_call(
        experts,
        out_shape=[o for o, _ in outs],
        in_specs=[ANY] * 8 + [VMEM],
        out_specs=[spec for _, spec in outs],
        scratch_shapes=[
            pltpu.VMEM((4, 2, 256, 1152), BF),
            pltpu.VMEM((4, 128, WIDTH), BF),
            pltpu.VMEM((4, 2, 16, 256), BF),
            pltpu.VMEM((4, ROWS, WIDTH), BF),
            pltpu.VMEM((4, ROWS, WIDTH), BF),
            pltpu.VMEM((4, 16, ROWS), BF),
            pltpu.VMEM((ROWS, 128), F32),
            pltpu.VMEM((ROWS, 128), F32),
            pltpu.VMEM((ROWS, 512), F32),
            pltpu.VMEM((4, ROWS, 1152), BF),
            pltpu.VMEM((4, ROWS, 512), BF),
            pltpu.VMEM((2, HALF, WIDTH), BF),
            pltpu.VMEM((4, HALF, WIDTH), BF),
            pltpu.VMEM((4, HALF, WIDTH), BF),
            pltpu.VMEM((2, 256, MCOLS), BF),
            pltpu.VMEM((2, 256, MCOLS), BF),
            pltpu.VMEM((3, 32, WIDTH), BF),
            pltpu.VMEM((3, 32, WIDTH), BF),
            pltpu.VMEM((HOME, WIDTH), BF),
            *scatter_buffers(),
            *scatter_buffers(),
            pltpu.SemaphoreType.REGULAR((2,)),
            pltpu.SemaphoreType.DMA((EXPERT_COPIES,)),
            pltpu.SemaphoreType.DMA((EXPERT_COPIES,)),
            pltpu.SemaphoreType.DMA((24,)),
        ],
        compiler_params=pltpu.CompilerParams(
            collective_id=2, has_side_effects=True, vmem_limit_bytes=62 * MIB
        ),
        name="experts",
    )(
        moe_in_all.reshape(4, ROWS, WIDTH),
        *rest,
    )


SMALL = 264


def back(
    grad_moe, grad_near, low_hbm, weights, others, mixed_hbm, rot_hbm, kv_hbm, kv_far_hbm, lse_hbm, pre_hbm,
    normed_hbm, tok_hbm,
    layer_ref, hidden_grad_ref, home_scale_ref, gain_ref, cosine_ref, sine_ref, segment_row,
    layer_all, input_all, groups_in, groups_out, moe_in,
    grad_q, grad_k, grad_v, grad_o, small_out, heads_out,
    w_ref, w_gains, low, mixed, rot, kv, kv_far, lse, pre, home_tok,
    bias, mixed_grad, dq, dkv, kv_give, kv_got, stacked,
    moe_after, moe_before, moe_near, pay_in, pay_out,
    attn_grad, attn_one, attn_two, attn_give, attn_keep, attn_y_one, attn_y_two,
    part, part_core, part_z, home_in,
    sums_ref, sums_x, sums_y, pair_ref, small_ref, small_z, small_c, routed,
    send_sems, recv_sems, local_sems,
):
    links = Links(send_sems, recv_sems)
    x, y, z, c = links.here
    ctx, y_low = y // 2, lax.rem(y, 2)
    x_after, x_before, x_far = lax.rem(x + 1, 4), lax.rem(x + 3, 4), lax.rem(x + 2, 4)
    own_rows, other_rows = at(c * HALF, HALF), at((1 - c) * HALF, HALF)
    loads = []

    def load(source, target):
        copy = pltpu.make_async_copy(source, target, local_sems.at[len(loads)])
        copy.start()
        loads.append(copy)
        return copy

    def pair_of(array, place):
        return array.at[at(place * 2, 2)]

    near_loads = [
        load(pair_of(grad_moe, x_after), moe_after),
        load(pair_of(grad_moe, x_before), moe_before),
        load(grad_near, moe_near),
    ]
    every = pl.ds(0, 256)
    out_loads = [
        load(low_hbm, low),
        load(others.at[:, :, :, pl.ds(128, 256)], w_ref.at[:, :, :, pl.ds(768, 256)]),
        load(mixed_hbm, mixed),
        load(rot_hbm, rot),
        load(kv_hbm, kv),
        load(kv_far_hbm, kv_far),
        load(lse_hbm, lse),
    ]
    next_loads = [
        load(pre_hbm, pre),
        load(weights.at[:, :, every, pl.ds(0, 768)], w_ref.at[:, :, :, pl.ds(0, 768)]),
        load(weights.at[:, :, pl.ds(256, 16), every], w_gains),
        load(tok_hbm.at[at(c * HALF + z * HOME, HOME)], home_tok),
    ]
    links.greet(STEPS_X + [(2, 0, 0, 0)] + STEPS_Y + STEPS_Z + STEPS_C)

    for copy in near_loads:
        copy.wait()
    moe_after[0] = (moe_after[0].astype(F32) + moe_near[0].astype(F32)).astype(BF)
    moe_before[1] = (moe_before[1].astype(F32) + moe_near[1].astype(F32)).astype(BF)
    moe_parts = pl.ds(0, 1152), pl.ds(1152, 512)
    moe_two = [
        [
            links.send(source.at[:, :, cols], moe_in.at[n, :, :, cols], dx=d)
            for n, (source, d) in enumerate(((moe_after, 1), (moe_before, -1)))
        ]
        for cols in moe_parts
    ]
    moe_own = moe_near
    own_load = load(pair_of(grad_moe, x), moe_own)

    place_layer = load(layer_ref, layer_all.at[c, z])
    layer_near = spread_home(links, layer_all, layer_ref)

    own_first = at(ctx * ROWS, ROWS)
    for copy in out_loads:
        copy.wait()
    total = jnp.zeros((ROWS, 256), F32)
    for s in range(8):
        total = total + dot_nt(low[:, s * 256 : s * 256 + 256], w_ref[s // 2, s % 2, :, 768:1024])
    mixed_grad[...] = total.astype(BF)

    score_scale = 128 ** (-0.5)
    deltas = []
    for h in range(2):
        lane = slice(h * 128, h * 128 + 128)
        deltas.append(
            jnp.sum(
                mixed_grad[:, lane].astype(F32) * mixed[:, lane].astype(F32), axis=-1, keepdims=True
            )
        )

    def scores_back(h, keys_values):
        lane = slice(h * 128, h * 128 + 128)
        keys, values = keys_values[:, lane], keys_values[:, 256 + h * 128 : 384 + h * 128]
        scores = dot_nt(rot[:, lane], keys) * score_scale + bias[...]
        probs = jnp.exp(scores - lse[h][:, 0:1])
        prob_grad = dot_nt(mixed_grad[:, lane], values)
        score_grad = (probs * (prob_grad - deltas[h])).astype(BF)
        query_part = dot(score_grad, keys) * score_scale
        key_part = dot_tn(score_grad, rot[:, lane]) * score_scale
        value_part = dot_tn(probs.astype(BF), mixed_grad[:, lane])
        return query_part, key_part, value_part

    earlier = links.send(kv_give, kv_got, dy=2, start=False)

    @pl.when(ctx == 1)
    def _():
        bias[...] = earlier_mask(segment_row, ctx * ROWS)
        for h in range(2):
            query_part, key_part, value_part = scores_back(h, kv_far)
            dq[:, h * 128 : h * 128 + 128] = query_part
            kv_give[:, h * 128 : h * 128 + 128] = key_part.astype(BF)
            kv_give[:, 256 + h * 128 : 384 + h * 128] = value_part.astype(BF)
        earlier.start()

    @pl.when(ctx == 0)
    def _():
        dq[...] = jnp.zeros_like(dq)

    bias[...] = own_mask(segment_row, ctx * ROWS)
    for h in range(2):
        query_part, key_part, value_part = scores_back(h, kv)
        dq[:, h * 128 : h * 128 + 128] += query_part
        dkv[:, h * 128 : h * 128 + 128] = key_part
        dkv[:, 256 + h * 128 : 384 + h * 128] = value_part

    def out_grad_block(s, carry):
        attn_grad[s, :, 0:256] = dot_tn(mixed[...], low[:, at(s * 256, 256)]).astype(BF)
        return carry

    lax.fori_loop(0, 8, out_grad_block, 0)
    normed = low
    normed_load = load(normed_hbm, normed)
    for copy in next_loads:
        copy.wait()
    head_gains = jnp.zeros((16, 128), F32)
    for s in range(8):
        head_gains = head_gains + w_gains[s // 2, s % 2, :, 0:128].astype(F32)
    cosine, sine = cosine_ref[own_first, :], sine_ref[own_first, :]

    def head_back(grads, first, first_gain):
        for h in range(2):
            lane = slice(first + h * 128, first + h * 128 + 128)
            unit_grad = turned(
                grads[:, h * 128 : h * 128 + 128].astype(BF).astype(F32), cosine, -sine
            )
            source = pre[:, lane]
            gain = head_gains[first_gain + h : first_gain + h + 1]
            grad, gain_rows = norm_back(unit_grad, source, rms_scale(source), gain)
            stacked[:, lane] = grad.astype(BF)
            row = first_gain - 2 + h
            heads_row = jnp.sum(gain_rows, axis=0, keepdims=True)
            for s in range(8):
                sums_ref[s // 2, s % 2, row + 2 : row + 3, 0:128] = heads_row
                sums_ref[s // 2, s % 2, row + 2 : row + 3, 128:256] = jnp.zeros_like(heads_row)

    head_back(dq, 0, 2)
    normed_load.wait()

    def query_block(s, carry):
        attn_grad[s, :, 256:512] = dot_tn(normed[:, at(s * 256, 256)], stacked[:, 0:256]).astype(BF)
        return carry

    lax.fori_loop(0, 8, query_block, 0)
    attn_parts = pl.ds(0, 512), pl.ds(512, 512)

    def attn_begin(part):
        cols = attn_parts[part]
        return [
            links.send(attn_grad.at[x_far * 2, :, cols], attn_one.at[0, :, cols], dx=1),
            links.send(attn_grad.at[x_far * 2 + 1, :, cols], attn_one.at[1, :, cols], dx=-1),
        ]

    attn_first = [attn_begin(0)]

    @pl.when(ctx == 0)
    def _():
        earlier.wait_recv()
        dkv[...] += kv_got[...].astype(F32)

    head_back(dkv, 256, 4)
    stacked[:, 512:768] = dkv[:, 256:512].astype(BF)

    def input_rows(rows, target):
        def one_block(s, carry):
            block = w_ref[s // 2, lax.rem(s, 2), :, 0:768]
            part[target, :, at(s * 256, 256)] = dot_nt(stacked[rows, :], block).astype(BF)
            return carry

        lax.fori_loop(0, 8, one_block, 0)

    input_rows(other_rows, 1)
    core_sum = links.send(part.at[1], part_core, dc=1)
    input_rows(own_rows, 0)

    def weight_block(slot):
        attn_grad[slot, :, 512:1024] = dot_tn(
            normed[:, at(slot * 256, 256)], stacked[:, 256:768]
        ).astype(BF)

    weight_block(x_far * 2)
    weight_block(x_far * 2 + 1)
    attn_first.append(attn_begin(1))
    core_sum.wait_recv()
    part[0] = (part[0].astype(F32) + part_core[...].astype(F32)).astype(BF)
    z_sum = [
        links.send(part.at[0, at(lax.rem(z + d + 4, 4) * HOME, HOME)], part_z.at[k], dz=d)
        for k, d in enumerate((1, -1, 2))
    ]

    def other_blocks(i, carry):
        weight_block(lax.rem(x_far * 2 + 2 + i, 8))
        return carry

    lax.fori_loop(0, 6, other_blocks, 0)
    own_load.wait()

    def moe_total(part):
        cols, arrivals = moe_parts[part], []
        arrived(moe_two[part])
        for n, target in enumerate((moe_after, moe_before)):
            links.left(moe_two[part][n])
            arrivals.append(load(moe_in.at[n, :, :, cols], target.at[:, :, cols]))
        for copy in arrivals:
            copy.wait()

        def total(i):
            return (
                moe_own[i, :, cols].astype(F32)
                + moe_after[i, :, cols].astype(F32)
                + moe_before[i, :, cols].astype(F32)
            )

        return total

    def to_groups(source, target):
        copies = [
            links.send(source.at[low_place], target.at[y], dy=d)
            for d, low_place in ((1, 1 - y_low), (-1, 1 - y_low), (2, y_low))
        ]
        return copies, load(source.at[y_low], target.at[y])

    moe_sum = moe_total(0)
    for i in range(2):
        total = moe_sum(i)
        for e in range(4):
            pay_in[i, e] = total[:, e * 256 : e * 256 + 128].astype(BF)
            pay_in[i, 4 + e] = total[:, e * 256 + 128 : e * 256 + 256].astype(BF)
        pay_in[i, 8] = total[:, 1024:1152].astype(BF)
    groups, place_in_groups = to_groups(pay_in, groups_in)
    arrived(layer_near)
    place_layer.wait()
    siblings = [links.send(layer_all.at[c], layer_all.at[c], dc=1)]

    arrived(z_sum)
    normed_grad = part[0, at(z * HOME, HOME), :].astype(F32)
    for k in range(3):
        normed_grad = normed_grad + part_z[k].astype(F32)
    gains = jnp.concatenate(
        [w_gains[s // 2, s % 2].astype(F32)[0:1] for s in range(8)], axis=1
    )
    input_back, gain_rows = norm_back(
        normed_grad, home_tok[...].astype(F32), home_scale_ref[:, 0:1], gains
    )
    home_in[...] = (hidden_grad_ref[...] + input_back).astype(BF)
    gain_row = jnp.sum(gain_rows, axis=0, keepdims=True)
    for s in range(8):
        columns = slice(s * 256, s * 256 + 256)
        sums_ref[s // 2, s % 2, 0:1, :] = gain_row[:, columns]
        sums_ref[s // 2, s % 2, 1:2, :] = gain_ref[0:1, columns]
        sums_ref[s // 2, s % 2, 6:16, :] = jnp.zeros((10, 256), F32)
    place_in = load(home_in, input_all.at[c, z])
    input_near = spread_home(links, input_all, home_in)
    sum_x = [
        links.send(sums_ref.at[lax.rem(x + d + 4, 4)], sums_x.at[k], dx=d)
        for k, d in enumerate((1, -1, 2))
    ]

    moe_sum = moe_total(1)
    for i in range(2):
        total = moe_sum(i)
        for e in range(4):
            pay_out[i, e] = total[:, e * 128 : e * 128 + 128].T.astype(BF)
    out_groups, place_out_groups = to_groups(pay_out, groups_out)

    def attn_onward(part):
        cols = attn_parts[part]
        arrived(attn_first[part])
        copies = []
        for n, (place, d) in enumerate(((x_after, 1), (x_before, -1))):
            slot = place * 2 + n
            attn_grad[slot, :, cols] = (
                attn_grad[slot, :, cols].astype(F32) + attn_one[n, :, cols].astype(F32)
            ).astype(BF)
            copies.append(
                links.send(
                    attn_grad.at[at(place * 2, 2), :, cols], attn_two.at[n, :, :, cols], dx=d
                )
            )
        return copies

    attn_next = [attn_onward(0), attn_onward(1)]

    arrived(input_near)
    place_in.wait()
    siblings.append(links.send(input_all.at[c], input_all.at[c], dc=1))

    arrived(sum_x)
    pair_ref[...] = sums_ref[x] + sums_x[0] + sums_x[1] + sums_x[2]
    sum_y = [
        links.send(pair_ref.at[low_place], sums_y.at[k], dy=d)
        for k, (d, low_place) in enumerate(((1, 1 - y_low), (-1, 1 - y_low), (2, y_low)))
    ]
    arrived(groups)
    place_in_groups.wait()
    get_routed = load(groups_in.at[:, 8], routed)
    arrived(sum_y)
    summed = pair_ref[y_low] + sums_y[0] + sums_y[1] + sums_y[2]
    heads_out[...] = jnp.concatenate([summed[2:6, 0:128], jnp.zeros((4, 128), F32)], axis=0)
    get_routed.wait()
    small_ref[0:256] = (
        routed[0].astype(F32) + routed[1].astype(F32) + routed[2].astype(F32) + routed[3].astype(F32)
    )
    small_ref[256:SMALL] = jnp.concatenate(
        [summed[0:2, 0:128], summed[0:2, 128:256], jnp.zeros((4, 128), F32)], axis=0
    )
    small_sums = [
        links.send(small_ref, small_z.at[k], dz=d) for k, d in enumerate((1, -1, 2))
    ]

    top, bottom = pl.ds(0, 128), pl.ds(128, 128)

    def attn_total(low_place, cols):
        slot = x * 2 + low_place
        return (
            attn_grad[slot, :, cols].astype(F32)
            + attn_two[0, low_place, :, cols].astype(F32)
            + attn_two[1, low_place, :, cols].astype(F32)
        )

    def attn_to_pair(part):
        cols = attn_parts[part]
        arrived(attn_next[part])
        attn_give[:, cols] = attn_total(1 - y_low, cols).astype(BF)
        return [
            links.send(attn_give.at[rows, cols], attn_y_one.at[rows, cols], dy=d)
            for rows, d in ((top, 1), (bottom, -1))
        ]

    def attn_to_far(part, copies):
        cols = attn_parts[part]
        kept = attn_total(y_low, cols)
        arrived(copies)
        attn_keep[:, cols] = (kept + attn_y_one[:, cols].astype(F32)).astype(BF)
        return links.send(attn_keep.at[:, cols], attn_y_two.at[:, cols], dy=2)

    to_pair = attn_to_pair(0)
    arrived(small_sums)
    small_ref_total = small_ref[...] + small_z[0] + small_z[1] + small_z[2]
    small_out[...] = small_ref_total
    small_core = links.send(small_out, small_c, dc=1)
    to_far = [attn_to_far(0, to_pair)]
    to_pair = attn_to_pair(1)
    small_core.wait()
    small_out[...] = small_ref_total + small_c[...]
    to_far.append(attn_to_far(1, to_pair))
    arrived(siblings + out_groups)
    place_out_groups.wait()
    arrived(to_far)
    for n, target in enumerate((grad_o, grad_q, grad_k, grad_v)):
        columns = slice(n * 256, n * 256 + 256)
        target[...] = attn_keep[:, columns].astype(F32) + attn_y_two[:, columns].astype(F32)

    for copy in links.made:
        if copy is not earlier and copy is not small_core:
            copy.wait_send()

    @pl.when(ctx == 1)
    def _():
        earlier.wait_send()


BACK_COPIES = 7 + 4 + 1 + 1 + 3 + 2 + 3 + 3 + 6 + 2 + 3 + 2 + 3 + 3 + 1 + 3


def run_back(hbm, vmem):
    shape = jax.ShapeDtypeStruct
    outs = (
        (shape((2, 4, HOME, WIDTH), BF), ANY),
        (shape((2, 4, HOME, WIDTH), BF), ANY),
        (shape((4, 9, 256, 128), BF), ANY),
        (shape((4, 4, 128, 256), BF), ANY),
        (shape((2, 2, 256, MCOLS), BF), ANY),
        (shape((256, 256), F32), VMEM),
        (shape((256, 256), F32), VMEM),
        (shape((256, 256), F32), VMEM),
        (shape((256, 256), F32), VMEM),
        (shape((SMALL, 128), F32), VMEM),
        (shape((8, 128), F32), VMEM),
    )

    def buffer(*dims, kind=BF):
        return pltpu.VMEM(dims, kind)

    return pl.pallas_call(
        back,
        out_shape=[o for o, _ in outs],
        in_specs=[ANY] * len(hbm) + [VMEM] * len(vmem),
        out_specs=[spec for _, spec in outs],
        scratch_shapes=[
            buffer(4, 2, 256, 1024),
            buffer(4, 2, 16, 256),
            buffer(ROWS, WIDTH),
            buffer(ROWS, 256),
            buffer(ROWS, 512),
            buffer(ROWS, 512),
            buffer(ROWS, 512),
            buffer(2, ROWS, 128, kind=F32),
            buffer(ROWS, 512, kind=F32),
            buffer(HOME, WIDTH),
            buffer(ROWS, ROWS, kind=F32),
            buffer(ROWS, 256),
            buffer(ROWS, 256, kind=F32),
            buffer(ROWS, 512, kind=F32),
            buffer(ROWS, 512),
            buffer(ROWS, 512),
            buffer(ROWS, 768),
            buffer(2, 256, MCOLS),
            buffer(2, 256, MCOLS),
            buffer(2, 256, MCOLS),
            buffer(2, 9, 256, 128),
            buffer(2, 4, 128, 256),
            buffer(8, 256, 1024),
            buffer(2, 256, 1024),
            buffer(2, 2, 256, 1024),
            buffer(256, 1024),
            buffer(256, 1024),
            buffer(256, 1024),
            buffer(256, 1024),
            buffer(2, HALF, WIDTH),
            buffer(HALF, WIDTH),
            buffer(3, HOME, WIDTH),
            buffer(HOME, WIDTH),
            buffer(4, 2, 16, 256, kind=F32),
            buffer(3, 2, 16, 256, kind=F32),
            buffer(3, 16, 256, kind=F32),
            buffer(2, 16, 256, kind=F32),
            buffer(SMALL, 128, kind=F32),
            buffer(3, SMALL, 128, kind=F32),
            buffer(SMALL, 128, kind=F32),
            buffer(4, 256, 128),
            pltpu.SemaphoreType.DMA((BACK_COPIES,)),
            pltpu.SemaphoreType.DMA((BACK_COPIES,)),
            pltpu.SemaphoreType.DMA((32,)),
        ],
        compiler_params=pltpu.CompilerParams(
            collective_id=3, has_side_effects=True, vmem_limit_bytes=62 * MIB
        ),
        name="back",
    )(*hbm, *vmem)


def results(
    layer, grad, groups_in, groups_out, grad_q, grad_k, grad_v, grad_o,
    layer_out, grad_out, gate_out, up_out, down_out, q_out, k_out, v_out, o_out,
):
    layer_out[...] = layer[...]
    grad_out[...] = grad[...]
    gate_out[...] = groups_in[0, 0:4].astype(F32)
    up_out[...] = groups_in[0, 4:8].astype(F32)
    down_out[...] = groups_out[0].astype(F32)
    for source, target in ((grad_q, q_out), (grad_k, k_out), (grad_v, v_out), (grad_o, o_out)):
        target[...] = source[...]


def run_results(layer_all, input_all, groups_in, groups_out, *grads):
    shape = jax.ShapeDtypeStruct
    rows = pl.BlockSpec((ROWS // 4, WIDTH), lambda i: (i, 0))
    some = pl.BlockSpec((64, 256), lambda i: (i, 0))
    wide = pl.BlockSpec((4, 256, 128), lambda i: (i, 0, 0))
    return pl.pallas_call(
        results,
        grid=(4,),
        out_shape=[shape((ROWS, WIDTH), BF)] * 2
        + [shape((16, 256, 128), F32)] * 2
        + [shape((16, 128, 256), F32)]
        + [shape((256, 256), F32)] * 4,
        in_specs=[rows] * 2
        + [
            pl.BlockSpec((1, 9, 256, 128), lambda i: (i, 0, 0, 0)),
            pl.BlockSpec((1, 4, 128, 256), lambda i: (i, 0, 0, 0)),
        ]
        + [some] * 4,
        out_specs=[rows] * 2
        + [wide] * 2
        + [pl.BlockSpec((4, 128, 256), lambda i: (i, 0, 0))]
        + [some] * 4,
        compiler_params=pltpu.CompilerParams(vmem_limit_bytes=62 * MIB),
        name="results",
    )(
        layer_all.reshape(ROWS, WIDTH),
        input_all.reshape(ROWS, WIDTH),
        groups_in,
        groups_out,
        *grads,
    )


def turn_tables():
    frequency = ROPE_BASE ** (-(np.arange(0, 128, 2, dtype=np.float64) / 128))
    angles = np.arange(1024, dtype=np.float64)[:, None] * frequency[None, :]
    cosine, sine = np.cos(angles), np.sin(angles)
    return (
        np.concatenate([cosine, cosine], axis=1).astype(np.float32),
        np.concatenate([-sine, sine], axis=1).astype(np.float32),
    )


def body(
    tokens,
    out_grad,
    segments,
    routes,
    query_weight,
    key_weight,
    value_weight,
    out_weight,
    router_weight,
    attn_gain,
    moe_gain,
    query_gain,
    key_gain,
    gate_weight,
    up_weight,
    down_weight,
):
    rows, width = tokens.shape[1], tokens.shape[2]
    experts_count = gate_weight.shape[0]
    shard = lax.axis_index("shard")

    own_grad = out_grad.reshape(rows, width)
    own_tokens = tokens.reshape(rows, width)
    tables = [jnp.asarray(table) for table in turn_tables()]
    (
        weights, others, experts_in, experts_out, grad_all, picked_all, moe_in_all,
        normed, pre, rot, key_value, key_value_far, mixed, lse, hidden, home_scale,
    ) = run_front(
        [
            own_tokens, router_weight.T, jnp.stack([attn_gain, moe_gain]), query_gain, key_gain, *tables,
            segments, routes.reshape(rows, -1).T,
        ],
        [
            query_weight, key_weight, value_weight, out_weight, gate_weight, up_weight, down_weight,
            own_grad,
        ],
    )
    grad_moe, grad_near, hidden_low, hidden_grad, gain_sum, layer_rows = run_experts(
        moe_in_all, grad_all, picked_all, own_grad, experts_in, experts_out, weights, others, hidden
    )
    (
        layer_all, input_all, groups_in, groups_out, _, grad_q, grad_k, grad_v, grad_o, small, heads,
    ) = run_back(
        [
            grad_moe, grad_near, hidden_low.reshape(rows, width), weights, others, mixed, rot, key_value,
            key_value_far, lse, pre, normed, own_tokens,
        ],
        [layer_rows, hidden_grad, home_scale, gain_sum, *tables, segments],
    )
    head_grads = lax.dynamic_slice_in_dim(heads[:4], shard * 16, 16, 1)

    layer_out, input_grad, gate_grad, up_grad, down_grad, grad_q, grad_k, grad_v, grad_o = run_results(
        layer_all, input_all, groups_in, groups_out, grad_q, grad_k, grad_v, grad_o
    )
    return (
        layer_out.reshape(tokens.shape),
        input_grad.reshape(tokens.shape),
        grad_q,
        grad_k,
        grad_v,
        grad_o,
        small[:256, :experts_count],
        small[256::2][:2].reshape(-1),
        small[257::2][:2].reshape(-1),
        head_grads[:2],
        head_grads[2:],
        gate_grad,
        up_grad,
        down_grad,
    )


def solution(mesh):
    return jax.shard_map(
        body,
        mesh=mesh,
        in_specs=(
            P("shard", "ctx", None),
            P("shard", "ctx", None),
            P("shard", None),
            P("shard", "ctx", None),
            P("shard", "tp"),
            P("shard", "tp"),
            P("shard", "tp"),
            P("tp", "shard"),
            P("shard", None),
            P("shard"),
            P("shard"),
            P("tp", "shard"),
            P("tp", "shard"),
            P(None, "shard", "tp"),
            P(None, "shard", "tp"),
            P(None, "tp", "shard"),
        ),
        out_specs=(
            P("shard", "ctx", None),
            P("shard", "ctx", None),
            P("shard", "tp"),
            P("shard", "tp"),
            P("shard", "tp"),
            P("tp", "shard"),
            P("shard", None),
            P("shard"),
            P("shard"),
            P("tp", "shard"),
            P("tp", "shard"),
            P(None, "shard", "tp"),
            P(None, "shard", "tp"),
            P(None, "tp", "shard"),
        ),
        check_vma=False,
    )
```
